32 devices in a mesh: dp: 16 (over z, y, core), mp: 2 (over x).
Axes of the slice: x: 2, y: 2, z: 4, core: 2. Of those that a mesh axis runs over, the one named last changes fastest.
Arguments:
- patches: bfloat16 [16384, 4096], P('dp', 'mp'), may hold values from -6 to 6
- labels: int32 [32, 4096], P(('dp', 'mp')), may hold values from 0 to 13
- batch_ids: int32 [32], P(('dp', 'mp')), may hold values from 0 to 3
- blocks: float32 [16, 2, 24, 128, 128], P('dp', 'mp'), may hold values from -0.21875 to 0.21875
- statistics: float32 [2, 16, 2, 24, 128, 128], P(None, 'dp', 'mp'), as said below
- roots: float32 [2, 16, 2, 24, 128, 128], P(None, 'dp', 'mp'), as said below
- moments: float32 [16, 2, 24, 128, 128], P('dp', 'mp'), may hold values from -1.9073486e-05 to 1.9073486e-05
- velocity: float32 [16, 2, 24, 128, 128], P('dp', 'mp'), may hold values from 1.9169148e-15 to 7.667659e-15
- aux: float32 [458878], replicated
- aux_moment: float32 [458878], replicated, may hold values from -1.1444092e-05 to 1.1444092e-05
- aux_velocity: float32 [458878], replicated, may hold values from 4.792287e-14 to 1.9169148e-13
Outputs:
- loss: float32 [], replicated
- grad_norm: float32 [], replicated
- new_blocks: float32 [16, 2, 24, 128, 128], P('dp', 'mp')
- new_statistics: float32 [2, 16, 2, 24, 128, 128], P(None, 'dp', 'mp')
- new_moments: float32 [16, 2, 24, 128, 128], P('dp', 'mp')
- new_velocity: float32 [16, 2, 24, 128, 128], P('dp', 'mp')
- new_aux: float32 [458878], replicated
- new_aux_moment: float32 [458878], replicated
- new_aux_velocity: float32 [458878], replicated
The draws below stay inside these ranges and needn't reach their ends.
Inputs may be any that keep to these rules, and one draw needn't show every extreme that they name: `statistics`: symmetric in the last two dimensions. `roots`: symmetric in the last two dimensions, diagonal entries positive.
All inputs are finite; a program needn't handle non-finite values.
Results may differ from the reference program's by a relative error of at most 0.00045.
The reference program's roundings to bfloat16 on the way count: a program that leaves them out, or rounds other values in their place, can miss the bound.
Values may be sent and summed in bfloat16 or wider, within the bound.
A program may use at most 320 MiB of HBM per device.

```python
import math
import jax
import jax.numpy as jnp
from jax import lax

D = 768
HEADS = 12
HDIM = 64
FF = 3072
PV = 4096
DEC = 128
CF = 16
NCLS = 14
GS = 8
MB = 4
STEP = 10
BS = 128
NTOK = 512
CELLS = 4096
CROPS = 32
NBM = 384
KB = 24
NAUX = 458878
NPARAM = 13041790
N_DP = 16
N_MP = 2


def draw_aux(key, part):
    key = jax.random.fold_in(key, 11)
    layout = [(NTOK * D, 0.3, 0.0), (D, 0.3, 0.0), (2 * D, 0.2, 1.0), (2 * D, 0.2, 0.0), (2 * D, 0.3, 0.0), (D, 0.3, 0.0), (FF, 0.3, 0.0), (D, 0.3, 0.0), (DEC, 0.3, 0.0), (27 * DEC * CF, (27 * DEC) ** (-0.5), 0.0), (CF, 0.3, 0.0), (CF * NCLS, CF ** (-0.5), 0.0), (NCLS, 0.3, 0.0)]
    spread = jnp.concatenate([jnp.full((length,), factor, jnp.float32) for length, factor, middle in layout])
    center = jnp.concatenate([jnp.full((length,), middle, jnp.float32) for length, factor, middle in layout])
    sample = jax.random.normal(key, (NAUX,), jnp.float32)
    return center + spread * sample


def draw_statistics(key, part):
    key = jax.random.fold_in(key, 12)
    key_diag, key_off = jax.random.split(key)
    extent = (2, N_DP, N_MP, KB, BS, BS)
    grad_size = 0.005 / NPARAM ** 0.5
    uniform_part = jax.random.uniform(key_diag, extent[:-1], jnp.float32)
    diagonal = jnp.exp(1.3862944 * uniform_part)
    offdiag = jax.random.normal(key_off, extent, jnp.float32)
    symmetric = (offdiag + jnp.swapaxes(offdiag, -1, -2)) * (0.25 * 0.70710678 / BS ** 0.5)
    identity = jnp.eye(BS, dtype=jnp.float32)
    return 0.05 / 0.95 * BS * grad_size * grad_size * (diagonal[..., None] * identity + symmetric)


def draw_roots(key, part):
    key = jax.random.fold_in(key, 13)
    key_diag, key_off = jax.random.split(key)
    extent = (2, N_DP, N_MP, KB, BS, BS)
    grad_size = 0.005 / NPARAM ** 0.5
    uniform_part = jax.random.uniform(key_diag, extent[:-1], jnp.float32)
    diagonal = jnp.exp(-0.6931472 + 1.3862944 * uniform_part)
    offdiag = jax.random.normal(key_off, extent, jnp.float32)
    symmetric = (offdiag + jnp.swapaxes(offdiag, -1, -2)) * (0.1 * 0.70710678 / BS ** 0.5)
    identity = jnp.eye(BS, dtype=jnp.float32)
    return grad_size ** (-0.5) * (diagonal[..., None] * identity + symmetric)


def touch_ends(drawn, own_key, smallest, top_value):
    shape = drawn.shape
    place = [jax.random.randint(jax.random.fold_in(own_key, axis), (), 0, shape[axis]) for axis in range(len(shape))]
    drawn = drawn.at[tuple(place)].set(smallest)
    longest = shape.index(max(shape))
    place[longest] = (place[longest] + 1) % shape[longest]
    return drawn.at[tuple(place)].set(top_value)


def shard_levels(own_key, dims, shards, low, high):
    level, own = 1.0, jax.random.fold_in(own_key, 6)
    for axis_at, shards_of in shards:
        steps = jnp.exp(jax.random.uniform(jax.random.fold_in(own, axis_at), (shards_of,), jnp.float32, low / len(shards), high / len(shards)))
        level = level * jnp.repeat(steps, dims[axis_at] // shards_of).reshape([-1 if axis == axis_at else 1 for axis in range(len(dims))])
    return level


def centred(key, dims, scale, bound, cuts=(), held_as=jnp.bfloat16):
    level = shard_levels(key, dims, cuts, -0.22, 0.18) if cuts else 1.0
    values = jax.random.normal(key, dims, jnp.float32) * scale * level
    return jnp.minimum(jnp.maximum(values, -bound), bound).astype(held_as)


def setup_inputs(seed: int = 0) -> dict:
    arg_keys = jax.random.split(jax.random.key(seed), 12)
    patches = centred(arg_keys[0], (CROPS * NTOK, PV), 1.0, 6.0, ((0, 16), (1, 2)))
    labels = touch_ends(jax.random.randint(arg_keys[1], (CROPS, CELLS), 0, NCLS), jax.random.fold_in(arg_keys[1], 1), 0, NCLS - 1).astype(jnp.int32)
    batch_ids = touch_ends(jax.random.randint(arg_keys[2], (CROPS,), 0, MB), jax.random.fold_in(arg_keys[2], 1), 0, MB - 1).astype(jnp.int32)
    blocks = centred(arg_keys[3], (N_DP, N_MP, KB, BS, BS), D ** -0.5, 0.21875, ((0, 16), (1, 2)), jnp.float32)
    statistics = draw_statistics(jax.random.fold_in(arg_keys[11], 71), 0)
    roots = draw_roots(jax.random.fold_in(arg_keys[11], 71), 0)
    moments = centred(arg_keys[6], (N_DP, N_MP, KB, BS, BS), (0.005 / NPARAM ** 0.5), 1.9073486328125e-05, ((0, 16), (1, 2)), jnp.float32)
    velocity = jnp.clip(jnp.exp(math.log(7.6676590288682e-15) - 1.3862944 * jax.random.uniform(arg_keys[7], (N_DP, N_MP, KB, BS, BS), jnp.float32) ** shard_levels(arg_keys[7], (N_DP, N_MP, KB, BS, BS), ((0, 16), (1, 2)), -0.2, 0.2)), 1.91691475721705e-15, 7.6676590288682e-15)
    aux = draw_aux(jax.random.fold_in(arg_keys[11], 71), 0)
    aux_moment = centred(arg_keys[9], (NAUX,), (0.11 * 0.025 / NPARAM ** 0.5), 1.1444091796875e-05, (), jnp.float32)
    aux_velocity = jnp.clip(jnp.exp(jax.random.uniform(arg_keys[10], (NAUX,), jnp.float32, math.log(4.7922871048008617e-14), math.log(1.9169148419203447e-13))), 4.7922871048008617e-14, 1.9169148419203447e-13)
    return dict(patches=patches, labels=labels, batch_ids=batch_ids, blocks=blocks, statistics=statistics, roots=roots, moments=moments, velocity=velocity, aux=aux, aux_moment=aux_moment, aux_velocity=aux_velocity)


@jax.custom_vjp
def low(v):
    return lax.optimization_barrier(v.astype(jnp.bfloat16)).astype(jnp.float32)

@jax.custom_vjp
def low_back(v):
    return v

def low_keep(v):
    return (low(v), None)

def low_pass(kept, grad):
    return (grad,)

def back_keep(v):
    return (v, None)

def back_low(kept, grad):
    return (low(grad),)
low.defvjp(low_keep, low_pass)
low_back.defvjp(back_keep, back_low)
HIGHEST = lax.Precision.HIGHEST
beta_one = 0.9
beta_two = 0.999
beta_stat = 0.95
learn_rate = 0.02
decay_rate = 0.01
clip_value = 0.005

def matmul(operand, factor):
    return jnp.dot(operand, factor, precision=HIGHEST, preferred_element_type=jnp.float32)

def layer_norm(values, norm_gain, norm_shift):
    center = values - lax.optimization_barrier(jnp.mean(values, -1, keepdims=True))
    spread = lax.optimization_barrier(jnp.mean(center * center, -1, keepdims=True))
    return center * lax.rsqrt(spread + 1e-06) * norm_gain + norm_shift

def gelu(values):
    return jax.nn.gelu(values, approximate=False)

def aux_layout():
    return [('positions', (NTOK, D)), ('embed_bias', (D,)), ('norm_gain', (2, D)), ('norm_bias', (2, D)), ('qv_bias', (2, D)), ('proj_bias', (D,)), ('up_bias', (FF,)), ('down_bias', (D,)), ('deconv_bias', (DEC,)), ('conv_weight', (27 * DEC, CF)), ('conv_bias', (CF,)), ('head_weight', (CF, NCLS)), ('head_bias', (NCLS,))]

def split_aux(vector):
    pieces = {}
    offset = 0
    for section_name, section_shape in aux_layout():
        length = math.prod(section_shape)
        pieces[section_name] = vector[offset:offset + length].reshape(section_shape)
        offset += length
    return pieces

def local_shapes(mp_count):
    return [(PV // mp_count, D), (D, 3 * D // mp_count), (D // mp_count, D), (D, FF // mp_count), (FF // mp_count, D), (3 * D // mp_count, 8 * DEC)]

def from_blocks(blocks, shapes):
    matrices = []
    offset = 0
    for height, breadth in shapes:
        number = height * breadth // (BS * BS)
        piece = blocks[offset:offset + number]
        matrices.append(piece.reshape(height // BS, breadth // BS, BS, BS).transpose(0, 2, 1, 3).reshape(height, breadth))
        offset += number
    return matrices

def full_weights(blocks):
    grouped = blocks.transpose(1, 0, 2, 3, 4).reshape(N_MP, NBM, BS, BS)
    halves = [from_blocks(grouped[which], local_shapes(N_MP)) for which in range(N_MP)]
    w_embed = jnp.concatenate([half[0] for half in halves], 0)
    w_qkv = jnp.stack([half[1].reshape(D, 3, D // N_MP) for half in halves], 2).reshape(D, 3 * D)
    w_proj = jnp.concatenate([half[2] for half in halves], 0)
    w_up = jnp.concatenate([half[3] for half in halves], 1)
    w_down = jnp.concatenate([half[4] for half in halves], 0)
    w_deconv = jnp.concatenate([half[5].reshape(3, D // N_MP, 8 * DEC) for half in halves], 1)
    return (w_embed, w_qkv, w_proj, w_up, w_down, w_deconv)

def to_grid(flat):
    volumes = flat.shape[0]
    shaped = flat.reshape(volumes, GS, GS, GS, 2, 2, 2, DEC).transpose(0, 1, 4, 2, 5, 3, 6, 7)
    return shaped.reshape(volumes, 2 * GS, 2 * GS, 2 * GS, DEC)

def crop_terms(patch_rows, label_row, weights, pieces):
    w_embed, w_qkv, w_proj, w_up, w_down, w_deconv = weights
    stream_zero = low_back(matmul(patch_rows, w_embed)) + pieces['embed_bias'] + pieces['positions']
    norm_gain = pieces['norm_gain']
    norm_shift = pieces['norm_bias']
    normed_one = low(layer_norm(stream_zero, norm_gain[0], norm_shift[0]))
    projected = matmul(normed_one, w_qkv)
    queries = low(low_back(projected[:, :D] + pieces['qv_bias'][0]))
    key_rows = low(low_back(projected[:, D:2 * D]))
    value_rows = low(low_back(projected[:, 2 * D:] + pieces['qv_bias'][1]))

    def split_heads(tensor):
        return tensor.reshape(NTOK, HEADS, HDIM).transpose(1, 0, 2)
    scores = low_back(jnp.einsum('hqd,hkd->hqk', split_heads(queries), split_heads(key_rows), precision=HIGHEST) * 0.125)
    attention = low(jax.nn.softmax(scores, -1))
    mixed_heads = low(low_back(jnp.einsum('hqk,hkd->hqd', attention, split_heads(value_rows), precision=HIGHEST)))
    mixed_heads = mixed_heads.transpose(1, 0, 2).reshape(NTOK, D)
    stream_one = stream_zero + low_back(matmul(mixed_heads, w_proj)) + pieces['proj_bias']
    normed_two = low(layer_norm(stream_one, norm_gain[1], norm_shift[1]))
    hidden = low_back(matmul(normed_two, w_up) + pieces['up_bias'])
    active = low(gelu(hidden))
    stream_two = stream_one + low_back(matmul(active, w_down)) + pieces['down_bias']
    upsampled = low_back(matmul(low(stream_zero), w_deconv[0]) + matmul(low(stream_one), w_deconv[1]) + matmul(low(stream_two), w_deconv[2]))
    cell_grid = to_grid(upsampled[None])[0] + pieces['deconv_bias']
    conv_in = low(gelu(cell_grid))
    kernel = low(pieces['conv_weight']).reshape(3, 3, 3, DEC, CF)
    conved = low_back(lax.conv_general_dilated(conv_in[None], kernel, (1, 1, 1), 'SAME', dimension_numbers=('NDHWC', 'DHWIO', 'NDHWC'), precision=HIGHEST, preferred_element_type=jnp.float32)[0]) + pieces['conv_bias']
    features = low(gelu(conved)).reshape(CELLS, CF)
    logits = low_back(matmul(features, low(pieces['head_weight']))) + pieces['head_bias']
    log_prob = jax.nn.log_softmax(logits, -1)
    target = (label_row[:, None] == jnp.arange(NCLS, dtype=jnp.int32)[None, :]).astype(jnp.float32)
    chance = jnp.exp(log_prob)
    return (lax.optimization_barrier(jnp.sum(chance * target, 0)), lax.optimization_barrier(jnp.sum(chance, 0)), lax.optimization_barrier(jnp.sum(target, 0)), -jnp.sum(log_prob * target))

def loss_of(blocks, aux, patch_data, labels, batch_onehot):
    weights = full_weights(low(blocks))
    pieces = split_aux(aux)
    crop_rows = patch_data.reshape(-1, NTOK, PV)

    def one_crop(pair):
        return crop_terms(pair[0], pair[1], weights, pieces)
    intersection, predicted, truth_sum, entropy = lax.map(jax.checkpoint(one_crop), (crop_rows, labels))
    intersection_mb = matmul(batch_onehot.T, intersection)
    predicted_mb = matmul(batch_onehot.T, predicted)
    truth_mb = matmul(batch_onehot.T, truth_sum)
    dice_ratio = (2 * intersection_mb + 1) / (predicted_mb + truth_mb + 1)
    return jnp.sum(entropy) / (crop_rows.shape[0] * CELLS) + jnp.mean(1 - lax.optimization_barrier(jnp.mean(dice_ratio, 1)))

def shampoo_step(blocks, grads, stat_pair, root_pair, moment, veloc):
    stat_left = beta_stat * stat_pair[0] + (1 - beta_stat) * jnp.einsum('abcij,abckj->abcik', grads, grads, precision=HIGHEST)
    stat_right = beta_stat * stat_pair[1] + (1 - beta_stat) * jnp.einsum('abcji,abcjk->abcik', grads, grads, precision=HIGHEST)
    moment_new = beta_one * moment + (1 - beta_one) * grads
    veloc_new = beta_two * veloc + (1 - beta_two) * grads * grads
    moment_hat = moment_new / (1 - beta_one ** STEP)
    adam_dir = moment_hat / (jnp.sqrt(veloc_new / (1 - beta_two ** STEP)) + 1e-08)
    left_side = jnp.einsum('abcij,abcjk->abcik', root_pair[0], moment_hat, precision=HIGHEST)
    precond = jnp.einsum('abcij,abcjk->abcik', left_side, root_pair[1], precision=HIGHEST)
    ratio = jnp.sqrt((lax.optimization_barrier(jnp.mean(adam_dir * adam_dir, (-2, -1), keepdims=True)) + 1e-06) / (lax.optimization_barrier(jnp.mean(precond * precond, (-2, -1), keepdims=True)) + 1e-06))
    block_new = blocks - learn_rate * (precond * ratio + decay_rate * blocks)
    return (block_new, jnp.stack([stat_left, stat_right]), moment_new, veloc_new)

def adam_step(param, grads, moment, veloc):
    moment_new = beta_one * moment + (1 - beta_one) * grads
    veloc_new = beta_two * veloc + (1 - beta_two) * grads * grads
    direction = moment_new / (1 - beta_one ** STEP) / (jnp.sqrt(veloc_new / (1 - beta_two ** STEP)) + 1e-08)
    return (param - learn_rate * direction, moment_new, veloc_new)

def reference(patches, labels, batch_ids, blocks, statistics, roots, moments, velocity, aux, aux_moment, aux_velocity):
    batch_onehot = (batch_ids[:, None] == jnp.arange(MB, dtype=jnp.int32)[None, :]).astype(jnp.float32)
    patch_data = patches.astype(jnp.float32)

    def objective(block_arg, aux_arg):
        return loss_of(block_arg, aux_arg, patch_data, labels, batch_onehot)
    loss_value, pullback = jax.vjp(objective, blocks, aux)
    grad_blocks, grad_aux = pullback(jnp.ones((), jnp.float32))
    norm_total = jnp.sqrt(jnp.sum(grad_blocks * grad_blocks) + jnp.sum(grad_aux * grad_aux))
    clip_scale = clip_value / jnp.maximum(norm_total, clip_value)
    block_new, stat_new, moment_new, veloc_new = shampoo_step(blocks, grad_blocks * clip_scale, statistics, roots, moments, velocity)
    aux_new, aux_moment_new, aux_veloc_new = adam_step(aux, grad_aux * clip_scale, aux_moment, aux_velocity)
    return (loss_value, norm_total, block_new, stat_new, moment_new, veloc_new, aux_new, aux_moment_new, aux_veloc_new)
```

```python
import functools
import math

import jax
import jax.numpy as jnp
from jax import lax
from jax.experimental import pallas as pl
from jax.experimental.pallas import tpu as pltpu
from jax.sharding import PartitionSpec as P

D = 768
HDIM = 64
FF = 3072
PV = 4096
DEC = 128
CF = 16
NCLS = 14
GS = 8
MB = 4
STEP = 10
BS = 128
NTOK = 512
CELLS = 4096
MP = 2
HALF = D // MP
E_BLOCKS = PV // MP * D // (BS * BS)

HIGHEST = lax.Precision.HIGHEST
MESH = pl.DeviceIdType.MESH
beta_one = 0.9
beta_two = 0.999
beta_stat = 0.95
learn_rate = 0.02
decay_rate = 0.01
clip_value = 0.005
MIB = 1024 * 1024

OFFSETS = [(a, b, c) for a in range(3) for b in range(3) for c in range(3)]
PARITIES = [(i, j, k) for i in range(2) for j in range(2) for k in range(2)]


def dot(a, b, dims):
    return lax.dot_general(a, b, (dims, ((), ())), preferred_element_type=jnp.float32)


def dot_nn(a, b):
    return dot(a, b, ((1,), (0,)))


def dot_nt(a, b):
    return dot(a, b, ((1,), (1,)))


def dot_tn(a, b):
    return dot(a, b, ((0,), (0,)))


def gelu_cdf(v):
    return 0.5 * (1.0 + lax.erf(v * (0.5**0.5)))


def gelu_and_slope(v):
    cdf = gelu_cdf(v)
    density = jnp.exp(-0.5 * v * v) * (1.0 / math.sqrt(2.0 * math.pi))
    return v * cdf, cdf + v * density


def aux_layout():
    return [
        ("positions", (NTOK, D)),
        ("embed_bias", (D,)),
        ("norm_gain", (2, D)),
        ("norm_bias", (2, D)),
        ("qv_bias", (2, D)),
        ("proj_bias", (D,)),
        ("up_bias", (FF,)),
        ("down_bias", (D,)),
        ("deconv_bias", (DEC,)),
        ("conv_weight", (27 * DEC, CF)),
        ("conv_bias", (CF,)),
        ("head_weight", (CF, NCLS)),
        ("head_bias", (NCLS,)),
    ]


NAUX = sum(math.prod(shape) for _, shape in aux_layout())


def split_aux(vector):
    pieces = {}
    offset = 0
    for section_name, section_shape in aux_layout():
        length = math.prod(section_shape)
        pieces[section_name] = vector[offset : offset + length].reshape(section_shape)
        offset += length
    return pieces


LOCAL_SHAPES = [
    (PV // MP, D),
    (D, 3 * HALF),
    (HALF, D),
    (D, FF // MP),
    (FF // MP, D),
    (3 * HALF, 8 * DEC),
]


def from_blocks(piece, height, breadth):
    return (
        piece.reshape(height // BS, breadth // BS, BS, BS)
        .transpose(0, 2, 1, 3)
        .reshape(height, breadth)
    )


def to_blocks(matrix):
    return (
        matrix.reshape(matrix.shape[0] // BS, BS, matrix.shape[1] // BS, BS)
        .transpose(0, 2, 1, 3)
        .reshape(-1, BS, BS)
    )


def attention_forward_kernel(qkv_q, qkv_k, qkv_v, mixed_ref, lse_ref):
    q, k, v = qkv_q[...], qkv_k[...], qkv_v[...]
    v_t = v.astype(jnp.float32).T.astype(jnp.bfloat16)
    outs = []
    for h in range(2):
        cols = slice(h * HDIM, (h + 1) * HDIM)
        scores = dot_nt(k[:, cols], q[:, cols]) * 0.125
        top = jnp.max(scores, 0, keepdims=True)
        weights = jnp.exp(scores - top)
        total = jnp.sum(weights, 0, keepdims=True)
        attention = (weights * (1.0 / total)).astype(jnp.bfloat16)
        outs.append(dot_nn(v_t[cols], attention))
        lse_ref[0, h : h + 1, :] = top + jnp.log(total)
    mixed_ref[...] = jnp.concatenate(outs, 0).T.astype(jnp.bfloat16)


def attention_backward_kernel(qkv_q, qkv_k, qkv_v, gm_ref, lse_ref, gq_ref, gk_ref, gv_ref):
    q, k, v, gm = qkv_q[...], qkv_k[...], qkv_v[...], gm_ref[...]
    k_t = k.astype(jnp.float32).T.astype(jnp.bfloat16)
    gq_t = []
    for h in range(2):
        cols = slice(h * HDIM, (h + 1) * HDIM)
        scores = dot_nt(k[:, cols], q[:, cols]) * 0.125
        attention = jnp.exp(scores - lse_ref[0, h : h + 1, :])
        back = dot_nt(v[:, cols], gm[:, cols])
        gv_ref[:, cols] = dot_nn(attention.astype(jnp.bfloat16), gm[:, cols]).astype(jnp.bfloat16)
        mean = jnp.sum(back * attention, 0, keepdims=True)
        gs = (attention * (back - mean)).astype(jnp.bfloat16)
        gk_ref[:, cols] = (dot_nn(gs, q[:, cols]) * 0.125).astype(jnp.bfloat16)
        gq_t.append(dot_nn(k_t[cols], gs) * 0.125)
    gq_ref[...] = jnp.concatenate(gq_t, 0).T.astype(jnp.bfloat16)


def qkv_spec(part):
    return pl.BlockSpec((NTOK, BS), lambda i, part=part: (0, (i // 3) * 9 + part * 3 + i % 3))


def attention_forward(qkv):
    return pl.pallas_call(
        attention_forward_kernel,
        grid=(6,),
        out_shape=(
            jax.ShapeDtypeStruct((NTOK, D), jnp.bfloat16),
            jax.ShapeDtypeStruct((6, 2, NTOK), jnp.float32),
        ),
        in_specs=[qkv_spec(0), qkv_spec(1), qkv_spec(2)],
        out_specs=(
            pl.BlockSpec((NTOK, BS), lambda i: (0, i)),
            pl.BlockSpec((1, 2, NTOK), lambda i: (i, 0, 0)),
        ),
        compiler_params=pltpu.CompilerParams(vmem_limit_bytes=32 * MIB),
        cost_estimate=pl.CostEstimate(
            flops=12 * 4 * NTOK * NTOK * HDIM,
            bytes_accessed=NTOK * D * 8,
            transcendentals=12 * NTOK * NTOK,
        ),
        name="attention_forward",
    )(qkv, qkv, qkv)


def attention_backward(qkv, gm, lse):
    pair = pl.BlockSpec((NTOK, BS), lambda i: (0, i))
    return pl.pallas_call(
        attention_backward_kernel,
        grid=(6,),
        out_shape=(jax.ShapeDtypeStruct((NTOK, D), jnp.bfloat16),) * 3,
        in_specs=[
            qkv_spec(0),
            qkv_spec(1),
            qkv_spec(2),
            pair,
            pl.BlockSpec((1, 2, NTOK), lambda i: (i, 0, 0)),
        ],
        out_specs=(pair,) * 3,
        compiler_params=pltpu.CompilerParams(vmem_limit_bytes=32 * MIB),
        cost_estimate=pl.CostEstimate(
            flops=12 * 10 * NTOK * NTOK * HDIM,
            bytes_accessed=NTOK * D * 14,
            transcendentals=12 * NTOK * NTOK,
        ),
        name="attention_backward",
    )(qkv, qkv, qkv, gm, lse)


def source_of(parity, step):
    at = parity + step
    if at < 0:
        return 1, -1
    if at > 1:
        return 0, 1
    return at, 0


def shift_plan(offset, parity, sign):
    found = [source_of(par, sign * (off - 1)) for off, par in zip(offset, parity)]
    bits = [f[0] for f in found]
    steps = [f[1] for f in found]
    return bits[0] * 4 + bits[1] * 2 + bits[2], steps


def token_masks(tokens):
    at = (tokens // (GS * GS), (tokens // GS) % GS, tokens % GS)
    masks = {}
    for axis in range(3):
        masks[axis, 1] = at[axis] < GS - 1
        masks[axis, -1] = at[axis] > 0
    return masks


def shifted(values, steps, masks):
    delta = steps[0] * GS * GS + steps[1] * GS + steps[2]
    if delta == 0 and not any(steps):
        return values
    moved = pltpu.roll(values, (-delta) % NTOK, 1)
    keep = None
    for axis in range(3):
        if steps[axis]:
            mask = masks[axis, steps[axis]]
            keep = mask if keep is None else keep & mask
    return jnp.where(keep, moved, 0.0)


def lanes(parity):
    return slice(parity * NTOK, (parity + 1) * NTOK)


def decoder_forward_kernel(
    up_ref,
    deconv_bias_ref,
    conv_ref,
    conv_bias_ref,
    head_ref,
    head_bias_ref,
    labels_ref,
    batch_ref,
    conv_in_ref,
    grid_slope_ref,
    conv_slope_ref,
    features_ref,
    chance_ref,
    sums_ref,
    conved_ref,
):
    tokens = lax.broadcasted_iota(jnp.int32, (CF, NTOK), 1)
    masks = token_masks(tokens)
    for parity in range(8):
        conved_ref[:, lanes(parity)] = jnp.broadcast_to(conv_bias_ref[...], (CF, NTOK))
    for parity in range(8):
        cell = up_ref[parity * DEC : (parity + 1) * DEC, :] + deconv_bias_ref[...]
        value, slope = gelu_and_slope(cell)
        low = value.astype(jnp.bfloat16)
        conv_in_ref[:, lanes(parity)] = low
        grid_slope_ref[:, lanes(parity)] = slope
        products = dot_nn(conv_ref[...], low)
        for at, offset in enumerate(OFFSETS):
            target, back_steps = shift_plan(offset, PARITIES[parity], -1)
            forward = [-s for s in back_steps]
            piece = shifted(products[at * CF : (at + 1) * CF, :], forward, masks)
            conved_ref[:, lanes(target)] += piece
    rows = lax.broadcasted_iota(jnp.int32, (CF, NTOK), 0)
    hit = jnp.zeros((CF, 1), jnp.float32)
    predicted = jnp.zeros((CF, 1), jnp.float32)
    truth = jnp.zeros((CF, 1), jnp.float32)
    entropy = jnp.zeros((CF, 1), jnp.float32)
    for parity in range(8):
        value, slope = gelu_and_slope(conved_ref[:, lanes(parity)])
        conv_slope_ref[:, lanes(parity)] = slope
        features = value.astype(jnp.bfloat16)
        features_ref[:, lanes(parity)] = features
        logits = dot_nn(head_ref[...], features) + head_bias_ref[...]
        logits = jnp.where(rows < NCLS, logits, -1e30)
        center = logits - jnp.max(logits, 0, keepdims=True)
        log_prob = center - jnp.log(jnp.sum(jnp.exp(center), 0, keepdims=True))
        chance = jnp.exp(log_prob)
        target = (rows == labels_ref[parity : parity + 1, :]).astype(jnp.float32)
        chance_ref[:, lanes(parity)] = chance
        hit += jnp.sum(chance * target, 1, keepdims=True)
        predicted += jnp.sum(chance, 1, keepdims=True)
        truth += jnp.sum(target, 1, keepdims=True)
        entropy -= jnp.sum(jnp.where(target > 0, log_prob, 0.0), 1, keepdims=True)
    lane = lax.broadcasted_iota(jnp.int32, (CF, BS), 1)
    base = batch_ref[...] * 3
    sums_ref[...] = (
        jnp.where(lane == base, hit, 0.0)
        + jnp.where(lane == base + 1, predicted, 0.0)
        + jnp.where(lane == base + 2, truth, 0.0)
        + jnp.where(lane == 3 * MB, entropy, 0.0)
    )


def decoder_backward_kernel(
    all_crops,
    sums_ref,
    batch_ref,
    labels_ref,
    chance_ref,
    features_ref,
    conv_slope_ref,
    grid_slope_ref,
    conv_in_ref,
    conv_t_ref,
    head_t_ref,
    gu_ref,
    conv_grad_ref,
    head_grad_ref,
    small_ref,
    deconv_grad_ref,
    spread_ref,
):
    sums = sums_ref[...]
    lane = lax.broadcasted_iota(jnp.int32, (CF, BS), 1)
    row = lax.broadcasted_iota(jnp.int32, (CF, BS), 0)
    live = (lane < 3 * MB) & (lane % 3 == 0) & (row < NCLS)
    under = pltpu.roll(sums, BS - 1, 1) + pltpu.roll(sums, BS - 2, 1) + 1.0
    under = jnp.where(live, under, 1.0)
    over = 2.0 * sums + 1.0
    dice = jnp.where(live, over / under, 0.0)
    mean_dice = jnp.sum(jnp.sum(dice, 1, keepdims=True), 0, keepdims=True) / (NCLS * MB)
    entropy_lane = jnp.where(lane == 3 * MB, sums, 0.0)
    entropy = jnp.sum(jnp.sum(entropy_lane, 1, keepdims=True), 0, keepdims=True)
    loss = entropy / (all_crops * CELLS) + (1.0 - mean_dice)
    own = live & (lane == batch_ref[...] * 3)
    d_hit = jnp.sum(jnp.where(own, -2.0 / (MB * NCLS) / under, 0.0), 1, keepdims=True)
    d_predicted = jnp.sum(
        jnp.where(own, (1.0 / (MB * NCLS)) * over / (under * under), 0.0), 1, keepdims=True
    )
    tokens = lax.broadcasted_iota(jnp.int32, (CF, NTOK), 1)
    masks = token_masks(tokens)
    rows = lax.broadcasted_iota(jnp.int32, (CF, NTOK), 0)
    head_bias = jnp.zeros((CF, 1), jnp.float32)
    conv_bias = jnp.zeros((CF, 1), jnp.float32)
    head_grad = jnp.zeros((CF, CF), jnp.float32)
    for parity in range(8):
        chance = chance_ref[:, lanes(parity)]
        target = (rows == labels_ref[parity : parity + 1, :]).astype(jnp.float32)
        back = (d_hit * target + d_predicted) * chance - target * (1.0 / (all_crops * CELLS))
        logits = back - chance * jnp.sum(back, 0, keepdims=True)
        head_bias += jnp.sum(logits, 1, keepdims=True)
        low = logits.astype(jnp.bfloat16)
        head_grad += dot_nt(features_ref[:, lanes(parity)], low)
        conved = conv_slope_ref[:, lanes(parity)] * dot_nn(head_t_ref[...], low)
        conv_bias += jnp.sum(conved, 1, keepdims=True)
        rounded = conved.astype(jnp.bfloat16).astype(jnp.float32)
        for at, offset in enumerate(OFFSETS):
            target_cell, steps = shift_plan(offset, PARITIES[parity], 1)
            piece = shifted(rounded, [-s for s in steps], masks)
            spread_ref[at * CF : (at + 1) * CF, lanes(target_cell)] = piece.astype(jnp.bfloat16)
    head_grad_ref[...] = head_grad
    small_ref[...] = (
        jnp.where(lane == 0, head_bias, 0.0)
        + jnp.where(lane == 1, conv_bias, 0.0)
        + jnp.where(lane == 2, loss, 0.0)
    )
    conv_grad = jnp.zeros((27 * CF, DEC), jnp.float32)
    deconv_grad = jnp.zeros((DEC, 1), jnp.float32)
    for parity in range(8):
        spread = spread_ref[:, lanes(parity)]
        conv_grad += dot_nt(spread, conv_in_ref[:, lanes(parity)])
        back = grid_slope_ref[:, lanes(parity)] * dot_nn(conv_t_ref[...], spread)
        deconv_grad += jnp.sum(back, 1, keepdims=True)
        gu_ref[parity * DEC : (parity + 1) * DEC, :] = back.astype(jnp.bfloat16)
    conv_grad_ref[...] = conv_grad
    deconv_grad_ref[...] = jnp.broadcast_to(deconv_grad, (DEC, BS))


def whole_specs(number):
    return [pl.BlockSpec(memory_space=pltpu.VMEM)] * number


def decoder_forward(up_t, deconv_bias, conv_low, conv_bias, head_low, head_bias, labels, batch):
    shapes = (
        jax.ShapeDtypeStruct((DEC, CELLS), jnp.bfloat16),
        jax.ShapeDtypeStruct((DEC, CELLS), jnp.float32),
        jax.ShapeDtypeStruct((CF, CELLS), jnp.float32),
        jax.ShapeDtypeStruct((CF, CELLS), jnp.bfloat16),
        jax.ShapeDtypeStruct((CF, CELLS), jnp.float32),
        jax.ShapeDtypeStruct((CF, BS), jnp.float32),
    )
    return pl.pallas_call(
        decoder_forward_kernel,
        out_shape=shapes,
        in_specs=whole_specs(8),
        out_specs=tuple(whole_specs(6)),
        scratch_shapes=[pltpu.VMEM((CF, CELLS), jnp.float32)],
        compiler_params=pltpu.CompilerParams(vmem_limit_bytes=40 * MIB),
        cost_estimate=pl.CostEstimate(
            flops=2 * 27 * CF * DEC * CELLS, bytes_accessed=6 * MIB, transcendentals=DEC * CELLS
        ),
        name="decoder_forward",
    )(up_t, deconv_bias, conv_low, conv_bias, head_low, head_bias, labels, batch)


def decoder_backward(
    all_crops, sums, batch, labels, chance, features, conv_slope, grid_slope, conv_in, conv_t, head_t
):
    shapes = (
        jax.ShapeDtypeStruct((8 * DEC, NTOK), jnp.bfloat16),
        jax.ShapeDtypeStruct((27 * CF, DEC), jnp.float32),
        jax.ShapeDtypeStruct((CF, CF), jnp.float32),
        jax.ShapeDtypeStruct((CF, BS), jnp.float32),
        jax.ShapeDtypeStruct((DEC, BS), jnp.float32),
    )
    return pl.pallas_call(
        functools.partial(decoder_backward_kernel, all_crops),
        out_shape=shapes,
        in_specs=whole_specs(10),
        out_specs=tuple(whole_specs(5)),
        scratch_shapes=[pltpu.VMEM((27 * CF, CELLS), jnp.bfloat16)],
        compiler_params=pltpu.CompilerParams(vmem_limit_bytes=40 * MIB),
        cost_estimate=pl.CostEstimate(
            flops=4 * 27 * CF * DEC * CELLS, bytes_accessed=6 * MIB, transcendentals=0
        ),
        name="decoder_backward",
    )(sums, batch, labels, chance, features, conv_slope, grid_slope, conv_in, conv_t, head_t)


def gather_weights(blocks):
    low = blocks.astype(jnp.bfloat16)[0]
    gathered = lax.all_gather(low, ("dp", "mp"), axis=0, tiled=True)
    return gathered.reshape(lax.axis_size("dp"), MP, -1, BS, BS)


def sum_small(values):
    return lax.psum(values, ("dp", "mp"))


def swap_mp(values):
    return lax.ppermute(values, "mp", [(0, 1), (1, 0)])


def reduce_blocks(embed_grad, block_grads):
    part = lax.axis_index("mp")
    own = (jnp.arange(MP) == part).astype(jnp.float32)
    first = embed_grad[None] * own[:, None, None, None]
    every = jnp.concatenate([first, block_grads], 1)
    dp = lax.axis_size("dp")
    every = every.reshape(MP, dp, -1, BS, BS).transpose(1, 0, 2, 3, 4)
    return lax.psum_scatter(
        every.reshape(dp * MP, -1, BS, BS), ("dp", "mp"), scatter_dimension=0, tiled=True
    )[0]


def layer_norm(values):
    center = values - jnp.mean(values, -1, keepdims=True)
    spread = jnp.mean(center * center, -1, keepdims=True)
    inverse = lax.rsqrt(spread + 1e-06)
    return center * inverse, inverse


def layer_norm_back(back, normal, inverse, gain):
    scaled = back * gain
    mean = jnp.mean(scaled, -1, keepdims=True)
    along = jnp.mean(scaled * normal, -1, keepdims=True)
    return inverse * (scaled - mean - normal * along)


def shampoo_step(blocks, grads, stat_pair, root_pair, moment, veloc):
    stat_left = beta_stat * stat_pair[0] + (1 - beta_stat) * jnp.einsum(
        "cij,ckj->cik", grads, grads, precision=HIGHEST
    )
    stat_right = beta_stat * stat_pair[1] + (1 - beta_stat) * jnp.einsum(
        "cji,cjk->cik", grads, grads, precision=HIGHEST
    )
    moment_new = beta_one * moment + (1 - beta_one) * grads
    veloc_new = beta_two * veloc + (1 - beta_two) * grads * grads
    moment_hat = moment_new / (1 - beta_one**STEP)
    adam_dir = moment_hat / (jnp.sqrt(veloc_new / (1 - beta_two**STEP)) + 1e-08)
    left_side = jnp.einsum("cij,cjk->cik", root_pair[0], moment_hat, precision=HIGHEST)
    precond = jnp.einsum("cij,cjk->cik", left_side, root_pair[1], precision=HIGHEST)
    ratio = jnp.sqrt(
        (jnp.mean(adam_dir * adam_dir, (-2, -1), keepdims=True) + 1e-06)
        / (jnp.mean(precond * precond, (-2, -1), keepdims=True) + 1e-06)
    )
    block_new = blocks - learn_rate * (precond * ratio + decay_rate * blocks)
    return (block_new, jnp.stack([stat_left, stat_right]), moment_new, veloc_new)


def adam_step(param, grads, moment, veloc):
    moment_new = beta_one * moment + (1 - beta_one) * grads
    veloc_new = beta_two * veloc + (1 - beta_two) * grads * grads
    direction = (
        moment_new / (1 - beta_one**STEP) / (jnp.sqrt(veloc_new / (1 - beta_two**STEP)) + 1e-08)
    )
    return (param - learn_rate * direction, moment_new, veloc_new)


def halves(matrix):
    return matrix[:, :HALF], matrix[:, HALF:]


def local(
    patches,
    labels,
    batch_ids,
    blocks,
    statistics,
    roots,
    moments,
    velocity,
    aux,
    aux_moment,
    aux_velocity,
):
    part = lax.axis_index("mp")
    all_crops = lax.axis_size("dp") * MP
    pieces = split_aux(aux)
    gain, shift = pieces["norm_gain"], pieces["norm_bias"]

    gathered = gather_weights(blocks)
    per_part = [gathered[:, m].reshape(-1, BS, BS) for m in range(MP)]
    starts = [0]
    for height, breadth in LOCAL_SHAPES:
        starts.append(starts[-1] + height * breadth // (BS * BS))

    def matrix_of(which, m):
        piece = per_part[m][starts[which] : starts[which + 1]]
        return from_blocks(piece, *LOCAL_SHAPES[which])

    own_embed = lax.dynamic_index_in_dim(gathered, part, 1, False).reshape(-1, BS, BS)
    w_embed = from_blocks(own_embed[:E_BLOCKS], *LOCAL_SHAPES[0])
    w_qkv = jnp.concatenate([matrix_of(1, m) for m in range(MP)], 1)
    w_proj = jnp.concatenate([matrix_of(2, m) for m in range(MP)], 0)
    w_up = jnp.concatenate([matrix_of(3, m) for m in range(MP)], 1)
    w_down = jnp.concatenate([matrix_of(4, m) for m in range(MP)], 0)
    w_deconv = jnp.concatenate([matrix_of(5, m) for m in range(MP)], 0)

    other_rows = lax.dynamic_slice_in_dim(patches, (1 - part) * NTOK, NTOK, 0)
    own_rows = lax.dynamic_slice_in_dim(patches, part * NTOK, NTOK, 0)
    received = swap_mp(dot_nn(other_rows, w_embed))
    stream_zero = (
        dot_nn(own_rows, w_embed) + received + pieces["positions"] + pieces["embed_bias"]
    )
    normal_one, inverse_one = layer_norm(stream_zero)
    normed_one = (normal_one * gain[0] + shift[0]).astype(jnp.bfloat16)
    q_bias, v_bias = pieces["qv_bias"][0], pieces["qv_bias"][1]
    nothing = jnp.zeros((HALF,), jnp.float32)
    qkv_bias = jnp.concatenate(
        [q_bias[:HALF], nothing, v_bias[:HALF], q_bias[HALF:], nothing, v_bias[HALF:]]
    )
    qkv = (dot_nn(normed_one, w_qkv) + qkv_bias).astype(jnp.bfloat16)
    mixed, lse = attention_forward(qkv)
    stream_one = stream_zero + dot_nn(mixed, w_proj) + pieces["proj_bias"]
    normal_two, inverse_two = layer_norm(stream_one)
    normed_two = (normal_two * gain[1] + shift[1]).astype(jnp.bfloat16)
    hidden = dot_nn(normed_two, w_up) + pieces["up_bias"]
    active_value, hidden_slope = gelu_and_slope(hidden)
    active = active_value.astype(jnp.bfloat16)
    stream_two = stream_one + dot_nn(active, w_down) + pieces["down_bias"]
    streams = [s.astype(jnp.bfloat16) for s in (stream_zero, stream_one, stream_two)]
    stacked = jnp.concatenate([halves(s)[m] for m in range(MP) for s in streams], 1)
    up_t = dot(w_deconv, stacked, ((0,), (1,)))

    conv_weight = pieces["conv_weight"].astype(jnp.bfloat16).reshape(27, DEC, CF)
    conv_low = conv_weight.transpose(0, 2, 1).reshape(27 * CF, DEC)
    conv_t = conv_weight.transpose(1, 0, 2).reshape(DEC, 27 * CF)
    head_weight = jnp.pad(pieces["head_weight"], ((0, 0), (0, CF - NCLS))).astype(jnp.bfloat16)
    head_bias = jnp.pad(pieces["head_bias"], (0, CF - NCLS)).reshape(CF, 1)
    grid_labels = (
        labels.reshape(GS, 2, GS, 2, GS, 2).transpose(1, 3, 5, 0, 2, 4).reshape(8, NTOK)
    )
    batch = jnp.broadcast_to(batch_ids.reshape(1, 1), (1, BS))
    conv_in, grid_slope, conv_slope, features, chance, sums = decoder_forward(
        up_t,
        pieces["deconv_bias"].reshape(DEC, 1),
        conv_low,
        pieces["conv_bias"].reshape(CF, 1),
        head_weight.T,
        head_bias,
        grid_labels,
        batch,
    )
    sums = sum_small(sums)
    gu_t, conv_grad, head_grad, small, deconv_bias_grad = decoder_backward(
        all_crops,
        sums,
        batch,
        grid_labels,
        chance,
        features,
        conv_slope,
        grid_slope,
        conv_in,
        conv_t,
        head_weight,
    )
    loss_value = small[0, 2]
    grad_head_bias = small[:NCLS, 0]
    grad_conv_bias = small[:, 1]
    grad_deconv_bias = deconv_bias_grad[:, 0]
    grad_conv_weight = conv_grad.reshape(27, CF, DEC).transpose(0, 2, 1)
    grad_head_weight = head_grad[:, :NCLS]

    grad_deconv = dot_tn(stacked, gu_t.T)
    stacked_back = dot(gu_t, w_deconv, ((0,), (1,)))
    back_zero_s, back_one_s, back_two = [
        jnp.concatenate([stacked_back[:, (3 * m + s) * HALF : (3 * m + s + 1) * HALF] for m in range(MP)], 1)
        for s in range(3)
    ]
    grad_down_bias = jnp.sum(back_two, 0)
    two_low = back_two.astype(jnp.bfloat16)
    back_hidden = (hidden_slope * dot_nt(two_low, w_down)).astype(jnp.bfloat16)
    grad_down = dot_tn(active, two_low)
    grad_up_bias = jnp.sum(back_hidden.astype(jnp.float32), 0)
    grad_up = dot_tn(normed_two, back_hidden)
    back_normed_two = dot_nt(back_hidden, w_up)
    grad_gain_two = jnp.sum(back_normed_two * normal_two, 0)
    grad_shift_two = jnp.sum(back_normed_two, 0)
    back_one = (
        back_two + back_one_s + layer_norm_back(back_normed_two, normal_two, inverse_two, gain[1])
    )
    grad_proj_bias = jnp.sum(back_one, 0)
    one_low = back_one.astype(jnp.bfloat16)
    grad_proj = dot_tn(mixed, one_low)
    back_mixed = dot_nt(one_low, w_proj).astype(jnp.bfloat16)
    back_q, back_k, back_v = attention_backward(qkv, back_mixed, lse)
    back_qkv = jnp.concatenate(
        [halves(piece)[m] for m in range(MP) for piece in (back_q, back_k, back_v)], 1
    )
    grad_qkv = dot_tn(normed_one, back_qkv)
    grad_query_bias = jnp.sum(back_q.astype(jnp.float32), 0)
    grad_value_bias = jnp.sum(back_v.astype(jnp.float32), 0)
    back_normed_one = dot_nt(back_qkv, w_qkv)
    grad_gain_one = jnp.sum(back_normed_one * normal_one, 0)
    grad_shift_one = jnp.sum(back_normed_one, 0)
    back_zero = (
        back_one + back_zero_s + layer_norm_back(back_normed_one, normal_one, inverse_one, gain[0])
    )
    zero_low = back_zero.astype(jnp.bfloat16)
    other_low = swap_mp(zero_low)
    grad_embed = dot_tn(own_rows, zero_low) + dot_tn(other_rows, other_low)

    block_grads = jnp.stack(
        [
            jnp.concatenate(
                [
                    to_blocks(grad_qkv[:, m * 3 * HALF : (m + 1) * 3 * HALF]),
                    to_blocks(grad_proj[m * HALF : (m + 1) * HALF]),
                    to_blocks(grad_up[:, m * FF // MP : (m + 1) * FF // MP]),
                    to_blocks(grad_down[m * FF // MP : (m + 1) * FF // MP]),
                    to_blocks(grad_deconv[m * 3 * HALF : (m + 1) * 3 * HALF]),
                ]
            )
            for m in range(MP)
        ]
    )
    owned = reduce_blocks(to_blocks(grad_embed), block_grads)
    late = jnp.stack(
        [
            grad_gain_one,
            grad_gain_two,
            grad_shift_one,
            grad_shift_two,
            grad_query_bias,
            grad_value_bias,
            grad_proj_bias,
        ]
    )
    rest = jnp.concatenate(
        [
            late.reshape(-1),
            grad_up_bias,
            grad_down_bias,
            grad_deconv_bias,
            grad_conv_weight.reshape(-1),
            grad_conv_bias,
            grad_head_weight.reshape(-1),
            grad_head_bias,
        ]
    )
    aux_sum = sum_small(jnp.concatenate([back_zero.reshape(-1), rest]))
    positions_sum = aux_sum[: NTOK * D]
    embed_bias_sum = jnp.sum(positions_sum.reshape(NTOK, D), 0)
    aux_total = jnp.concatenate([positions_sum, embed_bias_sum, aux_sum[NTOK * D :]])
    block_square = sum_small(jnp.sum(owned * owned))
    grad_norm = jnp.sqrt(block_square + jnp.sum(aux_total * aux_total))
    clip_scale = clip_value / jnp.maximum(grad_norm, clip_value)
    block_new, stat_new, moment_new, veloc_new = shampoo_step(
        blocks[0, 0],
        owned * clip_scale,
        statistics[:, 0, 0],
        roots[:, 0, 0],
        moments[0, 0],
        velocity[0, 0],
    )
    aux_new, aux_moment_new, aux_veloc_new = adam_step(
        aux, aux_total * clip_scale, aux_moment, aux_velocity
    )
    return (
        loss_value,
        grad_norm,
        block_new[None, None],
        stat_new[:, None, None],
        moment_new[None, None],
        veloc_new[None, None],
        aux_new,
        aux_moment_new,
        aux_veloc_new,
    )


def solution(mesh):
    block_spec = P("dp", "mp", None, None, None)
    pair_spec = P(None, "dp", "mp", None, None, None)
    placed = (
        P("dp", "mp"),
        P(("dp", "mp"), None),
        P(("dp", "mp")),
        block_spec,
        pair_spec,
        pair_spec,
        block_spec,
        block_spec,
        P(),
        P(),
        P(),
    )
    return jax.shard_map(
        local,
        mesh=mesh,
        in_specs=placed,
        out_specs=(P(), P(), block_spec, pair_spec, block_spec, block_spec, P(), P(), P()),
        check_vma=False,
    )
```

```python
import functools
import math

import jax
import jax.numpy as jnp
from jax import lax
from jax.experimental import pallas as pl
from jax.experimental.pallas import tpu as pltpu
from jax.sharding import PartitionSpec as P

D = 768
HDIM = 64
FF = 3072
PV = 4096
DEC = 128
CF = 16
NCLS = 14
GS = 8
MB = 4
STEP = 10
BS = 128
NTOK = 512
CELLS = 4096
MP = 2
HALF = D // MP
E_BLOCKS = PV // MP * D // (BS * BS)

HIGHEST = lax.Precision.HIGHEST
MESH = pl.DeviceIdType.MESH
beta_one = 0.9
beta_two = 0.999
beta_stat = 0.95
learn_rate = 0.02
decay_rate = 0.01
clip_value = 0.005
MIB = 1024 * 1024

OFFSETS = [(a, b, c) for a in range(3) for b in range(3) for c in range(3)]
PARITIES = [(i, j, k) for i in range(2) for j in range(2) for k in range(2)]


def dot(a, b, dims):
    return lax.dot_general(a, b, (dims, ((), ())), preferred_element_type=jnp.float32)


def dot_nn(a, b):
    return dot(a, b, ((1,), (0,)))


def dot_nt(a, b):
    return dot(a, b, ((1,), (1,)))


def dot_tn(a, b):
    return dot(a, b, ((0,), (0,)))


def gelu_cdf(v):
    return 0.5 * (1.0 + lax.erf(v * (0.5**0.5)))


def gelu_and_slope(v):
    cdf = gelu_cdf(v)
    density = jnp.exp(-0.5 * v * v) * (1.0 / math.sqrt(2.0 * math.pi))
    return v * cdf, cdf + v * density


def aux_layout():
    return [
        ("positions", (NTOK, D)),
        ("embed_bias", (D,)),
        ("norm_gain", (2, D)),
        ("norm_bias", (2, D)),
        ("qv_bias", (2, D)),
        ("proj_bias", (D,)),
        ("up_bias", (FF,)),
        ("down_bias", (D,)),
        ("deconv_bias", (DEC,)),
        ("conv_weight", (27 * DEC, CF)),
        ("conv_bias", (CF,)),
        ("head_weight", (CF, NCLS)),
        ("head_bias", (NCLS,)),
    ]


NAUX = sum(math.prod(shape) for _, shape in aux_layout())


def split_aux(vector):
    pieces = {}
    offset = 0
    for section_name, section_shape in aux_layout():
        length = math.prod(section_shape)
        pieces[section_name] = vector[offset : offset + length].reshape(section_shape)
        offset += length
    return pieces


LOCAL_SHAPES = [
    (PV // MP, D),
    (D, 3 * HALF),
    (HALF, D),
    (D, FF // MP),
    (FF // MP, D),
    (3 * HALF, 8 * DEC),
]


def from_blocks(piece, height, breadth):
    return (
        piece.reshape(height // BS, breadth // BS, BS, BS)
        .transpose(0, 2, 1, 3)
        .reshape(height, breadth)
    )


def to_blocks(matrix):
    return (
        matrix.reshape(matrix.shape[0] // BS, BS, matrix.shape[1] // BS, BS)
        .transpose(0, 2, 1, 3)
        .reshape(-1, BS, BS)
    )


def attention_forward_kernel(qkv_q, qkv_k, qkv_v, mixed_ref, lse_ref):
    q, k, v = qkv_q[...], qkv_k[...], qkv_v[...]
    v_t = v.astype(jnp.float32).T.astype(jnp.bfloat16)
    outs = []
    for h in range(2):
        cols = slice(h * HDIM, (h + 1) * HDIM)
        scores = dot_nt(k[:, cols], q[:, cols]) * 0.125
        top = jnp.max(scores, 0, keepdims=True)
        weights = jnp.exp(scores - top)
        total = jnp.sum(weights, 0, keepdims=True)
        attention = (weights * (1.0 / total)).astype(jnp.bfloat16)
        outs.append(dot_nn(v_t[cols], attention))
        lse_ref[0, h : h + 1, :] = top + jnp.log(total)
    mixed_ref[...] = jnp.concatenate(outs, 0).T.astype(jnp.bfloat16)


def attention_backward_kernel(qkv_q, qkv_k, qkv_v, gm_ref, lse_ref, gq_ref, gk_ref, gv_ref):
    q, k, v, gm = qkv_q[...], qkv_k[...], qkv_v[...], gm_ref[...]
    k_t = k.astype(jnp.float32).T.astype(jnp.bfloat16)
    gq_t = []
    for h in range(2):
        cols = slice(h * HDIM, (h + 1) * HDIM)
        scores = dot_nt(k[:, cols], q[:, cols]) * 0.125
        attention = jnp.exp(scores - lse_ref[0, h : h + 1, :])
        back = dot_nt(v[:, cols], gm[:, cols])
        gv_ref[:, cols] = dot_nn(attention.astype(jnp.bfloat16), gm[:, cols]).astype(jnp.bfloat16)
        mean = jnp.sum(back * attention, 0, keepdims=True)
        gs = (attention * (back - mean)).astype(jnp.bfloat16)
        gk_ref[:, cols] = (dot_nn(gs, q[:, cols]) * 0.125).astype(jnp.bfloat16)
        gq_t.append(dot_nn(k_t[cols], gs) * 0.125)
    gq_ref[...] = jnp.concatenate(gq_t, 0).T.astype(jnp.bfloat16)


def qkv_spec(part):
    return pl.BlockSpec((NTOK, BS), lambda i, part=part: (0, (i // 3) * 9 + part * 3 + i % 3))


def attention_forward(qkv):
    return pl.pallas_call(
        attention_forward_kernel,
        grid=(6,),
        out_shape=(
            jax.ShapeDtypeStruct((NTOK, D), jnp.bfloat16),
            jax.ShapeDtypeStruct((6, 2, NTOK), jnp.float32),
        ),
        in_specs=[qkv_spec(0), qkv_spec(1), qkv_spec(2)],
        out_specs=(
            pl.BlockSpec((NTOK, BS), lambda i: (0, i)),
            pl.BlockSpec((1, 2, NTOK), lambda i: (i, 0, 0)),
        ),
        compiler_params=pltpu.CompilerParams(vmem_limit_bytes=32 * MIB),
        cost_estimate=pl.CostEstimate(
            flops=12 * 4 * NTOK * NTOK * HDIM,
            bytes_accessed=NTOK * D * 8,
            transcendentals=12 * NTOK * NTOK,
        ),
        name="attention_forward",
    )(qkv, qkv, qkv)


def attention_backward(qkv, gm, lse):
    pair = pl.BlockSpec((NTOK, BS), lambda i: (0, i))
    return pl.pallas_call(
        attention_backward_kernel,
        grid=(6,),
        out_shape=(jax.ShapeDtypeStruct((NTOK, D), jnp.bfloat16),) * 3,
        in_specs=[
            qkv_spec(0),
            qkv_spec(1),
            qkv_spec(2),
            pair,
            pl.BlockSpec((1, 2, NTOK), lambda i: (i, 0, 0)),
        ],
        out_specs=(pair,) * 3,
        compiler_params=pltpu.CompilerParams(vmem_limit_bytes=32 * MIB),
        cost_estimate=pl.CostEstimate(
            flops=12 * 10 * NTOK * NTOK * HDIM,
            bytes_accessed=NTOK * D * 14,
            transcendentals=12 * NTOK * NTOK,
        ),
        name="attention_backward",
    )(qkv, qkv, qkv, gm, lse)


def source_of(parity, step):
    at = parity + step
    if at < 0:
        return 1, -1
    if at > 1:
        return 0, 1
    return at, 0


def shift_plan(offset, parity, sign):
    found = [source_of(par, sign * (off - 1)) for off, par in zip(offset, parity)]
    bits = [f[0] for f in found]
    steps = [f[1] for f in found]
    return bits[0] * 4 + bits[1] * 2 + bits[2], steps


def token_masks(tokens):
    at = (tokens // (GS * GS), (tokens // GS) % GS, tokens % GS)
    masks = {}
    for axis in range(3):
        masks[axis, 1] = at[axis] < GS - 1
        masks[axis, -1] = at[axis] > 0
    return masks


def shifted(values, steps, masks):
    delta = steps[0] * GS * GS + steps[1] * GS + steps[2]
    if delta == 0 and not any(steps):
        return values
    moved = pltpu.roll(values, (-delta) % NTOK, 1)
    keep = None
    for axis in range(3):
        if steps[axis]:
            mask = masks[axis, steps[axis]]
            keep = mask if keep is None else keep & mask
    return jnp.where(keep, moved, 0.0)


def lanes(parity):
    return slice(parity * NTOK, (parity + 1) * NTOK)


def decoder_forward_kernel(
    up_ref,
    deconv_bias_ref,
    conv_ref,
    conv_bias_ref,
    head_ref,
    head_bias_ref,
    labels_ref,
    batch_ref,
    conv_in_ref,
    grid_slope_ref,
    conv_slope_ref,
    features_ref,
    chance_ref,
    sums_ref,
    conved_ref,
):
    tokens = lax.broadcasted_iota(jnp.int32, (CF, NTOK), 1)
    masks = token_masks(tokens)
    for parity in range(8):
        conved_ref[:, lanes(parity)] = jnp.broadcast_to(conv_bias_ref[...], (CF, NTOK))
    for parity in range(8):
        cell = up_ref[parity * DEC : (parity + 1) * DEC, :] + deconv_bias_ref[...]
        value, slope = gelu_and_slope(cell)
        low = value.astype(jnp.bfloat16)
        conv_in_ref[:, lanes(parity)] = low
        grid_slope_ref[:, lanes(parity)] = slope
        products = dot_nn(conv_ref[...], low)
        for at, offset in enumerate(OFFSETS):
            target, back_steps = shift_plan(offset, PARITIES[parity], -1)
            forward = [-s for s in back_steps]
            piece = shifted(products[at * CF : (at + 1) * CF, :], forward, masks)
            conved_ref[:, lanes(target)] += piece
    rows = lax.broadcasted_iota(jnp.int32, (CF, NTOK), 0)
    hit = jnp.zeros((CF, 1), jnp.float32)
    predicted = jnp.zeros((CF, 1), jnp.float32)
    truth = jnp.zeros((CF, 1), jnp.float32)
    entropy = jnp.zeros((CF, 1), jnp.float32)
    for parity in range(8):
        value, slope = gelu_and_slope(conved_ref[:, lanes(parity)])
        conv_slope_ref[:, lanes(parity)] = slope
        features = value.astype(jnp.bfloat16)
        features_ref[:, lanes(parity)] = features
        logits = dot_nn(head_ref[...], features) + head_bias_ref[...]
        logits = jnp.where(rows < NCLS, logits, -1e30)
        center = logits - jnp.max(logits, 0, keepdims=True)
        log_prob = center - jnp.log(jnp.sum(jnp.exp(center), 0, keepdims=True))
        chance = jnp.exp(log_prob)
        target = (rows == labels_ref[parity : parity + 1, :]).astype(jnp.float32)
        chance_ref[:, lanes(parity)] = chance
        hit += jnp.sum(chance * target, 1, keepdims=True)
        predicted += jnp.sum(chance, 1, keepdims=True)
        truth += jnp.sum(target, 1, keepdims=True)
        entropy -= jnp.sum(jnp.where(target > 0, log_prob, 0.0), 1, keepdims=True)
    lane = lax.broadcasted_iota(jnp.int32, (CF, BS), 1)
    base = batch_ref[...] * 3
    sums_ref[...] = (
        jnp.where(lane == base, hit, 0.0)
        + jnp.where(lane == base + 1, predicted, 0.0)
        + jnp.where(lane == base + 2, truth, 0.0)
        + jnp.where(lane == 3 * MB, entropy, 0.0)
    )


def decoder_backward_kernel(
    all_crops,
    sums_ref,
    batch_ref,
    labels_ref,
    chance_ref,
    features_ref,
    conv_slope_ref,
    grid_slope_ref,
    conv_in_ref,
    conv_t_ref,
    head_t_ref,
    gu_ref,
    conv_grad_ref,
    head_grad_ref,
    small_ref,
    deconv_grad_ref,
    spread_ref,
):
    sums = sums_ref[...]
    lane = lax.broadcasted_iota(jnp.int32, (CF, BS), 1)
    row = lax.broadcasted_iota(jnp.int32, (CF, BS), 0)
    live = (lane < 3 * MB) & (lane % 3 == 0) & (row < NCLS)
    under = pltpu.roll(sums, BS - 1, 1) + pltpu.roll(sums, BS - 2, 1) + 1.0
    under = jnp.where(live, under, 1.0)
    over = 2.0 * sums + 1.0
    dice = jnp.where(live, over / under, 0.0)
    mean_dice = jnp.sum(jnp.sum(dice, 1, keepdims=True), 0, keepdims=True) / (NCLS * MB)
    entropy_lane = jnp.where(lane == 3 * MB, sums, 0.0)
    entropy = jnp.sum(jnp.sum(entropy_lane, 1, keepdims=True), 0, keepdims=True)
    loss = entropy / (all_crops * CELLS) + (1.0 - mean_dice)
    own = live & (lane == batch_ref[...] * 3)
    d_hit = jnp.sum(jnp.where(own, -2.0 / (MB * NCLS) / under, 0.0), 1, keepdims=True)
    d_predicted = jnp.sum(
        jnp.where(own, (1.0 / (MB * NCLS)) * over / (under * under), 0.0), 1, keepdims=True
    )
    tokens = lax.broadcasted_iota(jnp.int32, (CF, NTOK), 1)
    masks = token_masks(tokens)
    rows = lax.broadcasted_iota(jnp.int32, (CF, NTOK), 0)
    head_bias = jnp.zeros((CF, 1), jnp.float32)
    conv_bias = jnp.zeros((CF, 1), jnp.float32)
    head_grad = jnp.zeros((CF, CF), jnp.float32)
    for parity in range(8):
        chance = chance_ref[:, lanes(parity)]
        target = (rows == labels_ref[parity : parity + 1, :]).astype(jnp.float32)
        back = (d_hit * target + d_predicted) * chance - target * (1.0 / (all_crops * CELLS))
        logits = back - chance * jnp.sum(back, 0, keepdims=True)
        head_bias += jnp.sum(logits, 1, keepdims=True)
        low = logits.astype(jnp.bfloat16)
        head_grad += dot_nt(features_ref[:, lanes(parity)], low)
        conved = conv_slope_ref[:, lanes(parity)] * dot_nn(head_t_ref[...], low)
        conv_bias += jnp.sum(conved, 1, keepdims=True)
        rounded = conved.astype(jnp.bfloat16).astype(jnp.float32)
        for at, offset in enumerate(OFFSETS):
            target_cell, steps = shift_plan(offset, PARITIES[parity], 1)
            piece = shifted(rounded, [-s for s in steps], masks)
            spread_ref[at * CF : (at + 1) * CF, lanes(target_cell)] = piece.astype(jnp.bfloat16)
    head_grad_ref[...] = head_grad
    small_ref[...] = (
        jnp.where(lane == 0, head_bias, 0.0)
        + jnp.where(lane == 1, conv_bias, 0.0)
        + jnp.where(lane == 2, loss, 0.0)
    )
    conv_grad = jnp.zeros((27 * CF, DEC), jnp.float32)
    deconv_grad = jnp.zeros((DEC, 1), jnp.float32)
    for parity in range(8):
        spread = spread_ref[:, lanes(parity)]
        conv_grad += dot_nt(spread, conv_in_ref[:, lanes(parity)])
        back = grid_slope_ref[:, lanes(parity)] * dot_nn(conv_t_ref[...], spread)
        deconv_grad += jnp.sum(back, 1, keepdims=True)
        gu_ref[parity * DEC : (parity + 1) * DEC, :] = back.astype(jnp.bfloat16)
    conv_grad_ref[...] = conv_grad
    deconv_grad_ref[...] = jnp.broadcast_to(deconv_grad, (DEC, BS))


def whole_specs(number):
    return [pl.BlockSpec(memory_space=pltpu.VMEM)] * number


def decoder_forward(up_t, deconv_bias, conv_low, conv_bias, head_low, head_bias, labels, batch):
    shapes = (
        jax.ShapeDtypeStruct((DEC, CELLS), jnp.bfloat16),
        jax.ShapeDtypeStruct((DEC, CELLS), jnp.float32),
        jax.ShapeDtypeStruct((CF, CELLS), jnp.float32),
        jax.ShapeDtypeStruct((CF, CELLS), jnp.bfloat16),
        jax.ShapeDtypeStruct((CF, CELLS), jnp.float32),
        jax.ShapeDtypeStruct((CF, BS), jnp.float32),
    )
    return pl.pallas_call(
        decoder_forward_kernel,
        out_shape=shapes,
        in_specs=whole_specs(8),
        out_specs=tuple(whole_specs(6)),
        scratch_shapes=[pltpu.VMEM((CF, CELLS), jnp.float32)],
        compiler_params=pltpu.CompilerParams(vmem_limit_bytes=40 * MIB),
        cost_estimate=pl.CostEstimate(
            flops=2 * 27 * CF * DEC * CELLS, bytes_accessed=6 * MIB, transcendentals=DEC * CELLS
        ),
        name="decoder_forward",
    )(up_t, deconv_bias, conv_low, conv_bias, head_low, head_bias, labels, batch)


def decoder_backward(
    all_crops, sums, batch, labels, chance, features, conv_slope, grid_slope, conv_in, conv_t, head_t
):
    shapes = (
        jax.ShapeDtypeStruct((8 * DEC, NTOK), jnp.bfloat16),
        jax.ShapeDtypeStruct((27 * CF, DEC), jnp.float32),
        jax.ShapeDtypeStruct((CF, CF), jnp.float32),
        jax.ShapeDtypeStruct((CF, BS), jnp.float32),
        jax.ShapeDtypeStruct((DEC, BS), jnp.float32),
    )
    return pl.pallas_call(
        functools.partial(decoder_backward_kernel, all_crops),
        out_shape=shapes,
        in_specs=whole_specs(10),
        out_specs=tuple(whole_specs(5)),
        scratch_shapes=[pltpu.VMEM((27 * CF, CELLS), jnp.bfloat16)],
        compiler_params=pltpu.CompilerParams(vmem_limit_bytes=40 * MIB),
        cost_estimate=pl.CostEstimate(
            flops=4 * 27 * CF * DEC * CELLS, bytes_accessed=6 * MIB, transcendentals=0
        ),
        name="decoder_backward",
    )(sums, batch, labels, chance, features, conv_slope, grid_slope, conv_in, conv_t, head_t)


LAYERS = 4
PIECES = 24
ROWS_A = 272
ROWS_B = 136
ROWS_N = ROWS_A + ROWS_B
ROWS_E = 128
CHUNK = 8 * ROWS_N
AUX_ROWS = CHUNK - 24 * BS
LAG = 2
HOP_LAG = 1
CORE_SLOTS = 6
SEND_SLOTS = 4
KEEP = 8
SUM_SLOTS = 12


def remote(src, dst, send_sem, recv_sem, device):
    return pltpu.make_async_remote_copy(
        src_ref=src,
        dst_ref=dst,
        send_sem=send_sem,
        recv_sem=recv_sem,
        device_id=device,
        device_id_type=MESH,
    )


def places():
    dp, x = lax.axis_index("dp"), lax.axis_index("mp")
    z, y, c = dp // 4, (dp // 2) % 2, dp % 2
    return dict(
        dp=dp,
        x=x,
        y=y,
        z=z,
        c=c,
        at_core=(dp + 1 - 2 * c, x),
        at_x=(dp, 1 - x),
        at_y=(dp + 2 - 4 * y, x),
        above=(lax.rem(dp + 4, 4 * LAYERS), x),
        below=(lax.rem(dp + 4 * LAYERS - 4, 4 * LAYERS), x),
    )


def greet_neighbours(at):
    barrier = pltpu.get_barrier_semaphore()
    for name in ("at_core", "at_x", "at_y"):
        pl.semaphore_signal(barrier, inc=1, device_id=at[name], device_id_type=MESH)

    @pl.when(at["z"] < LAYERS - 1)
    def _():
        pl.semaphore_signal(barrier, inc=1, device_id=at["above"], device_id_type=MESH)

    @pl.when(at["z"] > 0)
    def _():
        pl.semaphore_signal(barrier, inc=1, device_id=at["below"], device_id_type=MESH)

    peers = 3 + jnp.minimum(at["z"], 1) + jnp.minimum(LAYERS - 1 - at["z"], 1)
    pl.semaphore_wait(barrier, peers)


def gather_kernel(rows, rows_a, skip, in_ref, out_ref, local_sem, up_sem, down_sem, z_recv, x_send, x_recv, y_send, y_recv, core_send, core_recv):
    at = places()
    x, y, z, c = at["x"], at["y"], at["z"], at["c"]
    last = LAYERS - 1
    every, a, b = pl.ds(0, rows), pl.ds(0, rows_a), pl.ds(rows_a, rows - rows_a)

    def spot(l, y_at, c_at, x_at, part):
        return out_ref.at[x_at, l * 4 + y_at * 2 + c_at, part]

    def send(ref, send_sem, recv_sem, device):
        return remote(ref, ref, send_sem, recv_sem, device)

    def up(l):
        return send(spot(l, y, c, x, every), up_sem.at[l], z_recv.at[l], at["above"])

    def down(l):
        return send(spot(l, y, c, x, every), down_sem.at[l], z_recv.at[l], at["below"])

    def x_a(l, x_at):
        return send(spot(l, y, c, x_at, a), x_send.at[l, 0], x_recv.at[l, 0], at["at_x"])

    def x_b(l, x_at):
        return send(spot(l, y, c, x_at, b), x_send.at[l, 1], x_recv.at[l, 1], at["at_x"])

    def x_relay(l, x_at):
        return send(spot(l, 1 - y, c, x_at, b), x_send.at[l, 2], x_recv.at[l, 2], at["at_x"])

    def y_a(l, y_at):
        return send(spot(l, y_at, c, x, a), y_send.at[l, 0], y_recv.at[l, 0], at["at_y"])

    def y_b(l, y_at):
        return send(spot(l, y_at, c, x, b), y_send.at[l, 1], y_recv.at[l, 1], at["at_y"])

    def y_relay(l, y_at):
        return send(spot(l, y_at, c, 1 - x, a), y_send.at[l, 2], y_recv.at[l, 2], at["at_y"])

    def core(l, kind, c_at):
        spots = (
            spot(l, y, c_at, x, every),
            spot(l, 1 - y, c_at, x, every),
            spot(l, y, c_at, 1 - x, every),
            spot(l, 1 - y, c_at, 1 - x, a),
            spot(l, 1 - y, c_at, 1 - x, b),
        )
        return send(spots[kind], core_send.at[l, kind], core_recv.at[l, kind], at["at_core"])

    def wide(l):
        return (l > 0) if skip else (l >= 0)

    own = pltpu.make_async_copy(in_ref, out_ref.at[x, at["dp"]], local_sem)
    own.start()
    greet_neighbours(at)
    own.wait()

    def arrive(l, came_up, came_down):
        if not (came_up and came_down):
            up(l).wait_recv()
        if came_up:

            @pl.when(z < last)
            def _():
                up(l).start()

        if came_down:

            @pl.when(z > 0)
            def _():
                down(l).start()

        y_b(l, y).start()

        @pl.when(wide(l))
        def _():
            x_a(l, x).start()
            x_b(l, x).start()

        y_a(l, y).start()
        core(l, 0, c).start()

    def relay(l):
        y_b(l, 1 - y).wait_recv()

        @pl.when(wide(l))
        def _():
            x_relay(l, x).start()
            x_a(l, 1 - x).wait_recv()
            y_relay(l, y).start()

        y_a(l, 1 - y).wait_recv()
        core(l, 1, c).start()

        @pl.when(wide(l))
        def _():
            x_b(l, 1 - x).wait_recv()
            core(l, 2, c).start()

    def finish(l):
        @pl.when(wide(l))
        def _():
            y_relay(l, 1 - y).wait_recv()
            core(l, 3, c).start()
            x_relay(l, 1 - x).wait_recv()
            core(l, 4, c).start()

    def both(r, run):
        if r < 0 or r >= LAYERS:
            return
        if r == 0:
            run(z, True, True)
            return

        @pl.when(z - r >= 0)
        def _():
            run(z - r, True, False)

        @pl.when(z + r <= last)
        def _():
            run(z + r, False, True)

    for r in range(LAYERS + 2):
        both(r, arrive)
        both(r - 1, lambda l, up_way, down_way: relay(l))
        both(r - 2, lambda l, up_way, down_way: finish(l))

    def settle(l, carry):
        for kind in (0, 1):
            core(l, kind, 1 - c).wait_recv()
            core(l, kind, c).wait_send()
        y_a(l, y).wait_send()
        y_b(l, y).wait_send()

        @pl.when(wide(l))
        def _():
            for kind in (2, 3, 4):
                core(l, kind, 1 - c).wait_recv()
                core(l, kind, c).wait_send()
            for copy in (x_a(l, x), x_b(l, x), x_relay(l, x), y_relay(l, y)):
                copy.wait_send()

        @pl.when((l <= z) & (z < last))
        def _():
            up(l).wait_send()

        @pl.when((l >= z) & (z > 0))
        def _():
            down(l).wait_send()

        return carry

    lax.fori_loop(0, LAYERS, settle, 0)


def gather_all(values, rows_a, skip, collective_id, name, memory=pl.ANY):
    rows = values.shape[0]

    def sems(*shape):
        return pltpu.SemaphoreType.DMA(shape)

    return pl.pallas_call(
        functools.partial(gather_kernel, rows, rows_a, skip),
        out_shape=jax.ShapeDtypeStruct((MP, 4 * LAYERS, rows, BS), values.dtype),
        in_specs=[pl.BlockSpec(memory_space=memory)],
        out_specs=pl.BlockSpec(memory_space=memory),
        scratch_shapes=[
            pltpu.SemaphoreType.DMA,
            sems(LAYERS),
            sems(LAYERS),
            sems(LAYERS),
            sems(LAYERS, 3),
            sems(LAYERS, 3),
            sems(LAYERS, 3),
            sems(LAYERS, 3),
            sems(LAYERS, 5),
            sems(LAYERS, 5),
        ],
        compiler_params=pltpu.CompilerParams(
            collective_id=collective_id, has_side_effects=True, vmem_limit_bytes=32 * MIB
        ),
        cost_estimate=pl.CostEstimate(flops=0, bytes_accessed=32 * rows * BS * 4, transcendentals=0),
        name=name,
    )(values)


def reduce_kernel(
    n_ref,
    e_ref,
    out_ref,
    own_n,
    own_e,
    core_n,
    core_e,
    keep_own,
    keep_a,
    keep_b,
    keep_e,
    xs_a,
    xs_b,
    ys_b,
    ys_a,
    ys_e,
    xr_a,
    xr_b,
    yr_b,
    yr_a,
    yr_e,
    sum_n,
    sum_e,
    up_n,
    down_n,
    down_e,
    own_sem,
    core_send,
    core_recv,
    credit,
    xs_a_sem,
    xs_b_sem,
    ys_b_sem,
    ys_a_sem,
    ys_e_sem,
    xr_a_sem,
    xr_b_sem,
    yr_b_sem,
    yr_a_sem,
    yr_e_sem,
    z_n_sem,
    z_e_sem,
    up_n_sem,
    down_n_sem,
    down_e_sem,
):
    at = places()
    x, y, z, c = at["x"], at["y"], at["z"], at["c"]

    def layer_of(s):
        return LAYERS - 1 - lax.rem(s, 3)

    def rows_of(s):
        return pl.ds(pl.multiple_of((s // 3) * ROWS_N, 8), ROWS_N)

    def rows_e(s):
        return pl.ds(pl.multiple_of(s * ROWS_E, 8), ROWS_E)

    def own_loads(s):
        slot = lax.rem(s, 3)
        return (
            pltpu.make_async_copy(
                n_ref.at[:, layer_of(s) - 1, :, c, rows_of(s)], own_n.at[slot], own_sem.at[slot, 0]
            ),
            pltpu.make_async_copy(e_ref.at[:, c, rows_e(s)], own_e.at[slot], own_sem.at[slot, 1]),
        )

    def core_copies(s):
        slot = lax.rem(s, CORE_SLOTS)
        return (
            remote(
                n_ref.at[:, layer_of(s) - 1, :, 1 - c, rows_of(s)],
                core_n.at[slot],
                core_send.at[s, 0],
                core_recv.at[slot, 0],
                at["at_core"],
            ),
            remote(
                e_ref.at[:, 1 - c, rows_e(s)],
                core_e.at[slot],
                core_send.at[s, 1],
                core_recv.at[slot, 1],
                at["at_core"],
            ),
        )

    def first_copies(s):
        slot = lax.rem(s, SEND_SLOTS)
        return (
            remote(xs_a.at[slot], xr_a.at[s], xs_a_sem.at[slot], xr_a_sem.at[s], at["at_x"]),
            remote(ys_b.at[slot], yr_b.at[s], ys_b_sem.at[slot], yr_b_sem.at[s], at["at_y"]),
            remote(ys_e.at[slot], yr_e.at[s], ys_e_sem.at[slot], yr_e_sem.at[s], at["at_y"]),
        )

    def second_copies(s):
        slot = lax.rem(s, SEND_SLOTS)
        return (
            remote(ys_a.at[slot], yr_a.at[s], ys_a_sem.at[slot], yr_a_sem.at[s], at["at_y"]),
            remote(xs_b.at[slot], xr_b.at[s], xs_b_sem.at[slot], xr_b_sem.at[s], at["at_x"]),
        )

    def up_copy(s):
        slot = lax.rem(s, SUM_SLOTS)
        return remote(sum_n.at[slot], up_n.at[s], z_n_sem.at[slot], up_n_sem.at[s], at["above"])

    def down_copy(s):
        slot = lax.rem(s, SUM_SLOTS)
        return remote(sum_n.at[slot], down_n.at[s], z_n_sem.at[slot], down_n_sem.at[s], at["below"])

    def down_copy_e(s):
        slot = lax.rem(s, SUM_SLOTS)
        return remote(sum_e.at[slot], down_e.at[s], z_e_sem.at[slot], down_e_sem.at[s], at["below"])

    for s in range(2):
        for copy in own_loads(s):
            copy.start()
    greet_neighbours(at)
    for s in range(2):
        for copy in core_copies(s):
            copy.start()

    def first(s):
        @pl.when(s + 2 < PIECES)
        def _():
            for copy in own_loads(s + 2):
                copy.start()

            @pl.when(s + 2 >= CORE_SLOTS)
            def _():
                pl.semaphore_wait(credit, 1)

            for copy in core_copies(s + 2):
                copy.start()

        for copy in own_loads(s):
            copy.wait()
        for copy in core_copies(s):
            copy.wait_recv()

        @pl.when(s >= SEND_SLOTS)
        def _():
            for copy in first_copies(s - SEND_SLOTS):
                copy.wait_send()

        own, core = lax.rem(s, 3), lax.rem(s, CORE_SLOTS)
        send, keep = lax.rem(s, SEND_SLOTS), lax.rem(s, KEEP)
        a, b = pl.ds(0, ROWS_A), pl.ds(ROWS_A, ROWS_B)
        for other in range(2):
            xs_a[send, other] = own_n[own, 1 - x, other, a] + core_n[core, 1 - x, other, a]
        to_x, to_y, to_y_e = first_copies(s)
        to_x.start()
        for other in range(2):
            ys_b[send, other] = own_n[own, other, 1 - y, b] + core_n[core, other, 1 - y, b]
        to_y.start()
        ys_e[send] = own_e[own, 1 - y] + core_e[core, 1 - y]
        to_y_e.start()
        keep_own[keep] = own_n[own, x, y] + core_n[core, x, y]
        keep_a[keep] = own_n[own, x, 1 - y, a] + core_n[core, x, 1 - y, a]
        keep_b[keep] = own_n[own, 1 - x, y, b] + core_n[core, 1 - x, y, b]
        keep_e[keep] = own_e[own, y] + core_e[core, y]

        @pl.when(s + CORE_SLOTS < PIECES)
        def _():
            pl.semaphore_signal(credit, inc=1, device_id=at["at_core"], device_id_type=MESH)

    def second(s):
        to_x, to_y, _ = first_copies(s)
        to_x.wait_recv()
        to_y.wait_recv()

        @pl.when(s >= SEND_SLOTS)
        def _():
            for copy in second_copies(s - SEND_SLOTS):
                copy.wait_send()

        send, keep = lax.rem(s, SEND_SLOTS), lax.rem(s, KEEP)
        a, b = pl.ds(0, ROWS_A), pl.ds(ROWS_A, ROWS_B)
        ys_a[send] = keep_a[keep] + xr_a[s, 1 - y]
        xs_b[send] = keep_b[keep] + yr_b[s, 1 - x]
        for copy in second_copies(s):
            copy.start()
        keep_own[keep, a] = keep_own[keep, a] + xr_a[s, y]
        keep_own[keep, b] = keep_own[keep, b] + yr_b[s, x]

    def third(s):
        first_copies(s)[2].wait_recv()
        for copy in second_copies(s):
            copy.wait_recv()

        @pl.when((s >= SUM_SLOTS) & (z != layer_of(s)))
        def _():
            up_copy(s - SUM_SLOTS).wait_send()

        @pl.when((s >= SUM_SLOTS) & (z > 0))
        def _():
            down_copy_e(s - SUM_SLOTS).wait_send()

        slot, keep = lax.rem(s, SUM_SLOTS), lax.rem(s, KEEP)
        a, b = pl.ds(0, ROWS_A), pl.ds(ROWS_A, ROWS_B)
        sum_n[slot, a] = keep_own[keep, a] + yr_a[s]
        sum_n[slot, b] = keep_own[keep, b] + xr_b[s]
        sum_e[slot] = keep_e[keep] + yr_e[s]

    def along(s, hop):
        slot = lax.rem(s, SUM_SLOTS)
        layer = layer_of(s)
        last = LAYERS - 1
        away = jnp.where(z < layer, z, jnp.where(z > layer, last - z, jnp.maximum(z, last - z)))

        @pl.when(away == hop)
        def _():
            @pl.when((z > 0) & (z <= layer))
            def _():
                up_copy(s).wait_recv()
                sum_n[slot] = sum_n[slot] + up_n[s]

            @pl.when((z < last) & (z >= layer))
            def _():
                down_copy(s).wait_recv()
                sum_n[slot] = sum_n[slot] + down_n[s]

            @pl.when(z < layer)
            def _():
                up_copy(s).start()

            @pl.when(z > layer)
            def _():
                down_copy(s).start()

            @pl.when(z == layer)
            def _():
                out_ref[rows_of(s)] = sum_n[slot]

        away_e = jnp.where(z == 0, last, last - z)

        @pl.when(away_e == hop)
        def _():
            @pl.when(z < last)
            def _():
                down_copy_e(s).wait_recv()
                sum_e[slot] = sum_e[slot] + down_e[s]

            @pl.when(z > 0)
            def _():
                down_copy_e(s).start()

            @pl.when(z == 0)
            def _():
                out_ref[rows_e(s)] = sum_e[slot]

    def guarded(run, s):
        @pl.when((s >= 0) & (s < PIECES))
        def _():
            run(s)

    def step(t, carry):
        guarded(first, t)
        guarded(second, t - LAG)
        guarded(third, t - 2 * LAG)
        for hop in range(LAYERS):
            guarded(functools.partial(along, hop=hop), t - 2 * LAG - hop * HOP_LAG)
        return carry

    lax.fori_loop(0, PIECES + 2 * LAG + (LAYERS - 1) * HOP_LAG, step, 0)

    def drain_sends(i, carry):
        s = PIECES - SEND_SLOTS + i
        for copy in first_copies(s) + second_copies(s):
            copy.wait_send()
        return carry

    lax.fori_loop(0, SEND_SLOTS, drain_sends, 0)

    def drain_sums(i, carry):
        s = PIECES - SUM_SLOTS + i

        @pl.when(z != layer_of(s))
        def _():
            up_copy(s).wait_send()

        @pl.when(z > 0)
        def _():
            down_copy_e(s).wait_send()

        return carry

    lax.fori_loop(0, SUM_SLOTS, drain_sums, 0)

    def drain_core(s, carry):
        for copy in core_copies(s):
            copy.wait_send()
        return carry

    lax.fori_loop(0, PIECES, drain_core, 0)

    @pl.when(z == 0)
    def _():
        out_ref[pl.ds(PIECES * ROWS_E, CHUNK - PIECES * ROWS_E)] = jnp.zeros(
            (CHUNK - PIECES * ROWS_E, BS), jnp.float32
        )


def reduce_to_owners(rest, embed):
    def room(*shape):
        return pltpu.VMEM(shape + (BS,), jnp.float32)

    def sems(*shape):
        return pltpu.SemaphoreType.DMA(shape)

    return pl.pallas_call(
        reduce_kernel,
        out_shape=jax.ShapeDtypeStruct((CHUNK, BS), jnp.float32),
        in_specs=[pl.BlockSpec(memory_space=pl.ANY)] * 2,
        out_specs=pl.BlockSpec(memory_space=pltpu.VMEM),
        scratch_shapes=[
            room(3, 2, 2, ROWS_N),
            room(3, 2, ROWS_E),
            room(CORE_SLOTS, 2, 2, ROWS_N),
            room(CORE_SLOTS, 2, ROWS_E),
            room(KEEP, ROWS_N),
            room(KEEP, ROWS_A),
            room(KEEP, ROWS_B),
            room(KEEP, ROWS_E),
            room(SEND_SLOTS, 2, ROWS_A),
            room(SEND_SLOTS, ROWS_B),
            room(SEND_SLOTS, 2, ROWS_B),
            room(SEND_SLOTS, ROWS_A),
            room(SEND_SLOTS, ROWS_E),
            room(PIECES, 2, ROWS_A),
            room(PIECES, ROWS_B),
            room(PIECES, 2, ROWS_B),
            room(PIECES, ROWS_A),
            room(PIECES, ROWS_E),
            room(SUM_SLOTS, ROWS_N),
            room(SUM_SLOTS, ROWS_E),
            room(PIECES, ROWS_N),
            room(PIECES, ROWS_N),
            room(PIECES, ROWS_E),
            sems(3, 2),
            sems(PIECES, 2),
            sems(CORE_SLOTS, 2),
            pltpu.SemaphoreType.REGULAR,
            sems(SEND_SLOTS),
            sems(SEND_SLOTS),
            sems(SEND_SLOTS),
            sems(SEND_SLOTS),
            sems(SEND_SLOTS),
            sems(PIECES),
            sems(PIECES),
            sems(PIECES),
            sems(PIECES),
            sems(PIECES),
            sems(SUM_SLOTS),
            sems(SUM_SLOTS),
            sems(PIECES),
            sems(PIECES),
            sems(PIECES),
        ],
        compiler_params=pltpu.CompilerParams(
            collective_id=1, has_side_effects=True, vmem_limit_bytes=58 * MIB
        ),
        cost_estimate=pl.CostEstimate(flops=0, bytes_accessed=100 * MIB, transcendentals=0),
        name="reduce_to_owners",
    )(rest, embed)


def blocks_kernel(first_block, per_row, step_rows, transposed, has_buffer, *refs):
    x_ref, g_ref = refs[:2]
    out_ref, tiles, sems = refs[-3:]
    m, i = pl.program_id(0), pl.program_id(1)
    steps = pl.num_programs(1)
    at = m * steps + i
    slot = lax.rem(at, 2)
    total = pl.num_programs(0) * steps

    def drain(which):
        pltpu.make_async_copy(tiles.at[which], tiles.at[which], sems.at[which]).wait()

    @pl.when(at >= 2)
    def _():
        drain(slot)

    tiles[slot] = dot(x_ref[...], g_ref[...], ((0,), (1,) if transposed else (0,)))
    for r in range(step_rows):
        for c in range(per_row):
            block = first_block + (i * step_rows + r) * per_row + c
            chunk, at_row = block // 24, lax.rem(block, 24) * BS
            pltpu.make_async_copy(
                tiles.at[slot, r * BS : (r + 1) * BS, c * BS : (c + 1) * BS],
                out_ref.at[m, chunk, pl.ds(pl.multiple_of(at_row, BS), BS)],
                sems.at[slot],
            ).start()

    @pl.when(at == total - 1)
    def _():
        drain(slot)

        @pl.when(total > 1)
        def _():
            drain(1 - slot)


def grad_blocks(x, g, parts, rows, per_row, step_rows, first_block, split_x, split_g, buffer, name, chunks=12, depth=CHUNK, transposed=False):
    steps = rows // step_rows
    tokens = x.shape[0]
    width = per_row * BS
    x_spec = pl.BlockSpec(
        (tokens, step_rows * BS), (lambda m, i: (0, m * steps + i)) if split_x else (lambda m, i: (0, i))
    )
    if transposed:
        g_spec = pl.BlockSpec((width, tokens), lambda m, i: (0, 0))
    else:
        g_spec = pl.BlockSpec((tokens, width), (lambda m, i: (0, m)) if split_g else (lambda m, i: (0, 0)))
    anywhere = pl.BlockSpec(memory_space=pl.ANY)
    operands = [x, g] + ([] if buffer is None else [buffer])
    return pl.pallas_call(
        functools.partial(
            blocks_kernel, first_block, per_row, step_rows, transposed, buffer is not None
        ),
        grid=(parts, steps),
        out_shape=jax.ShapeDtypeStruct((parts, chunks, depth, BS), jnp.float32),
        in_specs=[x_spec, g_spec] + ([] if buffer is None else [anywhere]),
        out_specs=anywhere,
        input_output_aliases={} if buffer is None else {2: 0},
        scratch_shapes=[
            pltpu.VMEM((2, step_rows * BS, width), jnp.float32),
            pltpu.SemaphoreType.DMA((2,)),
        ],
        compiler_params=pltpu.CompilerParams(vmem_limit_bytes=32 * MIB),
        cost_estimate=pl.CostEstimate(
            flops=2 * tokens * parts * rows * BS * width,
            bytes_accessed=parts * rows * BS * width * 4,
            transcendentals=0,
        ),
        name=name,
    )(*operands)


def fast_mesh():
    return lax.axis_size("dp") == 4 * LAYERS and lax.axis_size("mp") == MP


def gather_weights(blocks):
    low = blocks.astype(jnp.bfloat16)[0, 0]
    if fast_mesh():
        gathered = gather_all(low.reshape(-1, BS), 8 * BS, True, 2, "gather_weights")
    else:
        gathered = lax.all_gather(low, ("dp", "mp"), axis=0, tiled=False)
        gathered = gathered.reshape((-1, MP) + low.shape).swapaxes(0, 1)
    return gathered.reshape(MP, -1, BS, BS)


def sum_sums(values):
    if fast_mesh():
        return jnp.sum(gather_all(values, 8, False, 3, "gather_sums", pltpu.VMEM), (0, 1))
    return lax.psum(values, ("dp", "mp"))


def swap_mp(values):
    return lax.ppermute(values, "mp", [(0, 1), (1, 0)])


def reduce_plain(rest, embed):
    part = lax.axis_index("mp")
    own = (jnp.arange(MP) == part).astype(jnp.float32)
    first = embed.reshape(1, -1, BS, BS) * own[:, None, None, None]
    dp = lax.axis_size("dp")
    every = jnp.concatenate([first, rest], 1).reshape(MP, dp, -1, BS, BS).transpose(1, 0, 2, 3, 4)
    return lax.psum_scatter(
        every.reshape(dp * MP, -1, BS, BS), ("dp", "mp"), scatter_dimension=0, tiled=True
    )[0]


def layer_norm(values):
    center = values - jnp.mean(values, -1, keepdims=True)
    spread = jnp.mean(center * center, -1, keepdims=True)
    inverse = lax.rsqrt(spread + 1e-06)
    return center * inverse, inverse


def layer_norm_back(back, normal, inverse, gain):
    scaled = back * gain
    mean = jnp.mean(scaled, -1, keepdims=True)
    along = jnp.mean(scaled * normal, -1, keepdims=True)
    return inverse * (scaled - mean - normal * along)


def shampoo_step(blocks, grads, stat_pair, root_pair, moment, veloc):
    stat_left = beta_stat * stat_pair[0] + (1 - beta_stat) * jnp.einsum(
        "cij,ckj->cik", grads, grads, precision=HIGHEST
    )
    stat_right = beta_stat * stat_pair[1] + (1 - beta_stat) * jnp.einsum(
        "cji,cjk->cik", grads, grads, precision=HIGHEST
    )
    moment_new = beta_one * moment + (1 - beta_one) * grads
    veloc_new = beta_two * veloc + (1 - beta_two) * grads * grads
    moment_hat = moment_new / (1 - beta_one**STEP)
    adam_dir = moment_hat / (jnp.sqrt(veloc_new / (1 - beta_two**STEP)) + 1e-08)
    left_side = jnp.einsum("cij,cjk->cik", root_pair[0], moment_hat, precision=HIGHEST)
    precond = jnp.einsum("cij,cjk->cik", left_side, root_pair[1], precision=HIGHEST)
    ratio = jnp.sqrt(
        (jnp.mean(adam_dir * adam_dir, (-2, -1), keepdims=True) + 1e-06)
        / (jnp.mean(precond * precond, (-2, -1), keepdims=True) + 1e-06)
    )
    block_new = blocks - learn_rate * (precond * ratio + decay_rate * blocks)
    return (block_new, jnp.stack([stat_left, stat_right]), moment_new, veloc_new)


def adam_step(param, grads, moment, veloc):
    moment_new = beta_one * moment + (1 - beta_one) * grads
    veloc_new = beta_two * veloc + (1 - beta_two) * grads * grads
    direction = (
        moment_new / (1 - beta_one**STEP) / (jnp.sqrt(veloc_new / (1 - beta_two**STEP)) + 1e-08)
    )
    return (param - learn_rate * direction, moment_new, veloc_new)


def halves(matrix):
    return matrix[:, :HALF], matrix[:, HALF:]


def local(
    patches,
    labels,
    batch_ids,
    blocks,
    statistics,
    roots,
    moments,
    velocity,
    aux,
    aux_moment,
    aux_velocity,
):
    part = lax.axis_index("mp")
    all_crops = lax.axis_size("dp") * MP
    pieces = split_aux(aux)
    gain, shift = pieces["norm_gain"], pieces["norm_bias"]

    gathered = gather_weights(blocks)
    starts = [0]
    for height, breadth in LOCAL_SHAPES:
        starts.append(starts[-1] + height * breadth // (BS * BS))

    def matrix_of(which, m):
        return from_blocks(gathered[m, starts[which] : starts[which + 1]], *LOCAL_SHAPES[which])

    own_embed = lax.dynamic_index_in_dim(gathered[:, :E_BLOCKS], part, 0, False)
    w_embed = from_blocks(own_embed, *LOCAL_SHAPES[0])
    w_qkv = jnp.concatenate([matrix_of(1, m) for m in range(MP)], 1)
    w_proj = jnp.concatenate([matrix_of(2, m) for m in range(MP)], 0)
    w_up = jnp.concatenate([matrix_of(3, m) for m in range(MP)], 1)
    w_down = jnp.concatenate([matrix_of(4, m) for m in range(MP)], 0)
    w_deconv = jnp.concatenate([matrix_of(5, m) for m in range(MP)], 0)

    other_rows = lax.dynamic_slice_in_dim(patches, (1 - part) * NTOK, NTOK, 0)
    own_rows = lax.dynamic_slice_in_dim(patches, part * NTOK, NTOK, 0)
    received = swap_mp(dot_nn(other_rows, w_embed))
    stream_zero = (
        dot_nn(own_rows, w_embed) + received + pieces["positions"] + pieces["embed_bias"]
    )
    normal_one, inverse_one = layer_norm(stream_zero)
    normed_one = (normal_one * gain[0] + shift[0]).astype(jnp.bfloat16)
    q_bias, v_bias = pieces["qv_bias"][0], pieces["qv_bias"][1]
    nothing = jnp.zeros((HALF,), jnp.float32)
    qkv_bias = jnp.concatenate(
        [q_bias[:HALF], nothing, v_bias[:HALF], q_bias[HALF:], nothing, v_bias[HALF:]]
    )
    qkv = (dot_nn(normed_one, w_qkv) + qkv_bias).astype(jnp.bfloat16)
    mixed, lse = attention_forward(qkv)
    stream_one = stream_zero + dot_nn(mixed, w_proj) + pieces["proj_bias"]
    normal_two, inverse_two = layer_norm(stream_one)
    normed_two = (normal_two * gain[1] + shift[1]).astype(jnp.bfloat16)
    hidden = dot_nn(normed_two, w_up) + pieces["up_bias"]
    active_value, hidden_slope = gelu_and_slope(hidden)
    active = active_value.astype(jnp.bfloat16)
    stream_two = stream_one + dot_nn(active, w_down) + pieces["down_bias"]
    streams = [s.astype(jnp.bfloat16) for s in (stream_zero, stream_one, stream_two)]
    stacked = jnp.concatenate([halves(s)[m] for m in range(MP) for s in streams], 1)
    up_t = dot(w_deconv, stacked, ((0,), (1,)))

    conv_weight = pieces["conv_weight"].astype(jnp.bfloat16).reshape(27, DEC, CF)
    conv_low = conv_weight.transpose(0, 2, 1).reshape(27 * CF, DEC)
    conv_t = conv_weight.transpose(1, 0, 2).reshape(DEC, 27 * CF)
    head_weight = jnp.pad(pieces["head_weight"], ((0, 0), (0, CF - NCLS))).astype(jnp.bfloat16)
    head_bias = jnp.pad(pieces["head_bias"], (0, CF - NCLS)).reshape(CF, 1)
    grid_labels = (
        labels.reshape(GS, 2, GS, 2, GS, 2).transpose(1, 3, 5, 0, 2, 4).reshape(8, NTOK)
    )
    batch = jnp.broadcast_to(batch_ids.reshape(1, 1), (1, BS))
    conv_in, grid_slope, conv_slope, features, chance, sums = decoder_forward(
        up_t,
        pieces["deconv_bias"].reshape(DEC, 1),
        conv_low,
        pieces["conv_bias"].reshape(CF, 1),
        head_weight.T,
        head_bias,
        grid_labels,
        batch,
    )
    sums = sum_sums(sums)
    gu_t, conv_grad, head_grad, small, deconv_bias_grad = decoder_backward(
        all_crops,
        sums,
        batch,
        grid_labels,
        chance,
        features,
        conv_slope,
        grid_slope,
        conv_in,
        conv_t,
        head_weight,
    )
    loss_value = small[0, 2]
    grad_head_bias = small[:NCLS, 0]
    grad_conv_bias = small[:, 1]
    grad_deconv_bias = deconv_bias_grad[:, 0]
    grad_conv_weight = conv_grad.reshape(27, CF, DEC).transpose(0, 2, 1)
    grad_head_weight = head_grad[:, :NCLS]

    stacked_back = dot(gu_t, w_deconv, ((0,), (1,)))
    back_zero_s, back_one_s, back_two = [
        jnp.concatenate([stacked_back[:, (3 * m + s) * HALF : (3 * m + s + 1) * HALF] for m in range(MP)], 1)
        for s in range(3)
    ]
    grad_down_bias = jnp.sum(back_two, 0)
    two_low = back_two.astype(jnp.bfloat16)
    back_hidden = (hidden_slope * dot_nt(two_low, w_down)).astype(jnp.bfloat16)
    grad_up_bias = jnp.sum(back_hidden.astype(jnp.float32), 0)
    back_normed_two = dot_nt(back_hidden, w_up)
    grad_gain_two = jnp.sum(back_normed_two * normal_two, 0)
    grad_shift_two = jnp.sum(back_normed_two, 0)
    back_one = (
        back_two + back_one_s + layer_norm_back(back_normed_two, normal_two, inverse_two, gain[1])
    )
    grad_proj_bias = jnp.sum(back_one, 0)
    one_low = back_one.astype(jnp.bfloat16)
    back_mixed = dot_nt(one_low, w_proj).astype(jnp.bfloat16)
    back_q, back_k, back_v = attention_backward(qkv, back_mixed, lse)
    back_qkv = jnp.concatenate(
        [halves(piece)[m] for m in range(MP) for piece in (back_q, back_k, back_v)], 1
    )
    grad_query_bias = jnp.sum(back_q.astype(jnp.float32), 0)
    grad_value_bias = jnp.sum(back_v.astype(jnp.float32), 0)
    back_normed_one = dot_nt(back_qkv, w_qkv)
    grad_gain_one = jnp.sum(back_normed_one * normal_one, 0)
    grad_shift_one = jnp.sum(back_normed_one, 0)
    back_zero = (
        back_one + back_zero_s + layer_norm_back(back_normed_one, normal_one, inverse_one, gain[0])
    )
    zero_low = back_zero.astype(jnp.bfloat16)
    other_low = swap_mp(zero_low)
    zero_pair = jnp.where(
        part == 0,
        jnp.concatenate([zero_low, other_low]),
        jnp.concatenate([other_low, zero_low]),
    )

    fast = fast_mesh()
    depth = CHUNK if fast else 24 * BS
    rest_grads = None
    for name, x, g, rows, per_row, start, split_x, split_g in (
        ("grad_deconv", stacked, gu_t, 9, 8, 216, True, False),
        ("grad_down", active, two_low, 12, 6, 144, True, False),
        ("grad_up", normed_two, back_hidden, 6, 12, 72, False, True),
        ("grad_proj", mixed, one_low, 3, 6, 54, True, False),
        ("grad_qkv", normed_one, back_qkv, 6, 9, 0, False, True),
    ):
        rest_grads = grad_blocks(
            x, g, MP, rows, per_row, 3, start, split_x, split_g, rest_grads, name, 12, depth, g is gu_t
        )
    embed_grads = grad_blocks(
        patches, zero_pair, 1, 16, 6, 4, 0, False, False, None, "grad_embed", 4, 24 * BS
    )
    late = jnp.stack(
        [
            grad_gain_one,
            grad_gain_two,
            grad_shift_one,
            grad_shift_two,
            grad_query_bias,
            grad_value_bias,
            grad_proj_bias,
        ]
    )
    rest = jnp.concatenate(
        [
            late.reshape(-1),
            grad_up_bias,
            grad_down_bias,
            grad_deconv_bias,
            grad_conv_weight.reshape(-1),
            grad_conv_bias,
            grad_head_weight.reshape(-1),
            grad_head_bias,
        ]
    )
    aux_parts = jnp.concatenate([back_zero.reshape(-1), rest])
    if fast:
        room = 12 * MP * AUX_ROWS * BS
        aux_rows = jnp.pad(aux_parts, (0, room - aux_parts.shape[0])).reshape(MP, 12, AUX_ROWS, BS)
        rest_grads = lax.dynamic_update_slice(rest_grads, aux_rows, (0, 0, 24 * BS, 0))
        reduced = reduce_to_owners(
            rest_grads.reshape(MP, LAYERS - 1, 2, 2, CHUNK, BS), embed_grads.reshape(2, 2, 24 * BS, BS)
        )
        owned = reduced[: 24 * BS].reshape(24, BS, BS)
        square = jnp.broadcast_to(jnp.sum(owned * owned).reshape(1, 1), (8, BS))
        gathered_aux = gather_all(
            jnp.concatenate([reduced[24 * BS :], square]), 64, False, 4, "gather_aux"
        )
        block_square = jnp.sum(gathered_aux[:, :, AUX_ROWS, 0])
        aux_sum = gathered_aux[:, 4:, :AUX_ROWS].reshape(-1)
    else:
        owned = reduce_plain(rest_grads.reshape(MP, -1, BS, BS), embed_grads)
        aux_sum = lax.psum(aux_parts, ("dp", "mp"))
        block_square = lax.psum(jnp.sum(owned * owned), ("dp", "mp"))
    positions_sum = aux_sum[: NTOK * D]
    embed_bias_sum = jnp.sum(positions_sum.reshape(NTOK, D), 0)
    aux_total = jnp.concatenate([positions_sum, embed_bias_sum, aux_sum[NTOK * D : NAUX - D]])
    grad_norm = jnp.sqrt(block_square + jnp.sum(aux_total * aux_total))
    clip_scale = clip_value / jnp.maximum(grad_norm, clip_value)
    block_new, stat_new, moment_new, veloc_new = shampoo_step(
        blocks[0, 0],
        owned * clip_scale,
        statistics[:, 0, 0],
        roots[:, 0, 0],
        moments[0, 0],
        velocity[0, 0],
    )
    aux_new, aux_moment_new, aux_veloc_new = adam_step(
        aux, aux_total * clip_scale, aux_moment, aux_velocity
    )
    return (
        loss_value,
        grad_norm,
        block_new[None, None],
        stat_new[:, None, None],
        moment_new[None, None],
        veloc_new[None, None],
        aux_new,
        aux_moment_new,
        aux_veloc_new,
    )


def solution(mesh):
    block_spec = P("dp", "mp", None, None, None)
    pair_spec = P(None, "dp", "mp", None, None, None)
    placed = (
        P("dp", "mp"),
        P(("dp", "mp"), None),
        P(("dp", "mp")),
        block_spec,
        pair_spec,
        pair_spec,
        block_spec,
        block_spec,
        P(),
        P(),
        P(),
    )
    return jax.shard_map(
        local,
        mesh=mesh,
        in_specs=placed,
        out_specs=(P(), P(), block_spec, pair_spec, block_spec, block_spec, P(), P(), P()),
        check_vma=False,
    )
```

```python
import functools
import math

import jax
import jax.numpy as jnp
from jax import lax
from jax.experimental import pallas as pl
from jax.experimental.pallas import tpu as pltpu
from jax.sharding import PartitionSpec as P

D = 768
HDIM = 64
FF = 3072
PV = 4096
DEC = 128
CF = 16
NCLS = 14
GS = 8
MB = 4
STEP = 10
BS = 128
NTOK = 512
CELLS = 4096
MP = 2
HALF = D // MP
E_BLOCKS = PV // MP * D // (BS * BS)

HIGHEST = lax.Precision.HIGHEST
MESH = pl.DeviceIdType.MESH
beta_one = 0.9
beta_two = 0.999
beta_stat = 0.95
learn_rate = 0.02
decay_rate = 0.01
clip_value = 0.005
MIB = 1024 * 1024

OFFSETS = [(a, b, c) for a in range(3) for b in range(3) for c in range(3)]
PARITIES = [(i, j, k) for i in range(2) for j in range(2) for k in range(2)]


def dot(a, b, dims):
    return lax.dot_general(a, b, (dims, ((), ())), preferred_element_type=jnp.float32)


def dot_nn(a, b):
    return dot(a, b, ((1,), (0,)))


def dot_nt(a, b):
    return dot(a, b, ((1,), (1,)))


def dot_tn(a, b):
    return dot(a, b, ((0,), (0,)))


def gelu_cdf(v):
    return 0.5 * (1.0 + lax.erf(v * (0.5**0.5)))


def gelu_and_slope(v):
    cdf = gelu_cdf(v)
    density = jnp.exp(-0.5 * v * v) * (1.0 / math.sqrt(2.0 * math.pi))
    return v * cdf, cdf + v * density


def aux_layout():
    return [
        ("positions", (NTOK, D)),
        ("embed_bias", (D,)),
        ("norm_gain", (2, D)),
        ("norm_bias", (2, D)),
        ("qv_bias", (2, D)),
        ("proj_bias", (D,)),
        ("up_bias", (FF,)),
        ("down_bias", (D,)),
        ("deconv_bias", (DEC,)),
        ("conv_weight", (27 * DEC, CF)),
        ("conv_bias", (CF,)),
        ("head_weight", (CF, NCLS)),
        ("head_bias", (NCLS,)),
    ]


NAUX = sum(math.prod(shape) for _, shape in aux_layout())


def split_aux(vector):
    pieces = {}
    offset = 0
    for section_name, section_shape in aux_layout():
        length = math.prod(section_shape)
        pieces[section_name] = vector[offset : offset + length].reshape(section_shape)
        offset += length
    return pieces


def attention_forward_kernel(qkv_q, qkv_k, qkv_v, mixed_ref, lse_ref):
    q, k, v = qkv_q[...], qkv_k[...], qkv_v[...]
    v_t = v.astype(jnp.float32).T.astype(jnp.bfloat16)
    outs = []
    for h in range(2):
        cols = slice(h * HDIM, (h + 1) * HDIM)
        scores = dot_nt(k[:, cols], q[:, cols]) * 0.125
        top = jnp.max(scores, 0, keepdims=True)
        weights = jnp.exp(scores - top)
        total = jnp.sum(weights, 0, keepdims=True)
        attention = (weights * (1.0 / total)).astype(jnp.bfloat16)
        outs.append(dot_nn(v_t[cols], attention))
        lse_ref[0, h : h + 1, :] = top + jnp.log(total)
    mixed_ref[...] = jnp.concatenate(outs, 0).T.astype(jnp.bfloat16)


def attention_backward_kernel(qkv_q, qkv_k, qkv_v, gm_ref, lse_ref, gq_ref, gk_ref, gv_ref):
    q, k, v, gm = qkv_q[...], qkv_k[...], qkv_v[...], gm_ref[...]
    k_t = k.astype(jnp.float32).T.astype(jnp.bfloat16)
    gq_t = []
    for h in range(2):
        cols = slice(h * HDIM, (h + 1) * HDIM)
        scores = dot_nt(k[:, cols], q[:, cols]) * 0.125
        attention = jnp.exp(scores - lse_ref[0, h : h + 1, :])
        back = dot_nt(v[:, cols], gm[:, cols])
        gv_ref[:, cols] = dot_nn(attention.astype(jnp.bfloat16), gm[:, cols]).astype(jnp.bfloat16)
        mean = jnp.sum(back * attention, 0, keepdims=True)
        gs = (attention * (back - mean)).astype(jnp.bfloat16)
        gk_ref[:, cols] = (dot_nn(gs, q[:, cols]) * 0.125).astype(jnp.bfloat16)
        gq_t.append(dot_nn(k_t[cols], gs) * 0.125)
    gq_ref[...] = jnp.concatenate(gq_t, 0).T.astype(jnp.bfloat16)


def qkv_spec(part):
    return pl.BlockSpec((NTOK, BS), lambda i, part=part: (0, (i // 3) * 9 + part * 3 + i % 3))


def attention_forward(qkv):
    return pl.pallas_call(
        attention_forward_kernel,
        grid=(6,),
        out_shape=(
            jax.ShapeDtypeStruct((NTOK, D), jnp.bfloat16),
            jax.ShapeDtypeStruct((6, 2, NTOK), jnp.float32),
        ),
        in_specs=[qkv_spec(0), qkv_spec(1), qkv_spec(2)],
        out_specs=(
            pl.BlockSpec((NTOK, BS), lambda i: (0, i)),
            pl.BlockSpec((1, 2, NTOK), lambda i: (i, 0, 0)),
        ),
        compiler_params=pltpu.CompilerParams(vmem_limit_bytes=32 * MIB),
        cost_estimate=pl.CostEstimate(
            flops=12 * 4 * NTOK * NTOK * HDIM,
            bytes_accessed=NTOK * D * 8,
            transcendentals=12 * NTOK * NTOK,
        ),
        name="attention_forward",
    )(qkv, qkv, qkv)


def attention_backward(qkv, gm, lse):
    pair = pl.BlockSpec((NTOK, BS), lambda i: (0, i))
    return pl.pallas_call(
        attention_backward_kernel,
        grid=(6,),
        out_shape=(jax.ShapeDtypeStruct((NTOK, D), jnp.bfloat16),) * 3,
        in_specs=[
            qkv_spec(0),
            qkv_spec(1),
            qkv_spec(2),
            pair,
            pl.BlockSpec((1, 2, NTOK), lambda i: (i, 0, 0)),
        ],
        out_specs=(pair,) * 3,
        compiler_params=pltpu.CompilerParams(vmem_limit_bytes=32 * MIB),
        cost_estimate=pl.CostEstimate(
            flops=12 * 10 * NTOK * NTOK * HDIM,
            bytes_accessed=NTOK * D * 14,
            transcendentals=12 * NTOK * NTOK,
        ),
        name="attention_backward",
    )(qkv, qkv, qkv, gm, lse)


def source_of(parity, step):
    at = parity + step
    if at < 0:
        return 1, -1
    if at > 1:
        return 0, 1
    return at, 0


def shift_plan(offset, parity, sign):
    found = [source_of(par, sign * (off - 1)) for off, par in zip(offset, parity)]
    bits = [f[0] for f in found]
    steps = [f[1] for f in found]
    return bits[0] * 4 + bits[1] * 2 + bits[2], steps


def token_masks(tokens):
    at = (tokens // (GS * GS), (tokens // GS) % GS, tokens % GS)
    masks = {}
    for axis in range(3):
        masks[axis, 1] = at[axis] < GS - 1
        masks[axis, -1] = at[axis] > 0
    return masks


def shifted(values, steps, masks):
    delta = steps[0] * GS * GS + steps[1] * GS + steps[2]
    if delta == 0 and not any(steps):
        return values
    moved = pltpu.roll(values, (-delta) % NTOK, 1)
    keep = None
    for axis in range(3):
        if steps[axis]:
            mask = masks[axis, steps[axis]]
            keep = mask if keep is None else keep & mask
    return jnp.where(keep, moved, 0.0)


def lanes(parity):
    return slice(parity * NTOK, (parity + 1) * NTOK)


def decoder_forward_kernel(
    up_ref,
    deconv_bias_ref,
    conv_ref,
    conv_bias_ref,
    head_ref,
    head_bias_ref,
    labels_ref,
    batch_ref,
    conv_in_ref,
    grid_slope_ref,
    conv_slope_ref,
    features_ref,
    chance_ref,
    sums_ref,
    conved_ref,
):
    tokens = lax.broadcasted_iota(jnp.int32, (CF, NTOK), 1)
    masks = token_masks(tokens)
    for parity in range(8):
        conved_ref[:, lanes(parity)] = jnp.broadcast_to(conv_bias_ref[...], (CF, NTOK))
    for parity in range(8):
        cell = up_ref[parity * DEC : (parity + 1) * DEC, :] + deconv_bias_ref[...]
        value, slope = gelu_and_slope(cell)
        low = value.astype(jnp.bfloat16)
        conv_in_ref[:, lanes(parity)] = low
        grid_slope_ref[:, lanes(parity)] = slope
        products = dot_nn(conv_ref[...], low)
        for at, offset in enumerate(OFFSETS):
            target, back_steps = shift_plan(offset, PARITIES[parity], -1)
            forward = [-s for s in back_steps]
            piece = shifted(products[at * CF : (at + 1) * CF, :], forward, masks)
            conved_ref[:, lanes(target)] += piece
    rows = lax.broadcasted_iota(jnp.int32, (CF, NTOK), 0)
    hit = jnp.zeros((CF, 1), jnp.float32)
    predicted = jnp.zeros((CF, 1), jnp.float32)
    truth = jnp.zeros((CF, 1), jnp.float32)
    entropy = jnp.zeros((CF, 1), jnp.float32)
    for parity in range(8):
        value, slope = gelu_and_slope(conved_ref[:, lanes(parity)])
        conv_slope_ref[:, lanes(parity)] = slope
        features = value.astype(jnp.bfloat16)
        features_ref[:, lanes(parity)] = features
        logits = dot_nn(head_ref[...], features) + head_bias_ref[...]
        logits = jnp.where(rows < NCLS, logits, -1e30)
        center = logits - jnp.max(logits, 0, keepdims=True)
        log_prob = center - jnp.log(jnp.sum(jnp.exp(center), 0, keepdims=True))
        chance = jnp.exp(log_prob)
        target = (rows == labels_ref[parity : parity + 1, :]).astype(jnp.float32)
        chance_ref[:, lanes(parity)] = chance
        hit += jnp.sum(chance * target, 1, keepdims=True)
        predicted += jnp.sum(chance, 1, keepdims=True)
        truth += jnp.sum(target, 1, keepdims=True)
        entropy -= jnp.sum(jnp.where(target > 0, log_prob, 0.0), 1, keepdims=True)
    lane = lax.broadcasted_iota(jnp.int32, (CF, BS), 1)
    base = batch_ref[...] * 3
    sums_ref[...] = (
        jnp.where(lane == base, hit, 0.0)
        + jnp.where(lane == base + 1, predicted, 0.0)
        + jnp.where(lane == base + 2, truth, 0.0)
        + jnp.where(lane == 3 * MB, entropy, 0.0)
    )


def decoder_backward_kernel(
    all_crops,
    sums_ref,
    batch_ref,
    labels_ref,
    chance_ref,
    features_ref,
    conv_slope_ref,
    grid_slope_ref,
    conv_in_ref,
    conv_t_ref,
    head_t_ref,
    gu_ref,
    conv_grad_ref,
    head_grad_ref,
    small_ref,
    deconv_grad_ref,
    spread_ref,
):
    sums = sums_ref[...]
    lane = lax.broadcasted_iota(jnp.int32, (CF, BS), 1)
    row = lax.broadcasted_iota(jnp.int32, (CF, BS), 0)
    live = (lane < 3 * MB) & (lane % 3 == 0) & (row < NCLS)
    under = pltpu.roll(sums, BS - 1, 1) + pltpu.roll(sums, BS - 2, 1) + 1.0
    under = jnp.where(live, under, 1.0)
    over = 2.0 * sums + 1.0
    dice = jnp.where(live, over / under, 0.0)
    mean_dice = jnp.sum(jnp.sum(dice, 1, keepdims=True), 0, keepdims=True) / (NCLS * MB)
    entropy_lane = jnp.where(lane == 3 * MB, sums, 0.0)
    entropy = jnp.sum(jnp.sum(entropy_lane, 1, keepdims=True), 0, keepdims=True)
    loss = entropy / (all_crops * CELLS) + (1.0 - mean_dice)
    own = live & (lane == batch_ref[...] * 3)
    d_hit = jnp.sum(jnp.where(own, -2.0 / (MB * NCLS) / under, 0.0), 1, keepdims=True)
    d_predicted = jnp.sum(
        jnp.where(own, (1.0 / (MB * NCLS)) * over / (under * under), 0.0), 1, keepdims=True
    )
    tokens = lax.broadcasted_iota(jnp.int32, (CF, NTOK), 1)
    masks = token_masks(tokens)
    rows = lax.broadcasted_iota(jnp.int32, (CF, NTOK), 0)
    head_bias = jnp.zeros((CF, 1), jnp.float32)
    conv_bias = jnp.zeros((CF, 1), jnp.float32)
    head_grad = jnp.zeros((CF, CF), jnp.float32)
    for parity in range(8):
        chance = chance_ref[:, lanes(parity)]
        target = (rows == labels_ref[parity : parity + 1, :]).astype(jnp.float32)
        back = (d_hit * target + d_predicted) * chance - target * (1.0 / (all_crops * CELLS))
        logits = back - chance * jnp.sum(back, 0, keepdims=True)
        head_bias += jnp.sum(logits, 1, keepdims=True)
        low = logits.astype(jnp.bfloat16)
        head_grad += dot_nt(features_ref[:, lanes(parity)], low)
        conved = conv_slope_ref[:, lanes(parity)] * dot_nn(head_t_ref[...], low)
        conv_bias += jnp.sum(conved, 1, keepdims=True)
        rounded = conved.astype(jnp.bfloat16).astype(jnp.float32)
        for at, offset in enumerate(OFFSETS):
            target_cell, steps = shift_plan(offset, PARITIES[parity], 1)
            piece = shifted(rounded, [-s for s in steps], masks)
            spread_ref[at * CF : (at + 1) * CF, lanes(target_cell)] = piece.astype(jnp.bfloat16)
    head_grad_ref[...] = head_grad
    small_ref[...] = (
        jnp.where(lane == 0, head_bias, 0.0)
        + jnp.where(lane == 1, conv_bias, 0.0)
        + jnp.where(lane == 2, loss, 0.0)
    )
    conv_grad = jnp.zeros((27 * CF, DEC), jnp.float32)
    deconv_grad = jnp.zeros((DEC, 1), jnp.float32)
    for parity in range(8):
        spread = spread_ref[:, lanes(parity)]
        conv_grad += dot_nt(spread, conv_in_ref[:, lanes(parity)])
        back = grid_slope_ref[:, lanes(parity)] * dot_nn(conv_t_ref[...], spread)
        deconv_grad += jnp.sum(back, 1, keepdims=True)
        gu_ref[parity * DEC : (parity + 1) * DEC, :] = back.astype(jnp.bfloat16)
    conv_grad_ref[...] = conv_grad
    deconv_grad_ref[...] = jnp.broadcast_to(deconv_grad, (DEC, BS))


def whole_specs(number):
    return [pl.BlockSpec(memory_space=pltpu.VMEM)] * number


def decoder_forward(up_t, deconv_bias, conv_low, conv_bias, head_low, head_bias, labels, batch):
    shapes = (
        jax.ShapeDtypeStruct((DEC, CELLS), jnp.bfloat16),
        jax.ShapeDtypeStruct((DEC, CELLS), jnp.float32),
        jax.ShapeDtypeStruct((CF, CELLS), jnp.float32),
        jax.ShapeDtypeStruct((CF, CELLS), jnp.bfloat16),
        jax.ShapeDtypeStruct((CF, CELLS), jnp.float32),
        jax.ShapeDtypeStruct((CF, BS), jnp.float32),
    )
    return pl.pallas_call(
        decoder_forward_kernel,
        out_shape=shapes,
        in_specs=whole_specs(8),
        out_specs=tuple(whole_specs(6)),
        scratch_shapes=[pltpu.VMEM((CF, CELLS), jnp.float32)],
        compiler_params=pltpu.CompilerParams(vmem_limit_bytes=40 * MIB),
        cost_estimate=pl.CostEstimate(
            flops=2 * 27 * CF * DEC * CELLS, bytes_accessed=6 * MIB, transcendentals=DEC * CELLS
        ),
        name="decoder_forward",
    )(up_t, deconv_bias, conv_low, conv_bias, head_low, head_bias, labels, batch)


def decoder_backward(
    all_crops, sums, batch, labels, chance, features, conv_slope, grid_slope, conv_in, conv_t, head_t
):
    shapes = (
        jax.ShapeDtypeStruct((8 * DEC, NTOK), jnp.bfloat16),
        jax.ShapeDtypeStruct((27 * CF, DEC), jnp.float32),
        jax.ShapeDtypeStruct((CF, CF), jnp.float32),
        jax.ShapeDtypeStruct((CF, BS), jnp.float32),
        jax.ShapeDtypeStruct((DEC, BS), jnp.float32),
    )
    return pl.pallas_call(
        functools.partial(decoder_backward_kernel, all_crops),
        out_shape=shapes,
        in_specs=whole_specs(10),
        out_specs=tuple(whole_specs(5)),
        scratch_shapes=[pltpu.VMEM((27 * CF, CELLS), jnp.bfloat16)],
        compiler_params=pltpu.CompilerParams(vmem_limit_bytes=40 * MIB),
        cost_estimate=pl.CostEstimate(
            flops=4 * 27 * CF * DEC * CELLS, bytes_accessed=6 * MIB, transcendentals=0
        ),
        name="decoder_backward",
    )(sums, batch, labels, chance, features, conv_slope, grid_slope, conv_in, conv_t, head_t)


LAYERS = 4
GATHER_LAG = 2
PIECES = 32
BLOCK_ROWS = 24 * BS
AUX_ROWS = 256
CHUNK = BLOCK_ROWS + AUX_ROWS
ROWS_N = 2 * CHUNK // PIECES
ROWS_F = BLOCK_ROWS // PIECES
LAG = 2
HOP_LAG = 2
AHEAD = 3
CORE_SLOTS = 8
SEND_SLOTS = 4
KEEP = 8
SUM_SLOTS = 12


def remote(src, dst, send_sem, recv_sem, device):
    return pltpu.make_async_remote_copy(
        src_ref=src,
        dst_ref=dst,
        send_sem=send_sem,
        recv_sem=recv_sem,
        device_id=device,
        device_id_type=MESH,
    )


def places():
    dp, x = lax.axis_index("dp"), lax.axis_index("mp")
    z, y, c = dp // 4, (dp // 2) % 2, dp % 2
    return dict(
        dp=dp,
        x=x,
        y=y,
        z=z,
        c=c,
        at_core=(dp + 1 - 2 * c, x),
        at_x=(dp, 1 - x),
        at_y=(dp + 2 - 4 * y, x),
        above=(lax.rem(dp + 4, 4 * LAYERS), x),
        below=(lax.rem(dp + 4 * LAYERS - 4, 4 * LAYERS), x),
    )


def greet_neighbours(at):
    barrier = pltpu.get_barrier_semaphore()
    for name in ("at_core", "at_x", "at_y"):
        pl.semaphore_signal(barrier, inc=1, device_id=at[name], device_id_type=MESH)

    @pl.when(at["z"] < LAYERS - 1)
    def _():
        pl.semaphore_signal(barrier, inc=1, device_id=at["above"], device_id_type=MESH)

    @pl.when(at["z"] > 0)
    def _():
        pl.semaphore_signal(barrier, inc=1, device_id=at["below"], device_id_type=MESH)

    peers = 3 + jnp.minimum(at["z"], 1) + jnp.minimum(LAYERS - 1 - at["z"], 1)
    pl.semaphore_wait(barrier, peers)


def gather_kernel(rows, parts, skip, in_ref, out_ref, local_sem, up_sem, down_sem, z_recv, x_send, x_recv, y_send, y_recv, core_send, core_recv):
    at = places()
    x, y, z, c = at["x"], at["y"], at["z"], at["c"]
    last = LAYERS - 1
    size = rows // parts
    by_x = -(-parts // 3)

    def spot(l, y_at, c_at, x_at, p):
        return out_ref.at[x_at, l * 4 + y_at * 2 + c_at, pl.ds(p * size, size)]

    def send(ref, send_sem, recv_sem, device):
        return remote(ref, ref, send_sem, recv_sem, device)

    def up(l, p):
        return send(spot(l, y, c, x, p), up_sem.at[l, p], z_recv.at[l, p], at["above"])

    def down(l, p):
        return send(spot(l, y, c, x, p), down_sem.at[l, p], z_recv.at[l, p], at["below"])

    def x_direct(l, p, x_at):
        return send(spot(l, y, c, x_at, p), x_send.at[l, p, 0], x_recv.at[l, p, 0], at["at_x"])

    def y_direct(l, p, y_at):
        return send(spot(l, y_at, c, x, p), y_send.at[l, p, 0], y_recv.at[l, p, 0], at["at_y"])

    def diagonal(l, p, y_at, x_at):
        if p < by_x:
            return send(spot(l, y_at, c, x_at, p), y_send.at[l, p, 1], y_recv.at[l, p, 1], at["at_y"])
        return send(spot(l, y_at, c, x_at, p), x_send.at[l, p, 1], x_recv.at[l, p, 1], at["at_x"])

    def relayed(l, p):
        return diagonal(l, p, y, 1 - x) if p < by_x else diagonal(l, p, 1 - y, x)

    def core(l, p, kind, c_at):
        y_at, x_at = ((y, x), (1 - y, x), (y, 1 - x), (1 - y, 1 - x))[kind]
        return send(
            spot(l, y_at, c_at, x_at, p),
            core_send.at[l, p, kind],
            core_recv.at[l, p, kind],
            at["at_core"],
        )

    def wide(l):
        return (l > 0) if skip else (l >= 0)

    own = pltpu.make_async_copy(in_ref, out_ref.at[x, at["dp"]], local_sem)
    own.start()
    greet_neighbours(at)
    own.wait()

    def arrive(l, p, came_up, came_down):
        if not (came_up and came_down):
            up(l, p).wait_recv()
        if came_up:

            @pl.when(z < last)
            def _():
                up(l, p).start()

        if came_down:

            @pl.when(z > 0)
            def _():
                down(l, p).start()

        @pl.when(wide(l))
        def _():
            x_direct(l, p, x).start()

        y_direct(l, p, y).start()
        core(l, p, 0, c).start()

    def relay(l, p):
        y_direct(l, p, 1 - y).wait_recv()

        @pl.when(wide(l))
        def _():
            if p >= by_x:
                relayed(l, p).start()
            x_direct(l, p, 1 - x).wait_recv()
            if p < by_x:
                relayed(l, p).start()
            core(l, p, 2, c).start()

        core(l, p, 1, c).start()

    def finish(l, p):
        @pl.when(wide(l))
        def _():
            diagonal(l, p, 1 - y, 1 - x).wait_recv()
            core(l, p, 3, c).start()

    def both(tick, run):
        if tick < 0 or tick >= LAYERS * parts:
            return
        r, p = tick // parts, tick % parts
        if r == 0:
            run(z, p, True, True)
            return

        @pl.when(z - r >= 0)
        def _():
            run(z - r, p, True, False)

        @pl.when(z + r <= last)
        def _():
            run(z + r, p, False, True)

    for tick in range(LAYERS * parts + 2 * GATHER_LAG):
        both(tick, arrive)
        both(tick - GATHER_LAG, lambda l, p, up_way, down_way: relay(l, p))
        both(tick - 2 * GATHER_LAG, lambda l, p, up_way, down_way: finish(l, p))

    def settle(l, carry):
        for p in range(parts):
            for kind in (0, 1):
                core(l, p, kind, 1 - c).wait_recv()
                core(l, p, kind, c).wait_send()
            y_direct(l, p, y).wait_send()

            @pl.when(wide(l))
            def _(p=p):
                for kind in (2, 3):
                    core(l, p, kind, 1 - c).wait_recv()
                    core(l, p, kind, c).wait_send()
                x_direct(l, p, x).wait_send()
                relayed(l, p).wait_send()

            @pl.when((l <= z) & (z < last))
            def _(p=p):
                up(l, p).wait_send()

            @pl.when((l >= z) & (z > 0))
            def _(p=p):
                down(l, p).wait_send()

        return carry

    lax.fori_loop(0, LAYERS, settle, 0)


def gather_all(values, parts, skip, collective_id, name):
    rows = values.shape[0]

    def sems(*shape):
        return pltpu.SemaphoreType.DMA(shape)

    return pl.pallas_call(
        functools.partial(gather_kernel, rows, parts, skip),
        out_shape=jax.ShapeDtypeStruct((MP, 4 * LAYERS, rows, BS), values.dtype),
        in_specs=[pl.BlockSpec(memory_space=pl.ANY)],
        out_specs=pl.BlockSpec(memory_space=pl.ANY),
        scratch_shapes=[
            pltpu.SemaphoreType.DMA,
            sems(LAYERS, parts),
            sems(LAYERS, parts),
            sems(LAYERS, parts),
            sems(LAYERS, parts, 2),
            sems(LAYERS, parts, 2),
            sems(LAYERS, parts, 2),
            sems(LAYERS, parts, 2),
            sems(LAYERS, parts, 4),
            sems(LAYERS, parts, 4),
        ],
        compiler_params=pltpu.CompilerParams(
            collective_id=collective_id, has_side_effects=True, vmem_limit_bytes=32 * MIB
        ),
        cost_estimate=pl.CostEstimate(flops=0, bytes_accessed=32 * rows * BS * 4, transcendentals=0),
        name=name,
    )(values)


def reduce_kernel(
    n_ref,
    e_ref,
    f_ref,
    out_ref,
    square_ref,
    own_n,
    own_f,
    core_n,
    core_f,
    keep_n,
    keep_f,
    xs_n,
    ys_n,
    ys_f,
    xr_n,
    yr_n,
    yr_f,
    sum_n,
    sum_f,
    up_n,
    down_n,
    up_f,
    down_e,
    own_sem,
    core_send,
    core_recv,
    credit,
    xs_sem,
    ys_n_sem,
    ys_f_sem,
    xr_sem,
    yr_n_sem,
    yr_f_sem,
    z_n_sem,
    z_f_sem,
    up_n_sem,
    down_n_sem,
    up_f_sem,
    down_e_sem,
):
    at = places()
    x, y, z, c = at["x"], at["y"], at["z"], at["c"]
    last = LAYERS - 1

    def layer_of(s):
        return 1 + lax.rem(s, 2)

    def rows_of(s):
        return pl.ds(pl.multiple_of((s // 2) * ROWS_N, 8), ROWS_N)

    def rows_f(s):
        return pl.ds(pl.multiple_of(s * ROWS_F, 8), ROWS_F)

    def own_loads(s):
        slot = lax.rem(s, 3)
        mine = n_ref.at[:, layer_of(s) - 1, :, c, rows_of(s)]
        return (
            pltpu.make_async_copy(mine, own_n.at[slot], own_sem.at[slot, 0]),
            pltpu.make_async_copy(e_ref.at[:, c, rows_f(s)], own_f.at[slot, 0], own_sem.at[slot, 1]),
            pltpu.make_async_copy(f_ref.at[:, c, rows_f(s)], own_f.at[slot, 1], own_sem.at[slot, 2]),
        )

    def core_copies(s):
        slot = lax.rem(s, CORE_SLOTS)
        sources = (
            n_ref.at[:, layer_of(s) - 1, :, 1 - c, rows_of(s)],
            e_ref.at[:, 1 - c, rows_f(s)],
            f_ref.at[:, 1 - c, rows_f(s)],
        )
        targets = (core_n.at[slot], core_f.at[slot, 0], core_f.at[slot, 1])
        return [
            remote(source, target, core_send.at[s, i], core_recv.at[slot, i], at["at_core"])
            for i, (source, target) in enumerate(zip(sources, targets))
        ]

    def x_copy(s):
        slot = lax.rem(s, SEND_SLOTS)
        return remote(xs_n.at[slot], xr_n.at[s], xs_sem.at[slot], xr_sem.at[s], at["at_x"])

    def y_copy_f(s):
        slot = lax.rem(s, SEND_SLOTS)
        return remote(ys_f.at[slot], yr_f.at[s], ys_f_sem.at[slot], yr_f_sem.at[s], at["at_y"])

    def y_copy(s):
        slot = lax.rem(s, SEND_SLOTS)
        return remote(ys_n.at[slot], yr_n.at[s], ys_n_sem.at[slot], yr_n_sem.at[s], at["at_y"])

    def up_copy(s):
        slot = lax.rem(s, SUM_SLOTS)
        return remote(sum_n.at[slot], up_n.at[s], z_n_sem.at[slot], up_n_sem.at[s], at["above"])

    def down_copy(s):
        slot = lax.rem(s, SUM_SLOTS)
        return remote(sum_n.at[slot], down_n.at[s], z_n_sem.at[slot], down_n_sem.at[s], at["below"])

    def down_copy_e(s):
        slot = lax.rem(s, SUM_SLOTS)
        source, sem = sum_f.at[slot, 0], z_f_sem.at[slot, 0]
        return remote(source, down_e.at[s], sem, down_e_sem.at[s], at["below"])

    def up_copy_f(s):
        slot = lax.rem(s, SUM_SLOTS)
        source, sem = sum_f.at[slot, 1], z_f_sem.at[slot, 1]
        return remote(source, up_f.at[s], sem, up_f_sem.at[s], at["above"])

    def add_squares(values):
        square_ref[...] += jnp.sum((values * values).reshape(-1, 8, BS), 0)

    square_ref[...] = jnp.zeros((8, BS), jnp.float32)
    for s in range(2):
        for copy in own_loads(s):
            copy.start()
    greet_neighbours(at)
    for s in range(AHEAD):
        for copy in core_copies(s):
            copy.start()

    def first(s):
        @pl.when(s + 2 < PIECES)
        def _():
            for copy in own_loads(s + 2):
                copy.start()

        @pl.when(s + AHEAD < PIECES)
        def _():
            @pl.when(s + AHEAD >= CORE_SLOTS)
            def _():
                pl.semaphore_wait(credit, 1)

            for copy in core_copies(s + AHEAD):
                copy.start()

        for copy in own_loads(s):
            copy.wait()
        for copy in core_copies(s):
            copy.wait_recv()

        @pl.when(s >= SEND_SLOTS)
        def _():
            x_copy(s - SEND_SLOTS).wait_send()
            y_copy_f(s - SEND_SLOTS).wait_send()

        own, core = lax.rem(s, 3), lax.rem(s, CORE_SLOTS)
        send, keep = lax.rem(s, SEND_SLOTS), lax.rem(s, KEEP)
        xs_n[send] = own_n[own, 1 - x] + core_n[core, 1 - x]
        x_copy(s).start()
        for kind in range(2):
            ys_f[send, kind] = own_f[own, kind, 1 - y] + core_f[core, kind, 1 - y]
        y_copy_f(s).start()
        keep_n[keep] = own_n[own, x] + core_n[core, x]
        for kind in range(2):
            keep_f[keep, kind] = own_f[own, kind, y] + core_f[core, kind, y]

        @pl.when(s + CORE_SLOTS < PIECES)
        def _():
            pl.semaphore_signal(credit, inc=1, device_id=at["at_core"], device_id_type=MESH)

    def second(s):
        x_copy(s).wait_recv()

        @pl.when(s >= SEND_SLOTS)
        def _():
            y_copy(s - SEND_SLOTS).wait_send()

        send, keep = lax.rem(s, SEND_SLOTS), lax.rem(s, KEEP)
        ys_n[send] = keep_n[keep, 1 - y] + xr_n[s, 1 - y]
        y_copy(s).start()
        keep_n[keep, y] = keep_n[keep, y] + xr_n[s, y]

    def third(s):
        y_copy_f(s).wait_recv()
        y_copy(s).wait_recv()

        @pl.when((s >= SUM_SLOTS) & (z != layer_of(s)))
        def _():
            up_copy(s - SUM_SLOTS).wait_send()

        @pl.when((s >= SUM_SLOTS) & (z > 0))
        def _():
            down_copy_e(s - SUM_SLOTS).wait_send()

        @pl.when((s >= SUM_SLOTS) & (z < last))
        def _():
            up_copy_f(s - SUM_SLOTS).wait_send()

        slot, keep = lax.rem(s, SUM_SLOTS), lax.rem(s, KEEP)
        sum_n[slot] = keep_n[keep, y] + yr_n[s]
        sum_f[slot] = keep_f[keep] + yr_f[s]

    def along(s, hop):
        slot = lax.rem(s, SUM_SLOTS)
        layer = layer_of(s)
        away = jnp.where(z < layer, z, jnp.where(z > layer, last - z, jnp.maximum(z, last - z)))

        @pl.when(away == hop)
        def _():
            @pl.when((z > 0) & (z <= layer))
            def _():
                up_copy(s).wait_recv()
                sum_n[slot] = sum_n[slot] + up_n[s]

            @pl.when((z < last) & (z >= layer))
            def _():
                down_copy(s).wait_recv()
                sum_n[slot] = sum_n[slot] + down_n[s]

            @pl.when(z < layer)
            def _():
                up_copy(s).start()

            @pl.when(z > layer)
            def _():
                down_copy(s).start()

            @pl.when(z == layer)
            def _():
                out_ref[rows_of(s)] = sum_n[slot]
                piece = s // 2
                whole, cut = BLOCK_ROWS // ROWS_N, BLOCK_ROWS % ROWS_N

                @pl.when(piece <= whole)
                def _():
                    add_squares(sum_n[slot, pl.ds(0, cut)])

                @pl.when(piece < whole)
                def _():
                    add_squares(sum_n[slot, pl.ds(cut, ROWS_N - cut)])

        @pl.when(jnp.where(z == 0, last, last - z) == hop)
        def _():
            @pl.when(z < last)
            def _():
                down_copy_e(s).wait_recv()
                sum_f[slot, 0] = sum_f[slot, 0] + down_e[s]

            @pl.when(z > 0)
            def _():
                down_copy_e(s).start()

            @pl.when(z == 0)
            def _():
                out_ref[rows_f(s)] = sum_f[slot, 0]
                add_squares(sum_f[slot, 0])

        @pl.when(z == hop)
        def _():
            @pl.when(z > 0)
            def _():
                up_copy_f(s).wait_recv()
                sum_f[slot, 1] = sum_f[slot, 1] + up_f[s]

            @pl.when(z < last)
            def _():
                up_copy_f(s).start()

            @pl.when(z == last)
            def _():
                out_ref[rows_f(s)] = sum_f[slot, 1]
                add_squares(sum_f[slot, 1])

    def guarded(run, s):
        @pl.when((s >= 0) & (s < PIECES))
        def _():
            run(s)

    def step(t, carry):
        guarded(first, t)
        guarded(second, t - LAG)
        guarded(third, t - 2 * LAG)
        for hop in range(LAYERS):
            guarded(functools.partial(along, hop=hop), t - 2 * LAG - hop * HOP_LAG)
        return carry

    lax.fori_loop(0, PIECES + 2 * LAG + (LAYERS - 1) * HOP_LAG, step, 0)

    def drain_sends(i, carry):
        s = PIECES - SEND_SLOTS + i
        for copy in (x_copy(s), y_copy_f(s), y_copy(s)):
            copy.wait_send()
        return carry

    lax.fori_loop(0, SEND_SLOTS, drain_sends, 0)

    def drain_sums(i, carry):
        s = PIECES - SUM_SLOTS + i

        @pl.when(z != layer_of(s))
        def _():
            up_copy(s).wait_send()

        @pl.when(z > 0)
        def _():
            down_copy_e(s).wait_send()

        @pl.when(z < last)
        def _():
            up_copy_f(s).wait_send()

        return carry

    lax.fori_loop(0, SUM_SLOTS, drain_sums, 0)

    def drain_core(s, carry):
        for copy in core_copies(s):
            copy.wait_send()
        return carry

    lax.fori_loop(0, PIECES, drain_core, 0)

    @pl.when((z == 0) | (z == last))
    def _():
        out_ref[pl.ds(BLOCK_ROWS, AUX_ROWS)] = jnp.zeros((AUX_ROWS, BS), jnp.float32)


def reduce_to_owners(rest, first, final):
    def room(*shape):
        return pltpu.VMEM(shape + (BS,), jnp.float32)

    def sems(*shape):
        return pltpu.SemaphoreType.DMA(shape)

    return pl.pallas_call(
        reduce_kernel,
        out_shape=(
            jax.ShapeDtypeStruct((CHUNK, BS), jnp.float32),
            jax.ShapeDtypeStruct((8, BS), jnp.float32),
        ),
        in_specs=[pl.BlockSpec(memory_space=pl.ANY)] * 3,
        out_specs=(pl.BlockSpec(memory_space=pltpu.VMEM),) * 2,
        scratch_shapes=[
            room(3, 2, 2, ROWS_N),
            room(3, 2, 2, ROWS_F),
            room(CORE_SLOTS, 2, 2, ROWS_N),
            room(CORE_SLOTS, 2, 2, ROWS_F),
            room(KEEP, 2, ROWS_N),
            room(KEEP, 2, ROWS_F),
            room(SEND_SLOTS, 2, ROWS_N),
            room(SEND_SLOTS, ROWS_N),
            room(SEND_SLOTS, 2, ROWS_F),
            room(PIECES, 2, ROWS_N),
            room(PIECES, ROWS_N),
            room(PIECES, 2, ROWS_F),
            room(SUM_SLOTS, ROWS_N),
            room(SUM_SLOTS, 2, ROWS_F),
            room(PIECES, ROWS_N),
            room(PIECES, ROWS_N),
            room(PIECES, ROWS_F),
            room(PIECES, ROWS_F),
            sems(3, 3),
            sems(PIECES, 3),
            sems(CORE_SLOTS, 3),
            pltpu.SemaphoreType.REGULAR,
            sems(SEND_SLOTS),
            sems(SEND_SLOTS),
            sems(SEND_SLOTS),
            sems(PIECES),
            sems(PIECES),
            sems(PIECES),
            sems(SUM_SLOTS),
            sems(SUM_SLOTS, 2),
            sems(PIECES),
            sems(PIECES),
            sems(PIECES),
            sems(PIECES),
        ],
        compiler_params=pltpu.CompilerParams(
            collective_id=1, has_side_effects=True, vmem_limit_bytes=58 * MIB
        ),
        cost_estimate=pl.CostEstimate(flops=0, bytes_accessed=100 * MIB, transcendentals=0),
        name="reduce_to_owners",
    )(rest, first, final)


MATRICES = [
    (96, 6, 9, 3, True),
    (150, 3, 6, 3, False),
    (168, 6, 12, 3, True),
    (240, 12, 6, 4, False),
    (312, 9, 8, 3, False),
]
LOADS = 4


def unblock_kernel(plan, kinds, blocks_ref, *refs):
    outs, tiles = refs[:kinds], refs[kinds : 2 * kinds]
    loaded, load_sem, store_sem = refs[2 * kinds :]
    part = lax.axis_index("mp")

    def load(i):
        kind, m, first, rows, per_row, row, col = plan[i]
        number = rows * per_row
        return pltpu.make_async_copy(
            blocks_ref.at[part if m is None else m, pl.ds(first, number)],
            loaded.at[i % LOADS, pl.ds(0, number)],
            load_sem.at[i % LOADS],
        )

    def store(i, slot):
        kind, m, first, rows, per_row, row, col = plan[i]
        return pltpu.make_async_copy(
            tiles[kind].at[slot],
            outs[kind].at[pl.ds(row, rows * BS), pl.ds(col, per_row * BS)],
            store_sem.at[kind, slot],
        )

    history = [[] for _ in range(kinds)]
    for i in range(min(LOADS - 1, len(plan))):
        load(i).start()
    for i, (kind, m, first, rows, per_row, row, col) in enumerate(plan):
        if i + LOADS - 1 < len(plan):
            load(i + LOADS - 1).start()
        load(i).wait()
        slot = len(history[kind]) % 2
        if len(history[kind]) >= 2:
            store(*history[kind][-2]).wait()
        for r in range(rows):
            for c in range(per_row):
                tiles[kind][slot, r * BS : (r + 1) * BS, c * BS : (c + 1) * BS] = loaded[
                    i % LOADS, r * per_row + c
                ]
        history[kind].append((i, slot))
        store(i, slot).start()
    for done in history:
        for entry in done[-2:]:
            store(*entry).wait()


def unblock(gathered, embedding):
    plan, shapes, tiles = [], [], []
    if embedding:
        plan = [(0, None, 24 * i, 4, 6, 4 * BS * i, 0) for i in range(4)]
        shapes, tiles = [(PV // MP, D)], [(4 * BS, D)]
    else:
        for kind, (first, rows, per_row, step, beside) in enumerate(MATRICES):
            tall, wide = rows * BS, per_row * BS
            shapes.append((tall, MP * wide) if beside else (MP * tall, wide))
            tiles.append((step * BS, wide))
            for m in range(MP):
                for at in range(0, rows, step):
                    row = at * BS + (0 if beside else m * tall)
                    plan.append(
                        (kind, m, first + at * per_row, step, per_row, row, m * wide if beside else 0)
                    )
    anywhere = pl.BlockSpec(memory_space=pl.ANY)
    largest = max(entry[3] * entry[4] for entry in plan)
    return pl.pallas_call(
        functools.partial(unblock_kernel, plan, len(shapes)),
        out_shape=tuple(jax.ShapeDtypeStruct(shape, jnp.bfloat16) for shape in shapes),
        in_specs=[anywhere],
        out_specs=tuple([anywhere] * len(shapes)),
        scratch_shapes=[pltpu.VMEM((2,) + tile, jnp.bfloat16) for tile in tiles]
        + [
            pltpu.VMEM((LOADS, largest, BS, BS), jnp.bfloat16),
            pltpu.SemaphoreType.DMA((LOADS,)),
            pltpu.SemaphoreType.DMA((len(shapes), 2)),
        ],
        compiler_params=pltpu.CompilerParams(vmem_limit_bytes=32 * MIB),
        cost_estimate=pl.CostEstimate(
            flops=0, bytes_accessed=(6 if embedding else 38) * MIB, transcendentals=0
        ),
        name="unblock_embedding" if embedding else "unblock",
    )(gathered)


def blocks_kernel(first_block, per_row, step_rows, transposed, has_buffer, *refs):
    x_ref, g_ref = refs[:2]
    out_ref, tiles, sems = refs[-3:]
    m, i = pl.program_id(0), pl.program_id(1)
    steps = pl.num_programs(1)
    at = m * steps + i
    slot = lax.rem(at, 2)
    total = pl.num_programs(0) * steps

    def drain(which):
        pltpu.make_async_copy(tiles.at[which], tiles.at[which], sems.at[which]).wait()

    @pl.when(at >= 2)
    def _():
        drain(slot)

    tiles[slot] = dot(x_ref[...], g_ref[...], ((0,), (1,) if transposed else (0,)))
    for r in range(step_rows):
        for c in range(per_row):
            block = first_block + (i * step_rows + r) * per_row + c
            chunk, at_row = block // 24, lax.rem(block, 24) * BS
            pltpu.make_async_copy(
                tiles.at[slot, r * BS : (r + 1) * BS, c * BS : (c + 1) * BS],
                out_ref.at[m, chunk, pl.ds(pl.multiple_of(at_row, BS), BS)],
                sems.at[slot],
            ).start()

    @pl.when(at == total - 1)
    def _():
        drain(slot)

        @pl.when(total > 1)
        def _():
            drain(1 - slot)


def grad_blocks(x, g, parts, rows, per_row, step_rows, first_block, split_x, split_g, buffer, name, chunks, depth, transposed=False, x_stride=None):
    steps = rows // step_rows
    x_stride = x_stride or steps
    tokens = x.shape[0]
    width = per_row * BS
    x_spec = pl.BlockSpec(
        (tokens, step_rows * BS), (lambda m, i: (0, m * x_stride + i)) if split_x else (lambda m, i: (0, i))
    )
    if transposed:
        g_spec = pl.BlockSpec((width, tokens), lambda m, i: (0, 0))
    else:
        g_spec = pl.BlockSpec((tokens, width), (lambda m, i: (0, m)) if split_g else (lambda m, i: (0, 0)))
    anywhere = pl.BlockSpec(memory_space=pl.ANY)
    operands = [x, g] + ([] if buffer is None else [buffer])
    return pl.pallas_call(
        functools.partial(
            blocks_kernel, first_block, per_row, step_rows, transposed, buffer is not None
        ),
        grid=(parts, steps),
        out_shape=jax.ShapeDtypeStruct((parts, chunks, depth, BS), jnp.float32),
        in_specs=[x_spec, g_spec] + ([] if buffer is None else [anywhere]),
        out_specs=anywhere,
        input_output_aliases={} if buffer is None else {2: 0},
        scratch_shapes=[
            pltpu.VMEM((2, step_rows * BS, width), jnp.float32),
            pltpu.SemaphoreType.DMA((2,)),
        ],
        compiler_params=pltpu.CompilerParams(vmem_limit_bytes=32 * MIB),
        cost_estimate=pl.CostEstimate(
            flops=2 * tokens * parts * rows * BS * width,
            bytes_accessed=parts * rows * BS * width * 4,
            transcendentals=0,
        ),
        name=name,
    )(*operands)


def fast_mesh():
    return lax.axis_size("dp") == 4 * LAYERS and lax.axis_size("mp") == MP


def sum_kernel(devices, in_ref, out_ref, slots, send_sem, recv_sem):
    me = lax.axis_index("dp") * MP + lax.axis_index("mp")
    barrier = pltpu.get_barrier_semaphore()

    def place(k):
        peer = lax.rem(me + k, devices)
        return (peer // MP, lax.rem(peer, MP))

    def greet(k, carry):
        pl.semaphore_signal(barrier, inc=1, device_id=place(k), device_id_type=MESH)
        return carry

    def copy(k, slot):
        return remote(in_ref, slots.at[slot], send_sem.at[k], recv_sem.at[slot], place(k))

    lax.fori_loop(1, devices, greet, 0)
    slots[me] = in_ref[...]
    pl.semaphore_wait(barrier, devices - 1)

    def push(k, carry):
        copy(k, me).start()
        return carry

    def pull(k, carry):
        copy(k, lax.rem(me + devices - k, devices)).wait_recv()
        return carry

    def settle(k, carry):
        copy(k, me).wait_send()
        return carry

    lax.fori_loop(1, devices, push, 0)
    lax.fori_loop(1, devices, pull, 0)
    total = slots[0]
    for i in range(1, devices):
        total = total + slots[i]
    out_ref[...] = total
    lax.fori_loop(1, devices, settle, 0)


def gather_weights(blocks):
    low = blocks.astype(jnp.bfloat16)[0, 0]
    if fast_mesh():
        gathered = gather_all(low.reshape(-1, BS), 3, True, 2, "gather_weights")
    else:
        gathered = lax.all_gather(low, ("dp", "mp"), axis=0, tiled=False)
        gathered = gathered.reshape((-1, MP) + low.shape).swapaxes(0, 1)
    return gathered.reshape(MP, -1, BS, BS)


def sum_sums(values):
    if not fast_mesh():
        return lax.psum(values, ("dp", "mp"))
    devices = 4 * LAYERS * MP
    whole = pl.BlockSpec(memory_space=pltpu.VMEM)
    return pl.pallas_call(
        functools.partial(sum_kernel, devices),
        out_shape=jax.ShapeDtypeStruct(values.shape, jnp.float32),
        in_specs=[whole],
        out_specs=whole,
        scratch_shapes=[
            pltpu.VMEM((devices,) + values.shape, jnp.float32),
            pltpu.SemaphoreType.DMA((devices,)),
            pltpu.SemaphoreType.DMA((devices,)),
        ],
        compiler_params=pltpu.CompilerParams(collective_id=3, has_side_effects=True),
        name="sum_sums",
    )(values)


def swap_mp(values):
    return lax.ppermute(values, "mp", [(0, 1), (1, 0)])


def reduce_plain(rest, first, final):
    part = lax.axis_index("mp")
    own = (jnp.arange(MP) == part).astype(jnp.float32)
    ends = [piece.reshape(1, -1, BS, BS) * own[:, None, None, None] for piece in (first, final)]
    dp = lax.axis_size("dp")
    every = jnp.concatenate([ends[0], rest, ends[1]], 1)
    every = every.reshape(MP, dp, -1, BS, BS).transpose(1, 0, 2, 3, 4)
    return lax.psum_scatter(
        every.reshape(dp * MP, -1, BS, BS), ("dp", "mp"), scatter_dimension=0, tiled=True
    )[0]


def layer_norm(values):
    center = values - jnp.mean(values, -1, keepdims=True)
    spread = jnp.mean(center * center, -1, keepdims=True)
    inverse = lax.rsqrt(spread + 1e-06)
    return center * inverse, inverse


def layer_norm_back(back, normal, inverse, gain):
    scaled = back * gain
    mean = jnp.mean(scaled, -1, keepdims=True)
    along = jnp.mean(scaled * normal, -1, keepdims=True)
    return inverse * (scaled - mean - normal * along)


def shampoo_step(blocks, grads, stat_pair, root_pair, moment, veloc):
    stat_left = beta_stat * stat_pair[0] + (1 - beta_stat) * jnp.einsum(
        "cij,ckj->cik", grads, grads, precision=HIGHEST
    )
    stat_right = beta_stat * stat_pair[1] + (1 - beta_stat) * jnp.einsum(
        "cji,cjk->cik", grads, grads, precision=HIGHEST
    )
    moment_new = beta_one * moment + (1 - beta_one) * grads
    veloc_new = beta_two * veloc + (1 - beta_two) * grads * grads
    moment_hat = moment_new / (1 - beta_one**STEP)
    adam_dir = moment_hat / (jnp.sqrt(veloc_new / (1 - beta_two**STEP)) + 1e-08)
    left_side = jnp.einsum("cij,cjk->cik", root_pair[0], moment_hat, precision=HIGHEST)
    precond = jnp.einsum("cij,cjk->cik", left_side, root_pair[1], precision=HIGHEST)
    ratio = jnp.sqrt(
        (jnp.mean(adam_dir * adam_dir, (-2, -1), keepdims=True) + 1e-06)
        / (jnp.mean(precond * precond, (-2, -1), keepdims=True) + 1e-06)
    )
    block_new = blocks - learn_rate * (precond * ratio + decay_rate * blocks)
    return (block_new, jnp.stack([stat_left, stat_right]), moment_new, veloc_new)


def adam_step(param, grads, moment, veloc):
    moment_new = beta_one * moment + (1 - beta_one) * grads
    veloc_new = beta_two * veloc + (1 - beta_two) * grads * grads
    direction = (
        moment_new / (1 - beta_one**STEP) / (jnp.sqrt(veloc_new / (1 - beta_two**STEP)) + 1e-08)
    )
    return (param - learn_rate * direction, moment_new, veloc_new)


def halves(matrix):
    return matrix[:, :HALF], matrix[:, HALF:]


def local(
    patches,
    labels,
    batch_ids,
    blocks,
    statistics,
    roots,
    moments,
    velocity,
    aux,
    aux_moment,
    aux_velocity,
):
    part = lax.axis_index("mp")
    all_crops = lax.axis_size("dp") * MP
    pieces = split_aux(aux)
    gain, shift = pieces["norm_gain"], pieces["norm_bias"]

    gathered = gather_weights(blocks)
    (w_embed,) = unblock(gathered, True)
    w_qkv, w_proj, w_up, w_down, w_deconv = unblock(gathered, False)

    other_rows = lax.dynamic_slice_in_dim(patches, (1 - part) * NTOK, NTOK, 0)
    own_rows = lax.dynamic_slice_in_dim(patches, part * NTOK, NTOK, 0)
    received = swap_mp(dot_nn(other_rows, w_embed))
    stream_zero = (
        dot_nn(own_rows, w_embed) + received + pieces["positions"] + pieces["embed_bias"]
    )
    normal_one, inverse_one = layer_norm(stream_zero)
    normed_one = (normal_one * gain[0] + shift[0]).astype(jnp.bfloat16)
    q_bias, v_bias = pieces["qv_bias"][0], pieces["qv_bias"][1]
    nothing = jnp.zeros((HALF,), jnp.float32)
    qkv_bias = jnp.concatenate(
        [q_bias[:HALF], nothing, v_bias[:HALF], q_bias[HALF:], nothing, v_bias[HALF:]]
    )
    qkv = (dot_nn(normed_one, w_qkv) + qkv_bias).astype(jnp.bfloat16)
    mixed, lse = attention_forward(qkv)
    stream_one = stream_zero + dot_nn(mixed, w_proj) + pieces["proj_bias"]
    normal_two, inverse_two = layer_norm(stream_one)
    normed_two = (normal_two * gain[1] + shift[1]).astype(jnp.bfloat16)
    hidden = dot_nn(normed_two, w_up) + pieces["up_bias"]
    active_value, hidden_slope = gelu_and_slope(hidden)
    active = active_value.astype(jnp.bfloat16)
    stream_two = stream_one + dot_nn(active, w_down) + pieces["down_bias"]
    streams = [s.astype(jnp.bfloat16) for s in (stream_zero, stream_one, stream_two)]
    stacked = jnp.concatenate([halves(s)[m] for m in range(MP) for s in streams], 1)
    up_t = dot(w_deconv, stacked, ((0,), (1,)))

    def columns(array, which, width, start):
        return lax.dynamic_slice_in_dim(array, which * width + start, width - start, 1)

    down_start = 2 * FF // MP // 3
    stacked_pair = jnp.concatenate(
        [columns(stacked, part, 3 * HALF, 0), swap_mp(columns(stacked, 1 - part, 3 * HALF, 0))]
    )
    active_pair = jnp.concatenate(
        [
            columns(active, part, FF // MP, down_start),
            swap_mp(columns(active, 1 - part, FF // MP, down_start)),
        ]
    )

    conv_weight = pieces["conv_weight"].astype(jnp.bfloat16).reshape(27, DEC, CF)
    conv_low = conv_weight.transpose(0, 2, 1).reshape(27 * CF, DEC)
    conv_t = conv_weight.transpose(1, 0, 2).reshape(DEC, 27 * CF)
    head_weight = jnp.pad(pieces["head_weight"], ((0, 0), (0, CF - NCLS))).astype(jnp.bfloat16)
    head_bias = jnp.pad(pieces["head_bias"], (0, CF - NCLS)).reshape(CF, 1)
    grid_labels = (
        labels.reshape(GS, 2, GS, 2, GS, 2).transpose(1, 3, 5, 0, 2, 4).reshape(8, NTOK)
    )
    batch = jnp.broadcast_to(batch_ids.reshape(1, 1), (1, BS))
    conv_in, grid_slope, conv_slope, features, chance, sums = decoder_forward(
        up_t,
        pieces["deconv_bias"].reshape(DEC, 1),
        conv_low,
        pieces["conv_bias"].reshape(CF, 1),
        head_weight.T,
        head_bias,
        grid_labels,
        batch,
    )
    sums = sum_sums(sums)
    gu_t, conv_grad, head_grad, small, deconv_bias_grad = decoder_backward(
        all_crops,
        sums,
        batch,
        grid_labels,
        chance,
        features,
        conv_slope,
        grid_slope,
        conv_in,
        conv_t,
        head_weight,
    )
    loss_value = small[0, 2]

    gu_pair = jnp.concatenate([gu_t, swap_mp(gu_t)], 1)
    stacked_back = dot(gu_t, w_deconv, ((0,), (1,)))
    back_zero_s, back_one_s, back_two = [
        jnp.concatenate([stacked_back[:, (3 * m + s) * HALF : (3 * m + s + 1) * HALF] for m in range(MP)], 1)
        for s in range(3)
    ]
    grad_down_bias = jnp.sum(back_two, 0)
    two_low = back_two.astype(jnp.bfloat16)
    two_pair = jnp.concatenate([two_low, swap_mp(two_low)])
    back_hidden = (hidden_slope * dot_nt(two_low, w_down)).astype(jnp.bfloat16)
    grad_up_bias = jnp.sum(back_hidden.astype(jnp.float32), 0)
    back_normed_two = dot_nt(back_hidden, w_up)
    grad_gain_two = jnp.sum(back_normed_two * normal_two, 0)
    grad_shift_two = jnp.sum(back_normed_two, 0)
    back_one = (
        back_two + back_one_s + layer_norm_back(back_normed_two, normal_two, inverse_two, gain[1])
    )
    grad_proj_bias = jnp.sum(back_one, 0)
    one_low = back_one.astype(jnp.bfloat16)
    back_mixed = dot_nt(one_low, w_proj).astype(jnp.bfloat16)
    back_q, back_k, back_v = attention_backward(qkv, back_mixed, lse)
    back_qkv = jnp.concatenate(
        [halves(piece)[m] for m in range(MP) for piece in (back_q, back_k, back_v)], 1
    )
    grad_query_bias = jnp.sum(back_q.astype(jnp.float32), 0)
    grad_value_bias = jnp.sum(back_v.astype(jnp.float32), 0)
    back_normed_one = dot_nt(back_qkv, w_qkv)
    grad_gain_one = jnp.sum(back_normed_one * normal_one, 0)
    grad_shift_one = jnp.sum(back_normed_one, 0)
    back_zero = (
        back_one + back_zero_s + layer_norm_back(back_normed_one, normal_one, inverse_one, gain[0])
    )
    zero_low = back_zero.astype(jnp.bfloat16)
    other_low = swap_mp(zero_low)
    zero_pair = jnp.where(
        part == 0,
        jnp.concatenate([zero_low, other_low]),
        jnp.concatenate([other_low, zero_low]),
    )

    fast = fast_mesh()
    depth = CHUNK if fast else BLOCK_ROWS
    final_grads = grad_blocks(
        stacked_pair, gu_pair, 1, 9, 8, 3, 24, True, False, None, "grad_deconv", 4, BLOCK_ROWS, True
    )
    final_grads = grad_blocks(
        active_pair, two_pair, 1, 4, 6, 4, 0, True, False, final_grads, "grad_down_last", 4, BLOCK_ROWS
    )
    rest_grads = None
    for name, x, g, rows, per_row, step_rows, start, split_x, split_g, stride in (
        ("grad_down", active, two_low, 8, 6, 4, 144, True, False, 3),
        ("grad_up", normed_two, back_hidden, 6, 12, 3, 72, False, True, None),
        ("grad_proj", mixed, one_low, 3, 6, 3, 54, True, False, None),
        ("grad_qkv", normed_one, back_qkv, 6, 9, 3, 0, False, True, None),
    ):
        rest_grads = grad_blocks(
            x, g, MP, rows, per_row, step_rows, start, split_x, split_g, rest_grads, name, 8, depth,
            x_stride=stride,
        )
    first_grads = grad_blocks(
        patches, zero_pair, 1, 16, 6, 4, 0, False, False, None, "grad_embed", 4, BLOCK_ROWS
    )
    vectors = jnp.concatenate(
        [
            jnp.stack(
                [
                    grad_gain_one,
                    grad_gain_two,
                    grad_shift_one,
                    grad_shift_two,
                    grad_query_bias,
                    grad_value_bias,
                    grad_proj_bias,
                    grad_down_bias,
                ]
            ),
            jnp.pad(grad_up_bias.reshape(FF // D, D), ((0, 8 - FF // D), (0, 0))),
        ]
    )
    wide = jnp.concatenate([back_zero, vectors])
    tall = wide.shape[0]
    aux_rows = jnp.concatenate(
        [wide[:, j * BS : (j + 1) * BS] for j in range(D // BS)]
        + [conv_grad, jnp.pad(head_grad, ((0, 0), (0, BS - CF))), small, deconv_bias_grad]
    )
    if fast:
        room = 8 * MP * AUX_ROWS
        placed = jnp.pad(aux_rows, ((0, room - aux_rows.shape[0]), (0, 0)))
        placed = placed.reshape(MP, 8, AUX_ROWS, BS)
        rest_grads = lax.dynamic_update_slice(rest_grads, placed, (0, 0, BLOCK_ROWS, 0))
        reduced, squares = reduce_to_owners(
            rest_grads.reshape(MP, 2, 2, 2, CHUNK, BS),
            first_grads.reshape(2, 2, BLOCK_ROWS, BS),
            final_grads.reshape(2, 2, BLOCK_ROWS, BS),
        )
        owned = reduced[:BLOCK_ROWS].reshape(24, BS, BS)
        gathered_aux = gather_all(
            jnp.concatenate([reduced[BLOCK_ROWS:], squares]), 1, False, 4, "gather_aux"
        )
        block_square = jnp.sum(gathered_aux[:, :, AUX_ROWS:])
        aux_sum = gathered_aux[:, 4:12, :AUX_ROWS].reshape(-1, BS)
    else:
        owned = reduce_plain(rest_grads.reshape(MP, -1, BS, BS), first_grads, final_grads)
        aux_sum = lax.psum(aux_rows, ("dp", "mp"))
        block_square = lax.psum(jnp.sum(owned * owned), ("dp", "mp"))
    wide_sum = jnp.concatenate([aux_sum[j * tall : (j + 1) * tall] for j in range(D // BS)], 1)
    after = D // BS * tall
    conv_sum = aux_sum[after : after + 27 * CF]
    head_sum = aux_sum[after + 27 * CF : after + 28 * CF]
    small_sum = aux_sum[after + 28 * CF : after + 29 * CF]
    deconv_sum = aux_sum[after + 29 * CF : after + 29 * CF + DEC, 0]
    positions_sum = wide_sum[:NTOK]
    aux_total = jnp.concatenate(
        [
            positions_sum.reshape(-1),
            jnp.sum(positions_sum, 0),
            wide_sum[NTOK : NTOK + 7].reshape(-1),
            wide_sum[NTOK + 8 : NTOK + 8 + FF // D].reshape(-1),
            wide_sum[NTOK + 7],
            deconv_sum,
            conv_sum.reshape(27, CF, DEC).transpose(0, 2, 1).reshape(-1),
            small_sum[:, 1],
            head_sum[:, :NCLS].reshape(-1),
            small_sum[:NCLS, 0],
        ]
    )
    grad_norm = jnp.sqrt(block_square + jnp.sum(aux_total * aux_total))
    clip_scale = clip_value / jnp.maximum(grad_norm, clip_value)
    block_new, stat_new, moment_new, veloc_new = shampoo_step(
        blocks[0, 0],
        owned * clip_scale,
        statistics[:, 0, 0],
        roots[:, 0, 0],
        moments[0, 0],
        velocity[0, 0],
    )
    aux_new, aux_moment_new, aux_veloc_new = adam_step(
        aux, aux_total * clip_scale, aux_moment, aux_velocity
    )
    return (
        loss_value,
        grad_norm,
        block_new[None, None],
        stat_new[:, None, None],
        moment_new[None, None],
        veloc_new[None, None],
        aux_new,
        aux_moment_new,
        aux_veloc_new,
    )


def solution(mesh):
    block_spec = P("dp", "mp", None, None, None)
    pair_spec = P(None, "dp", "mp", None, None, None)
    placed = (
        P("dp", "mp"),
        P(("dp", "mp"), None),
        P(("dp", "mp")),
        block_spec,
        pair_spec,
        pair_spec,
        block_spec,
        block_spec,
        P(),
        P(),
        P(),
    )
    return jax.shard_map(
        local,
        mesh=mesh,
        in_specs=placed,
        out_specs=(P(), P(), block_spec, pair_spec, block_spec, block_spec, P(), P(), P()),
        check_vma=False,
    )
```

```python
import functools
import math

import jax
import jax.numpy as jnp
from jax import lax
from jax.experimental import pallas as pl
from jax.experimental.pallas import tpu as pltpu
from jax.sharding import PartitionSpec as P

D = 768
HDIM = 64
FF = 3072
PV = 4096
DEC = 128
CF = 16
NCLS = 14
GS = 8
MB = 4
STEP = 10
BS = 128
NTOK = 512
CELLS = 4096
MP = 2
HALF = D // MP
E_BLOCKS = PV // MP * D // (BS * BS)

HIGHEST = lax.Precision.HIGHEST
MESH = pl.DeviceIdType.MESH
beta_one = 0.9
beta_two = 0.999
beta_stat = 0.95
learn_rate = 0.02
decay_rate = 0.01
clip_value = 0.005
MIB = 1024 * 1024

OFFSETS = [(a, b, c) for a in range(3) for b in range(3) for c in range(3)]
PARITIES = [(i, j, k) for i in range(2) for j in range(2) for k in range(2)]


def dot(a, b, dims):
    return lax.dot_general(a, b, (dims, ((), ())), preferred_element_type=jnp.float32)


def dot_nn(a, b):
    return dot(a, b, ((1,), (0,)))


def dot_nt(a, b):
    return dot(a, b, ((1,), (1,)))


def dot_tn(a, b):
    return dot(a, b, ((0,), (0,)))


def gelu_cdf(v):
    return 0.5 * (1.0 + lax.erf(v * (0.5**0.5)))


def gelu_and_slope(v):
    cdf = gelu_cdf(v)
    density = jnp.exp(-0.5 * v * v) * (1.0 / math.sqrt(2.0 * math.pi))
    return v * cdf, cdf + v * density


def aux_layout():
    return [
        ("positions", (NTOK, D)),
        ("embed_bias", (D,)),
        ("norm_gain", (2, D)),
        ("norm_bias", (2, D)),
        ("qv_bias", (2, D)),
        ("proj_bias", (D,)),
        ("up_bias", (FF,)),
        ("down_bias", (D,)),
        ("deconv_bias", (DEC,)),
        ("conv_weight", (27 * DEC, CF)),
        ("conv_bias", (CF,)),
        ("head_weight", (CF, NCLS)),
        ("head_bias", (NCLS,)),
    ]


NAUX = sum(math.prod(shape) for _, shape in aux_layout())


def split_aux(vector):
    pieces = {}
    offset = 0
    for section_name, section_shape in aux_layout():
        length = math.prod(section_shape)
        pieces[section_name] = vector[offset : offset + length].reshape(section_shape)
        offset += length
    return pieces


def attention_forward_kernel(qkv_q, qkv_k, qkv_v, mixed_ref, lse_ref):
    q, k, v = qkv_q[...], qkv_k[...], qkv_v[...]
    v_t = v.astype(jnp.float32).T.astype(jnp.bfloat16)
    outs = []
    for h in range(2):
        cols = slice(h * HDIM, (h + 1) * HDIM)
        scores = dot_nt(k[:, cols], q[:, cols]) * 0.125
        top = jnp.max(scores, 0, keepdims=True)
        weights = jnp.exp(scores - top)
        total = jnp.sum(weights, 0, keepdims=True)
        attention = (weights * (1.0 / total)).astype(jnp.bfloat16)
        outs.append(dot_nn(v_t[cols], attention))
        lse_ref[0, h : h + 1, :] = top + jnp.log(total)
    mixed_ref[...] = jnp.concatenate(outs, 0).T.astype(jnp.bfloat16)


def attention_backward_kernel(qkv_q, qkv_k, qkv_v, gm_ref, lse_ref, gq_ref, gk_ref, gv_ref):
    q, k, v, gm = qkv_q[...], qkv_k[...], qkv_v[...], gm_ref[...]
    k_t = k.astype(jnp.float32).T.astype(jnp.bfloat16)
    gq_t = []
    for h in range(2):
        cols = slice(h * HDIM, (h + 1) * HDIM)
        scores = dot_nt(k[:, cols], q[:, cols]) * 0.125
        attention = jnp.exp(scores - lse_ref[0, h : h + 1, :])
        back = dot_nt(v[:, cols], gm[:, cols])
        gv_ref[:, cols] = dot_nn(attention.astype(jnp.bfloat16), gm[:, cols]).astype(jnp.bfloat16)
        mean = jnp.sum(back * attention, 0, keepdims=True)
        gs = (attention * (back - mean)).astype(jnp.bfloat16)
        gk_ref[:, cols] = (dot_nn(gs, q[:, cols]) * 0.125).astype(jnp.bfloat16)
        gq_t.append(dot_nn(k_t[cols], gs) * 0.125)
    gq_ref[...] = jnp.concatenate(gq_t, 0).T.astype(jnp.bfloat16)


def qkv_spec(part):
    return pl.BlockSpec((NTOK, BS), lambda i, part=part: (0, (i // 3) * 9 + part * 3 + i % 3))


def attention_forward(qkv):
    return pl.pallas_call(
        attention_forward_kernel,
        grid=(6,),
        out_shape=(
            jax.ShapeDtypeStruct((NTOK, D), jnp.bfloat16),
            jax.ShapeDtypeStruct((6, 2, NTOK), jnp.float32),
        ),
        in_specs=[qkv_spec(0), qkv_spec(1), qkv_spec(2)],
        out_specs=(
            pl.BlockSpec((NTOK, BS), lambda i: (0, i)),
            pl.BlockSpec((1, 2, NTOK), lambda i: (i, 0, 0)),
        ),
        compiler_params=pltpu.CompilerParams(vmem_limit_bytes=32 * MIB),
        cost_estimate=pl.CostEstimate(
            flops=12 * 4 * NTOK * NTOK * HDIM,
            bytes_accessed=NTOK * D * 8,
            transcendentals=12 * NTOK * NTOK,
        ),
        name="attention_forward",
    )(qkv, qkv, qkv)


def attention_backward(qkv, gm, lse):
    pair = pl.BlockSpec((NTOK, BS), lambda i: (0, i))
    return pl.pallas_call(
        attention_backward_kernel,
        grid=(6,),
        out_shape=(jax.ShapeDtypeStruct((NTOK, D), jnp.bfloat16),) * 3,
        in_specs=[
            qkv_spec(0),
            qkv_spec(1),
            qkv_spec(2),
            pair,
            pl.BlockSpec((1, 2, NTOK), lambda i: (i, 0, 0)),
        ],
        out_specs=(pair,) * 3,
        compiler_params=pltpu.CompilerParams(vmem_limit_bytes=32 * MIB),
        cost_estimate=pl.CostEstimate(
            flops=12 * 10 * NTOK * NTOK * HDIM,
            bytes_accessed=NTOK * D * 14,
            transcendentals=12 * NTOK * NTOK,
        ),
        name="attention_backward",
    )(qkv, qkv, qkv, gm, lse)


def source_of(parity, step):
    at = parity + step
    if at < 0:
        return 1, -1
    if at > 1:
        return 0, 1
    return at, 0


def shift_plan(offset, parity, sign):
    found = [source_of(par, sign * (off - 1)) for off, par in zip(offset, parity)]
    bits = [f[0] for f in found]
    steps = [f[1] for f in found]
    return bits[0] * 4 + bits[1] * 2 + bits[2], steps


def token_masks(tokens):
    at = (tokens // (GS * GS), (tokens // GS) % GS, tokens % GS)
    masks = {}
    for axis in range(3):
        masks[axis, 1] = at[axis] < GS - 1
        masks[axis, -1] = at[axis] > 0
    return masks


def shifted(values, steps, masks):
    delta = steps[0] * GS * GS + steps[1] * GS + steps[2]
    if delta == 0 and not any(steps):
        return values
    moved = pltpu.roll(values, (-delta) % NTOK, 1)
    keep = None
    for axis in range(3):
        if steps[axis]:
            mask = masks[axis, steps[axis]]
            keep = mask if keep is None else keep & mask
    return jnp.where(keep, moved, 0.0)


def lanes(parity):
    return slice(parity * NTOK, (parity + 1) * NTOK)


def decoder_forward_kernel(
    up_ref,
    deconv_bias_ref,
    conv_ref,
    conv_bias_ref,
    head_ref,
    head_bias_ref,
    labels_ref,
    batch_ref,
    conv_in_ref,
    grid_slope_ref,
    conv_slope_ref,
    features_ref,
    chance_ref,
    sums_ref,
    conved_ref,
):
    tokens = lax.broadcasted_iota(jnp.int32, (CF, NTOK), 1)
    masks = token_masks(tokens)
    for parity in range(8):
        conved_ref[:, lanes(parity)] = jnp.broadcast_to(conv_bias_ref[...], (CF, NTOK))
    for parity in range(8):
        cell = up_ref[parity * DEC : (parity + 1) * DEC, :] + deconv_bias_ref[...]
        value, slope = gelu_and_slope(cell)
        low = value.astype(jnp.bfloat16)
        conv_in_ref[:, lanes(parity)] = low
        grid_slope_ref[:, lanes(parity)] = slope
        products = dot_nn(conv_ref[...], low)
        for at, offset in enumerate(OFFSETS):
            target, back_steps = shift_plan(offset, PARITIES[parity], -1)
            forward = [-s for s in back_steps]
            piece = shifted(products[at * CF : (at + 1) * CF, :], forward, masks)
            conved_ref[:, lanes(target)] += piece
    rows = lax.broadcasted_iota(jnp.int32, (CF, NTOK), 0)
    hit = jnp.zeros((CF, 1), jnp.float32)
    predicted = jnp.zeros((CF, 1), jnp.float32)
    truth = jnp.zeros((CF, 1), jnp.float32)
    entropy = jnp.zeros((CF, 1), jnp.float32)
    for parity in range(8):
        value, slope = gelu_and_slope(conved_ref[:, lanes(parity)])
        conv_slope_ref[:, lanes(parity)] = slope
        features = value.astype(jnp.bfloat16)
        features_ref[:, lanes(parity)] = features
        logits = dot_nn(head_ref[...], features) + head_bias_ref[...]
        logits = jnp.where(rows < NCLS, logits, -1e30)
        center = logits - jnp.max(logits, 0, keepdims=True)
        log_prob = center - jnp.log(jnp.sum(jnp.exp(center), 0, keepdims=True))
        chance = jnp.exp(log_prob)
        target = (rows == labels_ref[parity : parity + 1, :]).astype(jnp.float32)
        chance_ref[:, lanes(parity)] = chance
        hit += jnp.sum(chance * target, 1, keepdims=True)
        predicted += jnp.sum(chance, 1, keepdims=True)
        truth += jnp.sum(target, 1, keepdims=True)
        entropy -= jnp.sum(jnp.where(target > 0, log_prob, 0.0), 1, keepdims=True)
    lane = lax.broadcasted_iota(jnp.int32, (CF, BS), 1)
    base = batch_ref[...] * 3
    sums_ref[...] = (
        jnp.where(lane == base, hit, 0.0)
        + jnp.where(lane == base + 1, predicted, 0.0)
        + jnp.where(lane == base + 2, truth, 0.0)
        + jnp.where(lane == 3 * MB, entropy, 0.0)
    )


def decoder_backward_kernel(
    all_crops,
    sums_ref,
    batch_ref,
    labels_ref,
    chance_ref,
    features_ref,
    conv_slope_ref,
    grid_slope_ref,
    conv_in_ref,
    conv_t_ref,
    head_t_ref,
    gu_ref,
    conv_grad_ref,
    head_grad_ref,
    small_ref,
    deconv_grad_ref,
    spread_ref,
):
    sums = sums_ref[...]
    lane = lax.broadcasted_iota(jnp.int32, (CF, BS), 1)
    row = lax.broadcasted_iota(jnp.int32, (CF, BS), 0)
    live = (lane < 3 * MB) & (lane % 3 == 0) & (row < NCLS)
    under = pltpu.roll(sums, BS - 1, 1) + pltpu.roll(sums, BS - 2, 1) + 1.0
    under = jnp.where(live, under, 1.0)
    over = 2.0 * sums + 1.0
    dice = jnp.where(live, over / under, 0.0)
    mean_dice = jnp.sum(jnp.sum(dice, 1, keepdims=True), 0, keepdims=True) / (NCLS * MB)
    entropy_lane = jnp.where(lane == 3 * MB, sums, 0.0)
    entropy = jnp.sum(jnp.sum(entropy_lane, 1, keepdims=True), 0, keepdims=True)
    loss = entropy / (all_crops * CELLS) + (1.0 - mean_dice)
    own = live & (lane == batch_ref[...] * 3)
    d_hit = jnp.sum(jnp.where(own, -2.0 / (MB * NCLS) / under, 0.0), 1, keepdims=True)
    d_predicted = jnp.sum(
        jnp.where(own, (1.0 / (MB * NCLS)) * over / (under * under), 0.0), 1, keepdims=True
    )
    tokens = lax.broadcasted_iota(jnp.int32, (CF, NTOK), 1)
    masks = token_masks(tokens)
    rows = lax.broadcasted_iota(jnp.int32, (CF, NTOK), 0)
    head_bias = jnp.zeros((CF, 1), jnp.float32)
    conv_bias = jnp.zeros((CF, 1), jnp.float32)
    head_grad = jnp.zeros((CF, CF), jnp.float32)
    for parity in range(8):
        chance = chance_ref[:, lanes(parity)]
        target = (rows == labels_ref[parity : parity + 1, :]).astype(jnp.float32)
        back = (d_hit * target + d_predicted) * chance - target * (1.0 / (all_crops * CELLS))
        logits = back - chance * jnp.sum(back, 0, keepdims=True)
        head_bias += jnp.sum(logits, 1, keepdims=True)
        low = logits.astype(jnp.bfloat16)
        head_grad += dot_nt(features_ref[:, lanes(parity)], low)
        conved = conv_slope_ref[:, lanes(parity)] * dot_nn(head_t_ref[...], low)
        conv_bias += jnp.sum(conved, 1, keepdims=True)
        rounded = conved.astype(jnp.bfloat16).astype(jnp.float32)
        for at, offset in enumerate(OFFSETS):
            target_cell, steps = shift_plan(offset, PARITIES[parity], 1)
            piece = shifted(rounded, [-s for s in steps], masks)
            spread_ref[at * CF : (at + 1) * CF, lanes(target_cell)] = piece.astype(jnp.bfloat16)
    head_grad_ref[...] = head_grad
    small_ref[...] = (
        jnp.where(lane == 0, head_bias, 0.0)
        + jnp.where(lane == 1, conv_bias, 0.0)
        + jnp.where(lane == 2, loss, 0.0)
    )
    conv_grad = jnp.zeros((27 * CF, DEC), jnp.float32)
    deconv_grad = jnp.zeros((DEC, 1), jnp.float32)
    for parity in range(8):
        spread = spread_ref[:, lanes(parity)]
        conv_grad += dot_nt(spread, conv_in_ref[:, lanes(parity)])
        back = grid_slope_ref[:, lanes(parity)] * dot_nn(conv_t_ref[...], spread)
        deconv_grad += jnp.sum(back, 1, keepdims=True)
        gu_ref[parity * DEC : (parity + 1) * DEC, :] = back.astype(jnp.bfloat16)
    conv_grad_ref[...] = conv_grad
    deconv_grad_ref[...] = jnp.broadcast_to(deconv_grad, (DEC, BS))


def whole_specs(number):
    return [pl.BlockSpec(memory_space=pltpu.VMEM)] * number


def decoder_forward(up_t, deconv_bias, conv_low, conv_bias, head_low, head_bias, labels, batch):
    shapes = (
        jax.ShapeDtypeStruct((DEC, CELLS), jnp.bfloat16),
        jax.ShapeDtypeStruct((DEC, CELLS), jnp.float32),
        jax.ShapeDtypeStruct((CF, CELLS), jnp.float32),
        jax.ShapeDtypeStruct((CF, CELLS), jnp.bfloat16),
        jax.ShapeDtypeStruct((CF, CELLS), jnp.float32),
        jax.ShapeDtypeStruct((CF, BS), jnp.float32),
    )
    return pl.pallas_call(
        decoder_forward_kernel,
        out_shape=shapes,
        in_specs=whole_specs(8),
        out_specs=tuple(whole_specs(6)),
        scratch_shapes=[pltpu.VMEM((CF, CELLS), jnp.float32)],
        compiler_params=pltpu.CompilerParams(vmem_limit_bytes=40 * MIB),
        cost_estimate=pl.CostEstimate(
            flops=2 * 27 * CF * DEC * CELLS, bytes_accessed=6 * MIB, transcendentals=DEC * CELLS
        ),
        name="decoder_forward",
    )(up_t, deconv_bias, conv_low, conv_bias, head_low, head_bias, labels, batch)


def decoder_backward(
    all_crops, sums, batch, labels, chance, features, conv_slope, grid_slope, conv_in, conv_t, head_t
):
    shapes = (
        jax.ShapeDtypeStruct((8 * DEC, NTOK), jnp.bfloat16),
        jax.ShapeDtypeStruct((27 * CF, DEC), jnp.float32),
        jax.ShapeDtypeStruct((CF, CF), jnp.float32),
        jax.ShapeDtypeStruct((CF, BS), jnp.float32),
        jax.ShapeDtypeStruct((DEC, BS), jnp.float32),
    )
    return pl.pallas_call(
        functools.partial(decoder_backward_kernel, all_crops),
        out_shape=shapes,
        in_specs=whole_specs(10),
        out_specs=tuple(whole_specs(5)),
        scratch_shapes=[pltpu.VMEM((27 * CF, CELLS), jnp.bfloat16)],
        compiler_params=pltpu.CompilerParams(vmem_limit_bytes=40 * MIB),
        cost_estimate=pl.CostEstimate(
            flops=4 * 27 * CF * DEC * CELLS, bytes_accessed=6 * MIB, transcendentals=0
        ),
        name="decoder_backward",
    )(sums, batch, labels, chance, features, conv_slope, grid_slope, conv_in, conv_t, head_t)


LAYERS = 4
GATHER_LAG = 2
THIRDS = tuple((8 * BS * i, 8 * BS) for i in range(3))
PIECES = 32
BLOCK_ROWS = 24 * BS
AUX_ROWS = 256
CHUNK = BLOCK_ROWS + AUX_ROWS
ROWS_N = 2 * CHUNK // PIECES
ROWS_F = BLOCK_ROWS // PIECES
LAG = 2
HOP_LAG = 2
AHEAD = 3
CORE_SLOTS = 8
SEND_SLOTS = 4
KEEP = 8
SUM_SLOTS = 12


def remote(src, dst, send_sem, recv_sem, device):
    return pltpu.make_async_remote_copy(
        src_ref=src,
        dst_ref=dst,
        send_sem=send_sem,
        recv_sem=recv_sem,
        device_id=device,
        device_id_type=MESH,
    )


def places():
    dp, x = lax.axis_index("dp"), lax.axis_index("mp")
    z, y, c = dp // 4, (dp // 2) % 2, dp % 2
    return dict(
        dp=dp,
        x=x,
        y=y,
        z=z,
        c=c,
        at_core=(dp + 1 - 2 * c, x),
        at_x=(dp, 1 - x),
        at_y=(dp + 2 - 4 * y, x),
        above=(lax.rem(dp + 4, 4 * LAYERS), x),
        below=(lax.rem(dp + 4 * LAYERS - 4, 4 * LAYERS), x),
    )


def greet_neighbours(at):
    barrier = pltpu.get_barrier_semaphore()
    for name in ("at_core", "at_x", "at_y"):
        pl.semaphore_signal(barrier, inc=1, device_id=at[name], device_id_type=MESH)

    @pl.when(at["z"] < LAYERS - 1)
    def _():
        pl.semaphore_signal(barrier, inc=1, device_id=at["above"], device_id_type=MESH)

    @pl.when(at["z"] > 0)
    def _():
        pl.semaphore_signal(barrier, inc=1, device_id=at["below"], device_id_type=MESH)

    peers = 3 + jnp.minimum(at["z"], 1) + jnp.minimum(LAYERS - 1 - at["z"], 1)
    pl.semaphore_wait(barrier, peers)


def gather_kernel(parts, by_x, skip, middle, in_ref, out_ref, local_sem, up_sem, down_sem, z_recv, x_send, x_recv, y_send, y_recv, core_send, core_recv):
    at = places()
    x, y, z, c = at["x"], at["y"], at["z"], at["c"]
    last = LAYERS - 1

    def spot(l, y_at, c_at, x_at, p):
        return out_ref.at[x_at, l * 4 + y_at * 2 + c_at, pl.ds(*parts[p])]

    def send(ref, send_sem, recv_sem, device):
        return remote(ref, ref, send_sem, recv_sem, device)

    def up(l, p):
        return send(spot(l, y, c, x, p), up_sem.at[l, p], z_recv.at[l, p], at["above"])

    def down(l, p):
        return send(spot(l, y, c, x, p), down_sem.at[l, p], z_recv.at[l, p], at["below"])

    def x_direct(l, p, x_at):
        return send(spot(l, y, c, x_at, p), x_send.at[l, p, 0], x_recv.at[l, p, 0], at["at_x"])

    def y_direct(l, p, y_at):
        return send(spot(l, y_at, c, x, p), y_send.at[l, p, 0], y_recv.at[l, p, 0], at["at_y"])

    def diagonal(l, p, y_at, x_at):
        if p < by_x:
            return send(spot(l, y_at, c, x_at, p), y_send.at[l, p, 1], y_recv.at[l, p, 1], at["at_y"])
        return send(spot(l, y_at, c, x_at, p), x_send.at[l, p, 1], x_recv.at[l, p, 1], at["at_x"])

    def relayed(l, p):
        return diagonal(l, p, y, 1 - x) if p < by_x else diagonal(l, p, 1 - y, x)

    def core(l, p, kind, c_at):
        y_at, x_at = ((y, x), (1 - y, x), (y, 1 - x), (1 - y, 1 - x))[kind]
        return send(
            spot(l, y_at, c_at, x_at, p),
            core_send.at[l, p, kind],
            core_recv.at[l, p, kind],
            at["at_core"],
        )

    def wide(l):
        return (l > 0) if skip else (l >= 0)

    own = pltpu.make_async_copy(in_ref, out_ref.at[x, at["dp"]], local_sem)
    own.start()
    greet_neighbours(at)
    own.wait()

    def arrive(l, p, came_up, came_down):
        if not (came_up and came_down):
            up(l, p).wait_recv()
        if came_up:

            @pl.when(z < last)
            def _():
                up(l, p).start()

        if came_down:

            @pl.when(z > 0)
            def _():
                down(l, p).start()

        @pl.when(wide(l))
        def _():
            x_direct(l, p, x).start()

        y_direct(l, p, y).start()
        core(l, p, 0, c).start()

    def relay(l, p):
        y_direct(l, p, 1 - y).wait_recv()

        @pl.when(wide(l))
        def _():
            if p >= by_x:
                relayed(l, p).start()
            x_direct(l, p, 1 - x).wait_recv()
            if p < by_x:
                relayed(l, p).start()
            core(l, p, 2, c).start()

        core(l, p, 1, c).start()

    def finish(l, p):
        @pl.when(wide(l))
        def _():
            diagonal(l, p, 1 - y, 1 - x).wait_recv()
            core(l, p, 3, c).start()

    def held(l, p):
        return ((l > 0) & (l < last)) if p in middle else ((l >= 0) & (l <= last))

    number = len(parts)

    def both(tick, run):
        if tick < 0 or tick >= LAYERS * number:
            return
        r, p = tick // number, tick % number
        if r == 0:

            @pl.when(held(z, p))
            def _():
                run(z, p, True, True)

            return

        @pl.when(held(z - r, p))
        def _():
            run(z - r, p, True, False)

        @pl.when(held(z + r, p))
        def _():
            run(z + r, p, False, True)

    for tick in range(LAYERS * number + 2 * GATHER_LAG):
        both(tick, arrive)
        both(tick - GATHER_LAG, lambda l, p, up_way, down_way: relay(l, p))
        both(tick - 2 * GATHER_LAG, lambda l, p, up_way, down_way: finish(l, p))

    def settle_part(l, p):
        for kind in (0, 1):
            core(l, p, kind, 1 - c).wait_recv()
            core(l, p, kind, c).wait_send()
        y_direct(l, p, y).wait_send()

        @pl.when(wide(l))
        def _():
            for kind in (2, 3):
                core(l, p, kind, 1 - c).wait_recv()
                core(l, p, kind, c).wait_send()
            x_direct(l, p, x).wait_send()
            relayed(l, p).wait_send()

        @pl.when((l <= z) & (z < last))
        def _():
            up(l, p).wait_send()

        @pl.when((l >= z) & (z > 0))
        def _():
            down(l, p).wait_send()

    def settle(l, carry):
        for p in range(number):
            pl.when(held(l, p))(functools.partial(settle_part, l, p))
        return carry

    lax.fori_loop(0, LAYERS, settle, 0)


def gather_all(values, parts, by_x, skip, middle, collective_id, name):
    rows = values.shape[0]
    number = len(parts)

    def sems(*shape):
        return pltpu.SemaphoreType.DMA(shape)

    return pl.pallas_call(
        functools.partial(gather_kernel, parts, by_x, skip, middle),
        out_shape=jax.ShapeDtypeStruct((MP, 4 * LAYERS, rows, BS), values.dtype),
        in_specs=[pl.BlockSpec(memory_space=pl.ANY)],
        out_specs=pl.BlockSpec(memory_space=pl.ANY),
        scratch_shapes=[
            pltpu.SemaphoreType.DMA,
            sems(LAYERS, number),
            sems(LAYERS, number),
            sems(LAYERS, number),
            sems(LAYERS, number, 2),
            sems(LAYERS, number, 2),
            sems(LAYERS, number, 2),
            sems(LAYERS, number, 2),
            sems(LAYERS, number, 4),
            sems(LAYERS, number, 4),
        ],
        compiler_params=pltpu.CompilerParams(
            collective_id=collective_id, has_side_effects=True, vmem_limit_bytes=32 * MIB
        ),
        cost_estimate=pl.CostEstimate(flops=0, bytes_accessed=32 * rows * BS * 4, transcendentals=0),
        name=name,
    )(values)


def reduce_kernel(
    n_ref,
    e_ref,
    f_ref,
    out_ref,
    square_ref,
    own_n,
    own_f,
    core_n,
    core_f,
    keep_n,
    keep_f,
    xs_n,
    ys_n,
    ys_f,
    xr_n,
    yr_n,
    yr_f,
    sum_n,
    sum_f,
    up_n,
    down_n,
    up_f,
    down_e,
    own_sem,
    core_send,
    core_recv,
    credit,
    xs_sem,
    ys_n_sem,
    ys_f_sem,
    xr_sem,
    yr_n_sem,
    yr_f_sem,
    z_n_sem,
    z_f_sem,
    up_n_sem,
    down_n_sem,
    up_f_sem,
    down_e_sem,
):
    at = places()
    x, y, z, c = at["x"], at["y"], at["z"], at["c"]
    last = LAYERS - 1

    def layer_of(s):
        return 1 + lax.rem(s, 2)

    def rows_of(s):
        return pl.ds(pl.multiple_of((s // 2) * ROWS_N, 8), ROWS_N)

    def rows_f(s):
        return pl.ds(pl.multiple_of(s * ROWS_F, 8), ROWS_F)

    def own_loads(s):
        slot = lax.rem(s, 3)
        mine = n_ref.at[:, layer_of(s) - 1, :, c, rows_of(s)]
        return (
            pltpu.make_async_copy(mine, own_n.at[slot], own_sem.at[slot, 0]),
            pltpu.make_async_copy(e_ref.at[:, c, rows_f(s)], own_f.at[slot, 0], own_sem.at[slot, 1]),
            pltpu.make_async_copy(f_ref.at[:, c, rows_f(s)], own_f.at[slot, 1], own_sem.at[slot, 2]),
        )

    def core_copies(s):
        slot = lax.rem(s, CORE_SLOTS)
        sources = (
            n_ref.at[:, layer_of(s) - 1, :, 1 - c, rows_of(s)],
            e_ref.at[:, 1 - c, rows_f(s)],
            f_ref.at[:, 1 - c, rows_f(s)],
        )
        targets = (core_n.at[slot], core_f.at[slot, 0], core_f.at[slot, 1])
        return [
            remote(source, target, core_send.at[s, i], core_recv.at[slot, i], at["at_core"])
            for i, (source, target) in enumerate(zip(sources, targets))
        ]

    def x_copy(s):
        slot = lax.rem(s, SEND_SLOTS)
        return remote(xs_n.at[slot], xr_n.at[s], xs_sem.at[slot], xr_sem.at[s], at["at_x"])

    def y_copy_f(s):
        slot = lax.rem(s, SEND_SLOTS)
        return remote(ys_f.at[slot], yr_f.at[s], ys_f_sem.at[slot], yr_f_sem.at[s], at["at_y"])

    def y_copy(s):
        slot = lax.rem(s, SEND_SLOTS)
        return remote(ys_n.at[slot], yr_n.at[s], ys_n_sem.at[slot], yr_n_sem.at[s], at["at_y"])

    def up_copy(s):
        slot = lax.rem(s, SUM_SLOTS)
        return remote(sum_n.at[slot], up_n.at[s], z_n_sem.at[slot], up_n_sem.at[s], at["above"])

    def down_copy(s):
        slot = lax.rem(s, SUM_SLOTS)
        return remote(sum_n.at[slot], down_n.at[s], z_n_sem.at[slot], down_n_sem.at[s], at["below"])

    def down_copy_e(s):
        slot = lax.rem(s, SUM_SLOTS)
        source, sem = sum_f.at[slot, 0], z_f_sem.at[slot, 0]
        return remote(source, down_e.at[s], sem, down_e_sem.at[s], at["below"])

    def up_copy_f(s):
        slot = lax.rem(s, SUM_SLOTS)
        source, sem = sum_f.at[slot, 1], z_f_sem.at[slot, 1]
        return remote(source, up_f.at[s], sem, up_f_sem.at[s], at["above"])

    def add_squares(values):
        square_ref[...] += jnp.sum((values * values).reshape(-1, 8, BS), 0)

    square_ref[...] = jnp.zeros((8, BS), jnp.float32)
    for s in range(2):
        for copy in own_loads(s):
            copy.start()
    greet_neighbours(at)
    for s in range(AHEAD):
        for copy in core_copies(s):
            copy.start()

    def first(s):
        @pl.when(s + 2 < PIECES)
        def _():
            for copy in own_loads(s + 2):
                copy.start()

        @pl.when(s + AHEAD < PIECES)
        def _():
            @pl.when(s + AHEAD >= CORE_SLOTS)
            def _():
                pl.semaphore_wait(credit, 1)

            for copy in core_copies(s + AHEAD):
                copy.start()

        for copy in own_loads(s):
            copy.wait()
        for copy in core_copies(s):
            copy.wait_recv()

        @pl.when(s >= SEND_SLOTS)
        def _():
            x_copy(s - SEND_SLOTS).wait_send()
            y_copy_f(s - SEND_SLOTS).wait_send()

        own, core = lax.rem(s, 3), lax.rem(s, CORE_SLOTS)
        send, keep = lax.rem(s, SEND_SLOTS), lax.rem(s, KEEP)
        xs_n[send] = own_n[own, 1 - x] + core_n[core, 1 - x]
        x_copy(s).start()
        for kind in range(2):
            ys_f[send, kind] = own_f[own, kind, 1 - y] + core_f[core, kind, 1 - y]
        y_copy_f(s).start()
        keep_n[keep] = own_n[own, x] + core_n[core, x]
        for kind in range(2):
            keep_f[keep, kind] = own_f[own, kind, y] + core_f[core, kind, y]

        @pl.when(s + CORE_SLOTS < PIECES)
        def _():
            pl.semaphore_signal(credit, inc=1, device_id=at["at_core"], device_id_type=MESH)

    def second(s):
        x_copy(s).wait_recv()

        @pl.when(s >= SEND_SLOTS)
        def _():
            y_copy(s - SEND_SLOTS).wait_send()

        send, keep = lax.rem(s, SEND_SLOTS), lax.rem(s, KEEP)
        ys_n[send] = keep_n[keep, 1 - y] + xr_n[s, 1 - y]
        y_copy(s).start()
        keep_n[keep, y] = keep_n[keep, y] + xr_n[s, y]

    def third(s):
        y_copy_f(s).wait_recv()
        y_copy(s).wait_recv()

        @pl.when((s >= SUM_SLOTS) & (z != layer_of(s)))
        def _():
            up_copy(s - SUM_SLOTS).wait_send()

        @pl.when((s >= SUM_SLOTS) & (z > 0))
        def _():
            down_copy_e(s - SUM_SLOTS).wait_send()

        @pl.when((s >= SUM_SLOTS) & (z < last))
        def _():
            up_copy_f(s - SUM_SLOTS).wait_send()

        slot, keep = lax.rem(s, SUM_SLOTS), lax.rem(s, KEEP)
        sum_n[slot] = keep_n[keep, y] + yr_n[s]
        sum_f[slot] = keep_f[keep] + yr_f[s]

    def along(s, hop):
        slot = lax.rem(s, SUM_SLOTS)
        layer = layer_of(s)
        away = jnp.where(z < layer, z, jnp.where(z > layer, last - z, jnp.maximum(z, last - z)))

        @pl.when(away == hop)
        def _():
            @pl.when((z > 0) & (z <= layer))
            def _():
                up_copy(s).wait_recv()
                sum_n[slot] = sum_n[slot] + up_n[s]

            @pl.when((z < last) & (z >= layer))
            def _():
                down_copy(s).wait_recv()
                sum_n[slot] = sum_n[slot] + down_n[s]

            @pl.when(z < layer)
            def _():
                up_copy(s).start()

            @pl.when(z > layer)
            def _():
                down_copy(s).start()

            @pl.when(z == layer)
            def _():
                out_ref[rows_of(s)] = sum_n[slot]
                piece = s // 2
                whole, cut = BLOCK_ROWS // ROWS_N, BLOCK_ROWS % ROWS_N

                @pl.when(piece <= whole)
                def _():
                    add_squares(sum_n[slot, pl.ds(0, cut)])

                @pl.when(piece < whole)
                def _():
                    add_squares(sum_n[slot, pl.ds(cut, ROWS_N - cut)])

        @pl.when(jnp.where(z == 0, last, last - z) == hop)
        def _():
            @pl.when(z < last)
            def _():
                down_copy_e(s).wait_recv()
                sum_f[slot, 0] = sum_f[slot, 0] + down_e[s]

            @pl.when(z > 0)
            def _():
                down_copy_e(s).start()

            @pl.when(z == 0)
            def _():
                out_ref[rows_f(s)] = sum_f[slot, 0]
                add_squares(sum_f[slot, 0])

        @pl.when(z == hop)
        def _():
            @pl.when(z > 0)
            def _():
                up_copy_f(s).wait_recv()
                sum_f[slot, 1] = sum_f[slot, 1] + up_f[s]

            @pl.when(z < last)
            def _():
                up_copy_f(s).start()

            @pl.when(z == last)
            def _():
                out_ref[rows_f(s)] = sum_f[slot, 1]
                add_squares(sum_f[slot, 1])

    def guarded(run, s):
        @pl.when((s >= 0) & (s < PIECES))
        def _():
            run(s)

    def step(t, carry):
        guarded(first, t)
        guarded(second, t - LAG)
        guarded(third, t - 2 * LAG)
        for hop in range(LAYERS):
            guarded(functools.partial(along, hop=hop), t - 2 * LAG - hop * HOP_LAG)
        return carry

    lax.fori_loop(0, PIECES + 2 * LAG + (LAYERS - 1) * HOP_LAG, step, 0)

    def drain_sends(i, carry):
        s = PIECES - SEND_SLOTS + i
        for copy in (x_copy(s), y_copy_f(s), y_copy(s)):
            copy.wait_send()
        return carry

    lax.fori_loop(0, SEND_SLOTS, drain_sends, 0)

    def drain_sums(i, carry):
        s = PIECES - SUM_SLOTS + i

        @pl.when(z != layer_of(s))
        def _():
            up_copy(s).wait_send()

        @pl.when(z > 0)
        def _():
            down_copy_e(s).wait_send()

        @pl.when(z < last)
        def _():
            up_copy_f(s).wait_send()

        return carry

    lax.fori_loop(0, SUM_SLOTS, drain_sums, 0)

    def drain_core(s, carry):
        for copy in core_copies(s):
            copy.wait_send()
        return carry

    lax.fori_loop(0, PIECES, drain_core, 0)

    @pl.when((z == 0) | (z == last))
    def _():
        out_ref[pl.ds(BLOCK_ROWS, AUX_ROWS)] = jnp.zeros((AUX_ROWS, BS), jnp.float32)


def reduce_to_owners(rest, first, final):
    def room(*shape):
        return pltpu.VMEM(shape + (BS,), jnp.float32)

    def sems(*shape):
        return pltpu.SemaphoreType.DMA(shape)

    return pl.pallas_call(
        reduce_kernel,
        out_shape=(
            jax.ShapeDtypeStruct((CHUNK, BS), jnp.float32),
            jax.ShapeDtypeStruct((8, BS), jnp.float32),
        ),
        in_specs=[pl.BlockSpec(memory_space=pl.ANY)] * 3,
        out_specs=(pl.BlockSpec(memory_space=pltpu.VMEM),) * 2,
        scratch_shapes=[
            room(3, 2, 2, ROWS_N),
            room(3, 2, 2, ROWS_F),
            room(CORE_SLOTS, 2, 2, ROWS_N),
            room(CORE_SLOTS, 2, 2, ROWS_F),
            room(KEEP, 2, ROWS_N),
            room(KEEP, 2, ROWS_F),
            room(SEND_SLOTS, 2, ROWS_N),
            room(SEND_SLOTS, ROWS_N),
            room(SEND_SLOTS, 2, ROWS_F),
            room(PIECES, 2, ROWS_N),
            room(PIECES, ROWS_N),
            room(PIECES, 2, ROWS_F),
            room(SUM_SLOTS, ROWS_N),
            room(SUM_SLOTS, 2, ROWS_F),
            room(PIECES, ROWS_N),
            room(PIECES, ROWS_N),
            room(PIECES, ROWS_F),
            room(PIECES, ROWS_F),
            sems(3, 3),
            sems(PIECES, 3),
            sems(CORE_SLOTS, 3),
            pltpu.SemaphoreType.REGULAR,
            sems(SEND_SLOTS),
            sems(SEND_SLOTS),
            sems(SEND_SLOTS),
            sems(PIECES),
            sems(PIECES),
            sems(PIECES),
            sems(SUM_SLOTS),
            sems(SUM_SLOTS, 2),
            sems(PIECES),
            sems(PIECES),
            sems(PIECES),
            sems(PIECES),
        ],
        compiler_params=pltpu.CompilerParams(
            collective_id=1, has_side_effects=True, vmem_limit_bytes=58 * MIB
        ),
        cost_estimate=pl.CostEstimate(flops=0, bytes_accessed=100 * MIB, transcendentals=0),
        name="reduce_to_owners",
    )(rest, first, final)


MATRICES = [
    (96, 6, 9, 3, True),
    (150, 3, 6, 3, False),
    (168, 6, 12, 3, True),
    (240, 12, 6, 4, False),
    (312, 9, 8, 3, False),
]
LOADS = 4


def unblock_kernel(plan, kinds, blocks_ref, *refs):
    outs, tiles = refs[:kinds], refs[kinds : 2 * kinds]
    loaded, load_sem, store_sem = refs[2 * kinds :]
    part = lax.axis_index("mp")

    def load(i):
        kind, m, first, rows, per_row, row, col = plan[i]
        number = rows * per_row
        return pltpu.make_async_copy(
            blocks_ref.at[part if m is None else m, pl.ds(first, number)],
            loaded.at[i % LOADS, pl.ds(0, number)],
            load_sem.at[i % LOADS],
        )

    def store(i, slot):
        kind, m, first, rows, per_row, row, col = plan[i]
        return pltpu.make_async_copy(
            tiles[kind].at[slot],
            outs[kind].at[pl.ds(row, rows * BS), pl.ds(col, per_row * BS)],
            store_sem.at[kind, slot],
        )

    history = [[] for _ in range(kinds)]
    for i in range(min(LOADS - 1, len(plan))):
        load(i).start()
    for i, (kind, m, first, rows, per_row, row, col) in enumerate(plan):
        if i + LOADS - 1 < len(plan):
            load(i + LOADS - 1).start()
        load(i).wait()
        slot = len(history[kind]) % 2
        if len(history[kind]) >= 2:
            store(*history[kind][-2]).wait()
        for r in range(rows):
            for c in range(per_row):
                tiles[kind][slot, r * BS : (r + 1) * BS, c * BS : (c + 1) * BS] = loaded[
                    i % LOADS, r * per_row + c
                ]
        history[kind].append((i, slot))
        store(i, slot).start()
    for done in history:
        for entry in done[-2:]:
            store(*entry).wait()


def unblock(gathered, embedding):
    plan, shapes, tiles = [], [], []
    if embedding:
        plan = [(0, None, 24 * i, 4, 6, 4 * BS * i, 0) for i in range(4)]
        shapes, tiles = [(PV // MP, D)], [(4 * BS, D)]
    else:
        for kind, (first, rows, per_row, step, beside) in enumerate(MATRICES):
            tall, wide = rows * BS, per_row * BS
            shapes.append((tall, MP * wide) if beside else (MP * tall, wide))
            tiles.append((step * BS, wide))
            for m in range(MP):
                for at in range(0, rows, step):
                    row = at * BS + (0 if beside else m * tall)
                    plan.append(
                        (kind, m, first + at * per_row, step, per_row, row, m * wide if beside else 0)
                    )
    anywhere = pl.BlockSpec(memory_space=pl.ANY)
    largest = max(entry[3] * entry[4] for entry in plan)
    return pl.pallas_call(
        functools.partial(unblock_kernel, plan, len(shapes)),
        out_shape=tuple(jax.ShapeDtypeStruct(shape, jnp.bfloat16) for shape in shapes),
        in_specs=[anywhere],
        out_specs=tuple([anywhere] * len(shapes)),
        scratch_shapes=[pltpu.VMEM((2,) + tile, jnp.bfloat16) for tile in tiles]
        + [
            pltpu.VMEM((LOADS, largest, BS, BS), jnp.bfloat16),
            pltpu.SemaphoreType.DMA((LOADS,)),
            pltpu.SemaphoreType.DMA((len(shapes), 2)),
        ],
        compiler_params=pltpu.CompilerParams(vmem_limit_bytes=32 * MIB),
        cost_estimate=pl.CostEstimate(
            flops=0, bytes_accessed=(6 if embedding else 38) * MIB, transcendentals=0
        ),
        name="unblock_embedding" if embedding else "unblock",
    )(gathered)


def blocks_kernel(first_block, per_row, step_rows, transposed, pairs, *refs):
    out_ref, tiles, sems = refs[-3:]
    m, i = pl.program_id(0), pl.program_id(1)
    steps = pl.num_programs(1)
    at = m * steps + i
    slot = lax.rem(at, 2)
    total = pl.num_programs(0) * steps

    def drain(which):
        pltpu.make_async_copy(tiles.at[which], tiles.at[which], sems.at[which]).wait()

    @pl.when(at >= 2)
    def _():
        drain(slot)

    total_product = None
    for pair in range(pairs):
        x_ref, g_ref = refs[2 * pair], refs[2 * pair + 1]
        term = dot(x_ref[...], g_ref[...], ((0,), (1,) if transposed else (0,)))
        total_product = term if total_product is None else total_product + term
    tiles[slot] = total_product
    for r in range(step_rows):
        for c in range(per_row):
            block = first_block + (i * step_rows + r) * per_row + c
            chunk, at_row = block // 24, lax.rem(block, 24) * BS
            pltpu.make_async_copy(
                tiles.at[slot, r * BS : (r + 1) * BS, c * BS : (c + 1) * BS],
                out_ref.at[m, chunk, pl.ds(pl.multiple_of(at_row, BS), BS)],
                sems.at[slot],
            ).start()

    @pl.when(at == total - 1)
    def _():
        drain(slot)

        @pl.when(total > 1)
        def _():
            drain(1 - slot)


def grad_blocks(xs, gs, parts, rows, per_row, step_rows, first_block, split_x, split_g, buffer, name, chunks, depth, transposed=False, x_stride=None):
    steps = rows // step_rows
    x_stride = x_stride or steps
    tokens = xs[0].shape[0]
    width = per_row * BS
    x_spec = pl.BlockSpec(
        (tokens, step_rows * BS), (lambda m, i: (0, m * x_stride + i)) if split_x else (lambda m, i: (0, i))
    )
    if transposed:
        g_spec = pl.BlockSpec((width, tokens), lambda m, i: (0, 0))
    else:
        g_spec = pl.BlockSpec((tokens, width), (lambda m, i: (0, m)) if split_g else (lambda m, i: (0, 0)))
    anywhere = pl.BlockSpec(memory_space=pl.ANY)
    operands = [array for pair in zip(xs, gs) for array in pair] + ([] if buffer is None else [buffer])
    return pl.pallas_call(
        functools.partial(
            blocks_kernel, first_block, per_row, step_rows, transposed, len(xs)
        ),
        grid=(parts, steps),
        out_shape=jax.ShapeDtypeStruct((parts, chunks, depth, BS), jnp.float32),
        in_specs=[x_spec, g_spec] * len(xs) + ([] if buffer is None else [anywhere]),
        out_specs=anywhere,
        input_output_aliases={} if buffer is None else {2 * len(xs): 0},
        scratch_shapes=[
            pltpu.VMEM((2, step_rows * BS, width), jnp.float32),
            pltpu.SemaphoreType.DMA((2,)),
        ],
        compiler_params=pltpu.CompilerParams(vmem_limit_bytes=32 * MIB),
        cost_estimate=pl.CostEstimate(
            flops=2 * len(xs) * tokens * parts * rows * BS * width,
            bytes_accessed=parts * rows * BS * width * 4,
            transcendentals=0,
        ),
        name=name,
    )(*operands)


def fast_mesh():
    return lax.axis_size("dp") == 4 * LAYERS and lax.axis_size("mp") == MP


def sum_kernel(devices, in_ref, out_ref, slots, send_sem, recv_sem):
    me = lax.axis_index("dp") * MP + lax.axis_index("mp")
    barrier = pltpu.get_barrier_semaphore()

    def place(k):
        peer = lax.rem(me + k, devices)
        return (peer // MP, lax.rem(peer, MP))

    def greet(k, carry):
        pl.semaphore_signal(barrier, inc=1, device_id=place(k), device_id_type=MESH)
        return carry

    def copy(k, slot):
        return remote(in_ref, slots.at[slot], send_sem.at[k], recv_sem.at[slot], place(k))

    lax.fori_loop(1, devices, greet, 0)
    slots[me] = in_ref[...]
    pl.semaphore_wait(barrier, devices - 1)

    def push(k, carry):
        copy(k, me).start()
        return carry

    def pull(k, carry):
        copy(k, lax.rem(me + devices - k, devices)).wait_recv()
        return carry

    def settle(k, carry):
        copy(k, me).wait_send()
        return carry

    lax.fori_loop(1, devices, push, 0)
    lax.fori_loop(1, devices, pull, 0)
    total = slots[0]
    for i in range(1, devices):
        total = total + slots[i]
    out_ref[...] = total
    lax.fori_loop(1, devices, settle, 0)


def gather_weights(blocks):
    low = blocks.astype(jnp.bfloat16)[0, 0]
    if fast_mesh():
        gathered = gather_all(low.reshape(-1, BS), THIRDS, 1, True, (), 2, "gather_weights")
    else:
        gathered = lax.all_gather(low, ("dp", "mp"), axis=0, tiled=False)
        gathered = gathered.reshape((-1, MP) + low.shape).swapaxes(0, 1)
    return gathered.reshape(MP, -1, BS, BS)


def sum_sums(values):
    if not fast_mesh():
        return lax.psum(values, ("dp", "mp"))
    devices = 4 * LAYERS * MP
    whole = pl.BlockSpec(memory_space=pltpu.VMEM)
    return pl.pallas_call(
        functools.partial(sum_kernel, devices),
        out_shape=jax.ShapeDtypeStruct(values.shape, jnp.float32),
        in_specs=[whole],
        out_specs=whole,
        scratch_shapes=[
            pltpu.VMEM((devices,) + values.shape, jnp.float32),
            pltpu.SemaphoreType.DMA((devices,)),
            pltpu.SemaphoreType.DMA((devices,)),
        ],
        compiler_params=pltpu.CompilerParams(collective_id=3, has_side_effects=True),
        name="sum_sums",
    )(values)


def swap_mp(values):
    return lax.ppermute(values, "mp", [(0, 1), (1, 0)])


def reduce_plain(rest, first, final):
    part = lax.axis_index("mp")
    own = (jnp.arange(MP) == part).astype(jnp.float32)
    ends = [piece.reshape(1, -1, BS, BS) * own[:, None, None, None] for piece in (first, final)]
    dp = lax.axis_size("dp")
    every = jnp.concatenate([ends[0], rest, ends[1]], 1)
    every = every.reshape(MP, dp, -1, BS, BS).transpose(1, 0, 2, 3, 4)
    return lax.psum_scatter(
        every.reshape(dp * MP, -1, BS, BS), ("dp", "mp"), scatter_dimension=0, tiled=True
    )[0]


TALL = NTOK + 16
TILES = D // BS
CONV_AT = TILES * TALL
HEAD_AT = CONV_AT + 27 * CF
SMALL_AT = HEAD_AT + CF
DECONV_AT = SMALL_AT + CF
PACKED = DECONV_AT + DEC
AUX_ROOM = 8 * MP * AUX_ROWS
FLAT_ROWS = -(-NAUX // (8 * BS)) * 8


def pack_kernel(zero_ref, *refs):
    vectors, up_ref, conv_ref, head_ref, small_ref, deconv_ref = refs[:8], *refs[8:13]
    out_ref, rows_ref, sems = refs[14:]
    for j in range(TILES):
        lanes_at = slice(j * BS, (j + 1) * BS)
        base = j * TALL
        rows_ref[base : base + NTOK] = zero_ref[:, lanes_at]
        small_rows = [vector[:, lanes_at] for vector in vectors]
        small_rows += [up_ref[:, i * D + j * BS : i * D + (j + 1) * BS] for i in range(FF // D)]
        small_rows += [jnp.zeros((16 - len(small_rows), BS), jnp.float32)]
        rows_ref[base + NTOK : base + TALL] = jnp.concatenate(small_rows, 0)
    lane = lax.broadcasted_iota(jnp.int32, (CF, BS), 1)
    wide_lane = lax.broadcasted_iota(jnp.int32, (DEC, BS), 1)
    rows_ref[CONV_AT:HEAD_AT] = conv_ref[...]
    rows_ref[HEAD_AT:SMALL_AT] = head_ref[...]
    rows_ref[SMALL_AT:DECONV_AT] = jnp.where(lane < 2, small_ref[...], 0.0)
    rows_ref[DECONV_AT:PACKED] = jnp.where(wide_lane < 1, deconv_ref[...], 0.0)
    rows_ref[PACKED:AUX_ROOM] = jnp.zeros((AUX_ROOM - PACKED, BS), jnp.float32)
    copies = [
        pltpu.make_async_copy(
            rows_ref.at[pl.ds((m * 8 + chunk) * AUX_ROWS, AUX_ROWS)],
            out_ref.at[m, chunk, pl.ds(BLOCK_ROWS, AUX_ROWS)],
            sems.at[m * 8 + chunk],
        )
        for m in range(MP)
        for chunk in range(8)
    ]
    for copy in copies:
        copy.start()
    for copy in copies:
        copy.wait()


def pack_aux(zero, vectors, up_bias, conv, head, small, deconv, buffer):
    whole = pl.BlockSpec(memory_space=pltpu.VMEM)
    anywhere = pl.BlockSpec(memory_space=pl.ANY)
    operands = [zero] + [vector.reshape(1, D) for vector in vectors]
    operands += [up_bias.reshape(1, FF), conv, head, small, deconv]
    return pl.pallas_call(
        pack_kernel,
        out_shape=jax.ShapeDtypeStruct(buffer.shape, jnp.float32),
        in_specs=[whole] * len(operands) + [anywhere],
        out_specs=anywhere,
        input_output_aliases={len(operands): 0},
        scratch_shapes=[
            pltpu.VMEM((AUX_ROOM, BS), jnp.float32),
            pltpu.SemaphoreType.DMA((8 * MP,)),
        ],
        compiler_params=pltpu.CompilerParams(vmem_limit_bytes=32 * MIB),
        cost_estimate=pl.CostEstimate(flops=0, bytes_accessed=4 * MIB, transcendentals=0),
        name="pack_aux",
    )(*operands, buffer)


def unpack_kernel(sums_ref, rows_ref, norm_ref, turned):
    def pieces(start, stop):
        at = start
        while at < stop:
            m, chunk = at // (8 * AUX_ROWS), at // AUX_ROWS % 8
            end = min(stop, (at // AUX_ROWS + 1) * AUX_ROWS)
            first = at % AUX_ROWS
            yield at - start, sums_ref[m, 4 + chunk, first : first + end - at]
            at = end

    def packed(start, stop):
        found = [piece for _, piece in pieces(start, stop)]
        return found[0] if len(found) == 1 else jnp.concatenate(found, 0)

    square = jnp.zeros((8, BS), jnp.float32)
    for m in range(MP):
        for owner in range(4 * LAYERS):
            square += sums_ref[m, owner, AUX_ROWS:]
    rows_ref[FLAT_ROWS - 16 :] = jnp.zeros((16, BS), jnp.float32)
    after = NTOK * TILES
    for j in range(TILES):
        token_sum = jnp.zeros((1, BS), jnp.float32)
        for offset, piece in pieces(j * TALL, j * TALL + NTOK):
            rows_ref[pl.ds(offset * TILES + j, piece.shape[0], stride=TILES)] = piece
            token_sum += jnp.sum(piece, 0, keepdims=True)
            square += jnp.sum((piece * piece).reshape(-1, 8, BS), 0)
        vectors = packed(j * TALL + NTOK, (j + 1) * TALL)
        square += jnp.sum((vectors * vectors).reshape(-1, 8, BS), 0)
        square += jnp.concatenate([token_sum * token_sum, jnp.zeros((7, BS), jnp.float32)], 0)
        rows_ref[after + j : after + j + 1] = token_sum
        order = list(range(7)) + list(range(8, 8 + FF // D)) + [7]
        for place, which in enumerate(order):
            at = after + TILES * (1 + place) + j
            rows_ref[at : at + 1] = vectors[which : which + 1]
    at = after + TILES * 13
    deconv = packed(DECONV_AT, PACKED)
    square += jnp.sum((deconv * deconv).reshape(-1, 8, BS), 0)
    rows_ref[at : at + 1] = deconv.T[0:1]
    at += 1
    for o in range(27):
        conv = packed(CONV_AT + o * CF, CONV_AT + (o + 1) * CF)
        square += jnp.sum((conv * conv).reshape(-1, 8, BS), 0)
        turned[:, 0:CF] = conv.T
        for f in range(8):
            rows_ref[at + o * CF : at + (o + 1) * CF, f * CF : (f + 1) * CF] = turned[
                pl.ds(f, CF, stride=8), 0:CF
            ]
    at += 27 * CF
    head = packed(HEAD_AT, SMALL_AT)
    small = packed(SMALL_AT, DECONV_AT)
    square += jnp.sum((head * head + small * small).reshape(-1, 8, BS), 0)
    turned_small = small.T
    segments = [(turned_small[1:2], CF)]
    segments += [(head[row : row + 1], NCLS) for row in range(CF)]
    segments += [(turned_small[0:1], NCLS)]
    lane = 0
    for values, length in segments:
        taken = 0
        while taken < length:
            row, col = lane // BS, lane % BS
            part = min(length - taken, BS - col)
            rows_ref[at + row : at + row + 1, col : col + part] = values[:, taken : taken + part]
            taken += part
            lane += part
    norm = jnp.sqrt(jnp.sum(jnp.sum(square, 0, keepdims=True), 1, keepdims=True))
    clip = clip_value / jnp.maximum(norm, clip_value)
    lanes_of = lax.broadcasted_iota(jnp.int32, (8, BS), 1)
    norm_ref[...] = jnp.where(lanes_of == 0, norm, clip)


def unpack_aux(gathered):
    whole = pl.BlockSpec(memory_space=pltpu.VMEM)
    return pl.pallas_call(
        unpack_kernel,
        out_shape=(
            jax.ShapeDtypeStruct((FLAT_ROWS, BS), jnp.float32),
            jax.ShapeDtypeStruct((8, BS), jnp.float32),
        ),
        in_specs=[whole],
        out_specs=(whole, whole),
        scratch_shapes=[pltpu.VMEM((BS, BS), jnp.float32)],
        compiler_params=pltpu.CompilerParams(vmem_limit_bytes=32 * MIB),
        cost_estimate=pl.CostEstimate(flops=0, bytes_accessed=7 * MIB, transcendentals=0),
        name="unpack_aux",
    )(gathered)


def layer_norm(values):
    center = values - jnp.mean(values, -1, keepdims=True)
    spread = jnp.mean(center * center, -1, keepdims=True)
    inverse = lax.rsqrt(spread + 1e-06)
    return center * inverse, inverse


def layer_norm_back(back, normal, inverse, gain):
    scaled = back * gain
    mean = jnp.mean(scaled, -1, keepdims=True)
    along = jnp.mean(scaled * normal, -1, keepdims=True)
    return inverse * (scaled - mean - normal * along)


def shampoo_kernel(per_step, clip_ref, g_ref, b_ref, s_ref, r_ref, m_ref, v_ref, nb_ref, ns_ref, nm_ref, nv_ref):
    def exact(a, b, dims):
        return lax.dot_general(
            a, b, (dims, ((), ())), precision=HIGHEST, preferred_element_type=jnp.float32
        )

    def mean_square(values):
        total = jnp.sum(jnp.sum(values * values, 0, keepdims=True), 1, keepdims=True)
        return total * (1.0 / (BS * BS))

    for i in range(per_step):
        grads = g_ref[i * BS : (i + 1) * BS] * clip_ref[0, 0]
        ns_ref[0, i] = beta_stat * s_ref[0, i] + (1 - beta_stat) * exact(grads, grads, ((1,), (1,)))
        ns_ref[1, i] = beta_stat * s_ref[1, i] + (1 - beta_stat) * exact(grads, grads, ((0,), (0,)))
        moment = beta_one * m_ref[i] + (1 - beta_one) * grads
        velocity = beta_two * v_ref[i] + (1 - beta_two) * grads * grads
        nm_ref[i] = moment
        nv_ref[i] = velocity
        hat = moment / (1 - beta_one**STEP)
        adam = hat / (jnp.sqrt(velocity / (1 - beta_two**STEP)) + 1e-08)
        left = exact(r_ref[0, i], hat, ((1,), (0,)))
        precond = exact(left, r_ref[1, i], ((1,), (0,)))
        ratio = jnp.sqrt((mean_square(adam) + 1e-06) / (mean_square(precond) + 1e-06))
        blocks = b_ref[i]
        nb_ref[i] = blocks - learn_rate * (precond * ratio + decay_rate * blocks)


def shampoo_step(clip, owned, blocks, stat_pair, root_pair, moment, velocity):
    number = blocks.shape[0]
    per_step = 3
    one = pl.BlockSpec((per_step, BS, BS), lambda i: (i, 0, 0))
    pair = pl.BlockSpec((2, per_step, BS, BS), lambda i: (0, i, 0, 0))
    single = jax.ShapeDtypeStruct((number, BS, BS), jnp.float32)
    return pl.pallas_call(
        functools.partial(shampoo_kernel, per_step),
        grid=(number // per_step,),
        out_shape=(single, jax.ShapeDtypeStruct((2, number, BS, BS), jnp.float32), single, single),
        in_specs=[
            pl.BlockSpec(memory_space=pltpu.SMEM),
            pl.BlockSpec((per_step * BS, BS), lambda i: (i, 0)),
            one,
            pair,
            pair,
            one,
            one,
        ],
        out_specs=(one, pair, one, one),
        compiler_params=pltpu.CompilerParams(vmem_limit_bytes=32 * MIB),
        cost_estimate=pl.CostEstimate(
            flops=number * 8 * BS**3 * 6, bytes_accessed=number * 12 * BS * BS * 4, transcendentals=0
        ),
        name="shampoo",
    )(clip.reshape(1, 1), owned, blocks, stat_pair, root_pair, moment, velocity)


def adam_step(param, grads, moment, veloc):
    moment_new = beta_one * moment + (1 - beta_one) * grads
    veloc_new = beta_two * veloc + (1 - beta_two) * grads * grads
    direction = (
        moment_new / (1 - beta_one**STEP) / (jnp.sqrt(veloc_new / (1 - beta_two**STEP)) + 1e-08)
    )
    return (param - learn_rate * direction, moment_new, veloc_new)


def halves(matrix):
    return matrix[:, :HALF], matrix[:, HALF:]


def local(
    patches,
    labels,
    batch_ids,
    blocks,
    statistics,
    roots,
    moments,
    velocity,
    aux,
    aux_moment,
    aux_velocity,
):
    part = lax.axis_index("mp")
    all_crops = lax.axis_size("dp") * MP
    pieces = split_aux(aux)
    gain, shift = pieces["norm_gain"], pieces["norm_bias"]

    gathered = gather_weights(blocks)
    (w_embed,) = unblock(gathered, True)
    w_qkv, w_proj, w_up, w_down, w_deconv = unblock(gathered, False)

    def columns(array, which, width, start):
        return lax.dynamic_slice_in_dim(array, which * width + start, width - start, 1)

    down_start = 2 * FF // MP // 3

    other_rows = lax.dynamic_slice_in_dim(patches, (1 - part) * NTOK, NTOK, 0)
    own_rows = lax.dynamic_slice_in_dim(patches, part * NTOK, NTOK, 0)
    received = swap_mp(dot_nn(other_rows, w_embed))
    stream_zero = (
        dot_nn(own_rows, w_embed) + received + pieces["positions"] + pieces["embed_bias"]
    )
    normal_one, inverse_one = layer_norm(stream_zero)
    normed_one = (normal_one * gain[0] + shift[0]).astype(jnp.bfloat16)
    q_bias, v_bias = pieces["qv_bias"][0], pieces["qv_bias"][1]
    nothing = jnp.zeros((HALF,), jnp.float32)
    qkv_bias = jnp.concatenate(
        [q_bias[:HALF], nothing, v_bias[:HALF], q_bias[HALF:], nothing, v_bias[HALF:]]
    )
    qkv = (dot_nn(normed_one, w_qkv) + qkv_bias).astype(jnp.bfloat16)
    zero_stream = stream_zero.astype(jnp.bfloat16)
    zero_half = swap_mp(columns(zero_stream, 1 - part, HALF, 0))
    mixed, lse = attention_forward(qkv)
    mixed, zero_half = lax.optimization_barrier((mixed, zero_half))
    stream_one = stream_zero + dot_nn(mixed, w_proj) + pieces["proj_bias"]
    one_stream = stream_one.astype(jnp.bfloat16)
    one_half = swap_mp(columns(one_stream, 1 - part, HALF, 0))
    normal_two, inverse_two = layer_norm(stream_one)
    normed_two = (normal_two * gain[1] + shift[1]).astype(jnp.bfloat16)
    hidden = dot_nn(normed_two, w_up) + pieces["up_bias"]
    active_value, hidden_slope = gelu_and_slope(hidden)
    active = active_value.astype(jnp.bfloat16)
    stream_two = stream_one + dot_nn(active, w_down) + pieces["down_bias"]
    streams = [zero_stream, one_stream, stream_two.astype(jnp.bfloat16)]
    stacked = jnp.concatenate([halves(s)[m] for m in range(MP) for s in streams], 1)
    up_t = dot(w_deconv, stacked, ((0,), (1,)))
    active_other = swap_mp(columns(active, 1 - part, FF // MP, down_start))

    conv_weight = pieces["conv_weight"].astype(jnp.bfloat16).reshape(27, DEC, CF)
    conv_low = conv_weight.transpose(0, 2, 1).reshape(27 * CF, DEC)
    conv_t = conv_weight.transpose(1, 0, 2).reshape(DEC, 27 * CF)
    head_weight = jnp.pad(pieces["head_weight"], ((0, 0), (0, CF - NCLS))).astype(jnp.bfloat16)
    head_bias = jnp.pad(pieces["head_bias"], (0, CF - NCLS)).reshape(CF, 1)
    grid_labels = (
        labels.reshape(GS, 2, GS, 2, GS, 2).transpose(1, 3, 5, 0, 2, 4).reshape(8, NTOK)
    )
    batch = jnp.broadcast_to(batch_ids.reshape(1, 1), (1, BS))
    conv_in, grid_slope, conv_slope, features, chance, sums = decoder_forward(
        up_t,
        pieces["deconv_bias"].reshape(DEC, 1),
        conv_low,
        pieces["conv_bias"].reshape(CF, 1),
        head_weight.T,
        head_bias,
        grid_labels,
        batch,
    )
    conv_in, one_half = lax.optimization_barrier((conv_in, one_half))
    sums, two_stream, active_other = lax.optimization_barrier(
        (sum_sums(sums), streams[2], active_other)
    )
    two_half = swap_mp(columns(two_stream, 1 - part, HALF, 0))
    gu_t, conv_grad, head_grad, small, deconv_bias_grad = decoder_backward(
        all_crops,
        sums,
        batch,
        grid_labels,
        chance,
        features,
        conv_slope,
        grid_slope,
        conv_in,
        conv_t,
        head_weight,
    )
    loss_value = small[0, 2]

    gu_other = swap_mp(gu_t)
    stacked_back = dot(gu_t, w_deconv, ((0,), (1,)))
    back_zero_s, back_one_s, back_two = [
        jnp.concatenate([stacked_back[:, (3 * m + s) * HALF : (3 * m + s + 1) * HALF] for m in range(MP)], 1)
        for s in range(3)
    ]
    grad_down_bias = jnp.sum(back_two, 0)
    two_low = back_two.astype(jnp.bfloat16)
    two_other = swap_mp(two_low)
    back_hidden = (hidden_slope * dot_nt(two_low, w_down)).astype(jnp.bfloat16)
    grad_up_bias = jnp.sum(back_hidden.astype(jnp.float32), 0)
    back_normed_two = dot_nt(back_hidden, w_up)
    grad_gain_two = jnp.sum(back_normed_two * normal_two, 0)
    grad_shift_two = jnp.sum(back_normed_two, 0)
    back_one = (
        back_two + back_one_s + layer_norm_back(back_normed_two, normal_two, inverse_two, gain[1])
    )
    grad_proj_bias = jnp.sum(back_one, 0)
    one_low = back_one.astype(jnp.bfloat16)
    back_mixed = dot_nt(one_low, w_proj).astype(jnp.bfloat16)
    back_q, back_k, back_v = attention_backward(qkv, back_mixed, lse)
    back_qkv = jnp.concatenate(
        [halves(piece)[m] for m in range(MP) for piece in (back_q, back_k, back_v)], 1
    )
    grad_query_bias = jnp.sum(back_q.astype(jnp.float32), 0)
    grad_value_bias = jnp.sum(back_v.astype(jnp.float32), 0)
    back_normed_one = dot_nt(back_qkv, w_qkv)
    grad_gain_one = jnp.sum(back_normed_one * normal_one, 0)
    grad_shift_one = jnp.sum(back_normed_one, 0)
    back_normed_one, two_half, gu_other, two_other = lax.optimization_barrier(
        (back_normed_one, two_half, gu_other, two_other)
    )
    back_zero = (
        back_one + back_zero_s + layer_norm_back(back_normed_one, normal_one, inverse_one, gain[0])
    )
    zero_low = back_zero.astype(jnp.bfloat16)
    other_low = swap_mp(zero_low)

    fast = fast_mesh()
    depth = CHUNK if fast else BLOCK_ROWS
    stacked_own = jnp.concatenate([columns(stream, part, HALF, 0) for stream in streams], 1)
    stacked_other = jnp.concatenate([zero_half, one_half, two_half], 1)
    active_own = columns(active, part, FF // MP, down_start)
    final_grads = grad_blocks(
        [stacked_own, stacked_other], [gu_t, gu_other], 1, 9, 8, 3, 24, True, False, None, "grad_deconv", 4, BLOCK_ROWS, True
    )
    final_grads = grad_blocks(
        [active_own, active_other], [two_low, two_other], 1, 4, 6, 4, 0, True, False, final_grads, "grad_down_last", 4, BLOCK_ROWS
    )
    rest_grads = None
    for name, x, g, rows, per_row, step_rows, start, split_x, split_g, stride in (
        ("grad_down", active, two_low, 8, 6, 4, 144, True, False, 3),
        ("grad_up", normed_two, back_hidden, 6, 12, 3, 72, False, True, None),
        ("grad_proj", mixed, one_low, 3, 6, 3, 54, True, False, None),
        ("grad_qkv", normed_one, back_qkv, 6, 9, 3, 0, False, True, None),
    ):
        rest_grads = grad_blocks(
            [x], [g], MP, rows, per_row, step_rows, start, split_x, split_g, rest_grads, name, 8, depth,
            x_stride=stride,
        )
    first_grads = grad_blocks(
        [own_rows, other_rows], [zero_low, other_low], 1, 16, 6, 4, 0, False, False, None, "grad_embed", 4, BLOCK_ROWS
    )
    vectors = [
        grad_gain_one,
        grad_gain_two,
        grad_shift_one,
        grad_shift_two,
        grad_query_bias,
        grad_value_bias,
        grad_proj_bias,
        grad_down_bias,
    ]
    if fast:
        head_wide = jnp.pad(head_grad, ((0, 0), (0, BS - CF)))
        rest_grads = pack_aux(
            back_zero, vectors, grad_up_bias, conv_grad, head_wide, small, deconv_bias_grad, rest_grads
        )
        owned, squares = reduce_to_owners(
            rest_grads.reshape(MP, 2, 2, 2, CHUNK, BS),
            first_grads.reshape(2, 2, BLOCK_ROWS, BS),
            final_grads.reshape(2, 2, BLOCK_ROWS, BS),
        )
        gathered_aux = gather_all(
            jnp.concatenate([owned[BLOCK_ROWS:], squares]),
            ((0, AUX_ROWS), (AUX_ROWS, 8)),
            1,
            False,
            (0,),
            4,
            "gather_aux",
        )
        in_rows, norm_clip = unpack_aux(gathered_aux)
        aux_total = in_rows.reshape(-1)[:NAUX]
        grad_norm, clip_scale = norm_clip[0, 0], norm_clip[0, 1]
    else:
        owned = reduce_plain(rest_grads.reshape(MP, -1, BS, BS), first_grads, final_grads)
        owned = owned.reshape(-1, BS)
        positions_sum, small_sum = lax.psum(
            (
                back_zero,
                jnp.concatenate(
                    vectors[:7]
                    + [
                        grad_up_bias,
                        grad_down_bias,
                        deconv_bias_grad[:, 0],
                        conv_grad.reshape(27, CF, DEC).transpose(0, 2, 1).reshape(-1),
                        small[:, 1],
                        head_grad[:, :NCLS].reshape(-1),
                        small[:NCLS, 0],
                    ]
                ),
            ),
            ("dp", "mp"),
        )
        aux_total = jnp.concatenate(
            [positions_sum.reshape(-1), jnp.sum(positions_sum, 0), small_sum]
        )
        block_square = lax.psum(jnp.sum(owned * owned), ("dp", "mp"))
        grad_norm = jnp.sqrt(block_square + jnp.sum(aux_total * aux_total))
        clip_scale = clip_value / jnp.maximum(grad_norm, clip_value)
    block_new, stat_new, moment_new, veloc_new = shampoo_step(
        clip_scale,
        owned,
        blocks[0, 0],
        statistics[:, 0, 0],
        roots[:, 0, 0],
        moments[0, 0],
        velocity[0, 0],
    )
    aux_new, aux_moment_new, aux_veloc_new = adam_step(
        aux, aux_total * clip_scale, aux_moment, aux_velocity
    )
    return (
        loss_value,
        grad_norm,
        block_new[None, None],
        stat_new[:, None, None],
        moment_new[None, None],
        veloc_new[None, None],
        aux_new,
        aux_moment_new,
        aux_veloc_new,
    )


def solution(mesh):
    block_spec = P("dp", "mp", None, None, None)
    pair_spec = P(None, "dp", "mp", None, None, None)
    placed = (
        P("dp", "mp"),
        P(("dp", "mp"), None),
        P(("dp", "mp")),
        block_spec,
        pair_spec,
        pair_spec,
        block_spec,
        block_spec,
        P(),
        P(),
        P(),
    )
    return jax.shard_map(
        local,
        mesh=mesh,
        in_specs=placed,
        out_specs=(P(), P(), block_spec, pair_spec, block_spec, block_spec, P(), P(), P()),
        check_vma=False,
    )
```

```python
import functools
import math

import jax
import jax.numpy as jnp
from jax import lax
from jax.experimental import pallas as pl
from jax.experimental.pallas import tpu as pltpu
from jax.sharding import PartitionSpec as P

D = 768
HDIM = 64
FF = 3072
PV = 4096
DEC = 128
CF = 16
NCLS = 14
GS = 8
MB = 4
STEP = 10
BS = 128
NTOK = 512
CELLS = 4096
MP = 2
HALF = D // MP
E_BLOCKS = PV // MP * D // (BS * BS)

HIGHEST = lax.Precision.HIGHEST
MESH = pl.DeviceIdType.MESH
beta_one = 0.9
beta_two = 0.999
beta_stat = 0.95
learn_rate = 0.02
decay_rate = 0.01
clip_value = 0.005
MIB = 1024 * 1024

OFFSETS = [(a, b, c) for a in range(3) for b in range(3) for c in range(3)]
PARITIES = [(i, j, k) for i in range(2) for j in range(2) for k in range(2)]


def dot(a, b, dims):
    return lax.dot_general(a, b, (dims, ((), ())), preferred_element_type=jnp.float32)


def dot_nn(a, b):
    return dot(a, b, ((1,), (0,)))


def dot_nt(a, b):
    return dot(a, b, ((1,), (1,)))


def dot_tn(a, b):
    return dot(a, b, ((0,), (0,)))


def gelu_cdf(v):
    return 0.5 * (1.0 + lax.erf(v * (0.5**0.5)))


def gelu_and_slope(v):
    cdf = gelu_cdf(v)
    density = jnp.exp(-0.5 * v * v) * (1.0 / math.sqrt(2.0 * math.pi))
    return v * cdf, cdf + v * density


def aux_layout():
    return [
        ("positions", (NTOK, D)),
        ("embed_bias", (D,)),
        ("norm_gain", (2, D)),
        ("norm_bias", (2, D)),
        ("qv_bias", (2, D)),
        ("proj_bias", (D,)),
        ("up_bias", (FF,)),
        ("down_bias", (D,)),
        ("deconv_bias", (DEC,)),
        ("conv_weight", (27 * DEC, CF)),
        ("conv_bias", (CF,)),
        ("head_weight", (CF, NCLS)),
        ("head_bias", (NCLS,)),
    ]


NAUX = sum(math.prod(shape) for _, shape in aux_layout())


def split_aux(vector):
    pieces = {}
    offset = 0
    for section_name, section_shape in aux_layout():
        length = math.prod(section_shape)
        pieces[section_name] = vector[offset : offset + length].reshape(section_shape)
        offset += length
    return pieces


def attention_forward_kernel(qkv_q, qkv_k, qkv_v, mixed_ref, lse_ref):
    q, k, v = qkv_q[...], qkv_k[...], qkv_v[...]
    v_t = v.astype(jnp.float32).T.astype(jnp.bfloat16)
    outs = []
    for h in range(2):
        cols = slice(h * HDIM, (h + 1) * HDIM)
        scores = dot_nt(k[:, cols], q[:, cols]) * 0.125
        top = jnp.max(scores, 0, keepdims=True)
        weights = jnp.exp(scores - top)
        total = jnp.sum(weights, 0, keepdims=True)
        attention = (weights * (1.0 / total)).astype(jnp.bfloat16)
        outs.append(dot_nn(v_t[cols], attention))
        lse_ref[0, h : h + 1, :] = top + jnp.log(total)
    mixed_ref[...] = jnp.concatenate(outs, 0).T.astype(jnp.bfloat16)


def attention_backward_kernel(qkv_q, qkv_k, qkv_v, gm_ref, lse_ref, gq_ref, gk_ref, gv_ref):
    q, k, v, gm = qkv_q[...], qkv_k[...], qkv_v[...], gm_ref[...]
    k_t = k.astype(jnp.float32).T.astype(jnp.bfloat16)
    gq_t = []
    for h in range(2):
        cols = slice(h * HDIM, (h + 1) * HDIM)
        scores = dot_nt(k[:, cols], q[:, cols]) * 0.125
        attention = jnp.exp(scores - lse_ref[0, h : h + 1, :])
        back = dot_nt(v[:, cols], gm[:, cols])
        gv_ref[:, cols] = dot_nn(attention.astype(jnp.bfloat16), gm[:, cols]).astype(jnp.bfloat16)
        mean = jnp.sum(back * attention, 0, keepdims=True)
        gs = (attention * (back - mean)).astype(jnp.bfloat16)
        gk_ref[:, cols] = (dot_nn(gs, q[:, cols]) * 0.125).astype(jnp.bfloat16)
        gq_t.append(dot_nn(k_t[cols], gs) * 0.125)
    gq_ref[...] = jnp.concatenate(gq_t, 0).T.astype(jnp.bfloat16)


def qkv_spec(part):
    return pl.BlockSpec((NTOK, BS), lambda i, part=part: (0, (i // 3) * 9 + part * 3 + i % 3))


def attention_forward(qkv):
    return pl.pallas_call(
        attention_forward_kernel,
        grid=(6,),
        out_shape=(
            jax.ShapeDtypeStruct((NTOK, D), jnp.bfloat16),
            jax.ShapeDtypeStruct((6, 2, NTOK), jnp.float32),
        ),
        in_specs=[qkv_spec(0), qkv_spec(1), qkv_spec(2)],
        out_specs=(
            pl.BlockSpec((NTOK, BS), lambda i: (0, i)),
            pl.BlockSpec((1, 2, NTOK), lambda i: (i, 0, 0)),
        ),
        compiler_params=pltpu.CompilerParams(vmem_limit_bytes=32 * MIB),
        cost_estimate=pl.CostEstimate(
            flops=12 * 4 * NTOK * NTOK * HDIM,
            bytes_accessed=NTOK * D * 8,
            transcendentals=12 * NTOK * NTOK,
        ),
        name="attention_forward",
    )(qkv, qkv, qkv)


def attention_backward(qkv, gm, lse):
    pair = pl.BlockSpec((NTOK, BS), lambda i: (0, i))
    return pl.pallas_call(
        attention_backward_kernel,
        grid=(6,),
        out_shape=(jax.ShapeDtypeStruct((NTOK, D), jnp.bfloat16),) * 3,
        in_specs=[
            qkv_spec(0),
            qkv_spec(1),
            qkv_spec(2),
            pair,
            pl.BlockSpec((1, 2, NTOK), lambda i: (i, 0, 0)),
        ],
        out_specs=(pair,) * 3,
        compiler_params=pltpu.CompilerParams(vmem_limit_bytes=32 * MIB),
        cost_estimate=pl.CostEstimate(
            flops=12 * 10 * NTOK * NTOK * HDIM,
            bytes_accessed=NTOK * D * 14,
            transcendentals=12 * NTOK * NTOK,
        ),
        name="attention_backward",
    )(qkv, qkv, qkv, gm, lse)


def source_of(parity, step):
    at = parity + step
    if at < 0:
        return 1, -1
    if at > 1:
        return 0, 1
    return at, 0


def shift_plan(offset, parity, sign):
    found = [source_of(par, sign * (off - 1)) for off, par in zip(offset, parity)]
    bits = [f[0] for f in found]
    steps = [f[1] for f in found]
    return bits[0] * 4 + bits[1] * 2 + bits[2], steps


def token_masks(tokens):
    at = (tokens // (GS * GS), (tokens // GS) % GS, tokens % GS)
    masks = {}
    for axis in range(3):
        masks[axis, 1] = at[axis] < GS - 1
        masks[axis, -1] = at[axis] > 0
    return masks


def shifted(values, steps, masks):
    delta = steps[0] * GS * GS + steps[1] * GS + steps[2]
    if delta == 0 and not any(steps):
        return values
    moved = pltpu.roll(values, (-delta) % NTOK, 1)
    keep = None
    for axis in range(3):
        if steps[axis]:
            mask = masks[axis, steps[axis]]
            keep = mask if keep is None else keep & mask
    return jnp.where(keep, moved, 0.0)


def lanes(parity):
    return slice(parity * NTOK, (parity + 1) * NTOK)


def decoder_forward_kernel(
    up_ref,
    deconv_bias_ref,
    conv_ref,
    conv_bias_ref,
    head_ref,
    head_bias_ref,
    labels_ref,
    batch_ref,
    conv_in_ref,
    grid_slope_ref,
    conv_slope_ref,
    features_ref,
    chance_ref,
    sums_ref,
    conved_ref,
):
    tokens = lax.broadcasted_iota(jnp.int32, (CF, NTOK), 1)
    masks = token_masks(tokens)
    for parity in range(8):
        conved_ref[:, lanes(parity)] = jnp.broadcast_to(conv_bias_ref[...], (CF, NTOK))
    for parity in range(8):
        cell = up_ref[parity * DEC : (parity + 1) * DEC, :] + deconv_bias_ref[...]
        value, slope = gelu_and_slope(cell)
        low = value.astype(jnp.bfloat16)
        conv_in_ref[:, lanes(parity)] = low
        grid_slope_ref[:, lanes(parity)] = slope
        products = dot_nn(conv_ref[...], low)
        for at, offset in enumerate(OFFSETS):
            target, back_steps = shift_plan(offset, PARITIES[parity], -1)
            forward = [-s for s in back_steps]
            piece = shifted(products[at * CF : (at + 1) * CF, :], forward, masks)
            conved_ref[:, lanes(target)] += piece
    rows = lax.broadcasted_iota(jnp.int32, (CF, NTOK), 0)
    hit = jnp.zeros((CF, 1), jnp.float32)
    predicted = jnp.zeros((CF, 1), jnp.float32)
    truth = jnp.zeros((CF, 1), jnp.float32)
    entropy = jnp.zeros((CF, 1), jnp.float32)
    for parity in range(8):
        value, slope = gelu_and_slope(conved_ref[:, lanes(parity)])
        conv_slope_ref[:, lanes(parity)] = slope
        features = value.astype(jnp.bfloat16)
        features_ref[:, lanes(parity)] = features
        logits = dot_nn(head_ref[...], features) + head_bias_ref[...]
        logits = jnp.where(rows < NCLS, logits, -1e30)
        center = logits - jnp.max(logits, 0, keepdims=True)
        log_prob = center - jnp.log(jnp.sum(jnp.exp(center), 0, keepdims=True))
        chance = jnp.exp(log_prob)
        target = (rows == labels_ref[parity : parity + 1, :]).astype(jnp.float32)
        chance_ref[:, lanes(parity)] = chance
        hit += jnp.sum(chance * target, 1, keepdims=True)
        predicted += jnp.sum(chance, 1, keepdims=True)
        truth += jnp.sum(target, 1, keepdims=True)
        entropy -= jnp.sum(jnp.where(target > 0, log_prob, 0.0), 1, keepdims=True)
    lane = lax.broadcasted_iota(jnp.int32, (CF, BS), 1)
    base = batch_ref[...] * 3
    sums_ref[...] = (
        jnp.where(lane == base, hit, 0.0)
        + jnp.where(lane == base + 1, predicted, 0.0)
        + jnp.where(lane == base + 2, truth, 0.0)
        + jnp.where(lane == 3 * MB, entropy, 0.0)
    )


def decoder_backward_kernel(
    all_crops,
    sums_ref,
    batch_ref,
    labels_ref,
    chance_ref,
    features_ref,
    conv_slope_ref,
    grid_slope_ref,
    conv_in_ref,
    conv_t_ref,
    head_t_ref,
    gu_ref,
    conv_grad_ref,
    head_grad_ref,
    small_ref,
    deconv_grad_ref,
    spread_ref,
):
    sums = sums_ref[...]
    lane = lax.broadcasted_iota(jnp.int32, (CF, BS), 1)
    row = lax.broadcasted_iota(jnp.int32, (CF, BS), 0)
    live = (lane < 3 * MB) & (lane % 3 == 0) & (row < NCLS)
    under = pltpu.roll(sums, BS - 1, 1) + pltpu.roll(sums, BS - 2, 1) + 1.0
    under = jnp.where(live, under, 1.0)
    over = 2.0 * sums + 1.0
    dice = jnp.where(live, over / under, 0.0)
    mean_dice = jnp.sum(jnp.sum(dice, 1, keepdims=True), 0, keepdims=True) / (NCLS * MB)
    entropy_lane = jnp.where(lane == 3 * MB, sums, 0.0)
    entropy = jnp.sum(jnp.sum(entropy_lane, 1, keepdims=True), 0, keepdims=True)
    loss = entropy / (all_crops * CELLS) + (1.0 - mean_dice)
    own = live & (lane == batch_ref[...] * 3)
    d_hit = jnp.sum(jnp.where(own, -2.0 / (MB * NCLS) / under, 0.0), 1, keepdims=True)
    d_predicted = jnp.sum(
        jnp.where(own, (1.0 / (MB * NCLS)) * over / (under * under), 0.0), 1, keepdims=True
    )
    tokens = lax.broadcasted_iota(jnp.int32, (CF, NTOK), 1)
    masks = token_masks(tokens)
    rows = lax.broadcasted_iota(jnp.int32, (CF, NTOK), 0)
    head_bias = jnp.zeros((CF, 1), jnp.float32)
    conv_bias = jnp.zeros((CF, 1), jnp.float32)
    head_grad = jnp.zeros((CF, CF), jnp.float32)
    for parity in range(8):
        chance = chance_ref[:, lanes(parity)]
        target = (rows == labels_ref[parity : parity + 1, :]).astype(jnp.float32)
        back = (d_hit * target + d_predicted) * chance - target * (1.0 / (all_crops * CELLS))
        logits = back - chance * jnp.sum(back, 0, keepdims=True)
        head_bias += jnp.sum(logits, 1, keepdims=True)
        low = logits.astype(jnp.bfloat16)
        head_grad += dot_nt(features_ref[:, lanes(parity)], low)
        conved = conv_slope_ref[:, lanes(parity)] * dot_nn(head_t_ref[...], low)
        conv_bias += jnp.sum(conved, 1, keepdims=True)
        rounded = conved.astype(jnp.bfloat16).astype(jnp.float32)
        for at, offset in enumerate(OFFSETS):
            target_cell, steps = shift_plan(offset, PARITIES[parity], 1)
            piece = shifted(rounded, [-s for s in steps], masks)
            spread_ref[at * CF : (at + 1) * CF, lanes(target_cell)] = piece.astype(jnp.bfloat16)
    head_grad_ref[...] = head_grad
    small_ref[...] = (
        jnp.where(lane == 0, head_bias, 0.0)
        + jnp.where(lane == 1, conv_bias, 0.0)
        + jnp.where(lane == 2, loss, 0.0)
    )
    conv_grad = jnp.zeros((27 * CF, DEC), jnp.float32)
    deconv_grad = jnp.zeros((DEC, 1), jnp.float32)
    for parity in range(8):
        spread = spread_ref[:, lanes(parity)]
        conv_grad += dot_nt(spread, conv_in_ref[:, lanes(parity)])
        back = grid_slope_ref[:, lanes(parity)] * dot_nn(conv_t_ref[...], spread)
        deconv_grad += jnp.sum(back, 1, keepdims=True)
        gu_ref[parity * DEC : (parity + 1) * DEC, :] = back.astype(jnp.bfloat16)
    conv_grad_ref[...] = conv_grad
    deconv_grad_ref[...] = jnp.broadcast_to(deconv_grad, (DEC, BS))


def whole_specs(number):
    return [pl.BlockSpec(memory_space=pltpu.VMEM)] * number


def decoder_forward(up_t, deconv_bias, conv_low, conv_bias, head_low, head_bias, labels, batch):
    shapes = (
        jax.ShapeDtypeStruct((DEC, CELLS), jnp.bfloat16),
        jax.ShapeDtypeStruct((DEC, CELLS), jnp.float32),
        jax.ShapeDtypeStruct((CF, CELLS), jnp.float32),
        jax.ShapeDtypeStruct((CF, CELLS), jnp.bfloat16),
        jax.ShapeDtypeStruct((CF, CELLS), jnp.float32),
        jax.ShapeDtypeStruct((CF, BS), jnp.float32),
    )
    return pl.pallas_call(
        decoder_forward_kernel,
        out_shape=shapes,
        in_specs=whole_specs(8),
        out_specs=tuple(whole_specs(6)),
        scratch_shapes=[pltpu.VMEM((CF, CELLS), jnp.float32)],
        compiler_params=pltpu.CompilerParams(vmem_limit_bytes=40 * MIB),
        cost_estimate=pl.CostEstimate(
            flops=2 * 27 * CF * DEC * CELLS, bytes_accessed=6 * MIB, transcendentals=DEC * CELLS
        ),
        name="decoder_forward",
    )(up_t, deconv_bias, conv_low, conv_bias, head_low, head_bias, labels, batch)


def decoder_backward(
    all_crops, sums, batch, labels, chance, features, conv_slope, grid_slope, conv_in, conv_t, head_t
):
    shapes = (
        jax.ShapeDtypeStruct((8 * DEC, NTOK), jnp.bfloat16),
        jax.ShapeDtypeStruct((27 * CF, DEC), jnp.float32),
        jax.ShapeDtypeStruct((CF, CF), jnp.float32),
        jax.ShapeDtypeStruct((CF, BS), jnp.float32),
        jax.ShapeDtypeStruct((DEC, BS), jnp.float32),
    )
    return pl.pallas_call(
        functools.partial(decoder_backward_kernel, all_crops),
        out_shape=shapes,
        in_specs=whole_specs(10),
        out_specs=tuple(whole_specs(5)),
        scratch_shapes=[pltpu.VMEM((27 * CF, CELLS), jnp.bfloat16)],
        compiler_params=pltpu.CompilerParams(vmem_limit_bytes=40 * MIB),
        cost_estimate=pl.CostEstimate(
            flops=4 * 27 * CF * DEC * CELLS, bytes_accessed=6 * MIB, transcendentals=0
        ),
        name="decoder_backward",
    )(sums, batch, labels, chance, features, conv_slope, grid_slope, conv_in, conv_t, head_t)


LAYERS = 4
GATHER_LAG = 2
THIRDS = tuple((8 * BS * i, 8 * BS) for i in range(3))
PIECES = 32
BLOCK_ROWS = 24 * BS
AUX_ROWS = 256
CHUNK = BLOCK_ROWS + AUX_ROWS
ROWS_N = 2 * CHUNK // PIECES
ROWS_F = BLOCK_ROWS // PIECES
LAG = 2
HOP_LAG = 2
AHEAD = 3
CORE_SLOTS = 8
SEND_SLOTS = 4
KEEP = 8
SUM_SLOTS = 12


def remote(src, dst, send_sem, recv_sem, device):
    return pltpu.make_async_remote_copy(
        src_ref=src,
        dst_ref=dst,
        send_sem=send_sem,
        recv_sem=recv_sem,
        device_id=device,
        device_id_type=MESH,
    )


def places():
    dp, x = lax.axis_index("dp"), lax.axis_index("mp")
    z, y, c = dp // 4, (dp // 2) % 2, dp % 2
    return dict(
        dp=dp,
        x=x,
        y=y,
        z=z,
        c=c,
        at_core=(dp + 1 - 2 * c, x),
        at_x=(dp, 1 - x),
        at_y=(dp + 2 - 4 * y, x),
        above=(lax.rem(dp + 4, 4 * LAYERS), x),
        below=(lax.rem(dp + 4 * LAYERS - 4, 4 * LAYERS), x),
    )


def greet_neighbours(at):
    barrier = pltpu.get_barrier_semaphore()
    for name in ("at_core", "at_x", "at_y"):
        pl.semaphore_signal(barrier, inc=1, device_id=at[name], device_id_type=MESH)

    @pl.when(at["z"] < LAYERS - 1)
    def _():
        pl.semaphore_signal(barrier, inc=1, device_id=at["above"], device_id_type=MESH)

    @pl.when(at["z"] > 0)
    def _():
        pl.semaphore_signal(barrier, inc=1, device_id=at["below"], device_id_type=MESH)

    peers = 3 + jnp.minimum(at["z"], 1) + jnp.minimum(LAYERS - 1 - at["z"], 1)
    pl.semaphore_wait(barrier, peers)


def gather_kernel(parts, by_x, skip, middle, in_ref, out_ref, local_sem, up_sem, down_sem, z_recv, x_send, x_recv, y_send, y_recv, core_send, core_recv):
    at = places()
    x, y, z, c = at["x"], at["y"], at["z"], at["c"]
    last = LAYERS - 1

    def spot(l, y_at, c_at, x_at, p):
        return out_ref.at[x_at, l * 4 + y_at * 2 + c_at, pl.ds(*parts[p])]

    def send(ref, send_sem, recv_sem, device):
        return remote(ref, ref, send_sem, recv_sem, device)

    def up(l, p):
        return send(spot(l, y, c, x, p), up_sem.at[l, p], z_recv.at[l, p], at["above"])

    def down(l, p):
        return send(spot(l, y, c, x, p), down_sem.at[l, p], z_recv.at[l, p], at["below"])

    def x_direct(l, p, x_at):
        return send(spot(l, y, c, x_at, p), x_send.at[l, p, 0], x_recv.at[l, p, 0], at["at_x"])

    def y_direct(l, p, y_at):
        return send(spot(l, y_at, c, x, p), y_send.at[l, p, 0], y_recv.at[l, p, 0], at["at_y"])

    def diagonal(l, p, y_at, x_at):
        if p < by_x:
            return send(spot(l, y_at, c, x_at, p), y_send.at[l, p, 1], y_recv.at[l, p, 1], at["at_y"])
        return send(spot(l, y_at, c, x_at, p), x_send.at[l, p, 1], x_recv.at[l, p, 1], at["at_x"])

    def relayed(l, p):
        return diagonal(l, p, y, 1 - x) if p < by_x else diagonal(l, p, 1 - y, x)

    def core(l, p, kind, c_at):
        y_at, x_at = ((y, x), (1 - y, x), (y, 1 - x), (1 - y, 1 - x))[kind]
        return send(
            spot(l, y_at, c_at, x_at, p),
            core_send.at[l, p, kind],
            core_recv.at[l, p, kind],
            at["at_core"],
        )

    def wide(l):
        return (l > 0) if skip else (l >= 0)

    own = pltpu.make_async_copy(in_ref, out_ref.at[x, at["dp"]], local_sem)
    own.start()
    greet_neighbours(at)
    own.wait()

    def arrive(l, p, came_up, came_down):
        if not (came_up and came_down):
            up(l, p).wait_recv()
        if came_up:

            @pl.when(z < last)
            def _():
                up(l, p).start()

        if came_down:

            @pl.when(z > 0)
            def _():
                down(l, p).start()

        @pl.when(wide(l))
        def _():
            x_direct(l, p, x).start()

        y_direct(l, p, y).start()
        core(l, p, 0, c).start()

    def relay(l, p):
        y_direct(l, p, 1 - y).wait_recv()

        @pl.when(wide(l))
        def _():
            if p >= by_x:
                relayed(l, p).start()
            x_direct(l, p, 1 - x).wait_recv()
            if p < by_x:
                relayed(l, p).start()
            core(l, p, 2, c).start()

        core(l, p, 1, c).start()

    def finish(l, p):
        @pl.when(wide(l))
        def _():
            diagonal(l, p, 1 - y, 1 - x).wait_recv()
            core(l, p, 3, c).start()

    def held(l, p):
        return ((l > 0) & (l < last)) if p in middle else ((l >= 0) & (l <= last))

    number = len(parts)

    def both(tick, run):
        if tick < 0 or tick >= LAYERS * number:
            return
        r, p = tick // number, tick % number
        if r == 0:

            @pl.when(held(z, p))
            def _():
                run(z, p, True, True)

            return

        @pl.when(held(z - r, p))
        def _():
            run(z - r, p, True, False)

        @pl.when(held(z + r, p))
        def _():
            run(z + r, p, False, True)

    for tick in range(LAYERS * number + 2 * GATHER_LAG):
        both(tick, arrive)
        both(tick - GATHER_LAG, lambda l, p, up_way, down_way: relay(l, p))
        both(tick - 2 * GATHER_LAG, lambda l, p, up_way, down_way: finish(l, p))

    def settle_part(l, p):
        for kind in (0, 1):
            core(l, p, kind, 1 - c).wait_recv()
            core(l, p, kind, c).wait_send()
        y_direct(l, p, y).wait_send()

        @pl.when(wide(l))
        def _():
            for kind in (2, 3):
                core(l, p, kind, 1 - c).wait_recv()
                core(l, p, kind, c).wait_send()
            x_direct(l, p, x).wait_send()
            relayed(l, p).wait_send()

        @pl.when((l <= z) & (z < last))
        def _():
            up(l, p).wait_send()

        @pl.when((l >= z) & (z > 0))
        def _():
            down(l, p).wait_send()

    def settle(l, carry):
        for p in range(number):
            pl.when(held(l, p))(functools.partial(settle_part, l, p))
        return carry

    lax.fori_loop(0, LAYERS, settle, 0)


def gather_all(values, parts, by_x, skip, middle, collective_id, name):
    rows = values.shape[0]
    number = len(parts)

    def sems(*shape):
        return pltpu.SemaphoreType.DMA(shape)

    return pl.pallas_call(
        functools.partial(gather_kernel, parts, by_x, skip, middle),
        out_shape=jax.ShapeDtypeStruct((MP, 4 * LAYERS, rows, BS), values.dtype),
        in_specs=[pl.BlockSpec(memory_space=pl.ANY)],
        out_specs=pl.BlockSpec(memory_space=pl.ANY),
        scratch_shapes=[
            pltpu.SemaphoreType.DMA,
            sems(LAYERS, number),
            sems(LAYERS, number),
            sems(LAYERS, number),
            sems(LAYERS, number, 2),
            sems(LAYERS, number, 2),
            sems(LAYERS, number, 2),
            sems(LAYERS, number, 2),
            sems(LAYERS, number, 4),
            sems(LAYERS, number, 4),
        ],
        compiler_params=pltpu.CompilerParams(
            collective_id=collective_id, has_side_effects=True, vmem_limit_bytes=32 * MIB
        ),
        cost_estimate=pl.CostEstimate(flops=0, bytes_accessed=32 * rows * BS * 4, transcendentals=0),
        name=name,
    )(values)


def reduce_kernel(
    n_ref,
    e_ref,
    f_ref,
    out_ref,
    square_ref,
    own_n,
    own_f,
    core_n,
    core_f,
    keep_n,
    keep_f,
    xs_n,
    ys_n,
    ys_f,
    xr_n,
    yr_n,
    yr_f,
    sum_n,
    sum_f,
    up_n,
    down_n,
    up_f,
    down_e,
    own_sem,
    core_send,
    core_recv,
    credit,
    xs_sem,
    ys_n_sem,
    ys_f_sem,
    xr_sem,
    yr_n_sem,
    yr_f_sem,
    z_n_sem,
    z_f_sem,
    up_n_sem,
    down_n_sem,
    up_f_sem,
    down_e_sem,
):
    at = places()
    x, y, z, c = at["x"], at["y"], at["z"], at["c"]
    last = LAYERS - 1

    def layer_of(s):
        return 1 + lax.rem(s, 2)

    def rows_of(s):
        return pl.ds(pl.multiple_of((s // 2) * ROWS_N, 8), ROWS_N)

    def rows_f(s):
        return pl.ds(pl.multiple_of(s * ROWS_F, 8), ROWS_F)

    def own_loads(s):
        slot = lax.rem(s, 3)
        mine = n_ref.at[:, layer_of(s) - 1, :, c, rows_of(s)]
        return (
            pltpu.make_async_copy(mine, own_n.at[slot], own_sem.at[slot, 0]),
            pltpu.make_async_copy(e_ref.at[:, c, rows_f(s)], own_f.at[slot, 0], own_sem.at[slot, 1]),
            pltpu.make_async_copy(f_ref.at[:, c, rows_f(s)], own_f.at[slot, 1], own_sem.at[slot, 2]),
        )

    def core_copies(s):
        slot = lax.rem(s, CORE_SLOTS)
        sources = (
            n_ref.at[:, layer_of(s) - 1, :, 1 - c, rows_of(s)],
            e_ref.at[:, 1 - c, rows_f(s)],
            f_ref.at[:, 1 - c, rows_f(s)],
        )
        targets = (core_n.at[slot], core_f.at[slot, 0], core_f.at[slot, 1])
        return [
            remote(source, target, core_send.at[s, i], core_recv.at[slot, i], at["at_core"])
            for i, (source, target) in enumerate(zip(sources, targets))
        ]

    def x_copy(s):
        slot = lax.rem(s, SEND_SLOTS)
        return remote(xs_n.at[slot], xr_n.at[s], xs_sem.at[slot], xr_sem.at[s], at["at_x"])

    def y_copy_f(s):
        slot = lax.rem(s, SEND_SLOTS)
        return remote(ys_f.at[slot], yr_f.at[s], ys_f_sem.at[slot], yr_f_sem.at[s], at["at_y"])

    def y_copy(s):
        slot = lax.rem(s, SEND_SLOTS)
        return remote(ys_n.at[slot], yr_n.at[s], ys_n_sem.at[slot], yr_n_sem.at[s], at["at_y"])

    def up_copy(s):
        slot = lax.rem(s, SUM_SLOTS)
        return remote(sum_n.at[slot], up_n.at[s], z_n_sem.at[slot], up_n_sem.at[s], at["above"])

    def down_copy(s):
        slot = lax.rem(s, SUM_SLOTS)
        return remote(sum_n.at[slot], down_n.at[s], z_n_sem.at[slot], down_n_sem.at[s], at["below"])

    def down_copy_e(s):
        slot = lax.rem(s, SUM_SLOTS)
        source, sem = sum_f.at[slot, 0], z_f_sem.at[slot, 0]
        return remote(source, down_e.at[s], sem, down_e_sem.at[s], at["below"])

    def up_copy_f(s):
        slot = lax.rem(s, SUM_SLOTS)
        source, sem = sum_f.at[slot, 1], z_f_sem.at[slot, 1]
        return remote(source, up_f.at[s], sem, up_f_sem.at[s], at["above"])

    def add_squares(values):
        square_ref[...] += jnp.sum((values * values).reshape(-1, 8, BS), 0)

    square_ref[...] = jnp.zeros((8, BS), jnp.float32)
    for s in range(2):
        for copy in own_loads(s):
            copy.start()
    greet_neighbours(at)
    for s in range(AHEAD):
        for copy in core_copies(s):
            copy.start()

    def first(s):
        @pl.when(s + 2 < PIECES)
        def _():
            for copy in own_loads(s + 2):
                copy.start()

        @pl.when(s + AHEAD < PIECES)
        def _():
            @pl.when(s + AHEAD >= CORE_SLOTS)
            def _():
                pl.semaphore_wait(credit, 1)

            for copy in core_copies(s + AHEAD):
                copy.start()

        for copy in own_loads(s):
            copy.wait()
        for copy in core_copies(s):
            copy.wait_recv()

        @pl.when(s >= SEND_SLOTS)
        def _():
            x_copy(s - SEND_SLOTS).wait_send()
            y_copy_f(s - SEND_SLOTS).wait_send()

        own, core = lax.rem(s, 3), lax.rem(s, CORE_SLOTS)
        send, keep = lax.rem(s, SEND_SLOTS), lax.rem(s, KEEP)
        xs_n[send] = own_n[own, 1 - x] + core_n[core, 1 - x]
        x_copy(s).start()
        for kind in range(2):
            ys_f[send, kind] = own_f[own, kind, 1 - y] + core_f[core, kind, 1 - y]
        y_copy_f(s).start()
        keep_n[keep] = own_n[own, x] + core_n[core, x]
        for kind in range(2):
            keep_f[keep, kind] = own_f[own, kind, y] + core_f[core, kind, y]

        @pl.when(s + CORE_SLOTS < PIECES)
        def _():
            pl.semaphore_signal(credit, inc=1, device_id=at["at_core"], device_id_type=MESH)

    def second(s):
        x_copy(s).wait_recv()

        @pl.when(s >= SEND_SLOTS)
        def _():
            y_copy(s - SEND_SLOTS).wait_send()

        send, keep = lax.rem(s, SEND_SLOTS), lax.rem(s, KEEP)
        ys_n[send] = keep_n[keep, 1 - y] + xr_n[s, 1 - y]
        y_copy(s).start()
        keep_n[keep, y] = keep_n[keep, y] + xr_n[s, y]

    def third(s):
        y_copy_f(s).wait_recv()
        y_copy(s).wait_recv()

        @pl.when((s >= SUM_SLOTS) & (z != layer_of(s)))
        def _():
            up_copy(s - SUM_SLOTS).wait_send()

        @pl.when((s >= SUM_SLOTS) & (z > 0))
        def _():
            down_copy_e(s - SUM_SLOTS).wait_send()

        @pl.when((s >= SUM_SLOTS) & (z < last))
        def _():
            up_copy_f(s - SUM_SLOTS).wait_send()

        slot, keep = lax.rem(s, SUM_SLOTS), lax.rem(s, KEEP)
        sum_n[slot] = keep_n[keep, y] + yr_n[s]
        sum_f[slot] = keep_f[keep] + yr_f[s]

    def along(s, hop):
        slot = lax.rem(s, SUM_SLOTS)
        layer = layer_of(s)
        away = jnp.where(z < layer, z, jnp.where(z > layer, last - z, jnp.maximum(z, last - z)))

        @pl.when(away == hop)
        def _():
            @pl.when((z > 0) & (z <= layer))
            def _():
                up_copy(s).wait_recv()
                sum_n[slot] = sum_n[slot] + up_n[s]

            @pl.when((z < last) & (z >= layer))
            def _():
                down_copy(s).wait_recv()
                sum_n[slot] = sum_n[slot] + down_n[s]

            @pl.when(z < layer)
            def _():
                up_copy(s).start()

            @pl.when(z > layer)
            def _():
                down_copy(s).start()

            @pl.when(z == layer)
            def _():
                out_ref[rows_of(s)] = sum_n[slot]
                piece = s // 2
                whole, cut = BLOCK_ROWS // ROWS_N, BLOCK_ROWS % ROWS_N

                @pl.when(piece <= whole)
                def _():
                    add_squares(sum_n[slot, pl.ds(0, cut)])

                @pl.when(piece < whole)
                def _():
                    add_squares(sum_n[slot, pl.ds(cut, ROWS_N - cut)])

        @pl.when(jnp.where(z == 0, last, last - z) == hop)
        def _():
            @pl.when(z < last)
            def _():
                down_copy_e(s).wait_recv()
                sum_f[slot, 0] = sum_f[slot, 0] + down_e[s]

            @pl.when(z > 0)
            def _():
                down_copy_e(s).start()

            @pl.when(z == 0)
            def _():
                out_ref[rows_f(s)] = sum_f[slot, 0]
                add_squares(sum_f[slot, 0])

        @pl.when(z == hop)
        def _():
            @pl.when(z > 0)
            def _():
                up_copy_f(s).wait_recv()
                sum_f[slot, 1] = sum_f[slot, 1] + up_f[s]

            @pl.when(z < last)
            def _():
                up_copy_f(s).start()

            @pl.when(z == last)
            def _():
                out_ref[rows_f(s)] = sum_f[slot, 1]
                add_squares(sum_f[slot, 1])

    def guarded(run, s):
        @pl.when((s >= 0) & (s < PIECES))
        def _():
            run(s)

    def step(t, carry):
        guarded(first, t)
        guarded(second, t - LAG)
        guarded(third, t - 2 * LAG)
        for hop in range(LAYERS):
            guarded(functools.partial(along, hop=hop), t - 2 * LAG - hop * HOP_LAG)
        return carry

    lax.fori_loop(0, PIECES + 2 * LAG + (LAYERS - 1) * HOP_LAG, step, 0)

    def drain_sends(i, carry):
        s = PIECES - SEND_SLOTS + i
        for copy in (x_copy(s), y_copy_f(s), y_copy(s)):
            copy.wait_send()
        return carry

    lax.fori_loop(0, SEND_SLOTS, drain_sends, 0)

    def drain_sums(i, carry):
        s = PIECES - SUM_SLOTS + i

        @pl.when(z != layer_of(s))
        def _():
            up_copy(s).wait_send()

        @pl.when(z > 0)
        def _():
            down_copy_e(s).wait_send()

        @pl.when(z < last)
        def _():
            up_copy_f(s).wait_send()

        return carry

    lax.fori_loop(0, SUM_SLOTS, drain_sums, 0)

    def drain_core(s, carry):
        for copy in core_copies(s):
            copy.wait_send()
        return carry

    lax.fori_loop(0, PIECES, drain_core, 0)

    @pl.when((z == 0) | (z == last))
    def _():
        out_ref[pl.ds(BLOCK_ROWS, AUX_ROWS)] = jnp.zeros((AUX_ROWS, BS), jnp.float32)


def reduce_to_owners(rest, first, final):
    def room(*shape):
        return pltpu.VMEM(shape + (BS,), jnp.float32)

    def sems(*shape):
        return pltpu.SemaphoreType.DMA(shape)

    return pl.pallas_call(
        reduce_kernel,
        out_shape=(
            jax.ShapeDtypeStruct((CHUNK, BS), jnp.float32),
            jax.ShapeDtypeStruct((8, BS), jnp.float32),
        ),
        in_specs=[pl.BlockSpec(memory_space=pltpu.HBM)] * 3,
        out_specs=(pl.BlockSpec(memory_space=pltpu.VMEM),) * 2,
        scratch_shapes=[
            room(3, 2, 2, ROWS_N),
            room(3, 2, 2, ROWS_F),
            room(CORE_SLOTS, 2, 2, ROWS_N),
            room(CORE_SLOTS, 2, 2, ROWS_F),
            room(KEEP, 2, ROWS_N),
            room(KEEP, 2, ROWS_F),
            room(SEND_SLOTS, 2, ROWS_N),
            room(SEND_SLOTS, ROWS_N),
            room(SEND_SLOTS, 2, ROWS_F),
            room(PIECES, 2, ROWS_N),
            room(PIECES, ROWS_N),
            room(PIECES, 2, ROWS_F),
            room(SUM_SLOTS, ROWS_N),
            room(SUM_SLOTS, 2, ROWS_F),
            room(PIECES, ROWS_N),
            room(PIECES, ROWS_N),
            room(PIECES, ROWS_F),
            room(PIECES, ROWS_F),
            sems(3, 3),
            sems(PIECES, 3),
            sems(CORE_SLOTS, 3),
            pltpu.SemaphoreType.REGULAR,
            sems(SEND_SLOTS),
            sems(SEND_SLOTS),
            sems(SEND_SLOTS),
            sems(PIECES),
            sems(PIECES),
            sems(PIECES),
            sems(SUM_SLOTS),
            sems(SUM_SLOTS, 2),
            sems(PIECES),
            sems(PIECES),
            sems(PIECES),
            sems(PIECES),
        ],
        compiler_params=pltpu.CompilerParams(
            collective_id=1, has_side_effects=True, vmem_limit_bytes=58 * MIB
        ),
        cost_estimate=pl.CostEstimate(flops=0, bytes_accessed=100 * MIB, transcendentals=0),
        name="reduce_to_owners",
    )(rest, first, final)


MATRICES = [
    (96, 6, 9, 3, True),
    (150, 3, 6, 3, False),
    (168, 6, 12, 3, True),
    (240, 12, 6, 4, False),
    (312, 9, 8, 3, False),
]
LOADS = 4


def unblock_kernel(plan, kinds, blocks_ref, *refs):
    outs, tiles = refs[:kinds], refs[kinds : 2 * kinds]
    loaded, load_sem, store_sem = refs[2 * kinds :]
    part = lax.axis_index("mp")

    def load(i):
        kind, m, first, rows, per_row, row, col = plan[i]
        number = rows * per_row
        return pltpu.make_async_copy(
            blocks_ref.at[part if m is None else m, pl.ds(first, number)],
            loaded.at[i % LOADS, pl.ds(0, number)],
            load_sem.at[i % LOADS],
        )

    def store(i, slot):
        kind, m, first, rows, per_row, row, col = plan[i]
        return pltpu.make_async_copy(
            tiles[kind].at[slot],
            outs[kind].at[pl.ds(row, rows * BS), pl.ds(col, per_row * BS)],
            store_sem.at[kind, slot],
        )

    history = [[] for _ in range(kinds)]
    for i in range(min(LOADS - 1, len(plan))):
        load(i).start()
    for i, (kind, m, first, rows, per_row, row, col) in enumerate(plan):
        if i + LOADS - 1 < len(plan):
            load(i + LOADS - 1).start()
        load(i).wait()
        slot = len(history[kind]) % 2
        if len(history[kind]) >= 2:
            store(*history[kind][-2]).wait()
        for r in range(rows):
            for c in range(per_row):
                tiles[kind][slot, r * BS : (r + 1) * BS, c * BS : (c + 1) * BS] = loaded[
                    i % LOADS, r * per_row + c
                ]
        history[kind].append((i, slot))
        store(i, slot).start()
    for done in history:
        for entry in done[-2:]:
            store(*entry).wait()


def unblock(gathered, embedding):
    plan, shapes, tiles = [], [], []
    if embedding:
        plan = [(0, None, 24 * i, 4, 6, 4 * BS * i, 0) for i in range(4)]
        shapes, tiles = [(PV // MP, D)], [(4 * BS, D)]
    else:
        for kind, (first, rows, per_row, step, beside) in enumerate(MATRICES):
            tall, wide = rows * BS, per_row * BS
            shapes.append((tall, MP * wide) if beside else (MP * tall, wide))
            tiles.append((step * BS, wide))
            for m in range(MP):
                for at in range(0, rows, step):
                    row = at * BS + (0 if beside else m * tall)
                    plan.append(
                        (kind, m, first + at * per_row, step, per_row, row, m * wide if beside else 0)
                    )
    anywhere = pl.BlockSpec(memory_space=pl.ANY)
    largest = max(entry[3] * entry[4] for entry in plan)
    return pl.pallas_call(
        functools.partial(unblock_kernel, plan, len(shapes)),
        out_shape=tuple(jax.ShapeDtypeStruct(shape, jnp.bfloat16) for shape in shapes),
        in_specs=[anywhere],
        out_specs=tuple([anywhere] * len(shapes)),
        scratch_shapes=[pltpu.VMEM((2,) + tile, jnp.bfloat16) for tile in tiles]
        + [
            pltpu.VMEM((LOADS, largest, BS, BS), jnp.bfloat16),
            pltpu.SemaphoreType.DMA((LOADS,)),
            pltpu.SemaphoreType.DMA((len(shapes), 2)),
        ],
        compiler_params=pltpu.CompilerParams(vmem_limit_bytes=32 * MIB),
        cost_estimate=pl.CostEstimate(
            flops=0, bytes_accessed=(6 if embedding else 38) * MIB, transcendentals=0
        ),
        name="unblock_embedding" if embedding else "unblock",
    )(gathered)


def blocks_kernel(first_block, per_row, step_rows, transposed, pairs, *refs):
    out_ref, tiles, sems = refs[-3:]
    m, i = pl.program_id(0), pl.program_id(1)
    steps = pl.num_programs(1)
    at = m * steps + i
    slot = lax.rem(at, 2)
    total = pl.num_programs(0) * steps

    def drain(which):
        pltpu.make_async_copy(tiles.at[which], tiles.at[which], sems.at[which]).wait()

    @pl.when(at >= 2)
    def _():
        drain(slot)

    total_product = None
    for pair in range(pairs):
        x_ref, g_ref = refs[2 * pair], refs[2 * pair + 1]
        term = dot(x_ref[...], g_ref[...], ((0,), (1,) if transposed else (0,)))
        total_product = term if total_product is None else total_product + term
    tiles[slot] = total_product
    for r in range(step_rows):
        for c in range(per_row):
            block = first_block + (i * step_rows + r) * per_row + c
            chunk, at_row = block // 24, lax.rem(block, 24) * BS
            pltpu.make_async_copy(
                tiles.at[slot, r * BS : (r + 1) * BS, c * BS : (c + 1) * BS],
                out_ref.at[m, chunk, pl.ds(pl.multiple_of(at_row, BS), BS)],
                sems.at[slot],
            ).start()

    @pl.when(at == total - 1)
    def _():
        drain(slot)

        @pl.when(total > 1)
        def _():
            drain(1 - slot)


def grad_blocks(xs, gs, parts, rows, per_row, step_rows, first_block, split_x, split_g, buffer, name, chunks, depth, transposed=False, x_stride=None):
    steps = rows // step_rows
    x_stride = x_stride or steps
    tokens = xs[0].shape[0]
    width = per_row * BS
    x_spec = pl.BlockSpec(
        (tokens, step_rows * BS), (lambda m, i: (0, m * x_stride + i)) if split_x else (lambda m, i: (0, i))
    )
    if transposed:
        g_spec = pl.BlockSpec((width, tokens), lambda m, i: (0, 0))
    else:
        g_spec = pl.BlockSpec((tokens, width), (lambda m, i: (0, m)) if split_g else (lambda m, i: (0, 0)))
    anywhere = pl.BlockSpec(memory_space=pl.ANY)
    operands = [array for pair in zip(xs, gs) for array in pair] + ([] if buffer is None else [buffer])
    return pl.pallas_call(
        functools.partial(
            blocks_kernel, first_block, per_row, step_rows, transposed, len(xs)
        ),
        grid=(parts, steps),
        out_shape=jax.ShapeDtypeStruct((parts, chunks, depth, BS), jnp.float32),
        in_specs=[x_spec, g_spec] * len(xs) + ([] if buffer is None else [anywhere]),
        out_specs=anywhere,
        input_output_aliases={} if buffer is None else {2 * len(xs): 0},
        scratch_shapes=[
            pltpu.VMEM((2, step_rows * BS, width), jnp.float32),
            pltpu.SemaphoreType.DMA((2,)),
        ],
        compiler_params=pltpu.CompilerParams(vmem_limit_bytes=32 * MIB),
        cost_estimate=pl.CostEstimate(
            flops=2 * len(xs) * tokens * parts * rows * BS * width,
            bytes_accessed=parts * rows * BS * width * 4,
            transcendentals=0,
        ),
        name=name,
    )(*operands)


def fast_mesh():
    return lax.axis_size("dp") == 4 * LAYERS and lax.axis_size("mp") == MP


def gather_weights(blocks):
    low = blocks.astype(jnp.bfloat16)[0, 0]
    if fast_mesh():
        gathered = gather_all(low.reshape(-1, BS), THIRDS, 1, True, (), 2, "gather_weights")
    else:
        gathered = lax.all_gather(low, ("dp", "mp"), axis=0, tiled=False)
        gathered = gathered.reshape((-1, MP) + low.shape).swapaxes(0, 1)
    return gathered.reshape(MP, -1, BS, BS)


def swap_mp(values):
    return lax.ppermute(values, "mp", [(0, 1), (1, 0)])


def reduce_plain(rest, first, final):
    part = lax.axis_index("mp")
    own = (jnp.arange(MP) == part).astype(jnp.float32)
    ends = [piece.reshape(1, -1, BS, BS) * own[:, None, None, None] for piece in (first, final)]
    dp = lax.axis_size("dp")
    every = jnp.concatenate([ends[0], rest, ends[1]], 1)
    every = every.reshape(MP, dp, -1, BS, BS).transpose(1, 0, 2, 3, 4)
    return lax.psum_scatter(
        every.reshape(dp * MP, -1, BS, BS), ("dp", "mp"), scatter_dimension=0, tiled=True
    )[0]


TALL = NTOK + 16
TILES = D // BS
CONV_AT = TILES * TALL
HEAD_AT = CONV_AT + 27 * CF
SMALL_AT = HEAD_AT + CF
DECONV_AT = SMALL_AT + CF
PACKED = DECONV_AT + DEC
AUX_ROOM = 8 * MP * AUX_ROWS
FLAT_ROWS = -(-NAUX // (8 * BS)) * 8


def pack_kernel(zero_ref, *refs):
    vectors, up_ref, conv_ref, head_ref, small_ref, deconv_ref = refs[:8], *refs[8:13]
    out_ref, rows_ref, sems = refs[14:]
    for j in range(TILES):
        lanes_at = slice(j * BS, (j + 1) * BS)
        base = j * TALL
        rows_ref[base : base + NTOK] = zero_ref[:, lanes_at]
        small_rows = [vector[:, lanes_at] for vector in vectors]
        small_rows += [up_ref[:, i * D + j * BS : i * D + (j + 1) * BS] for i in range(FF // D)]
        small_rows += [jnp.zeros((16 - len(small_rows), BS), jnp.float32)]
        rows_ref[base + NTOK : base + TALL] = jnp.concatenate(small_rows, 0)
    lane = lax.broadcasted_iota(jnp.int32, (CF, BS), 1)
    wide_lane = lax.broadcasted_iota(jnp.int32, (DEC, BS), 1)
    rows_ref[CONV_AT:HEAD_AT] = conv_ref[...]
    rows_ref[HEAD_AT:SMALL_AT] = head_ref[...]
    rows_ref[SMALL_AT:DECONV_AT] = jnp.where(lane < 2, small_ref[...], 0.0)
    rows_ref[DECONV_AT:PACKED] = jnp.where(wide_lane < 1, deconv_ref[...], 0.0)
    rows_ref[PACKED:AUX_ROOM] = jnp.zeros((AUX_ROOM - PACKED, BS), jnp.float32)
    copies = [
        pltpu.make_async_copy(
            rows_ref.at[pl.ds((m * 8 + chunk) * AUX_ROWS, AUX_ROWS)],
            out_ref.at[m, chunk, pl.ds(BLOCK_ROWS, AUX_ROWS)],
            sems.at[m * 8 + chunk],
        )
        for m in range(MP)
        for chunk in range(8)
    ]
    for copy in copies:
        copy.start()
    for copy in copies:
        copy.wait()


def pack_aux(zero, vectors, up_bias, conv, head, small, deconv, buffer):
    whole = pl.BlockSpec(memory_space=pltpu.VMEM)
    anywhere = pl.BlockSpec(memory_space=pl.ANY)
    operands = [zero] + [vector.reshape(1, D) for vector in vectors]
    operands += [up_bias.reshape(1, FF), conv, head, small, deconv]
    return pl.pallas_call(
        pack_kernel,
        out_shape=jax.ShapeDtypeStruct(buffer.shape, jnp.float32),
        in_specs=[whole] * len(operands) + [anywhere],
        out_specs=anywhere,
        input_output_aliases={len(operands): 0},
        scratch_shapes=[
            pltpu.VMEM((AUX_ROOM, BS), jnp.float32),
            pltpu.SemaphoreType.DMA((8 * MP,)),
        ],
        compiler_params=pltpu.CompilerParams(vmem_limit_bytes=32 * MIB),
        cost_estimate=pl.CostEstimate(flops=0, bytes_accessed=4 * MIB, transcendentals=0),
        name="pack_aux",
    )(*operands, buffer)


def unpack_kernel(sums_ref, rows_ref, norm_ref, turned):
    def pieces(start, stop):
        at = start
        while at < stop:
            m, chunk = at // (8 * AUX_ROWS), at // AUX_ROWS % 8
            end = min(stop, (at // AUX_ROWS + 1) * AUX_ROWS)
            first = at % AUX_ROWS
            yield at - start, sums_ref[m, 4 + chunk, first : first + end - at]
            at = end

    def packed(start, stop):
        found = [piece for _, piece in pieces(start, stop)]
        return found[0] if len(found) == 1 else jnp.concatenate(found, 0)

    square = jnp.zeros((8, BS), jnp.float32)
    for m in range(MP):
        for owner in range(4 * LAYERS):
            square += sums_ref[m, owner, AUX_ROWS:]
    rows_ref[FLAT_ROWS - 16 :] = jnp.zeros((16, BS), jnp.float32)
    after = NTOK * TILES
    for j in range(TILES):
        token_sum = jnp.zeros((1, BS), jnp.float32)
        for offset, piece in pieces(j * TALL, j * TALL + NTOK):
            rows_ref[pl.ds(offset * TILES + j, piece.shape[0], stride=TILES)] = piece
            token_sum += jnp.sum(piece, 0, keepdims=True)
            square += jnp.sum((piece * piece).reshape(-1, 8, BS), 0)
        vectors = packed(j * TALL + NTOK, (j + 1) * TALL)
        square += jnp.sum((vectors * vectors).reshape(-1, 8, BS), 0)
        square += jnp.concatenate([token_sum * token_sum, jnp.zeros((7, BS), jnp.float32)], 0)
        rows_ref[after + j : after + j + 1] = token_sum
        order = list(range(7)) + list(range(8, 8 + FF // D)) + [7]
        for place, which in enumerate(order):
            at = after + TILES * (1 + place) + j
            rows_ref[at : at + 1] = vectors[which : which + 1]
    at = after + TILES * 13
    deconv = packed(DECONV_AT, PACKED)
    square += jnp.sum((deconv * deconv).reshape(-1, 8, BS), 0)
    rows_ref[at : at + 1] = deconv.T[0:1]
    at += 1
    for o in range(27):
        conv = packed(CONV_AT + o * CF, CONV_AT + (o + 1) * CF)
        square += jnp.sum((conv * conv).reshape(-1, 8, BS), 0)
        turned[:, 0:CF] = conv.T
        for f in range(8):
            rows_ref[at + o * CF : at + (o + 1) * CF, f * CF : (f + 1) * CF] = turned[
                pl.ds(f, CF, stride=8), 0:CF
            ]
    at += 27 * CF
    head = packed(HEAD_AT, SMALL_AT)
    small = packed(SMALL_AT, DECONV_AT)
    square += jnp.sum((head * head + small * small).reshape(-1, 8, BS), 0)
    turned_small = small.T
    segments = [(turned_small[1:2], CF)]
    segments += [(head[row : row + 1], NCLS) for row in range(CF)]
    segments += [(turned_small[0:1], NCLS)]
    lane = 0
    for values, length in segments:
        taken = 0
        while taken < length:
            row, col = lane // BS, lane % BS
            part = min(length - taken, BS - col)
            rows_ref[at + row : at + row + 1, col : col + part] = values[:, taken : taken + part]
            taken += part
            lane += part
    norm = jnp.sqrt(jnp.sum(jnp.sum(square, 0, keepdims=True), 1, keepdims=True))
    clip = clip_value / jnp.maximum(norm, clip_value)
    lanes_of = lax.broadcasted_iota(jnp.int32, (8, BS), 1)
    norm_ref[...] = jnp.where(lanes_of == 0, norm, clip)


def unpack_aux(gathered):
    whole = pl.BlockSpec(memory_space=pltpu.VMEM)
    return pl.pallas_call(
        unpack_kernel,
        out_shape=(
            jax.ShapeDtypeStruct((FLAT_ROWS, BS), jnp.float32),
            jax.ShapeDtypeStruct((8, BS), jnp.float32),
        ),
        in_specs=[whole],
        out_specs=(whole, whole),
        scratch_shapes=[pltpu.VMEM((BS, BS), jnp.float32)],
        compiler_params=pltpu.CompilerParams(vmem_limit_bytes=32 * MIB),
        cost_estimate=pl.CostEstimate(flops=0, bytes_accessed=7 * MIB, transcendentals=0),
        name="unpack_aux",
    )(gathered)


def greet_all(devices):
    me = lax.axis_index("dp") * MP + lax.axis_index("mp")
    barrier = pltpu.get_barrier_semaphore()

    def greet(k, carry):
        peer = lax.rem(me + k, devices)
        place = (peer // MP, lax.rem(peer, MP))
        pl.semaphore_signal(barrier, inc=1, device_id=place, device_id_type=MESH)
        return carry

    lax.fori_loop(1, devices, greet, 0)


def sum_over_all(devices, in_ref, out_ref, slots, send_sem, recv_sem):
    me = lax.axis_index("dp") * MP + lax.axis_index("mp")

    def copy(k, slot):
        peer = lax.rem(me + k, devices)
        place = (peer // MP, lax.rem(peer, MP))
        return remote(in_ref, slots.at[slot], send_sem.at[k], recv_sem.at[slot], place)

    slots[me] = in_ref[...]
    pl.semaphore_wait(pltpu.get_barrier_semaphore(), devices - 1)

    def push(k, carry):
        copy(k, me).start()
        return carry

    def pull(k, carry):
        copy(k, lax.rem(me + devices - k, devices)).wait_recv()
        return carry

    def settle(k, carry):
        copy(k, me).wait_send()
        return carry

    lax.fori_loop(1, devices, push, 0)
    lax.fori_loop(1, devices, pull, 0)
    total = slots[0]
    for i in range(1, devices):
        total = total + slots[i]
    out_ref[...] = total
    lax.fori_loop(1, devices, settle, 0)


def decoder_kernel(
    all_crops,
    devices,
    up_ref,
    deconv_bias_ref,
    conv_ref,
    conv_bias_ref,
    head_ref,
    head_bias_ref,
    labels_ref,
    batch_ref,
    conv_t_ref,
    head_t_ref,
    gu_ref,
    conv_grad_ref,
    head_grad_ref,
    small_ref,
    deconv_grad_ref,
    conv_in,
    grid_slope,
    conv_slope,
    features,
    chance,
    sums,
    conved,
    spread,
    total,
    slots,
    send_sem,
    recv_sem,
):
    greet_all(devices)
    decoder_forward_kernel(
        up_ref,
        deconv_bias_ref,
        conv_ref,
        conv_bias_ref,
        head_ref,
        head_bias_ref,
        labels_ref,
        batch_ref,
        conv_in,
        grid_slope,
        conv_slope,
        features,
        chance,
        sums,
        conved,
    )
    sum_over_all(devices, sums, total, slots, send_sem, recv_sem)
    decoder_backward_kernel(
        all_crops,
        total,
        batch_ref,
        labels_ref,
        chance,
        features,
        conv_slope,
        grid_slope,
        conv_in,
        conv_t_ref,
        head_t_ref,
        gu_ref,
        conv_grad_ref,
        head_grad_ref,
        small_ref,
        deconv_grad_ref,
        spread,
    )


def decoder(all_crops, *operands):
    devices = 4 * LAYERS * MP
    shapes = (
        jax.ShapeDtypeStruct((8 * DEC, NTOK), jnp.bfloat16),
        jax.ShapeDtypeStruct((27 * CF, DEC), jnp.float32),
        jax.ShapeDtypeStruct((CF, CF), jnp.float32),
        jax.ShapeDtypeStruct((CF, BS), jnp.float32),
        jax.ShapeDtypeStruct((DEC, BS), jnp.float32),
    )
    return pl.pallas_call(
        functools.partial(decoder_kernel, all_crops, devices),
        out_shape=shapes,
        in_specs=whole_specs(10),
        out_specs=tuple(whole_specs(5)),
        scratch_shapes=[
            pltpu.VMEM((DEC, CELLS), jnp.bfloat16),
            pltpu.VMEM((DEC, CELLS), jnp.float32),
            pltpu.VMEM((CF, CELLS), jnp.float32),
            pltpu.VMEM((CF, CELLS), jnp.bfloat16),
            pltpu.VMEM((CF, CELLS), jnp.float32),
            pltpu.VMEM((CF, BS), jnp.float32),
            pltpu.VMEM((CF, CELLS), jnp.float32),
            pltpu.VMEM((27 * CF, CELLS), jnp.bfloat16),
            pltpu.VMEM((CF, BS), jnp.float32),
            pltpu.VMEM((devices, CF, BS), jnp.float32),
            pltpu.SemaphoreType.DMA((devices,)),
            pltpu.SemaphoreType.DMA((devices,)),
        ],
        compiler_params=pltpu.CompilerParams(
            collective_id=3, has_side_effects=True, vmem_limit_bytes=40 * MIB
        ),
        cost_estimate=pl.CostEstimate(
            flops=6 * 27 * CF * DEC * CELLS, bytes_accessed=6 * MIB, transcendentals=DEC * CELLS
        ),
        name="decoder",
    )(*operands)


def layer_norm(values):
    center = values - jnp.mean(values, -1, keepdims=True)
    spread = jnp.mean(center * center, -1, keepdims=True)
    inverse = lax.rsqrt(spread + 1e-06)
    return center * inverse, inverse


def layer_norm_back(back, normal, inverse, gain):
    scaled = back * gain
    mean = jnp.mean(scaled, -1, keepdims=True)
    along = jnp.mean(scaled * normal, -1, keepdims=True)
    return inverse * (scaled - mean - normal * along)


def shampoo_kernel(per_step, clip_ref, g_ref, b_ref, s_ref, r_ref, m_ref, v_ref, nb_ref, ns_ref, nm_ref, nv_ref):
    def exact(a, b, dims):
        return lax.dot_general(
            a, b, (dims, ((), ())), precision=HIGHEST, preferred_element_type=jnp.float32
        )

    def mean_square(values):
        total = jnp.sum(jnp.sum(values * values, 0, keepdims=True), 1, keepdims=True)
        return total * (1.0 / (BS * BS))

    for i in range(per_step):
        grads = g_ref[i * BS : (i + 1) * BS] * clip_ref[0, 0]
        ns_ref[0, i] = beta_stat * s_ref[0, i] + (1 - beta_stat) * exact(grads, grads, ((1,), (1,)))
        ns_ref[1, i] = beta_stat * s_ref[1, i] + (1 - beta_stat) * exact(grads, grads, ((0,), (0,)))
        moment = beta_one * m_ref[i] + (1 - beta_one) * grads
        velocity = beta_two * v_ref[i] + (1 - beta_two) * grads * grads
        nm_ref[i] = moment
        nv_ref[i] = velocity
        hat = moment / (1 - beta_one**STEP)
        adam = hat / (jnp.sqrt(velocity / (1 - beta_two**STEP)) + 1e-08)
        left = exact(r_ref[0, i], hat, ((1,), (0,)))
        precond = exact(left, r_ref[1, i], ((1,), (0,)))
        ratio = jnp.sqrt((mean_square(adam) + 1e-06) / (mean_square(precond) + 1e-06))
        blocks = b_ref[i]
        nb_ref[i] = blocks - learn_rate * (precond * ratio + decay_rate * blocks)


def shampoo_step(clip, owned, blocks, stat_pair, root_pair, moment, velocity):
    number = blocks.shape[0]
    per_step = 3
    one = pl.BlockSpec((per_step, BS, BS), lambda i: (i, 0, 0))
    pair = pl.BlockSpec((2, per_step, BS, BS), lambda i: (0, i, 0, 0))
    single = jax.ShapeDtypeStruct((number, BS, BS), jnp.float32)
    return pl.pallas_call(
        functools.partial(shampoo_kernel, per_step),
        grid=(number // per_step,),
        out_shape=(single, jax.ShapeDtypeStruct((2, number, BS, BS), jnp.float32), single, single),
        in_specs=[
            pl.BlockSpec(memory_space=pltpu.SMEM),
            pl.BlockSpec((per_step * BS, BS), lambda i: (i, 0)),
            one,
            pair,
            pair,
            one,
            one,
        ],
        out_specs=(one, pair, one, one),
        compiler_params=pltpu.CompilerParams(vmem_limit_bytes=32 * MIB),
        cost_estimate=pl.CostEstimate(
            flops=number * 8 * BS**3 * 6, bytes_accessed=number * 12 * BS * BS * 4, transcendentals=0
        ),
        name="shampoo",
    )(clip.reshape(1, 1), owned, blocks, stat_pair, root_pair, moment, velocity)


def adam_step(param, grads, moment, veloc):
    moment_new = beta_one * moment + (1 - beta_one) * grads
    veloc_new = beta_two * veloc + (1 - beta_two) * grads * grads
    direction = (
        moment_new / (1 - beta_one**STEP) / (jnp.sqrt(veloc_new / (1 - beta_two**STEP)) + 1e-08)
    )
    return (param - learn_rate * direction, moment_new, veloc_new)


def halves(matrix):
    return matrix[:, :HALF], matrix[:, HALF:]


def local(
    patches,
    labels,
    batch_ids,
    blocks,
    statistics,
    roots,
    moments,
    velocity,
    aux,
    aux_moment,
    aux_velocity,
):
    part = lax.axis_index("mp")
    all_crops = lax.axis_size("dp") * MP
    pieces = split_aux(aux)
    gain, shift = pieces["norm_gain"], pieces["norm_bias"]

    gathered = gather_weights(blocks)
    (w_embed,) = unblock(gathered, True)
    w_qkv, w_proj, w_up, w_down, w_deconv = unblock(gathered, False)

    def columns(array, which, width, start):
        return lax.dynamic_slice_in_dim(array, which * width + start, width - start, 1)

    down_start = 2 * FF // MP // 3

    other_rows = lax.dynamic_slice_in_dim(patches, (1 - part) * NTOK, NTOK, 0)
    own_rows = lax.dynamic_slice_in_dim(patches, part * NTOK, NTOK, 0)
    received = swap_mp(dot_nn(other_rows, w_embed))
    stream_zero = (
        dot_nn(own_rows, w_embed) + received + pieces["positions"] + pieces["embed_bias"]
    )
    normal_one, inverse_one = layer_norm(stream_zero)
    normed_one = (normal_one * gain[0] + shift[0]).astype(jnp.bfloat16)
    q_bias, v_bias = pieces["qv_bias"][0], pieces["qv_bias"][1]
    nothing = jnp.zeros((HALF,), jnp.float32)
    qkv_bias = jnp.concatenate(
        [q_bias[:HALF], nothing, v_bias[:HALF], q_bias[HALF:], nothing, v_bias[HALF:]]
    )
    qkv = (dot_nn(normed_one, w_qkv) + qkv_bias).astype(jnp.bfloat16)
    zero_stream = stream_zero.astype(jnp.bfloat16)
    zero_half = swap_mp(columns(zero_stream, 1 - part, HALF, 0))
    mixed, lse = attention_forward(qkv)
    mixed, zero_half = lax.optimization_barrier((mixed, zero_half))
    stream_one = stream_zero + dot_nn(mixed, w_proj) + pieces["proj_bias"]
    one_stream = stream_one.astype(jnp.bfloat16)
    one_half = swap_mp(columns(one_stream, 1 - part, HALF, 0))
    normal_two, inverse_two = layer_norm(stream_one)
    normed_two = (normal_two * gain[1] + shift[1]).astype(jnp.bfloat16)
    hidden = dot_nn(normed_two, w_up) + pieces["up_bias"]
    active_value, hidden_slope = gelu_and_slope(hidden)
    active = active_value.astype(jnp.bfloat16)
    active, one_half = lax.optimization_barrier((active, one_half))
    active_other = swap_mp(columns(active, 1 - part, FF // MP, down_start))
    stream_two = stream_one + dot_nn(active, w_down) + pieces["down_bias"]
    streams = [zero_stream, one_stream, stream_two.astype(jnp.bfloat16)]
    stacked = jnp.concatenate([halves(s)[m] for m in range(MP) for s in streams], 1)
    up_t = dot(w_deconv, stacked, ((0,), (1,)))

    conv_weight = pieces["conv_weight"].astype(jnp.bfloat16).reshape(27, DEC, CF)
    conv_low = conv_weight.transpose(0, 2, 1).reshape(27 * CF, DEC)
    conv_t = conv_weight.transpose(1, 0, 2).reshape(DEC, 27 * CF)
    head_weight = jnp.pad(pieces["head_weight"], ((0, 0), (0, CF - NCLS))).astype(jnp.bfloat16)
    head_bias = jnp.pad(pieces["head_bias"], (0, CF - NCLS)).reshape(CF, 1)
    grid_labels = (
        labels.reshape(GS, 2, GS, 2, GS, 2).transpose(1, 3, 5, 0, 2, 4).reshape(8, NTOK)
    )
    batch = jnp.broadcast_to(batch_ids.reshape(1, 1), (1, BS))
    operands = (
        up_t,
        pieces["deconv_bias"].reshape(DEC, 1),
        conv_low,
        pieces["conv_bias"].reshape(CF, 1),
        head_weight.T,
        head_bias,
        grid_labels,
        batch,
    )
    if fast_mesh():
        gu_t, conv_grad, head_grad, small, deconv_bias_grad = decoder(
            all_crops, *operands, conv_t, head_weight
        )
    else:
        conv_in, grid_slope, conv_slope, features, chance, sums = decoder_forward(*operands)
        gu_t, conv_grad, head_grad, small, deconv_bias_grad = decoder_backward(
            all_crops,
            lax.psum(sums, ("dp", "mp")),
            batch,
            grid_labels,
            chance,
            features,
            conv_slope,
            grid_slope,
            conv_in,
            conv_t,
            head_weight,
        )
    gu_t, two_stream, active_other = lax.optimization_barrier((gu_t, streams[2], active_other))
    two_half = swap_mp(columns(two_stream, 1 - part, HALF, 0))
    loss_value = small[0, 2]

    gu_other = swap_mp(gu_t)
    stacked_back = dot(gu_t, w_deconv, ((0,), (1,)))
    back_zero_s, back_one_s, back_two = [
        jnp.concatenate([stacked_back[:, (3 * m + s) * HALF : (3 * m + s + 1) * HALF] for m in range(MP)], 1)
        for s in range(3)
    ]
    grad_down_bias = jnp.sum(back_two, 0)
    two_low = back_two.astype(jnp.bfloat16)
    two_other = swap_mp(two_low)
    back_hidden = (hidden_slope * dot_nt(two_low, w_down)).astype(jnp.bfloat16)
    grad_up_bias = jnp.sum(back_hidden.astype(jnp.float32), 0)
    back_normed_two = dot_nt(back_hidden, w_up)
    grad_gain_two = jnp.sum(back_normed_two * normal_two, 0)
    grad_shift_two = jnp.sum(back_normed_two, 0)
    back_one = (
        back_two + back_one_s + layer_norm_back(back_normed_two, normal_two, inverse_two, gain[1])
    )
    grad_proj_bias = jnp.sum(back_one, 0)
    one_low = back_one.astype(jnp.bfloat16)
    back_mixed = dot_nt(one_low, w_proj).astype(jnp.bfloat16)
    back_q, back_k, back_v = attention_backward(qkv, back_mixed, lse)
    back_qkv = jnp.concatenate(
        [halves(piece)[m] for m in range(MP) for piece in (back_q, back_k, back_v)], 1
    )
    grad_query_bias = jnp.sum(back_q.astype(jnp.float32), 0)
    grad_value_bias = jnp.sum(back_v.astype(jnp.float32), 0)
    back_normed_one = dot_nt(back_qkv, w_qkv)
    grad_gain_one = jnp.sum(back_normed_one * normal_one, 0)
    grad_shift_one = jnp.sum(back_normed_one, 0)
    back_normed_one, two_half, gu_other, two_other = lax.optimization_barrier(
        (back_normed_one, two_half, gu_other, two_other)
    )
    back_zero = (
        back_one + back_zero_s + layer_norm_back(back_normed_one, normal_one, inverse_one, gain[0])
    )
    zero_low = back_zero.astype(jnp.bfloat16)
    other_low = swap_mp(zero_low)

    fast = fast_mesh()
    depth = CHUNK if fast else BLOCK_ROWS
    stacked_own = jnp.concatenate([columns(stream, part, HALF, 0) for stream in streams], 1)
    stacked_other = jnp.concatenate([zero_half, one_half, two_half], 1)
    active_own = columns(active, part, FF // MP, down_start)
    final_grads = grad_blocks(
        [stacked_own, stacked_other], [gu_t, gu_other], 1, 9, 8, 3, 24, True, False, None, "grad_deconv", 4, BLOCK_ROWS, True
    )
    final_grads = grad_blocks(
        [active_own, active_other], [two_low, two_other], 1, 4, 6, 4, 0, True, False, final_grads, "grad_down_last", 4, BLOCK_ROWS
    )
    rest_grads = None
    for name, x, g, rows, per_row, step_rows, start, split_x, split_g, stride in (
        ("grad_down", active, two_low, 8, 6, 4, 144, True, False, 3),
        ("grad_up", normed_two, back_hidden, 6, 12, 3, 72, False, True, None),
        ("grad_proj", mixed, one_low, 3, 6, 3, 54, True, False, None),
        ("grad_qkv", normed_one, back_qkv, 6, 9, 3, 0, False, True, None),
    ):
        rest_grads = grad_blocks(
            [x], [g], MP, rows, per_row, step_rows, start, split_x, split_g, rest_grads, name, 8, depth,
            x_stride=stride,
        )
    first_grads = grad_blocks(
        [own_rows, other_rows], [zero_low, other_low], 1, 16, 6, 4, 0, False, False, None, "grad_embed", 4, BLOCK_ROWS
    )
    vectors = [
        grad_gain_one,
        grad_gain_two,
        grad_shift_one,
        grad_shift_two,
        grad_query_bias,
        grad_value_bias,
        grad_proj_bias,
        grad_down_bias,
    ]
    if fast:
        head_wide = jnp.pad(head_grad, ((0, 0), (0, BS - CF)))
        rest_grads = pack_aux(
            back_zero, vectors, grad_up_bias, conv_grad, head_wide, small, deconv_bias_grad, rest_grads
        )
        owned, squares = reduce_to_owners(
            rest_grads.reshape(MP, 2, 2, 2, CHUNK, BS),
            first_grads.reshape(2, 2, BLOCK_ROWS, BS),
            final_grads.reshape(2, 2, BLOCK_ROWS, BS),
        )
        gathered_aux = gather_all(
            jnp.concatenate([owned[BLOCK_ROWS:], squares]),
            ((0, AUX_ROWS), (AUX_ROWS, 8)),
            1,
            False,
            (0,),
            4,
            "gather_aux",
        )
        in_rows, norm_clip = unpack_aux(gathered_aux)
        aux_total = in_rows.reshape(-1)[:NAUX]
        grad_norm, clip_scale = norm_clip[0, 0], norm_clip[0, 1]
    else:
        owned = reduce_plain(rest_grads.reshape(MP, -1, BS, BS), first_grads, final_grads)
        owned = owned.reshape(-1, BS)
        positions_sum, small_sum = lax.psum(
            (
                back_zero,
                jnp.concatenate(
                    vectors[:7]
                    + [
                        grad_up_bias,
                        grad_down_bias,
                        deconv_bias_grad[:, 0],
                        conv_grad.reshape(27, CF, DEC).transpose(0, 2, 1).reshape(-1),
                        small[:, 1],
                        head_grad[:, :NCLS].reshape(-1),
                        small[:NCLS, 0],
                    ]
                ),
            ),
            ("dp", "mp"),
        )
        aux_total = jnp.concatenate(
            [positions_sum.reshape(-1), jnp.sum(positions_sum, 0), small_sum]
        )
        block_square = lax.psum(jnp.sum(owned * owned), ("dp", "mp"))
        grad_norm = jnp.sqrt(block_square + jnp.sum(aux_total * aux_total))
        clip_scale = clip_value / jnp.maximum(grad_norm, clip_value)
    block_new, stat_new, moment_new, veloc_new = shampoo_step(
        clip_scale,
        owned,
        blocks[0, 0],
        statistics[:, 0, 0],
        roots[:, 0, 0],
        moments[0, 0],
        velocity[0, 0],
    )
    aux_new, aux_moment_new, aux_veloc_new = adam_step(
        aux, aux_total * clip_scale, aux_moment, aux_velocity
    )
    return (
        loss_value,
        grad_norm,
        block_new[None, None],
        stat_new[:, None, None],
        moment_new[None, None],
        veloc_new[None, None],
        aux_new,
        aux_moment_new,
        aux_veloc_new,
    )


def solution(mesh):
    block_spec = P("dp", "mp", None, None, None)
    pair_spec = P(None, "dp", "mp", None, None, None)
    placed = (
        P("dp", "mp"),
        P(("dp", "mp"), None),
        P(("dp", "mp")),
        block_spec,
        pair_spec,
        pair_spec,
        block_spec,
        block_spec,
        P(),
        P(),
        P(),
    )
    return jax.shard_map(
        local,
        mesh=mesh,
        in_specs=placed,
        out_specs=(P(), P(), block_spec, pair_spec, block_spec, block_spec, P(), P(), P()),
        check_vma=False,
    )
```

```python
import functools
import math

import jax
import jax.numpy as jnp
from jax import lax
from jax.experimental import pallas as pl
from jax.experimental.pallas import tpu as pltpu
from jax.sharding import PartitionSpec as P

D = 768
HDIM = 64
FF = 3072
PV = 4096
DEC = 128
CF = 16
NCLS = 14
GS = 8
MB = 4
STEP = 10
BS = 128
NTOK = 512
CELLS = 4096
MP = 2
HALF = D // MP
E_BLOCKS = PV // MP * D // (BS * BS)

HIGHEST = lax.Precision.HIGHEST
MESH = pl.DeviceIdType.MESH
beta_one = 0.9
beta_two = 0.999
beta_stat = 0.95
learn_rate = 0.02
decay_rate = 0.01
clip_value = 0.005
MIB = 1024 * 1024

OFFSETS = [(a, b, c) for a in range(3) for b in range(3) for c in range(3)]
PARITIES = [(i, j, k) for i in range(2) for j in range(2) for k in range(2)]


def dot(a, b, dims):
    return lax.dot_general(a, b, (dims, ((), ())), preferred_element_type=jnp.float32)


def dot_nn(a, b):
    return dot(a, b, ((1,), (0,)))


def dot_nt(a, b):
    return dot(a, b, ((1,), (1,)))


def dot_tn(a, b):
    return dot(a, b, ((0,), (0,)))


def gelu_cdf(v):
    return 0.5 * (1.0 + lax.erf(v * (0.5**0.5)))


def gelu_and_slope(v):
    cdf = gelu_cdf(v)
    density = jnp.exp(-0.5 * v * v) * (1.0 / math.sqrt(2.0 * math.pi))
    return v * cdf, cdf + v * density


def aux_layout():
    return [
        ("positions", (NTOK, D)),
        ("embed_bias", (D,)),
        ("norm_gain", (2, D)),
        ("norm_bias", (2, D)),
        ("qv_bias", (2, D)),
        ("proj_bias", (D,)),
        ("up_bias", (FF,)),
        ("down_bias", (D,)),
        ("deconv_bias", (DEC,)),
        ("conv_weight", (27 * DEC, CF)),
        ("conv_bias", (CF,)),
        ("head_weight", (CF, NCLS)),
        ("head_bias", (NCLS,)),
    ]


NAUX = sum(math.prod(shape) for _, shape in aux_layout())


def split_aux(vector):
    pieces = {}
    offset = 0
    for section_name, section_shape in aux_layout():
        length = math.prod(section_shape)
        pieces[section_name] = vector[offset : offset + length].reshape(section_shape)
        offset += length
    return pieces


def attention_forward_kernel(qkv_q, qkv_k, qkv_v, mixed_ref, lse_ref):
    q, k, v = qkv_q[...], qkv_k[...], qkv_v[...]
    v_t = v.astype(jnp.float32).T.astype(jnp.bfloat16)
    outs = []
    for h in range(2):
        cols = slice(h * HDIM, (h + 1) * HDIM)
        scores = dot_nt(k[:, cols], q[:, cols]) * 0.125
        top = jnp.max(scores, 0, keepdims=True)
        weights = jnp.exp(scores - top)
        total = jnp.sum(weights, 0, keepdims=True)
        attention = (weights * (1.0 / total)).astype(jnp.bfloat16)
        outs.append(dot_nn(v_t[cols], attention))
        lse_ref[0, h : h + 1, :] = top + jnp.log(total)
    mixed_ref[...] = jnp.concatenate(outs, 0).T.astype(jnp.bfloat16)


def attention_backward_kernel(qkv_q, qkv_k, qkv_v, gm_ref, lse_ref, gq_ref, gk_ref, gv_ref):
    q, k, v, gm = qkv_q[...], qkv_k[...], qkv_v[...], gm_ref[...]
    k_t = k.astype(jnp.float32).T.astype(jnp.bfloat16)
    gq_t = []
    for h in range(2):
        cols = slice(h * HDIM, (h + 1) * HDIM)
        scores = dot_nt(k[:, cols], q[:, cols]) * 0.125
        attention = jnp.exp(scores - lse_ref[0, h : h + 1, :])
        back = dot_nt(v[:, cols], gm[:, cols])
        gv_ref[:, cols] = dot_nn(attention.astype(jnp.bfloat16), gm[:, cols]).astype(jnp.bfloat16)
        mean = jnp.sum(back * attention, 0, keepdims=True)
        gs = (attention * (back - mean)).astype(jnp.bfloat16)
        gk_ref[:, cols] = (dot_nn(gs, q[:, cols]) * 0.125).astype(jnp.bfloat16)
        gq_t.append(dot_nn(k_t[cols], gs) * 0.125)
    gq_ref[...] = jnp.concatenate(gq_t, 0).T.astype(jnp.bfloat16)


def qkv_spec(part):
    return pl.BlockSpec((NTOK, BS), lambda i, part=part: (0, (i // 3) * 9 + part * 3 + i % 3))


def attention_forward(qkv):
    return pl.pallas_call(
        attention_forward_kernel,
        grid=(6,),
        out_shape=(
            jax.ShapeDtypeStruct((NTOK, D), jnp.bfloat16),
            jax.ShapeDtypeStruct((6, 2, NTOK), jnp.float32),
        ),
        in_specs=[qkv_spec(0), qkv_spec(1), qkv_spec(2)],
        out_specs=(
            pl.BlockSpec((NTOK, BS), lambda i: (0, i)),
            pl.BlockSpec((1, 2, NTOK), lambda i: (i, 0, 0)),
        ),
        compiler_params=pltpu.CompilerParams(vmem_limit_bytes=32 * MIB),
        cost_estimate=pl.CostEstimate(
            flops=12 * 4 * NTOK * NTOK * HDIM,
            bytes_accessed=NTOK * D * 8,
            transcendentals=12 * NTOK * NTOK,
        ),
        name="attention_forward",
    )(qkv, qkv, qkv)


def attention_backward(qkv, gm, lse):
    pair = pl.BlockSpec((NTOK, BS), lambda i: (0, i))
    return pl.pallas_call(
        attention_backward_kernel,
        grid=(6,),
        out_shape=(jax.ShapeDtypeStruct((NTOK, D), jnp.bfloat16),) * 3,
        in_specs=[
            qkv_spec(0),
            qkv_spec(1),
            qkv_spec(2),
            pair,
            pl.BlockSpec((1, 2, NTOK), lambda i: (i, 0, 0)),
        ],
        out_specs=(pair,) * 3,
        compiler_params=pltpu.CompilerParams(vmem_limit_bytes=32 * MIB),
        cost_estimate=pl.CostEstimate(
            flops=12 * 10 * NTOK * NTOK * HDIM,
            bytes_accessed=NTOK * D * 14,
            transcendentals=12 * NTOK * NTOK,
        ),
        name="attention_backward",
    )(qkv, qkv, qkv, gm, lse)


def source_of(parity, step):
    at = parity + step
    if at < 0:
        return 1, -1
    if at > 1:
        return 0, 1
    return at, 0


def shift_plan(offset, parity, sign):
    found = [source_of(par, sign * (off - 1)) for off, par in zip(offset, parity)]
    bits = [f[0] for f in found]
    steps = [f[1] for f in found]
    return bits[0] * 4 + bits[1] * 2 + bits[2], steps


def token_masks(tokens):
    at = (tokens // (GS * GS), (tokens // GS) % GS, tokens % GS)
    masks = {}
    for axis in range(3):
        masks[axis, 1] = at[axis] < GS - 1
        masks[axis, -1] = at[axis] > 0
    return masks


def shifted(values, steps, masks):
    delta = steps[0] * GS * GS + steps[1] * GS + steps[2]
    if delta == 0 and not any(steps):
        return values
    moved = pltpu.roll(values, (-delta) % NTOK, 1)
    keep = None
    for axis in range(3):
        if steps[axis]:
            mask = masks[axis, steps[axis]]
            keep = mask if keep is None else keep & mask
    return jnp.where(keep, moved, 0.0)


def lanes(parity):
    return slice(parity * NTOK, (parity + 1) * NTOK)


def decoder_forward_kernel(
    up_ref,
    deconv_bias_ref,
    conv_ref,
    conv_bias_ref,
    head_ref,
    head_bias_ref,
    labels_ref,
    batch_ref,
    conv_in_ref,
    grid_slope_ref,
    conv_slope_ref,
    features_ref,
    chance_ref,
    sums_ref,
    conved_ref,
):
    tokens = lax.broadcasted_iota(jnp.int32, (CF, NTOK), 1)
    masks = token_masks(tokens)
    for parity in range(8):
        conved_ref[:, lanes(parity)] = jnp.broadcast_to(conv_bias_ref[...], (CF, NTOK))
    for parity in range(8):
        cell = up_ref[parity * DEC : (parity + 1) * DEC, :] + deconv_bias_ref[...]
        value, slope = gelu_and_slope(cell)
        low = value.astype(jnp.bfloat16)
        conv_in_ref[:, lanes(parity)] = low
        grid_slope_ref[:, lanes(parity)] = slope
        products = dot_nn(conv_ref[...], low)
        for at, offset in enumerate(OFFSETS):
            target, back_steps = shift_plan(offset, PARITIES[parity], -1)
            forward = [-s for s in back_steps]
            piece = shifted(products[at * CF : (at + 1) * CF, :], forward, masks)
            conved_ref[:, lanes(target)] += piece
    rows = lax.broadcasted_iota(jnp.int32, (CF, NTOK), 0)
    hit = jnp.zeros((CF, 1), jnp.float32)
    predicted = jnp.zeros((CF, 1), jnp.float32)
    truth = jnp.zeros((CF, 1), jnp.float32)
    entropy = jnp.zeros((CF, 1), jnp.float32)
    for parity in range(8):
        value, slope = gelu_and_slope(conved_ref[:, lanes(parity)])
        conv_slope_ref[:, lanes(parity)] = slope
        features = value.astype(jnp.bfloat16)
        features_ref[:, lanes(parity)] = features
        logits = dot_nn(head_ref[...], features) + head_bias_ref[...]
        logits = jnp.where(rows < NCLS, logits, -1e30)
        center = logits - jnp.max(logits, 0, keepdims=True)
        log_prob = center - jnp.log(jnp.sum(jnp.exp(center), 0, keepdims=True))
        chance = jnp.exp(log_prob)
        target = (rows == labels_ref[parity : parity + 1, :]).astype(jnp.float32)
        chance_ref[:, lanes(parity)] = chance
        hit += jnp.sum(chance * target, 1, keepdims=True)
        predicted += jnp.sum(chance, 1, keepdims=True)
        truth += jnp.sum(target, 1, keepdims=True)
        entropy -= jnp.sum(jnp.where(target > 0, log_prob, 0.0), 1, keepdims=True)
    lane = lax.broadcasted_iota(jnp.int32, (CF, BS), 1)
    base = batch_ref[...] * 3
    sums_ref[...] = (
        jnp.where(lane == base, hit, 0.0)
        + jnp.where(lane == base + 1, predicted, 0.0)
        + jnp.where(lane == base + 2, truth, 0.0)
        + jnp.where(lane == 3 * MB, entropy, 0.0)
    )


def decoder_backward_kernel(
    all_crops,
    sums_ref,
    batch_ref,
    labels_ref,
    chance_ref,
    features_ref,
    conv_slope_ref,
    grid_slope_ref,
    conv_in_ref,
    conv_t_ref,
    head_t_ref,
    gu_ref,
    conv_grad_ref,
    head_grad_ref,
    small_ref,
    deconv_grad_ref,
    spread_ref,
):
    sums = sums_ref[...]
    lane = lax.broadcasted_iota(jnp.int32, (CF, BS), 1)
    row = lax.broadcasted_iota(jnp.int32, (CF, BS), 0)
    live = (lane < 3 * MB) & (lane % 3 == 0) & (row < NCLS)
    under = pltpu.roll(sums, BS - 1, 1) + pltpu.roll(sums, BS - 2, 1) + 1.0
    under = jnp.where(live, under, 1.0)
    over = 2.0 * sums + 1.0
    dice = jnp.where(live, over / under, 0.0)
    mean_dice = jnp.sum(jnp.sum(dice, 1, keepdims=True), 0, keepdims=True) / (NCLS * MB)
    entropy_lane = jnp.where(lane == 3 * MB, sums, 0.0)
    entropy = jnp.sum(jnp.sum(entropy_lane, 1, keepdims=True), 0, keepdims=True)
    loss = entropy / (all_crops * CELLS) + (1.0 - mean_dice)
    own = live & (lane == batch_ref[...] * 3)
    d_hit = jnp.sum(jnp.where(own, -2.0 / (MB * NCLS) / under, 0.0), 1, keepdims=True)
    d_predicted = jnp.sum(
        jnp.where(own, (1.0 / (MB * NCLS)) * over / (under * under), 0.0), 1, keepdims=True
    )
    tokens = lax.broadcasted_iota(jnp.int32, (CF, NTOK), 1)
    masks = token_masks(tokens)
    rows = lax.broadcasted_iota(jnp.int32, (CF, NTOK), 0)
    head_bias = jnp.zeros((CF, 1), jnp.float32)
    conv_bias = jnp.zeros((CF, 1), jnp.float32)
    head_grad = jnp.zeros((CF, CF), jnp.float32)
    for parity in range(8):
        chance = chance_ref[:, lanes(parity)]
        target = (rows == labels_ref[parity : parity + 1, :]).astype(jnp.float32)
        back = (d_hit * target + d_predicted) * chance - target * (1.0 / (all_crops * CELLS))
        logits = back - chance * jnp.sum(back, 0, keepdims=True)
        head_bias += jnp.sum(logits, 1, keepdims=True)
        low = logits.astype(jnp.bfloat16)
        head_grad += dot_nt(features_ref[:, lanes(parity)], low)
        conved = conv_slope_ref[:, lanes(parity)] * dot_nn(head_t_ref[...], low)
        conv_bias += jnp.sum(conved, 1, keepdims=True)
        rounded = conved.astype(jnp.bfloat16).astype(jnp.float32)
        for at, offset in enumerate(OFFSETS):
            target_cell, steps = shift_plan(offset, PARITIES[parity], 1)
            piece = shifted(rounded, [-s for s in steps], masks)
            spread_ref[at * CF : (at + 1) * CF, lanes(target_cell)] = piece.astype(jnp.bfloat16)
    head_grad_ref[...] = head_grad
    small_ref[...] = (
        jnp.where(lane == 0, head_bias, 0.0)
        + jnp.where(lane == 1, conv_bias, 0.0)
        + jnp.where(lane == 2, loss, 0.0)
    )
    conv_grad = jnp.zeros((27 * CF, DEC), jnp.float32)
    deconv_grad = jnp.zeros((DEC, 1), jnp.float32)
    for parity in range(8):
        spread = spread_ref[:, lanes(parity)]
        conv_grad += dot_nt(spread, conv_in_ref[:, lanes(parity)])
        back = grid_slope_ref[:, lanes(parity)] * dot_nn(conv_t_ref[...], spread)
        deconv_grad += jnp.sum(back, 1, keepdims=True)
        gu_ref[parity * DEC : (parity + 1) * DEC, :] = back.astype(jnp.bfloat16)
    conv_grad_ref[...] = conv_grad
    deconv_grad_ref[...] = jnp.broadcast_to(deconv_grad, (DEC, BS))


def whole_specs(number):
    return [pl.BlockSpec(memory_space=pltpu.VMEM)] * number


def decoder_forward(up_t, deconv_bias, conv_low, conv_bias, head_low, head_bias, labels, batch):
    shapes = (
        jax.ShapeDtypeStruct((DEC, CELLS), jnp.bfloat16),
        jax.ShapeDtypeStruct((DEC, CELLS), jnp.float32),
        jax.ShapeDtypeStruct((CF, CELLS), jnp.float32),
        jax.ShapeDtypeStruct((CF, CELLS), jnp.bfloat16),
        jax.ShapeDtypeStruct((CF, CELLS), jnp.float32),
        jax.ShapeDtypeStruct((CF, BS), jnp.float32),
    )
    return pl.pallas_call(
        decoder_forward_kernel,
        out_shape=shapes,
        in_specs=whole_specs(8),
        out_specs=tuple(whole_specs(6)),
        scratch_shapes=[pltpu.VMEM((CF, CELLS), jnp.float32)],
        compiler_params=pltpu.CompilerParams(vmem_limit_bytes=40 * MIB),
        cost_estimate=pl.CostEstimate(
            flops=2 * 27 * CF * DEC * CELLS, bytes_accessed=6 * MIB, transcendentals=DEC * CELLS
        ),
        name="decoder_forward",
    )(up_t, deconv_bias, conv_low, conv_bias, head_low, head_bias, labels, batch)


def decoder_backward(
    all_crops, sums, batch, labels, chance, features, conv_slope, grid_slope, conv_in, conv_t, head_t
):
    shapes = (
        jax.ShapeDtypeStruct((8 * DEC, NTOK), jnp.bfloat16),
        jax.ShapeDtypeStruct((27 * CF, DEC), jnp.float32),
        jax.ShapeDtypeStruct((CF, CF), jnp.float32),
        jax.ShapeDtypeStruct((CF, BS), jnp.float32),
        jax.ShapeDtypeStruct((DEC, BS), jnp.float32),
    )
    return pl.pallas_call(
        functools.partial(decoder_backward_kernel, all_crops),
        out_shape=shapes,
        in_specs=whole_specs(10),
        out_specs=tuple(whole_specs(5)),
        scratch_shapes=[pltpu.VMEM((27 * CF, CELLS), jnp.bfloat16)],
        compiler_params=pltpu.CompilerParams(vmem_limit_bytes=40 * MIB),
        cost_estimate=pl.CostEstimate(
            flops=4 * 27 * CF * DEC * CELLS, bytes_accessed=6 * MIB, transcendentals=0
        ),
        name="decoder_backward",
    )(sums, batch, labels, chance, features, conv_slope, grid_slope, conv_in, conv_t, head_t)


LAYERS = 4
GATHER_LAG = 2
THIRDS = tuple((8 * BS * i, 8 * BS) for i in range(3))
PIECES = 32
BLOCK_ROWS = 24 * BS
AUX_ROWS = 256
CHUNK = BLOCK_ROWS + AUX_ROWS
ROWS_N = 2 * CHUNK // PIECES
ROWS_F = BLOCK_ROWS // PIECES
LAG = 2
HOP_LAG = 2
AHEAD = 3
CORE_SLOTS = 8
SEND_SLOTS = 4
KEEP = 8
SUM_SLOTS = 12


def remote(src, dst, send_sem, recv_sem, device):
    return pltpu.make_async_remote_copy(
        src_ref=src,
        dst_ref=dst,
        send_sem=send_sem,
        recv_sem=recv_sem,
        device_id=device,
        device_id_type=MESH,
    )


def places():
    dp, x = lax.axis_index("dp"), lax.axis_index("mp")
    z, y, c = dp // 4, (dp // 2) % 2, dp % 2
    return dict(
        dp=dp,
        x=x,
        y=y,
        z=z,
        c=c,
        at_core=(dp + 1 - 2 * c, x),
        at_x=(dp, 1 - x),
        at_y=(dp + 2 - 4 * y, x),
        above=(lax.rem(dp + 4, 4 * LAYERS), x),
        below=(lax.rem(dp + 4 * LAYERS - 4, 4 * LAYERS), x),
    )


def greet_neighbours(at):
    barrier = pltpu.get_barrier_semaphore()
    for name in ("at_core", "at_x", "at_y"):
        pl.semaphore_signal(barrier, inc=1, device_id=at[name], device_id_type=MESH)

    @pl.when(at["z"] < LAYERS - 1)
    def _():
        pl.semaphore_signal(barrier, inc=1, device_id=at["above"], device_id_type=MESH)

    @pl.when(at["z"] > 0)
    def _():
        pl.semaphore_signal(barrier, inc=1, device_id=at["below"], device_id_type=MESH)

    peers = 3 + jnp.minimum(at["z"], 1) + jnp.minimum(LAYERS - 1 - at["z"], 1)
    pl.semaphore_wait(barrier, peers)


def gather_kernel(parts, by_x, skip, middle, in_ref, out_ref, local_sem, up_sem, down_sem, z_recv, x_send, x_recv, y_send, y_recv, core_send, core_recv):
    at = places()
    x, y, z, c = at["x"], at["y"], at["z"], at["c"]
    last = LAYERS - 1

    def spot(l, y_at, c_at, x_at, p):
        return out_ref.at[x_at, l * 4 + y_at * 2 + c_at, pl.ds(*parts[p])]

    def send(ref, send_sem, recv_sem, device):
        return remote(ref, ref, send_sem, recv_sem, device)

    def up(l, p):
        return send(spot(l, y, c, x, p), up_sem.at[l, p], z_recv.at[l, p], at["above"])

    def down(l, p):
        return send(spot(l, y, c, x, p), down_sem.at[l, p], z_recv.at[l, p], at["below"])

    def x_direct(l, p, x_at):
        return send(spot(l, y, c, x_at, p), x_send.at[l, p, 0], x_recv.at[l, p, 0], at["at_x"])

    def y_direct(l, p, y_at):
        return send(spot(l, y_at, c, x, p), y_send.at[l, p, 0], y_recv.at[l, p, 0], at["at_y"])

    def diagonal(l, p, y_at, x_at):
        if p < by_x:
            return send(spot(l, y_at, c, x_at, p), y_send.at[l, p, 1], y_recv.at[l, p, 1], at["at_y"])
        return send(spot(l, y_at, c, x_at, p), x_send.at[l, p, 1], x_recv.at[l, p, 1], at["at_x"])

    def relayed(l, p):
        return diagonal(l, p, y, 1 - x) if p < by_x else diagonal(l, p, 1 - y, x)

    def core(l, p, kind, c_at):
        y_at, x_at = ((y, x), (1 - y, x), (y, 1 - x), (1 - y, 1 - x))[kind]
        return send(
            spot(l, y_at, c_at, x_at, p),
            core_send.at[l, p, kind],
            core_recv.at[l, p, kind],
            at["at_core"],
        )

    def wide(l):
        return (l > 0) if skip else (l >= 0)

    own = pltpu.make_async_copy(in_ref, out_ref.at[x, at["dp"]], local_sem)
    own.start()
    greet_neighbours(at)
    own.wait()

    def arrive(l, p, came_up, came_down):
        if not (came_up and came_down):
            up(l, p).wait_recv()
        if came_up:

            @pl.when(z < last)
            def _():
                up(l, p).start()

        if came_down:

            @pl.when(z > 0)
            def _():
                down(l, p).start()

        @pl.when(wide(l))
        def _():
            x_direct(l, p, x).start()

        y_direct(l, p, y).start()
        core(l, p, 0, c).start()

    def relay(l, p):
        y_direct(l, p, 1 - y).wait_recv()

        @pl.when(wide(l))
        def _():
            if p >= by_x:
                relayed(l, p).start()
            x_direct(l, p, 1 - x).wait_recv()
            if p < by_x:
                relayed(l, p).start()
            core(l, p, 2, c).start()

        core(l, p, 1, c).start()

    def finish(l, p):
        @pl.when(wide(l))
        def _():
            diagonal(l, p, 1 - y, 1 - x).wait_recv()
            core(l, p, 3, c).start()

    def held(l, p):
        return ((l > 0) & (l < last)) if p in middle else ((l >= 0) & (l <= last))

    number = len(parts)

    def both(tick, run):
        if tick < 0 or tick >= LAYERS * number:
            return
        r, p = tick // number, tick % number
        if r == 0:

            @pl.when(held(z, p))
            def _():
                run(z, p, True, True)

            return

        @pl.when(held(z - r, p))
        def _():
            run(z - r, p, True, False)

        @pl.when(held(z + r, p))
        def _():
            run(z + r, p, False, True)

    for tick in range(LAYERS * number + 2 * GATHER_LAG):
        both(tick, arrive)
        both(tick - GATHER_LAG, lambda l, p, up_way, down_way: relay(l, p))
        both(tick - 2 * GATHER_LAG, lambda l, p, up_way, down_way: finish(l, p))

    def settle_part(l, p):
        for kind in (0, 1):
            core(l, p, kind, 1 - c).wait_recv()
            core(l, p, kind, c).wait_send()
        y_direct(l, p, y).wait_send()

        @pl.when(wide(l))
        def _():
            for kind in (2, 3):
                core(l, p, kind, 1 - c).wait_recv()
                core(l, p, kind, c).wait_send()
            x_direct(l, p, x).wait_send()
            relayed(l, p).wait_send()

        @pl.when((l <= z) & (z < last))
        def _():
            up(l, p).wait_send()

        @pl.when((l >= z) & (z > 0))
        def _():
            down(l, p).wait_send()

    def settle(l, carry):
        for p in range(number):
            pl.when(held(l, p))(functools.partial(settle_part, l, p))
        return carry

    lax.fori_loop(0, LAYERS, settle, 0)


def gather_all(values, parts, by_x, skip, middle, collective_id, name):
    rows = values.shape[0]
    number = len(parts)

    def sems(*shape):
        return pltpu.SemaphoreType.DMA(shape)

    return pl.pallas_call(
        functools.partial(gather_kernel, parts, by_x, skip, middle),
        out_shape=jax.ShapeDtypeStruct((MP, 4 * LAYERS, rows, BS), values.dtype),
        in_specs=[pl.BlockSpec(memory_space=pl.ANY)],
        out_specs=pl.BlockSpec(memory_space=pl.ANY),
        scratch_shapes=[
            pltpu.SemaphoreType.DMA,
            sems(LAYERS, number),
            sems(LAYERS, number),
            sems(LAYERS, number),
            sems(LAYERS, number, 2),
            sems(LAYERS, number, 2),
            sems(LAYERS, number, 2),
            sems(LAYERS, number, 2),
            sems(LAYERS, number, 4),
            sems(LAYERS, number, 4),
        ],
        compiler_params=pltpu.CompilerParams(
            collective_id=collective_id, has_side_effects=True, vmem_limit_bytes=32 * MIB
        ),
        cost_estimate=pl.CostEstimate(flops=0, bytes_accessed=32 * rows * BS * 4, transcendentals=0),
        name=name,
    )(values)


def reduce_kernel(
    n_ref,
    e_ref,
    f_ref,
    out_ref,
    square_ref,
    own_n,
    own_f,
    core_n,
    core_f,
    keep_n,
    keep_f,
    xs_n,
    ys_n,
    ys_f,
    xr_n,
    yr_n,
    yr_f,
    sum_n,
    sum_f,
    up_n,
    down_n,
    up_f,
    down_e,
    own_sem,
    core_send,
    core_recv,
    credit,
    xs_sem,
    ys_n_sem,
    ys_f_sem,
    xr_sem,
    yr_n_sem,
    yr_f_sem,
    z_n_sem,
    z_f_sem,
    up_n_sem,
    down_n_sem,
    up_f_sem,
    down_e_sem,
):
    at = places()
    x, y, z, c = at["x"], at["y"], at["z"], at["c"]
    last = LAYERS - 1

    def layer_of(s):
        return 1 + lax.rem(s, 2)

    def rows_of(s):
        return pl.ds(pl.multiple_of((s // 2) * ROWS_N, 8), ROWS_N)

    def rows_f(s):
        return pl.ds(pl.multiple_of(s * ROWS_F, 8), ROWS_F)

    def own_loads(s):
        slot = lax.rem(s, 3)
        mine = n_ref.at[:, layer_of(s) - 1, :, c, rows_of(s)]
        return (
            pltpu.make_async_copy(mine, own_n.at[slot], own_sem.at[slot, 0]),
            pltpu.make_async_copy(e_ref.at[:, c, rows_f(s)], own_f.at[slot, 0], own_sem.at[slot, 1]),
            pltpu.make_async_copy(f_ref.at[:, c, rows_f(s)], own_f.at[slot, 1], own_sem.at[slot, 2]),
        )

    def core_copies(s):
        slot = lax.rem(s, CORE_SLOTS)
        sources = (
            n_ref.at[:, layer_of(s) - 1, :, 1 - c, rows_of(s)],
            e_ref.at[:, 1 - c, rows_f(s)],
            f_ref.at[:, 1 - c, rows_f(s)],
        )
        targets = (core_n.at[slot], core_f.at[slot, 0], core_f.at[slot, 1])
        return [
            remote(source, target, core_send.at[s, i], core_recv.at[slot, i], at["at_core"])
            for i, (source, target) in enumerate(zip(sources, targets))
        ]

    def x_copy(s):
        slot = lax.rem(s, SEND_SLOTS)
        return remote(xs_n.at[slot], xr_n.at[s], xs_sem.at[slot], xr_sem.at[s], at["at_x"])

    def y_copy_f(s):
        slot = lax.rem(s, SEND_SLOTS)
        return remote(ys_f.at[slot], yr_f.at[s], ys_f_sem.at[slot], yr_f_sem.at[s], at["at_y"])

    def y_copy(s):
        slot = lax.rem(s, SEND_SLOTS)
        return remote(ys_n.at[slot], yr_n.at[s], ys_n_sem.at[slot], yr_n_sem.at[s], at["at_y"])

    def up_copy(s):
        slot = lax.rem(s, SUM_SLOTS)
        return remote(sum_n.at[slot], up_n.at[s], z_n_sem.at[slot], up_n_sem.at[s], at["above"])

    def down_copy(s):
        slot = lax.rem(s, SUM_SLOTS)
        return remote(sum_n.at[slot], down_n.at[s], z_n_sem.at[slot], down_n_sem.at[s], at["below"])

    def down_copy_e(s):
        slot = lax.rem(s, SUM_SLOTS)
        source, sem = sum_f.at[slot, 0], z_f_sem.at[slot, 0]
        return remote(source, down_e.at[s], sem, down_e_sem.at[s], at["below"])

    def up_copy_f(s):
        slot = lax.rem(s, SUM_SLOTS)
        source, sem = sum_f.at[slot, 1], z_f_sem.at[slot, 1]
        return remote(source, up_f.at[s], sem, up_f_sem.at[s], at["above"])

    def add_squares(values):
        square_ref[...] += jnp.sum((values * values).reshape(-1, 8, BS), 0)

    square_ref[...] = jnp.zeros((8, BS), jnp.float32)
    for s in range(2):
        for copy in own_loads(s):
            copy.start()
    greet_neighbours(at)
    for s in range(AHEAD):
        for copy in core_copies(s):
            copy.start()

    def first(s):
        @pl.when(s + 2 < PIECES)
        def _():
            for copy in own_loads(s + 2):
                copy.start()

        @pl.when(s + AHEAD < PIECES)
        def _():
            @pl.when(s + AHEAD >= CORE_SLOTS)
            def _():
                pl.semaphore_wait(credit, 1)

            for copy in core_copies(s + AHEAD):
                copy.start()

        for copy in own_loads(s):
            copy.wait()
        for copy in core_copies(s):
            copy.wait_recv()

        @pl.when(s >= SEND_SLOTS)
        def _():
            x_copy(s - SEND_SLOTS).wait_send()
            y_copy_f(s - SEND_SLOTS).wait_send()

        own, core = lax.rem(s, 3), lax.rem(s, CORE_SLOTS)
        send, keep = lax.rem(s, SEND_SLOTS), lax.rem(s, KEEP)
        xs_n[send] = own_n[own, 1 - x] + core_n[core, 1 - x]
        x_copy(s).start()
        for kind in range(2):
            ys_f[send, kind] = own_f[own, kind, 1 - y] + core_f[core, kind, 1 - y]
        y_copy_f(s).start()
        keep_n[keep] = own_n[own, x] + core_n[core, x]
        for kind in range(2):
            keep_f[keep, kind] = own_f[own, kind, y] + core_f[core, kind, y]

        @pl.when(s + CORE_SLOTS < PIECES)
        def _():
            pl.semaphore_signal(credit, inc=1, device_id=at["at_core"], device_id_type=MESH)

    def second(s):
        x_copy(s).wait_recv()

        @pl.when(s >= SEND_SLOTS)
        def _():
            y_copy(s - SEND_SLOTS).wait_send()

        send, keep = lax.rem(s, SEND_SLOTS), lax.rem(s, KEEP)
        ys_n[send] = keep_n[keep, 1 - y] + xr_n[s, 1 - y]
        y_copy(s).start()
        keep_n[keep, y] = keep_n[keep, y] + xr_n[s, y]

    def third(s):
        y_copy_f(s).wait_recv()
        y_copy(s).wait_recv()

        @pl.when((s >= SUM_SLOTS) & (z != layer_of(s)))
        def _():
            up_copy(s - SUM_SLOTS).wait_send()

        @pl.when((s >= SUM_SLOTS) & (z > 0))
        def _():
            down_copy_e(s - SUM_SLOTS).wait_send()

        @pl.when((s >= SUM_SLOTS) & (z < last))
        def _():
            up_copy_f(s - SUM_SLOTS).wait_send()

        slot, keep = lax.rem(s, SUM_SLOTS), lax.rem(s, KEEP)
        sum_n[slot] = keep_n[keep, y] + yr_n[s]
        sum_f[slot] = keep_f[keep] + yr_f[s]

    def along(s, hop):
        slot = lax.rem(s, SUM_SLOTS)
        layer = layer_of(s)
        away = jnp.where(z < layer, z, jnp.where(z > layer, last - z, jnp.maximum(z, last - z)))

        @pl.when(away == hop)
        def _():
            @pl.when((z > 0) & (z <= layer))
            def _():
                up_copy(s).wait_recv()
                sum_n[slot] = sum_n[slot] + up_n[s]

            @pl.when((z < last) & (z >= layer))
            def _():
                down_copy(s).wait_recv()
                sum_n[slot] = sum_n[slot] + down_n[s]

            @pl.when(z < layer)
            def _():
                up_copy(s).start()

            @pl.when(z > layer)
            def _():
                down_copy(s).start()

            @pl.when(z == layer)
            def _():
                out_ref[rows_of(s)] = sum_n[slot]
                piece = s // 2
                whole, cut = BLOCK_ROWS // ROWS_N, BLOCK_ROWS % ROWS_N

                @pl.when(piece <= whole)
                def _():
                    add_squares(sum_n[slot, pl.ds(0, cut)])

                @pl.when(piece < whole)
                def _():
                    add_squares(sum_n[slot, pl.ds(cut, ROWS_N - cut)])

        @pl.when(jnp.where(z == 0, last, last - z) == hop)
        def _():
            @pl.when(z < last)
            def _():
                down_copy_e(s).wait_recv()
                sum_f[slot, 0] = sum_f[slot, 0] + down_e[s]

            @pl.when(z > 0)
            def _():
                down_copy_e(s).start()

            @pl.when(z == 0)
            def _():
                out_ref[rows_f(s)] = sum_f[slot, 0]
                add_squares(sum_f[slot, 0])

        @pl.when(z == hop)
        def _():
            @pl.when(z > 0)
            def _():
                up_copy_f(s).wait_recv()
                sum_f[slot, 1] = sum_f[slot, 1] + up_f[s]

            @pl.when(z < last)
            def _():
                up_copy_f(s).start()

            @pl.when(z == last)
            def _():
                out_ref[rows_f(s)] = sum_f[slot, 1]
                add_squares(sum_f[slot, 1])

    def guarded(run, s):
        @pl.when((s >= 0) & (s < PIECES))
        def _():
            run(s)

    def step(t, carry):
        guarded(first, t)
        guarded(second, t - LAG)
        guarded(third, t - 2 * LAG)
        for hop in range(LAYERS):
            guarded(functools.partial(along, hop=hop), t - 2 * LAG - hop * HOP_LAG)
        return carry

    lax.fori_loop(0, PIECES + 2 * LAG + (LAYERS - 1) * HOP_LAG, step, 0)

    def drain_sends(i, carry):
        s = PIECES - SEND_SLOTS + i
        for copy in (x_copy(s), y_copy_f(s), y_copy(s)):
            copy.wait_send()
        return carry

    lax.fori_loop(0, SEND_SLOTS, drain_sends, 0)

    def drain_sums(i, carry):
        s = PIECES - SUM_SLOTS + i

        @pl.when(z != layer_of(s))
        def _():
            up_copy(s).wait_send()

        @pl.when(z > 0)
        def _():
            down_copy_e(s).wait_send()

        @pl.when(z < last)
        def _():
            up_copy_f(s).wait_send()

        return carry

    lax.fori_loop(0, SUM_SLOTS, drain_sums, 0)

    def drain_core(s, carry):
        for copy in core_copies(s):
            copy.wait_send()
        return carry

    lax.fori_loop(0, PIECES, drain_core, 0)

    @pl.when((z == 0) | (z == last))
    def _():
        out_ref[pl.ds(BLOCK_ROWS, AUX_ROWS)] = jnp.zeros((AUX_ROWS, BS), jnp.float32)


def reduce_to_owners(rest, first, final):
    def room(*shape):
        return pltpu.VMEM(shape + (BS,), jnp.float32)

    def sems(*shape):
        return pltpu.SemaphoreType.DMA(shape)

    return pl.pallas_call(
        reduce_kernel,
        out_shape=(
            jax.ShapeDtypeStruct((CHUNK, BS), jnp.float32),
            jax.ShapeDtypeStruct((8, BS), jnp.float32),
        ),
        in_specs=[pl.BlockSpec(memory_space=pltpu.HBM)] * 3,
        out_specs=(pl.BlockSpec(memory_space=pltpu.VMEM),) * 2,
        scratch_shapes=[
            room(3, 2, 2, ROWS_N),
            room(3, 2, 2, ROWS_F),
            room(CORE_SLOTS, 2, 2, ROWS_N),
            room(CORE_SLOTS, 2, 2, ROWS_F),
            room(KEEP, 2, ROWS_N),
            room(KEEP, 2, ROWS_F),
            room(SEND_SLOTS, 2, ROWS_N),
            room(SEND_SLOTS, ROWS_N),
            room(SEND_SLOTS, 2, ROWS_F),
            room(PIECES, 2, ROWS_N),
            room(PIECES, ROWS_N),
            room(PIECES, 2, ROWS_F),
            room(SUM_SLOTS, ROWS_N),
            room(SUM_SLOTS, 2, ROWS_F),
            room(PIECES, ROWS_N),
            room(PIECES, ROWS_N),
            room(PIECES, ROWS_F),
            room(PIECES, ROWS_F),
            sems(3, 3),
            sems(PIECES, 3),
            sems(CORE_SLOTS, 3),
            pltpu.SemaphoreType.REGULAR,
            sems(SEND_SLOTS),
            sems(SEND_SLOTS),
            sems(SEND_SLOTS),
            sems(PIECES),
            sems(PIECES),
            sems(PIECES),
            sems(SUM_SLOTS),
            sems(SUM_SLOTS, 2),
            sems(PIECES),
            sems(PIECES),
            sems(PIECES),
            sems(PIECES),
        ],
        compiler_params=pltpu.CompilerParams(
            collective_id=1, has_side_effects=True, vmem_limit_bytes=58 * MIB
        ),
        cost_estimate=pl.CostEstimate(flops=0, bytes_accessed=100 * MIB, transcendentals=0),
        name="reduce_to_owners",
    )(rest, first, final)


MATRICES = [
    (96, 6, 9, 3, True),
    (150, 3, 6, 3, False),
    (168, 6, 12, 3, True),
    (240, 12, 6, 4, False),
    (312, 9, 8, 3, False),
]
LOADS = 4


def unblock_kernel(plan, kinds, blocks_ref, *refs):
    outs, tiles = refs[:kinds], refs[kinds : 2 * kinds]
    loaded, load_sem, store_sem = refs[2 * kinds :]

    def load(i):
        kind, m, first, rows, per_row, row, col = plan[i]
        number = rows * per_row
        return pltpu.make_async_copy(
            blocks_ref.at[m, pl.ds(first, number)],
            loaded.at[i % LOADS, pl.ds(0, number)],
            load_sem.at[i % LOADS],
        )

    def store(i, slot):
        kind, m, first, rows, per_row, row, col = plan[i]
        return pltpu.make_async_copy(
            tiles[kind].at[slot],
            outs[kind].at[pl.ds(row, rows * BS), pl.ds(col, per_row * BS)],
            store_sem.at[kind, slot],
        )

    history = [[] for _ in range(kinds)]
    for i in range(min(LOADS - 1, len(plan))):
        load(i).start()
    for i, (kind, m, first, rows, per_row, row, col) in enumerate(plan):
        if i + LOADS - 1 < len(plan):
            load(i + LOADS - 1).start()
        load(i).wait()
        slot = len(history[kind]) % 2
        if len(history[kind]) >= 2:
            store(*history[kind][-2]).wait()
        for r in range(rows):
            for c in range(per_row):
                tiles[kind][slot, r * BS : (r + 1) * BS, c * BS : (c + 1) * BS] = loaded[
                    i % LOADS, r * per_row + c
                ]
        history[kind].append((i, slot))
        store(i, slot).start()
    for done in history:
        for entry in done[-2:]:
            store(*entry).wait()


def unblock(gathered):
    plan, shapes, tiles = [], [], []
    for kind, (first, rows, per_row, step, beside) in enumerate(MATRICES):
        tall, wide = rows * BS, per_row * BS
        shapes.append((tall, MP * wide) if beside else (MP * tall, wide))
        tiles.append((step * BS, wide))
        for m in range(MP):
            for at in range(0, rows, step):
                row = at * BS + (0 if beside else m * tall)
                plan.append((kind, m, first + at * per_row, step, per_row, row, m * wide if beside else 0))
    anywhere = pl.BlockSpec(memory_space=pl.ANY)
    largest = max(entry[3] * entry[4] for entry in plan)
    return pl.pallas_call(
        functools.partial(unblock_kernel, plan, len(shapes)),
        out_shape=tuple(jax.ShapeDtypeStruct(shape, jnp.bfloat16) for shape in shapes),
        in_specs=[anywhere],
        out_specs=tuple([anywhere] * len(shapes)),
        scratch_shapes=[pltpu.VMEM((2,) + tile, jnp.bfloat16) for tile in tiles]
        + [
            pltpu.VMEM((LOADS, largest, BS, BS), jnp.bfloat16),
            pltpu.SemaphoreType.DMA((LOADS,)),
            pltpu.SemaphoreType.DMA((len(shapes), 2)),
        ],
        compiler_params=pltpu.CompilerParams(vmem_limit_bytes=60 * MIB),
        cost_estimate=pl.CostEstimate(
            flops=0, bytes_accessed=38 * MIB, transcendentals=0
        ),
        name="unblock",
    )(gathered)


def embed_kernel(which_ref, rows_ref, blocks_ref, out_ref, matrix_ref):
    step = pl.program_id(0)
    for r in range(4):
        for c in range(6):
            matrix_ref[r * BS : (r + 1) * BS, c * BS : (c + 1) * BS] = blocks_ref[0, r * 6 + c]
    product = dot_nn(rows_ref[...], matrix_ref[...])

    @pl.when(step == 0)
    def _():
        out_ref[...] = product

    @pl.when(step > 0)
    def _():
        out_ref[...] += product


def embed_other(patches, gathered):
    part = lax.axis_index("mp")
    tall = 4 * BS
    return pl.pallas_call(
        embed_kernel,
        grid_spec=pltpu.PrefetchScalarGridSpec(
            num_scalar_prefetch=1,
            grid=(PV // MP // tall,),
            in_specs=[
                pl.BlockSpec((NTOK, tall), lambda k, which: (which[0], k)),
                pl.BlockSpec((1, 24, BS, BS), lambda k, which: (which[1], k, 0, 0)),
            ],
            out_specs=(
                pl.BlockSpec((NTOK, D), lambda k, which: (0, 0)),
                pl.BlockSpec((tall, D), lambda k, which: (k, 0)),
            ),
        ),
        out_shape=(
            jax.ShapeDtypeStruct((NTOK, D), jnp.float32),
            jax.ShapeDtypeStruct((PV // MP, D), jnp.bfloat16),
        ),
        compiler_params=pltpu.CompilerParams(vmem_limit_bytes=56 * MIB),
        cost_estimate=pl.CostEstimate(
            flops=2 * NTOK * D * PV // MP, bytes_accessed=10 * MIB, transcendentals=0
        ),
        name="embed_other",
    )(jnp.stack([1 - part, part]).astype(jnp.int32), patches, gathered)


def labels_kernel(labels_ref, out_ref):
    side = 2 * GS
    plane = side * side
    rows = jnp.concatenate([labels_ref[:, z * plane : (z + 1) * plane] for z in range(side)], 0)
    cell = lax.broadcasted_iota(jnp.int32, (plane, plane), 0)
    place = lax.broadcasted_iota(jnp.int32, (plane, plane), 1)
    parity, patch = place // (GS * GS), place % (GS * GS)
    match = (cell // side == 2 * (patch // GS) + parity // 2) & (
        cell % side == 2 * (patch % GS) + parity % 2
    )
    low = rows.astype(jnp.float32).astype(jnp.bfloat16)
    moved = dot_nn(low, match.astype(jnp.float32).astype(jnp.bfloat16)).astype(jnp.int32)
    width = GS * GS
    for i in range(2):
        for inner in range(4):
            for a in range(GS):
                out_ref[i * 4 + inner : i * 4 + inner + 1, a * width : (a + 1) * width] = moved[
                    2 * a + i : 2 * a + i + 1, inner * width : (inner + 1) * width
                ]


def arrange_labels(labels):
    return pl.pallas_call(
        labels_kernel,
        out_shape=jax.ShapeDtypeStruct((8, NTOK), jnp.int32),
        in_specs=whole_specs(1),
        out_specs=whole_specs(1)[0],
        cost_estimate=pl.CostEstimate(flops=2 * 16 * 256 * 256, bytes_accessed=65536, transcendentals=0),
        name="arrange_labels",
    )(labels)


def blocks_kernel(first_block, per_row, step_rows, transposed, pairs, *refs):
    out_ref, tiles, sems = refs[-3:]
    m, i = pl.program_id(0), pl.program_id(1)
    steps = pl.num_programs(1)
    at = m * steps + i
    slot = lax.rem(at, 2)
    total = pl.num_programs(0) * steps

    def drain(which):
        pltpu.make_async_copy(tiles.at[which], tiles.at[which], sems.at[which]).wait()

    @pl.when(at >= 2)
    def _():
        drain(slot)

    total_product = None
    for pair in range(pairs):
        x_ref, g_ref = refs[2 * pair], refs[2 * pair + 1]
        term = dot(x_ref[...], g_ref[...], ((0,), (1,) if transposed else (0,)))
        total_product = term if total_product is None else total_product + term
    tiles[slot] = total_product
    for r in range(step_rows):
        for c in range(per_row):
            block = first_block + (i * step_rows + r) * per_row + c
            chunk, at_row = block // 24, lax.rem(block, 24) * BS
            pltpu.make_async_copy(
                tiles.at[slot, r * BS : (r + 1) * BS, c * BS : (c + 1) * BS],
                out_ref.at[m, chunk, pl.ds(pl.multiple_of(at_row, BS), BS)],
                sems.at[slot],
            ).start()

    @pl.when(at == total - 1)
    def _():
        drain(slot)

        @pl.when(total > 1)
        def _():
            drain(1 - slot)


def grad_blocks(xs, gs, parts, rows, per_row, step_rows, first_block, split_x, split_g, buffer, name, chunks, depth, transposed=False, x_stride=None):
    steps = rows // step_rows
    x_stride = x_stride or steps
    tokens = xs[0].shape[0]
    width = per_row * BS
    x_spec = pl.BlockSpec(
        (tokens, step_rows * BS), (lambda m, i: (0, m * x_stride + i)) if split_x else (lambda m, i: (0, i))
    )
    if transposed:
        g_spec = pl.BlockSpec((width, tokens), lambda m, i: (0, 0))
    else:
        g_spec = pl.BlockSpec((tokens, width), (lambda m, i: (0, m)) if split_g else (lambda m, i: (0, 0)))
    anywhere = pl.BlockSpec(memory_space=pltpu.HBM)
    operands = [array for pair in zip(xs, gs) for array in pair] + ([] if buffer is None else [buffer])
    return pl.pallas_call(
        functools.partial(
            blocks_kernel, first_block, per_row, step_rows, transposed, len(xs)
        ),
        grid=(parts, steps),
        out_shape=jax.ShapeDtypeStruct((parts, chunks, depth, BS), jnp.float32),
        in_specs=[x_spec, g_spec] * len(xs) + ([] if buffer is None else [anywhere]),
        out_specs=anywhere,
        input_output_aliases={} if buffer is None else {2 * len(xs): 0},
        scratch_shapes=[
            pltpu.VMEM((2, step_rows * BS, width), jnp.float32),
            pltpu.SemaphoreType.DMA((2,)),
        ],
        compiler_params=pltpu.CompilerParams(vmem_limit_bytes=32 * MIB),
        cost_estimate=pl.CostEstimate(
            flops=2 * len(xs) * tokens * parts * rows * BS * width,
            bytes_accessed=parts * rows * BS * width * 4,
            transcendentals=0,
        ),
        name=name,
    )(*operands)


def fast_mesh():
    return lax.axis_size("dp") == 4 * LAYERS and lax.axis_size("mp") == MP


def gather_weights(blocks):
    low = blocks.astype(jnp.bfloat16)[0, 0]
    if fast_mesh():
        gathered = gather_all(low.reshape(-1, BS), THIRDS, 1, True, (), 2, "gather_weights")
    else:
        gathered = lax.all_gather(low, ("dp", "mp"), axis=0, tiled=False)
        gathered = gathered.reshape((-1, MP) + low.shape).swapaxes(0, 1)
    return gathered.reshape(MP, -1, BS, BS)


def swap_mp(values):
    return lax.ppermute(values, "mp", [(0, 1), (1, 0)])


def reduce_plain(rest, first, final):
    part = lax.axis_index("mp")
    own = (jnp.arange(MP) == part).astype(jnp.float32)
    ends = [piece.reshape(1, -1, BS, BS) * own[:, None, None, None] for piece in (first, final)]
    dp = lax.axis_size("dp")
    every = jnp.concatenate([ends[0], rest, ends[1]], 1)
    every = every.reshape(MP, dp, -1, BS, BS).transpose(1, 0, 2, 3, 4)
    return lax.psum_scatter(
        every.reshape(dp * MP, -1, BS, BS), ("dp", "mp"), scatter_dimension=0, tiled=True
    )[0]


TALL = NTOK + 16
TILES = D // BS
CONV_AT = TILES * TALL
HEAD_AT = CONV_AT + 27 * CF
SMALL_AT = HEAD_AT + CF
DECONV_AT = SMALL_AT + CF
PACKED = DECONV_AT + DEC
AUX_ROOM = 8 * MP * AUX_ROWS
FLAT_ROWS = -(-NAUX // (8 * BS)) * 8


def pack_kernel(zero_ref, *refs):
    vectors, up_ref, conv_ref, head_ref, small_ref, deconv_ref = refs[:8], *refs[8:13]
    out_ref, rows_ref, sems = refs[14:]
    for j in range(TILES):
        lanes_at = slice(j * BS, (j + 1) * BS)
        base = j * TALL
        rows_ref[base : base + NTOK] = zero_ref[:, lanes_at]
        small_rows = [vector[:, lanes_at] for vector in vectors]
        small_rows += [up_ref[:, i * D + j * BS : i * D + (j + 1) * BS] for i in range(FF // D)]
        small_rows += [jnp.zeros((16 - len(small_rows), BS), jnp.float32)]
        rows_ref[base + NTOK : base + TALL] = jnp.concatenate(small_rows, 0)
    lane = lax.broadcasted_iota(jnp.int32, (CF, BS), 1)
    wide_lane = lax.broadcasted_iota(jnp.int32, (DEC, BS), 1)
    rows_ref[CONV_AT:HEAD_AT] = conv_ref[...]
    rows_ref[HEAD_AT:SMALL_AT] = head_ref[...]
    rows_ref[SMALL_AT:DECONV_AT] = jnp.where(lane < 2, small_ref[...], 0.0)
    rows_ref[DECONV_AT:PACKED] = jnp.where(wide_lane < 1, deconv_ref[...], 0.0)
    rows_ref[PACKED:AUX_ROOM] = jnp.zeros((AUX_ROOM - PACKED, BS), jnp.float32)
    copies = [
        pltpu.make_async_copy(
            rows_ref.at[pl.ds((m * 8 + chunk) * AUX_ROWS, AUX_ROWS)],
            out_ref.at[m, chunk, pl.ds(BLOCK_ROWS, AUX_ROWS)],
            sems.at[m * 8 + chunk],
        )
        for m in range(MP)
        for chunk in range(8)
    ]
    for copy in copies:
        copy.start()
    for copy in copies:
        copy.wait()


def pack_aux(zero, vectors, up_bias, conv, head, small, deconv, buffer):
    whole = pl.BlockSpec(memory_space=pltpu.VMEM)
    anywhere = pl.BlockSpec(memory_space=pl.ANY)
    operands = [zero] + [vector.reshape(1, D) for vector in vectors]
    operands += [up_bias.reshape(1, FF), conv, head, small, deconv]
    return pl.pallas_call(
        pack_kernel,
        out_shape=jax.ShapeDtypeStruct(buffer.shape, jnp.float32),
        in_specs=[whole] * len(operands) + [anywhere],
        out_specs=anywhere,
        input_output_aliases={len(operands): 0},
        scratch_shapes=[
            pltpu.VMEM((AUX_ROOM, BS), jnp.float32),
            pltpu.SemaphoreType.DMA((8 * MP,)),
        ],
        compiler_params=pltpu.CompilerParams(vmem_limit_bytes=32 * MIB),
        cost_estimate=pl.CostEstimate(flops=0, bytes_accessed=4 * MIB, transcendentals=0),
        name="pack_aux",
    )(*operands, buffer)


def unpack_kernel(sums_ref, rows_ref, norm_ref, turned):
    def pieces(start, stop):
        at = start
        while at < stop:
            m, chunk = at // (8 * AUX_ROWS), at // AUX_ROWS % 8
            end = min(stop, (at // AUX_ROWS + 1) * AUX_ROWS)
            first = at % AUX_ROWS
            yield at - start, sums_ref[m, 4 + chunk, first : first + end - at]
            at = end

    def packed(start, stop):
        found = [piece for _, piece in pieces(start, stop)]
        return found[0] if len(found) == 1 else jnp.concatenate(found, 0)

    square = jnp.zeros((8, BS), jnp.float32)
    for m in range(MP):
        for owner in range(4 * LAYERS):
            square += sums_ref[m, owner, AUX_ROWS:]
    rows_ref[FLAT_ROWS - 16 :] = jnp.zeros((16, BS), jnp.float32)
    after = NTOK * TILES
    for j in range(TILES):
        token_sum = jnp.zeros((1, BS), jnp.float32)
        for offset, piece in pieces(j * TALL, j * TALL + NTOK):
            rows_ref[pl.ds(offset * TILES + j, piece.shape[0], stride=TILES)] = piece
            token_sum += jnp.sum(piece, 0, keepdims=True)
            square += jnp.sum((piece * piece).reshape(-1, 8, BS), 0)
        vectors = packed(j * TALL + NTOK, (j + 1) * TALL)
        square += jnp.sum((vectors * vectors).reshape(-1, 8, BS), 0)
        square += jnp.concatenate([token_sum * token_sum, jnp.zeros((7, BS), jnp.float32)], 0)
        rows_ref[after + j : after + j + 1] = token_sum
        order = list(range(7)) + list(range(8, 8 + FF // D)) + [7]
        for place, which in enumerate(order):
            at = after + TILES * (1 + place) + j
            rows_ref[at : at + 1] = vectors[which : which + 1]
    at = after + TILES * 13
    deconv = packed(DECONV_AT, PACKED)
    square += jnp.sum((deconv * deconv).reshape(-1, 8, BS), 0)
    rows_ref[at : at + 1] = deconv.T[0:1]
    at += 1
    for o in range(27):
        conv = packed(CONV_AT + o * CF, CONV_AT + (o + 1) * CF)
        square += jnp.sum((conv * conv).reshape(-1, 8, BS), 0)
        turned[:, 0:CF] = conv.T
        for f in range(8):
            rows_ref[at + o * CF : at + (o + 1) * CF, f * CF : (f + 1) * CF] = turned[
                pl.ds(f, CF, stride=8), 0:CF
            ]
    at += 27 * CF
    head = packed(HEAD_AT, SMALL_AT)
    small = packed(SMALL_AT, DECONV_AT)
    square += jnp.sum((head * head + small * small).reshape(-1, 8, BS), 0)
    turned_small = small.T
    segments = [(turned_small[1:2], CF)]
    segments += [(head[row : row + 1], NCLS) for row in range(CF)]
    segments += [(turned_small[0:1], NCLS)]
    lane = 0
    for values, length in segments:
        taken = 0
        while taken < length:
            row, col = lane // BS, lane % BS
            part = min(length - taken, BS - col)
            rows_ref[at + row : at + row + 1, col : col + part] = values[:, taken : taken + part]
            taken += part
            lane += part
    norm = jnp.sqrt(jnp.sum(jnp.sum(square, 0, keepdims=True), 1, keepdims=True))
    clip = clip_value / jnp.maximum(norm, clip_value)
    lanes_of = lax.broadcasted_iota(jnp.int32, (8, BS), 1)
    norm_ref[...] = jnp.where(lanes_of == 0, norm, clip)


def unpack_aux(gathered):
    whole = pl.BlockSpec(memory_space=pltpu.VMEM)
    return pl.pallas_call(
        unpack_kernel,
        out_shape=(
            jax.ShapeDtypeStruct((FLAT_ROWS, BS), jnp.float32),
            jax.ShapeDtypeStruct((8, BS), jnp.float32),
        ),
        in_specs=[whole],
        out_specs=(whole, whole),
        scratch_shapes=[pltpu.VMEM((BS, BS), jnp.float32)],
        compiler_params=pltpu.CompilerParams(vmem_limit_bytes=32 * MIB),
        cost_estimate=pl.CostEstimate(flops=0, bytes_accessed=7 * MIB, transcendentals=0),
        name="unpack_aux",
    )(gathered)


def greet_all(devices):
    me = lax.axis_index("dp") * MP + lax.axis_index("mp")
    barrier = pltpu.get_barrier_semaphore()

    def greet(k, carry):
        peer = lax.rem(me + k, devices)
        place = (peer // MP, lax.rem(peer, MP))
        pl.semaphore_signal(barrier, inc=1, device_id=place, device_id_type=MESH)
        return carry

    lax.fori_loop(1, devices, greet, 0)


def sum_over_all(devices, in_ref, out_ref, slots, send_sem, recv_sem):
    me = lax.axis_index("dp") * MP + lax.axis_index("mp")

    def copy(k, slot):
        peer = lax.rem(me + k, devices)
        place = (peer // MP, lax.rem(peer, MP))
        return remote(in_ref, slots.at[slot], send_sem.at[k], recv_sem.at[slot], place)

    slots[me] = in_ref[...]
    pl.semaphore_wait(pltpu.get_barrier_semaphore(), devices - 1)

    def push(k, carry):
        copy(k, me).start()
        return carry

    def pull(k, carry):
        copy(k, lax.rem(me + devices - k, devices)).wait_recv()
        return carry

    def settle(k, carry):
        copy(k, me).wait_send()
        return carry

    lax.fori_loop(1, devices, push, 0)
    lax.fori_loop(1, devices, pull, 0)
    total = slots[0]
    for i in range(1, devices):
        total = total + slots[i]
    out_ref[...] = total
    lax.fori_loop(1, devices, settle, 0)


def decoder_kernel(
    all_crops,
    devices,
    up_ref,
    deconv_bias_ref,
    conv_ref,
    conv_bias_ref,
    head_ref,
    head_bias_ref,
    labels_ref,
    batch_ref,
    conv_t_ref,
    head_t_ref,
    gu_ref,
    conv_grad_ref,
    head_grad_ref,
    small_ref,
    deconv_grad_ref,
    conv_in,
    grid_slope,
    conv_slope,
    features,
    chance,
    sums,
    conved,
    spread,
    total,
    slots,
    send_sem,
    recv_sem,
):
    greet_all(devices)
    decoder_forward_kernel(
        up_ref,
        deconv_bias_ref,
        conv_ref,
        conv_bias_ref,
        head_ref,
        head_bias_ref,
        labels_ref,
        batch_ref,
        conv_in,
        grid_slope,
        conv_slope,
        features,
        chance,
        sums,
        conved,
    )
    sum_over_all(devices, sums, total, slots, send_sem, recv_sem)
    decoder_backward_kernel(
        all_crops,
        total,
        batch_ref,
        labels_ref,
        chance,
        features,
        conv_slope,
        grid_slope,
        conv_in,
        conv_t_ref,
        head_t_ref,
        gu_ref,
        conv_grad_ref,
        head_grad_ref,
        small_ref,
        deconv_grad_ref,
        spread,
    )


def decoder(all_crops, *operands):
    devices = 4 * LAYERS * MP
    shapes = (
        jax.ShapeDtypeStruct((8 * DEC, NTOK), jnp.bfloat16),
        jax.ShapeDtypeStruct((27 * CF, DEC), jnp.float32),
        jax.ShapeDtypeStruct((CF, CF), jnp.float32),
        jax.ShapeDtypeStruct((CF, BS), jnp.float32),
        jax.ShapeDtypeStruct((DEC, BS), jnp.float32),
    )
    return pl.pallas_call(
        functools.partial(decoder_kernel, all_crops, devices),
        out_shape=shapes,
        in_specs=whole_specs(10),
        out_specs=tuple(whole_specs(5)),
        scratch_shapes=[
            pltpu.VMEM((DEC, CELLS), jnp.bfloat16),
            pltpu.VMEM((DEC, CELLS), jnp.float32),
            pltpu.VMEM((CF, CELLS), jnp.float32),
            pltpu.VMEM((CF, CELLS), jnp.bfloat16),
            pltpu.VMEM((CF, CELLS), jnp.float32),
            pltpu.VMEM((CF, BS), jnp.float32),
            pltpu.VMEM((CF, CELLS), jnp.float32),
            pltpu.VMEM((27 * CF, CELLS), jnp.bfloat16),
            pltpu.VMEM((CF, BS), jnp.float32),
            pltpu.VMEM((devices, CF, BS), jnp.float32),
            pltpu.SemaphoreType.DMA((devices,)),
            pltpu.SemaphoreType.DMA((devices,)),
        ],
        compiler_params=pltpu.CompilerParams(
            collective_id=3, has_side_effects=True, vmem_limit_bytes=40 * MIB
        ),
        cost_estimate=pl.CostEstimate(
            flops=6 * 27 * CF * DEC * CELLS, bytes_accessed=6 * MIB, transcendentals=DEC * CELLS
        ),
        name="decoder",
    )(*operands)


def layer_norm(values):
    center = values - jnp.mean(values, -1, keepdims=True)
    spread = jnp.mean(center * center, -1, keepdims=True)
    inverse = lax.rsqrt(spread + 1e-06)
    return center * inverse, inverse


def layer_norm_back(back, normal, inverse, gain):
    scaled = back * gain
    mean = jnp.mean(scaled, -1, keepdims=True)
    along = jnp.mean(scaled * normal, -1, keepdims=True)
    return inverse * (scaled - mean - normal * along)


def shampoo_kernel(per_step, clip_ref, g_ref, b_ref, s_ref, r_ref, m_ref, v_ref, nb_ref, ns_ref, nm_ref, nv_ref):
    def exact(a, b, dims):
        return lax.dot_general(
            a, b, (dims, ((), ())), precision=HIGHEST, preferred_element_type=jnp.float32
        )

    def mean_square(values):
        total = jnp.sum(jnp.sum(values * values, 0, keepdims=True), 1, keepdims=True)
        return total * (1.0 / (BS * BS))

    for i in range(per_step):
        grads = g_ref[i * BS : (i + 1) * BS] * clip_ref[0, 0]
        ns_ref[0, i] = beta_stat * s_ref[0, i] + (1 - beta_stat) * exact(grads, grads, ((1,), (1,)))
        ns_ref[1, i] = beta_stat * s_ref[1, i] + (1 - beta_stat) * exact(grads, grads, ((0,), (0,)))
        moment = beta_one * m_ref[i] + (1 - beta_one) * grads
        velocity = beta_two * v_ref[i] + (1 - beta_two) * grads * grads
        nm_ref[i] = moment
        nv_ref[i] = velocity
        hat = moment / (1 - beta_one**STEP)
        adam = hat / (jnp.sqrt(velocity / (1 - beta_two**STEP)) + 1e-08)
        left = exact(r_ref[0, i], hat, ((1,), (0,)))
        precond = exact(left, r_ref[1, i], ((1,), (0,)))
        ratio = jnp.sqrt((mean_square(adam) + 1e-06) / (mean_square(precond) + 1e-06))
        blocks = b_ref[i]
        nb_ref[i] = blocks - learn_rate * (precond * ratio + decay_rate * blocks)


def shampoo_step(clip, owned, blocks, stat_pair, root_pair, moment, velocity):
    number = blocks.shape[0]
    per_step = 3
    one = pl.BlockSpec((per_step, BS, BS), lambda i: (i, 0, 0))
    pair = pl.BlockSpec((2, per_step, BS, BS), lambda i: (0, i, 0, 0))
    single = jax.ShapeDtypeStruct((number, BS, BS), jnp.float32)
    return pl.pallas_call(
        functools.partial(shampoo_kernel, per_step),
        grid=(number // per_step,),
        out_shape=(single, jax.ShapeDtypeStruct((2, number, BS, BS), jnp.float32), single, single),
        in_specs=[
            pl.BlockSpec(memory_space=pltpu.SMEM),
            pl.BlockSpec((per_step * BS, BS), lambda i: (i, 0)),
            one,
            pair,
            pair,
            one,
            one,
        ],
        out_specs=(one, pair, one, one),
        compiler_params=pltpu.CompilerParams(vmem_limit_bytes=32 * MIB),
        cost_estimate=pl.CostEstimate(
            flops=number * 8 * BS**3 * 6, bytes_accessed=number * 12 * BS * BS * 4, transcendentals=0
        ),
        name="shampoo",
    )(clip.reshape(1, 1), owned, blocks, stat_pair, root_pair, moment, velocity)


def adam_step(param, grads, moment, veloc):
    moment_new = beta_one * moment + (1 - beta_one) * grads
    veloc_new = beta_two * veloc + (1 - beta_two) * grads * grads
    direction = (
        moment_new / (1 - beta_one**STEP) / (jnp.sqrt(veloc_new / (1 - beta_two**STEP)) + 1e-08)
    )
    return (param - learn_rate * direction, moment_new, veloc_new)


def halves(matrix):
    return matrix[:, :HALF], matrix[:, HALF:]


def local(
    patches,
    labels,
    batch_ids,
    blocks,
    statistics,
    roots,
    moments,
    velocity,
    aux,
    aux_moment,
    aux_velocity,
):
    part = lax.axis_index("mp")
    all_crops = lax.axis_size("dp") * MP
    pieces = split_aux(aux)
    gain, shift = pieces["norm_gain"], pieces["norm_bias"]

    gathered = gather_weights(blocks)
    other_embedding, w_embed = embed_other(patches, gathered)
    w_qkv, w_proj, w_up, w_down, w_deconv = unblock(gathered)

    def columns(array, which, width, start):
        return lax.dynamic_slice_in_dim(array, which * width + start, width - start, 1)

    down_start = 2 * FF // MP // 3

    other_rows = lax.dynamic_slice_in_dim(patches, (1 - part) * NTOK, NTOK, 0)
    own_rows = lax.dynamic_slice_in_dim(patches, part * NTOK, NTOK, 0)
    received = swap_mp(other_embedding)
    stream_zero = (
        dot_nn(own_rows, w_embed) + received + pieces["positions"] + pieces["embed_bias"]
    )
    normal_one, inverse_one = layer_norm(stream_zero)
    normed_one = (normal_one * gain[0] + shift[0]).astype(jnp.bfloat16)
    q_bias, v_bias = pieces["qv_bias"][0], pieces["qv_bias"][1]
    nothing = jnp.zeros((HALF,), jnp.float32)
    qkv_bias = jnp.concatenate(
        [q_bias[:HALF], nothing, v_bias[:HALF], q_bias[HALF:], nothing, v_bias[HALF:]]
    )
    qkv = (dot_nn(normed_one, w_qkv) + qkv_bias).astype(jnp.bfloat16)
    zero_stream = stream_zero.astype(jnp.bfloat16)
    zero_half = swap_mp(columns(zero_stream, 1 - part, HALF, 0))
    mixed, lse = attention_forward(qkv)
    mixed, zero_half = lax.optimization_barrier((mixed, zero_half))
    stream_one = stream_zero + dot_nn(mixed, w_proj) + pieces["proj_bias"]
    one_stream = stream_one.astype(jnp.bfloat16)
    one_half = swap_mp(columns(one_stream, 1 - part, HALF, 0))
    normal_two, inverse_two = layer_norm(stream_one)
    normed_two = (normal_two * gain[1] + shift[1]).astype(jnp.bfloat16)
    hidden = dot_nn(normed_two, w_up) + pieces["up_bias"]
    active_value, hidden_slope = gelu_and_slope(hidden)
    active = active_value.astype(jnp.bfloat16)
    active, one_half = lax.optimization_barrier((active, one_half))
    active_other = swap_mp(columns(active, 1 - part, FF // MP, down_start))
    stream_two = stream_one + dot_nn(active, w_down) + pieces["down_bias"]
    streams = [zero_stream, one_stream, stream_two.astype(jnp.bfloat16)]
    stacked = jnp.concatenate([halves(s)[m] for m in range(MP) for s in streams], 1)
    up_t = dot(w_deconv, stacked, ((0,), (1,)))

    conv_weight = pieces["conv_weight"].astype(jnp.bfloat16).reshape(27, DEC, CF)
    conv_low = conv_weight.transpose(0, 2, 1).reshape(27 * CF, DEC)
    conv_t = conv_weight.transpose(1, 0, 2).reshape(DEC, 27 * CF)
    head_weight = jnp.pad(pieces["head_weight"], ((0, 0), (0, CF - NCLS))).astype(jnp.bfloat16)
    head_bias = jnp.pad(pieces["head_bias"], (0, CF - NCLS)).reshape(CF, 1)
    grid_labels = arrange_labels(labels)
    batch = jnp.broadcast_to(batch_ids.reshape(1, 1), (1, BS))
    operands = (
        up_t,
        pieces["deconv_bias"].reshape(DEC, 1),
        conv_low,
        pieces["conv_bias"].reshape(CF, 1),
        head_weight.T,
        head_bias,
        grid_labels,
        batch,
    )
    if fast_mesh():
        gu_t, conv_grad, head_grad, small, deconv_bias_grad = decoder(
            all_crops, *operands, conv_t, head_weight
        )
    else:
        conv_in, grid_slope, conv_slope, features, chance, sums = decoder_forward(*operands)
        gu_t, conv_grad, head_grad, small, deconv_bias_grad = decoder_backward(
            all_crops,
            lax.psum(sums, ("dp", "mp")),
            batch,
            grid_labels,
            chance,
            features,
            conv_slope,
            grid_slope,
            conv_in,
            conv_t,
            head_weight,
        )
    gu_t, two_stream, active_other = lax.optimization_barrier((gu_t, streams[2], active_other))
    two_half = swap_mp(columns(two_stream, 1 - part, HALF, 0))
    loss_value = small[0, 2]

    gu_other = swap_mp(gu_t)
    stacked_back = dot(gu_t, w_deconv, ((0,), (1,)))
    back_zero_s, back_one_s, back_two = [
        jnp.concatenate([stacked_back[:, (3 * m + s) * HALF : (3 * m + s + 1) * HALF] for m in range(MP)], 1)
        for s in range(3)
    ]
    grad_down_bias = jnp.sum(back_two, 0)
    two_low = back_two.astype(jnp.bfloat16)
    two_other = swap_mp(two_low)
    back_hidden = (hidden_slope * dot_nt(two_low, w_down)).astype(jnp.bfloat16)
    grad_up_bias = jnp.sum(back_hidden.astype(jnp.float32), 0)
    back_normed_two = dot_nt(back_hidden, w_up)
    grad_gain_two = jnp.sum(back_normed_two * normal_two, 0)
    grad_shift_two = jnp.sum(back_normed_two, 0)
    back_one = (
        back_two + back_one_s + layer_norm_back(back_normed_two, normal_two, inverse_two, gain[1])
    )
    grad_proj_bias = jnp.sum(back_one, 0)
    one_low = back_one.astype(jnp.bfloat16)
    back_mixed = dot_nt(one_low, w_proj).astype(jnp.bfloat16)
    back_q, back_k, back_v = attention_backward(qkv, back_mixed, lse)
    back_qkv = jnp.concatenate(
        [halves(piece)[m] for m in range(MP) for piece in (back_q, back_k, back_v)], 1
    )
    grad_query_bias = jnp.sum(back_q.astype(jnp.float32), 0)
    grad_value_bias = jnp.sum(back_v.astype(jnp.float32), 0)
    back_normed_one = dot_nt(back_qkv, w_qkv)
    grad_gain_one = jnp.sum(back_normed_one * normal_one, 0)
    grad_shift_one = jnp.sum(back_normed_one, 0)
    back_normed_one, two_half, gu_other, two_other = lax.optimization_barrier(
        (back_normed_one, two_half, gu_other, two_other)
    )
    back_zero = (
        back_one + back_zero_s + layer_norm_back(back_normed_one, normal_one, inverse_one, gain[0])
    )
    zero_low = back_zero.astype(jnp.bfloat16)
    other_low = swap_mp(zero_low)

    fast = fast_mesh()
    depth = CHUNK if fast else BLOCK_ROWS
    stacked_own = jnp.concatenate([columns(stream, part, HALF, 0) for stream in streams], 1)
    stacked_other = jnp.concatenate([zero_half, one_half, two_half], 1)
    active_own = columns(active, part, FF // MP, down_start)
    final_grads = grad_blocks(
        [stacked_own, stacked_other], [gu_t, gu_other], 1, 9, 8, 3, 24, True, False, None, "grad_deconv", 4, BLOCK_ROWS, True
    )
    final_grads = grad_blocks(
        [active_own, active_other], [two_low, two_other], 1, 4, 6, 4, 0, True, False, final_grads, "grad_down_last", 4, BLOCK_ROWS
    )
    rest_grads = None
    for name, x, g, rows, per_row, step_rows, start, split_x, split_g, stride in (
        ("grad_down", active, two_low, 8, 6, 4, 144, True, False, 3),
        ("grad_up", normed_two, back_hidden, 6, 12, 3, 72, False, True, None),
        ("grad_proj", mixed, one_low, 3, 6, 3, 54, True, False, None),
        ("grad_qkv", normed_one, back_qkv, 6, 9, 3, 0, False, True, None),
    ):
        rest_grads = grad_blocks(
            [x], [g], MP, rows, per_row, step_rows, start, split_x, split_g, rest_grads, name, 8, depth,
            x_stride=stride,
        )
    first_grads = grad_blocks(
        [own_rows, other_rows], [zero_low, other_low], 1, 16, 6, 4, 0, False, False, None, "grad_embed", 4, BLOCK_ROWS
    )
    vectors = [
        grad_gain_one,
        grad_gain_two,
        grad_shift_one,
        grad_shift_two,
        grad_query_bias,
        grad_value_bias,
        grad_proj_bias,
        grad_down_bias,
    ]
    if fast:
        head_wide = jnp.pad(head_grad, ((0, 0), (0, BS - CF)))
        rest_grads = pack_aux(
            back_zero, vectors, grad_up_bias, conv_grad, head_wide, small, deconv_bias_grad, rest_grads
        )
        owned, squares = reduce_to_owners(
            rest_grads.reshape(MP, 2, 2, 2, CHUNK, BS),
            first_grads.reshape(2, 2, BLOCK_ROWS, BS),
            final_grads.reshape(2, 2, BLOCK_ROWS, BS),
        )
        gathered_aux = gather_all(
            jnp.concatenate([owned[BLOCK_ROWS:], squares]),
            ((0, AUX_ROWS), (AUX_ROWS, 8)),
            1,
            False,
            (0,),
            4,
            "gather_aux",
        )
        in_rows, norm_clip = unpack_aux(gathered_aux)
        aux_total = in_rows.reshape(-1)[:NAUX]
        grad_norm, clip_scale = norm_clip[0, 0], norm_clip[0, 1]
    else:
        owned = reduce_plain(rest_grads.reshape(MP, -1, BS, BS), first_grads, final_grads)
        owned = owned.reshape(-1, BS)
        positions_sum, small_sum = lax.psum(
            (
                back_zero,
                jnp.concatenate(
                    vectors[:7]
                    + [
                        grad_up_bias,
                        grad_down_bias,
                        deconv_bias_grad[:, 0],
                        conv_grad.reshape(27, CF, DEC).transpose(0, 2, 1).reshape(-1),
                        small[:, 1],
                        head_grad[:, :NCLS].reshape(-1),
                        small[:NCLS, 0],
                    ]
                ),
            ),
            ("dp", "mp"),
        )
        aux_total = jnp.concatenate(
            [positions_sum.reshape(-1), jnp.sum(positions_sum, 0), small_sum]
        )
        block_square = lax.psum(jnp.sum(owned * owned), ("dp", "mp"))
        grad_norm = jnp.sqrt(block_square + jnp.sum(aux_total * aux_total))
        clip_scale = clip_value / jnp.maximum(grad_norm, clip_value)
    block_new, stat_new, moment_new, veloc_new = shampoo_step(
        clip_scale,
        owned,
        blocks[0, 0],
        statistics[:, 0, 0],
        roots[:, 0, 0],
        moments[0, 0],
        velocity[0, 0],
    )
    aux_new, aux_moment_new, aux_veloc_new = adam_step(
        aux, aux_total * clip_scale, aux_moment, aux_velocity
    )
    return (
        loss_value,
        grad_norm,
        block_new[None, None],
        stat_new[:, None, None],
        moment_new[None, None],
        veloc_new[None, None],
        aux_new,
        aux_moment_new,
        aux_veloc_new,
    )


def solution(mesh):
    block_spec = P("dp", "mp", None, None, None)
    pair_spec = P(None, "dp", "mp", None, None, None)
    placed = (
        P("dp", "mp"),
        P(("dp", "mp"), None),
        P(("dp", "mp")),
        block_spec,
        pair_spec,
        pair_spec,
        block_spec,
        block_spec,
        P(),
        P(),
        P(),
    )
    return jax.shard_map(
        local,
        mesh=mesh,
        in_specs=placed,
        out_specs=(P(), P(), block_spec, pair_spec, block_spec, block_spec, P(), P(), P()),
        check_vma=False,
    )
```

```python
import functools
import math

import jax
import jax.numpy as jnp
from jax import lax
from jax.experimental import pallas as pl
from jax.experimental.pallas import tpu as pltpu
from jax.sharding import PartitionSpec as P

D = 768
HDIM = 64
FF = 3072
PV = 4096
DEC = 128
CF = 16
NCLS = 14
GS = 8
MB = 4
STEP = 10
BS = 128
NTOK = 512
CELLS = 4096
MP = 2
HALF = D // MP
E_BLOCKS = PV // MP * D // (BS * BS)

HIGHEST = lax.Precision.HIGHEST
MESH = pl.DeviceIdType.MESH
beta_one = 0.9
beta_two = 0.999
beta_stat = 0.95
learn_rate = 0.02
decay_rate = 0.01
clip_value = 0.005
MIB = 1024 * 1024

OFFSETS = [(a, b, c) for a in range(3) for b in range(3) for c in range(3)]
PARITIES = [(i, j, k) for i in range(2) for j in range(2) for k in range(2)]


def dot(a, b, dims):
    return lax.dot_general(a, b, (dims, ((), ())), preferred_element_type=jnp.float32)


def dot_nn(a, b):
    return dot(a, b, ((1,), (0,)))


def dot_nt(a, b):
    return dot(a, b, ((1,), (1,)))


def dot_tn(a, b):
    return dot(a, b, ((0,), (0,)))


def gelu_cdf(v):
    return 0.5 * (1.0 + lax.erf(v * (0.5**0.5)))


def gelu_and_slope(v):
    cdf = gelu_cdf(v)
    density = jnp.exp(-0.5 * v * v) * (1.0 / math.sqrt(2.0 * math.pi))
    return v * cdf, cdf + v * density


def aux_layout():
    return [
        ("positions", (NTOK, D)),
        ("embed_bias", (D,)),
        ("norm_gain", (2, D)),
        ("norm_bias", (2, D)),
        ("qv_bias", (2, D)),
        ("proj_bias", (D,)),
        ("up_bias", (FF,)),
        ("down_bias", (D,)),
        ("deconv_bias", (DEC,)),
        ("conv_weight", (27 * DEC, CF)),
        ("conv_bias", (CF,)),
        ("head_weight", (CF, NCLS)),
        ("head_bias", (NCLS,)),
    ]


NAUX = sum(math.prod(shape) for _, shape in aux_layout())


def split_aux(vector):
    pieces = {}
    offset = 0
    for section_name, section_shape in aux_layout():
        length = math.prod(section_shape)
        pieces[section_name] = vector[offset : offset + length].reshape(section_shape)
        offset += length
    return pieces


def attention_forward_kernel(qkv_q, qkv_k, qkv_v, mixed_ref, lse_ref):
    q, k, v = qkv_q[...], qkv_k[...], qkv_v[...]
    v_t = v.astype(jnp.float32).T.astype(jnp.bfloat16)
    outs = []
    for h in range(2):
        cols = slice(h * HDIM, (h + 1) * HDIM)
        scores = dot_nt(k[:, cols], q[:, cols]) * 0.125
        top = jnp.max(scores, 0, keepdims=True)
        weights = jnp.exp(scores - top)
        total = jnp.sum(weights, 0, keepdims=True)
        attention = (weights * (1.0 / total)).astype(jnp.bfloat16)
        outs.append(dot_nn(v_t[cols], attention))
        lse_ref[0, h : h + 1, :] = top + jnp.log(total)
    mixed_ref[...] = jnp.concatenate(outs, 0).T.astype(jnp.bfloat16)


def attention_backward_kernel(qkv_q, qkv_k, qkv_v, gm_ref, lse_ref, gq_ref, gk_ref, gv_ref):
    q, k, v, gm = qkv_q[...], qkv_k[...], qkv_v[...], gm_ref[...]
    k_t = k.astype(jnp.float32).T.astype(jnp.bfloat16)
    gq_t = []
    for h in range(2):
        cols = slice(h * HDIM, (h + 1) * HDIM)
        scores = dot_nt(k[:, cols], q[:, cols]) * 0.125
        attention = jnp.exp(scores - lse_ref[0, h : h + 1, :])
        back = dot_nt(v[:, cols], gm[:, cols])
        gv_ref[:, cols] = dot_nn(attention.astype(jnp.bfloat16), gm[:, cols]).astype(jnp.bfloat16)
        mean = jnp.sum(back * attention, 0, keepdims=True)
        gs = (attention * (back - mean)).astype(jnp.bfloat16)
        gk_ref[:, cols] = (dot_nn(gs, q[:, cols]) * 0.125).astype(jnp.bfloat16)
        gq_t.append(dot_nn(k_t[cols], gs) * 0.125)
    gq_ref[...] = jnp.concatenate(gq_t, 0).T.astype(jnp.bfloat16)


def qkv_spec(part):
    return pl.BlockSpec((NTOK, BS), lambda i, part=part: (0, (i // 3) * 9 + part * 3 + i % 3))


def attention_forward(qkv):
    return pl.pallas_call(
        attention_forward_kernel,
        grid=(6,),
        out_shape=(
            jax.ShapeDtypeStruct((NTOK, D), jnp.bfloat16),
            jax.ShapeDtypeStruct((6, 2, NTOK), jnp.float32),
        ),
        in_specs=[qkv_spec(0), qkv_spec(1), qkv_spec(2)],
        out_specs=(
            pl.BlockSpec((NTOK, BS), lambda i: (0, i)),
            pl.BlockSpec((1, 2, NTOK), lambda i: (i, 0, 0)),
        ),
        compiler_params=pltpu.CompilerParams(vmem_limit_bytes=32 * MIB),
        cost_estimate=pl.CostEstimate(
            flops=12 * 4 * NTOK * NTOK * HDIM,
            bytes_accessed=NTOK * D * 8,
            transcendentals=12 * NTOK * NTOK,
        ),
        name="attention_forward",
    )(qkv, qkv, qkv)


def attention_backward(qkv, gm, lse):
    pair = pl.BlockSpec((NTOK, BS), lambda i: (0, i))
    return pl.pallas_call(
        attention_backward_kernel,
        grid=(6,),
        out_shape=(jax.ShapeDtypeStruct((NTOK, D), jnp.bfloat16),) * 3,
        in_specs=[
            qkv_spec(0),
            qkv_spec(1),
            qkv_spec(2),
            pair,
            pl.BlockSpec((1, 2, NTOK), lambda i: (i, 0, 0)),
        ],
        out_specs=(pair,) * 3,
        compiler_params=pltpu.CompilerParams(vmem_limit_bytes=32 * MIB),
        cost_estimate=pl.CostEstimate(
            flops=12 * 10 * NTOK * NTOK * HDIM,
            bytes_accessed=NTOK * D * 14,
            transcendentals=12 * NTOK * NTOK,
        ),
        name="attention_backward",
    )(qkv, qkv, qkv, gm, lse)


def source_of(parity, step):
    at = parity + step
    if at < 0:
        return 1, -1
    if at > 1:
        return 0, 1
    return at, 0


def shift_plan(offset, parity, sign):
    found = [source_of(par, sign * (off - 1)) for off, par in zip(offset, parity)]
    bits = [f[0] for f in found]
    steps = [f[1] for f in found]
    return bits[0] * 4 + bits[1] * 2 + bits[2], steps


def token_masks(tokens):
    at = (tokens // (GS * GS), (tokens // GS) % GS, tokens % GS)
    masks = {}
    for axis in range(3):
        masks[axis, 1] = at[axis] < GS - 1
        masks[axis, -1] = at[axis] > 0
    return masks


def shifted(values, steps, masks):
    delta = steps[0] * GS * GS + steps[1] * GS + steps[2]
    if delta == 0 and not any(steps):
        return values
    moved = pltpu.roll(values, (-delta) % NTOK, 1)
    keep = None
    for axis in range(3):
        if steps[axis]:
            mask = masks[axis, steps[axis]]
            keep = mask if keep is None else keep & mask
    return jnp.where(keep, moved, 0.0)


def lanes(parity):
    return slice(parity * NTOK, (parity + 1) * NTOK)


def decoder_forward_kernel(
    up_ref,
    deconv_bias_ref,
    conv_ref,
    conv_bias_ref,
    head_ref,
    head_bias_ref,
    labels_ref,
    batch_ref,
    conv_in_ref,
    grid_slope_ref,
    conv_slope_ref,
    features_ref,
    chance_ref,
    sums_ref,
    conved_ref,
):
    tokens = lax.broadcasted_iota(jnp.int32, (CF, NTOK), 1)
    masks = token_masks(tokens)
    for parity in range(8):
        conved_ref[:, lanes(parity)] = jnp.broadcast_to(conv_bias_ref[...], (CF, NTOK))
    for parity in range(8):
        cell = up_ref[parity * DEC : (parity + 1) * DEC, :] + deconv_bias_ref[...]
        value, slope = gelu_and_slope(cell)
        low = value.astype(jnp.bfloat16)
        conv_in_ref[:, lanes(parity)] = low
        grid_slope_ref[:, lanes(parity)] = slope
        products = dot_nn(conv_ref[...], low)
        for at, offset in enumerate(OFFSETS):
            target, back_steps = shift_plan(offset, PARITIES[parity], -1)
            forward = [-s for s in back_steps]
            piece = shifted(products[at * CF : (at + 1) * CF, :], forward, masks)
            conved_ref[:, lanes(target)] += piece
    rows = lax.broadcasted_iota(jnp.int32, (CF, NTOK), 0)
    hit = jnp.zeros((CF, 1), jnp.float32)
    predicted = jnp.zeros((CF, 1), jnp.float32)
    truth = jnp.zeros((CF, 1), jnp.float32)
    entropy = jnp.zeros((CF, 1), jnp.float32)
    for parity in range(8):
        value, slope = gelu_and_slope(conved_ref[:, lanes(parity)])
        conv_slope_ref[:, lanes(parity)] = slope
        features = value.astype(jnp.bfloat16)
        features_ref[:, lanes(parity)] = features
        logits = dot_nn(head_ref[...], features) + head_bias_ref[...]
        logits = jnp.where(rows < NCLS, logits, -1e30)
        center = logits - jnp.max(logits, 0, keepdims=True)
        log_prob = center - jnp.log(jnp.sum(jnp.exp(center), 0, keepdims=True))
        chance = jnp.exp(log_prob)
        target = (rows == labels_ref[parity : parity + 1, :]).astype(jnp.float32)
        chance_ref[:, lanes(parity)] = chance
        hit += jnp.sum(chance * target, 1, keepdims=True)
        predicted += jnp.sum(chance, 1, keepdims=True)
        truth += jnp.sum(target, 1, keepdims=True)
        entropy -= jnp.sum(jnp.where(target > 0, log_prob, 0.0), 1, keepdims=True)
    lane = lax.broadcasted_iota(jnp.int32, (CF, BS), 1)
    base = batch_ref[...] * 3
    sums_ref[...] = (
        jnp.where(lane == base, hit, 0.0)
        + jnp.where(lane == base + 1, predicted, 0.0)
        + jnp.where(lane == base + 2, truth, 0.0)
        + jnp.where(lane == 3 * MB, entropy, 0.0)
    )


def decoder_backward_kernel(
    all_crops,
    sums_ref,
    batch_ref,
    labels_ref,
    chance_ref,
    features_ref,
    conv_slope_ref,
    grid_slope_ref,
    conv_in_ref,
    conv_t_ref,
    head_t_ref,
    gu_ref,
    conv_grad_ref,
    head_grad_ref,
    small_ref,
    deconv_grad_ref,
    spread_ref,
):
    sums = sums_ref[...]
    lane = lax.broadcasted_iota(jnp.int32, (CF, BS), 1)
    row = lax.broadcasted_iota(jnp.int32, (CF, BS), 0)
    live = (lane < 3 * MB) & (lane % 3 == 0) & (row < NCLS)
    under = pltpu.roll(sums, BS - 1, 1) + pltpu.roll(sums, BS - 2, 1) + 1.0
    under = jnp.where(live, under, 1.0)
    over = 2.0 * sums + 1.0
    dice = jnp.where(live, over / under, 0.0)
    mean_dice = jnp.sum(jnp.sum(dice, 1, keepdims=True), 0, keepdims=True) / (NCLS * MB)
    entropy_lane = jnp.where(lane == 3 * MB, sums, 0.0)
    entropy = jnp.sum(jnp.sum(entropy_lane, 1, keepdims=True), 0, keepdims=True)
    loss = entropy / (all_crops * CELLS) + (1.0 - mean_dice)
    own = live & (lane == batch_ref[...] * 3)
    d_hit = jnp.sum(jnp.where(own, -2.0 / (MB * NCLS) / under, 0.0), 1, keepdims=True)
    d_predicted = jnp.sum(
        jnp.where(own, (1.0 / (MB * NCLS)) * over / (under * under), 0.0), 1, keepdims=True
    )
    tokens = lax.broadcasted_iota(jnp.int32, (CF, NTOK), 1)
    masks = token_masks(tokens)
    rows = lax.broadcasted_iota(jnp.int32, (CF, NTOK), 0)
    head_bias = jnp.zeros((CF, 1), jnp.float32)
    conv_bias = jnp.zeros((CF, 1), jnp.float32)
    head_grad = jnp.zeros((CF, CF), jnp.float32)
    for parity in range(8):
        chance = chance_ref[:, lanes(parity)]
        target = (rows == labels_ref[parity : parity + 1, :]).astype(jnp.float32)
        back = (d_hit * target + d_predicted) * chance - target * (1.0 / (all_crops * CELLS))
        logits = back - chance * jnp.sum(back, 0, keepdims=True)
        head_bias += jnp.sum(logits, 1, keepdims=True)
        low = logits.astype(jnp.bfloat16)
        head_grad += dot_nt(features_ref[:, lanes(parity)], low)
        conved = conv_slope_ref[:, lanes(parity)] * dot_nn(head_t_ref[...], low)
        conv_bias += jnp.sum(conved, 1, keepdims=True)
        rounded = conved.astype(jnp.bfloat16).astype(jnp.float32)
        for at, offset in enumerate(OFFSETS):
            target_cell, steps = shift_plan(offset, PARITIES[parity], 1)
            piece = shifted(rounded, [-s for s in steps], masks)
            spread_ref[at * CF : (at + 1) * CF, lanes(target_cell)] = piece.astype(jnp.bfloat16)
    head_grad_ref[...] = head_grad
    small_ref[...] = (
        jnp.where(lane == 0, head_bias, 0.0)
        + jnp.where(lane == 1, conv_bias, 0.0)
        + jnp.where(lane == 2, loss, 0.0)
    )
    conv_grad = jnp.zeros((27 * CF, DEC), jnp.float32)
    deconv_grad = jnp.zeros((DEC, 1), jnp.float32)
    for parity in range(8):
        spread = spread_ref[:, lanes(parity)]
        conv_grad += dot_nt(spread, conv_in_ref[:, lanes(parity)])
        back = grid_slope_ref[:, lanes(parity)] * dot_nn(conv_t_ref[...], spread)
        deconv_grad += jnp.sum(back, 1, keepdims=True)
        gu_ref[parity * DEC : (parity + 1) * DEC, :] = back.astype(jnp.bfloat16)
    conv_grad_ref[...] = conv_grad
    deconv_grad_ref[...] = jnp.broadcast_to(deconv_grad, (DEC, BS))


def whole_specs(number):
    return [pl.BlockSpec(memory_space=pltpu.VMEM)] * number


def decoder_forward(up_t, deconv_bias, conv_low, conv_bias, head_low, head_bias, labels, batch):
    shapes = (
        jax.ShapeDtypeStruct((DEC, CELLS), jnp.bfloat16),
        jax.ShapeDtypeStruct((DEC, CELLS), jnp.float32),
        jax.ShapeDtypeStruct((CF, CELLS), jnp.float32),
        jax.ShapeDtypeStruct((CF, CELLS), jnp.bfloat16),
        jax.ShapeDtypeStruct((CF, CELLS), jnp.float32),
        jax.ShapeDtypeStruct((CF, BS), jnp.float32),
    )
    return pl.pallas_call(
        decoder_forward_kernel,
        out_shape=shapes,
        in_specs=whole_specs(8),
        out_specs=tuple(whole_specs(6)),
        scratch_shapes=[pltpu.VMEM((CF, CELLS), jnp.float32)],
        compiler_params=pltpu.CompilerParams(vmem_limit_bytes=40 * MIB),
        cost_estimate=pl.CostEstimate(
            flops=2 * 27 * CF * DEC * CELLS, bytes_accessed=6 * MIB, transcendentals=DEC * CELLS
        ),
        name="decoder_forward",
    )(up_t, deconv_bias, conv_low, conv_bias, head_low, head_bias, labels, batch)


def decoder_backward(
    all_crops, sums, batch, labels, chance, features, conv_slope, grid_slope, conv_in, conv_t, head_t
):
    shapes = (
        jax.ShapeDtypeStruct((8 * DEC, NTOK), jnp.bfloat16),
        jax.ShapeDtypeStruct((27 * CF, DEC), jnp.float32),
        jax.ShapeDtypeStruct((CF, CF), jnp.float32),
        jax.ShapeDtypeStruct((CF, BS), jnp.float32),
        jax.ShapeDtypeStruct((DEC, BS), jnp.float32),
    )
    return pl.pallas_call(
        functools.partial(decoder_backward_kernel, all_crops),
        out_shape=shapes,
        in_specs=whole_specs(10),
        out_specs=tuple(whole_specs(5)),
        scratch_shapes=[pltpu.VMEM((27 * CF, CELLS), jnp.bfloat16)],
        compiler_params=pltpu.CompilerParams(vmem_limit_bytes=40 * MIB),
        cost_estimate=pl.CostEstimate(
            flops=4 * 27 * CF * DEC * CELLS, bytes_accessed=6 * MIB, transcendentals=0
        ),
        name="decoder_backward",
    )(sums, batch, labels, chance, features, conv_slope, grid_slope, conv_in, conv_t, head_t)


LAYERS = 4
GATHER_LAG = 2
THIRDS = tuple((8 * BS * i, 8 * BS) for i in range(3))
PIECES = 32
BLOCK_ROWS = 24 * BS
AUX_ROWS = 256
CHUNK = BLOCK_ROWS + AUX_ROWS
ROWS_N = 2 * CHUNK // PIECES
ROWS_F = BLOCK_ROWS // PIECES
LAG = 1
HOP_LAG = 1
AHEAD = 3
CORE_SLOTS = 8
SEND_SLOTS = 4
KEEP = 8
SUM_SLOTS = 12


def remote(src, dst, send_sem, recv_sem, device):
    return pltpu.make_async_remote_copy(
        src_ref=src,
        dst_ref=dst,
        send_sem=send_sem,
        recv_sem=recv_sem,
        device_id=device,
        device_id_type=MESH,
    )


def places():
    dp, x = lax.axis_index("dp"), lax.axis_index("mp")
    z, y, c = dp // 4, (dp // 2) % 2, dp % 2
    return dict(
        dp=dp,
        x=x,
        y=y,
        z=z,
        c=c,
        at_core=(dp + 1 - 2 * c, x),
        at_x=(dp, 1 - x),
        at_y=(dp + 2 - 4 * y, x),
        above=(lax.rem(dp + 4, 4 * LAYERS), x),
        below=(lax.rem(dp + 4 * LAYERS - 4, 4 * LAYERS), x),
    )


def greet_neighbours(at):
    barrier = pltpu.get_barrier_semaphore()
    for name in ("at_core", "at_x", "at_y"):
        pl.semaphore_signal(barrier, inc=1, device_id=at[name], device_id_type=MESH)

    @pl.when(at["z"] < LAYERS - 1)
    def _():
        pl.semaphore_signal(barrier, inc=1, device_id=at["above"], device_id_type=MESH)

    @pl.when(at["z"] > 0)
    def _():
        pl.semaphore_signal(barrier, inc=1, device_id=at["below"], device_id_type=MESH)

    peers = 3 + jnp.minimum(at["z"], 1) + jnp.minimum(LAYERS - 1 - at["z"], 1)
    pl.semaphore_wait(barrier, peers)


def gather_kernel(parts, by_x, skip, middle, in_ref, out_ref, local_sem, up_sem, down_sem, z_recv, x_send, x_recv, y_send, y_recv, core_send, core_recv):
    at = places()
    x, y, z, c = at["x"], at["y"], at["z"], at["c"]
    last = LAYERS - 1

    def spot(l, y_at, c_at, x_at, p):
        return out_ref.at[x_at, l * 4 + y_at * 2 + c_at, pl.ds(*parts[p])]

    def send(ref, send_sem, recv_sem, device):
        return remote(ref, ref, send_sem, recv_sem, device)

    def up(l, p):
        return send(spot(l, y, c, x, p), up_sem.at[l, p], z_recv.at[l, p], at["above"])

    def down(l, p):
        return send(spot(l, y, c, x, p), down_sem.at[l, p], z_recv.at[l, p], at["below"])

    def x_direct(l, p, x_at):
        return send(spot(l, y, c, x_at, p), x_send.at[l, p, 0], x_recv.at[l, p, 0], at["at_x"])

    def y_direct(l, p, y_at):
        return send(spot(l, y_at, c, x, p), y_send.at[l, p, 0], y_recv.at[l, p, 0], at["at_y"])

    def diagonal(l, p, y_at, x_at):
        if p < by_x:
            return send(spot(l, y_at, c, x_at, p), y_send.at[l, p, 1], y_recv.at[l, p, 1], at["at_y"])
        return send(spot(l, y_at, c, x_at, p), x_send.at[l, p, 1], x_recv.at[l, p, 1], at["at_x"])

    def relayed(l, p):
        return diagonal(l, p, y, 1 - x) if p < by_x else diagonal(l, p, 1 - y, x)

    def core(l, p, kind, c_at):
        y_at, x_at = ((y, x), (1 - y, x), (y, 1 - x), (1 - y, 1 - x))[kind]
        return send(
            spot(l, y_at, c_at, x_at, p),
            core_send.at[l, p, kind],
            core_recv.at[l, p, kind],
            at["at_core"],
        )

    def wide(l):
        return (l > 0) if skip else (l >= 0)

    own = pltpu.make_async_copy(in_ref, out_ref.at[x, at["dp"]], local_sem)
    own.start()
    greet_neighbours(at)
    own.wait()

    def arrive(l, p, came_up, came_down):
        if not (came_up and came_down):
            up(l, p).wait_recv()
        if came_up:

            @pl.when(z < last)
            def _():
                up(l, p).start()

        if came_down:

            @pl.when(z > 0)
            def _():
                down(l, p).start()

        @pl.when(wide(l))
        def _():
            x_direct(l, p, x).start()

        y_direct(l, p, y).start()
        core(l, p, 0, c).start()

    def relay(l, p):
        y_direct(l, p, 1 - y).wait_recv()

        @pl.when(wide(l))
        def _():
            if p >= by_x:
                relayed(l, p).start()
            x_direct(l, p, 1 - x).wait_recv()
            if p < by_x:
                relayed(l, p).start()
            core(l, p, 2, c).start()

        core(l, p, 1, c).start()

    def finish(l, p):
        @pl.when(wide(l))
        def _():
            diagonal(l, p, 1 - y, 1 - x).wait_recv()
            core(l, p, 3, c).start()

    def held(l, p):
        return ((l > 0) & (l < last)) if p in middle else ((l >= 0) & (l <= last))

    number = len(parts)

    def both(tick, run):
        if tick < 0 or tick >= LAYERS * number:
            return
        r, p = tick // number, tick % number
        if r == 0:

            @pl.when(held(z, p))
            def _():
                run(z, p, True, True)

            return

        @pl.when(held(z - r, p))
        def _():
            run(z - r, p, True, False)

        @pl.when(held(z + r, p))
        def _():
            run(z + r, p, False, True)

    for tick in range(LAYERS * number + 2 * GATHER_LAG):
        both(tick, arrive)
        both(tick - GATHER_LAG, lambda l, p, up_way, down_way: relay(l, p))
        both(tick - 2 * GATHER_LAG, lambda l, p, up_way, down_way: finish(l, p))

    def settle_part(l, p):
        for kind in (0, 1):
            core(l, p, kind, 1 - c).wait_recv()
            core(l, p, kind, c).wait_send()
        y_direct(l, p, y).wait_send()

        @pl.when(wide(l))
        def _():
            for kind in (2, 3):
                core(l, p, kind, 1 - c).wait_recv()
                core(l, p, kind, c).wait_send()
            x_direct(l, p, x).wait_send()
            relayed(l, p).wait_send()

        @pl.when((l <= z) & (z < last))
        def _():
            up(l, p).wait_send()

        @pl.when((l >= z) & (z > 0))
        def _():
            down(l, p).wait_send()

    def settle(l, carry):
        for p in range(number):
            pl.when(held(l, p))(functools.partial(settle_part, l, p))
        return carry

    lax.fori_loop(0, LAYERS, settle, 0)


def gather_all(values, parts, by_x, skip, middle, collective_id, name):
    rows = values.shape[0]
    number = len(parts)

    def sems(*shape):
        return pltpu.SemaphoreType.DMA(shape)

    return pl.pallas_call(
        functools.partial(gather_kernel, parts, by_x, skip, middle),
        out_shape=jax.ShapeDtypeStruct((MP, 4 * LAYERS, rows, BS), values.dtype),
        in_specs=[pl.BlockSpec(memory_space=pl.ANY)],
        out_specs=pl.BlockSpec(memory_space=pl.ANY),
        scratch_shapes=[
            pltpu.SemaphoreType.DMA,
            sems(LAYERS, number),
            sems(LAYERS, number),
            sems(LAYERS, number),
            sems(LAYERS, number, 2),
            sems(LAYERS, number, 2),
            sems(LAYERS, number, 2),
            sems(LAYERS, number, 2),
            sems(LAYERS, number, 4),
            sems(LAYERS, number, 4),
        ],
        compiler_params=pltpu.CompilerParams(
            collective_id=collective_id, has_side_effects=True, vmem_limit_bytes=32 * MIB
        ),
        cost_estimate=pl.CostEstimate(flops=0, bytes_accessed=32 * rows * BS * 4, transcendentals=0),
        name=name,
    )(values)


def reduce_kernel(
    n_ref,
    e_ref,
    f_ref,
    out_ref,
    square_ref,
    own_n,
    own_f,
    core_n,
    core_f,
    keep_n,
    keep_f,
    xs_n,
    ys_n,
    ys_f,
    xr_n,
    yr_n,
    yr_f,
    sum_n,
    sum_f,
    up_n,
    down_n,
    up_f,
    down_e,
    own_sem,
    core_send,
    core_recv,
    credit,
    xs_sem,
    ys_n_sem,
    ys_f_sem,
    xr_sem,
    yr_n_sem,
    yr_f_sem,
    z_n_sem,
    z_f_sem,
    up_n_sem,
    down_n_sem,
    up_f_sem,
    down_e_sem,
):
    at = places()
    x, y, z, c = at["x"], at["y"], at["z"], at["c"]
    last = LAYERS - 1

    def layer_of(s):
        return 1 + lax.rem(s, 2)

    def rows_of(s):
        return pl.ds(pl.multiple_of((s // 2) * ROWS_N, 8), ROWS_N)

    def rows_f(s):
        return pl.ds(pl.multiple_of(s * ROWS_F, 8), ROWS_F)

    def own_loads(s):
        slot = lax.rem(s, 3)
        mine = n_ref.at[:, layer_of(s) - 1, :, c, rows_of(s)]
        return (
            pltpu.make_async_copy(mine, own_n.at[slot], own_sem.at[slot, 0]),
            pltpu.make_async_copy(e_ref.at[:, c, rows_f(s)], own_f.at[slot, 0], own_sem.at[slot, 1]),
            pltpu.make_async_copy(f_ref.at[:, c, rows_f(s)], own_f.at[slot, 1], own_sem.at[slot, 2]),
        )

    def core_copies(s):
        slot = lax.rem(s, CORE_SLOTS)
        sources = (
            n_ref.at[:, layer_of(s) - 1, :, 1 - c, rows_of(s)],
            e_ref.at[:, 1 - c, rows_f(s)],
            f_ref.at[:, 1 - c, rows_f(s)],
        )
        targets = (core_n.at[slot], core_f.at[slot, 0], core_f.at[slot, 1])
        return [
            remote(source, target, core_send.at[s, i], core_recv.at[slot, i], at["at_core"])
            for i, (source, target) in enumerate(zip(sources, targets))
        ]

    def x_copy(s):
        slot = lax.rem(s, SEND_SLOTS)
        return remote(xs_n.at[slot], xr_n.at[s], xs_sem.at[slot], xr_sem.at[s], at["at_x"])

    def y_copy_f(s):
        slot = lax.rem(s, SEND_SLOTS)
        return remote(ys_f.at[slot], yr_f.at[s], ys_f_sem.at[slot], yr_f_sem.at[s], at["at_y"])

    def y_copy(s):
        slot = lax.rem(s, SEND_SLOTS)
        return remote(ys_n.at[slot], yr_n.at[s], ys_n_sem.at[slot], yr_n_sem.at[s], at["at_y"])

    def up_copy(s):
        slot = lax.rem(s, SUM_SLOTS)
        return remote(sum_n.at[slot], up_n.at[s], z_n_sem.at[slot], up_n_sem.at[s], at["above"])

    def down_copy(s):
        slot = lax.rem(s, SUM_SLOTS)
        return remote(sum_n.at[slot], down_n.at[s], z_n_sem.at[slot], down_n_sem.at[s], at["below"])

    def down_copy_e(s):
        slot = lax.rem(s, SUM_SLOTS)
        source, sem = sum_f.at[slot, 0], z_f_sem.at[slot, 0]
        return remote(source, down_e.at[s], sem, down_e_sem.at[s], at["below"])

    def up_copy_f(s):
        slot = lax.rem(s, SUM_SLOTS)
        source, sem = sum_f.at[slot, 1], z_f_sem.at[slot, 1]
        return remote(source, up_f.at[s], sem, up_f_sem.at[s], at["above"])

    def add_squares(values):
        square_ref[...] += jnp.sum((values * values).reshape(-1, 8, BS), 0)

    square_ref[...] = jnp.zeros((8, BS), jnp.float32)
    for s in range(2):
        for copy in own_loads(s):
            copy.start()
    greet_neighbours(at)
    for s in range(AHEAD):
        for copy in core_copies(s):
            copy.start()

    def first(s):
        @pl.when(s + 2 < PIECES)
        def _():
            for copy in own_loads(s + 2):
                copy.start()

        @pl.when(s + AHEAD < PIECES)
        def _():
            @pl.when(s + AHEAD >= CORE_SLOTS)
            def _():
                pl.semaphore_wait(credit, 1)

            for copy in core_copies(s + AHEAD):
                copy.start()

        for copy in own_loads(s):
            copy.wait()
        for copy in core_copies(s):
            copy.wait_recv()

        @pl.when(s >= SEND_SLOTS)
        def _():
            x_copy(s - SEND_SLOTS).wait_send()
            y_copy_f(s - SEND_SLOTS).wait_send()

        own, core = lax.rem(s, 3), lax.rem(s, CORE_SLOTS)
        send, keep = lax.rem(s, SEND_SLOTS), lax.rem(s, KEEP)
        xs_n[send] = own_n[own, 1 - x] + core_n[core, 1 - x]
        x_copy(s).start()
        for kind in range(2):
            ys_f[send, kind] = own_f[own, kind, 1 - y] + core_f[core, kind, 1 - y]
        y_copy_f(s).start()
        keep_n[keep] = own_n[own, x] + core_n[core, x]
        for kind in range(2):
            keep_f[keep, kind] = own_f[own, kind, y] + core_f[core, kind, y]

        @pl.when(s + CORE_SLOTS < PIECES)
        def _():
            pl.semaphore_signal(credit, inc=1, device_id=at["at_core"], device_id_type=MESH)

    def second(s):
        x_copy(s).wait_recv()

        @pl.when(s >= SEND_SLOTS)
        def _():
            y_copy(s - SEND_SLOTS).wait_send()

        send, keep = lax.rem(s, SEND_SLOTS), lax.rem(s, KEEP)
        ys_n[send] = keep_n[keep, 1 - y] + xr_n[s, 1 - y]
        y_copy(s).start()
        keep_n[keep, y] = keep_n[keep, y] + xr_n[s, y]

    def third(s):
        y_copy_f(s).wait_recv()
        y_copy(s).wait_recv()

        @pl.when((s >= SUM_SLOTS) & (z != layer_of(s)))
        def _():
            up_copy(s - SUM_SLOTS).wait_send()

        @pl.when((s >= SUM_SLOTS) & (z > 0))
        def _():
            down_copy_e(s - SUM_SLOTS).wait_send()

        @pl.when((s >= SUM_SLOTS) & (z < last))
        def _():
            up_copy_f(s - SUM_SLOTS).wait_send()

        slot, keep = lax.rem(s, SUM_SLOTS), lax.rem(s, KEEP)
        sum_n[slot] = keep_n[keep, y] + yr_n[s]
        sum_f[slot] = keep_f[keep] + yr_f[s]

    def along(s, hop):
        slot = lax.rem(s, SUM_SLOTS)
        layer = layer_of(s)
        away = jnp.where(z < layer, z, jnp.where(z > layer, last - z, jnp.maximum(z, last - z)))

        @pl.when(away == hop)
        def _():
            @pl.when((z > 0) & (z <= layer))
            def _():
                up_copy(s).wait_recv()
                sum_n[slot] = sum_n[slot] + up_n[s]

            @pl.when((z < last) & (z >= layer))
            def _():
                down_copy(s).wait_recv()
                sum_n[slot] = sum_n[slot] + down_n[s]

            @pl.when(z < layer)
            def _():
                up_copy(s).start()

            @pl.when(z > layer)
            def _():
                down_copy(s).start()

            @pl.when(z == layer)
            def _():
                out_ref[rows_of(s)] = sum_n[slot]
                piece = s // 2
                whole, cut = BLOCK_ROWS // ROWS_N, BLOCK_ROWS % ROWS_N

                @pl.when(piece <= whole)
                def _():
                    add_squares(sum_n[slot, pl.ds(0, cut)])

                @pl.when(piece < whole)
                def _():
                    add_squares(sum_n[slot, pl.ds(cut, ROWS_N - cut)])

        @pl.when(jnp.where(z == 0, last, last - z) == hop)
        def _():
            @pl.when(z < last)
            def _():
                down_copy_e(s).wait_recv()
                sum_f[slot, 0] = sum_f[slot, 0] + down_e[s]

            @pl.when(z > 0)
            def _():
                down_copy_e(s).start()

            @pl.when(z == 0)
            def _():
                out_ref[rows_f(s)] = sum_f[slot, 0]
                add_squares(sum_f[slot, 0])

        @pl.when(z == hop)
        def _():
            @pl.when(z > 0)
            def _():
                up_copy_f(s).wait_recv()
                sum_f[slot, 1] = sum_f[slot, 1] + up_f[s]

            @pl.when(z < last)
            def _():
                up_copy_f(s).start()

            @pl.when(z == last)
            def _():
                out_ref[rows_f(s)] = sum_f[slot, 1]
                add_squares(sum_f[slot, 1])

    def guarded(run, s):
        @pl.when((s >= 0) & (s < PIECES))
        def _():
            run(s)

    def step(t, carry):
        guarded(first, t)
        guarded(second, t - LAG)
        guarded(third, t - 2 * LAG)
        for hop in range(LAYERS):
            guarded(functools.partial(along, hop=hop), t - 2 * LAG - hop * HOP_LAG)
        return carry

    lax.fori_loop(0, PIECES + 2 * LAG + (LAYERS - 1) * HOP_LAG, step, 0)

    def drain_sends(i, carry):
        s = PIECES - SEND_SLOTS + i
        for copy in (x_copy(s), y_copy_f(s), y_copy(s)):
            copy.wait_send()
        return carry

    lax.fori_loop(0, SEND_SLOTS, drain_sends, 0)

    def drain_sums(i, carry):
        s = PIECES - SUM_SLOTS + i

        @pl.when(z != layer_of(s))
        def _():
            up_copy(s).wait_send()

        @pl.when(z > 0)
        def _():
            down_copy_e(s).wait_send()

        @pl.when(z < last)
        def _():
            up_copy_f(s).wait_send()

        return carry

    lax.fori_loop(0, SUM_SLOTS, drain_sums, 0)

    def drain_core(s, carry):
        for copy in core_copies(s):
            copy.wait_send()
        return carry

    lax.fori_loop(0, PIECES, drain_core, 0)

    @pl.when((z == 0) | (z == last))
    def _():
        out_ref[pl.ds(BLOCK_ROWS, AUX_ROWS)] = jnp.zeros((AUX_ROWS, BS), jnp.float32)


def reduce_to_owners(rest, first, final):
    def room(*shape):
        return pltpu.VMEM(shape + (BS,), jnp.float32)

    def sems(*shape):
        return pltpu.SemaphoreType.DMA(shape)

    return pl.pallas_call(
        reduce_kernel,
        out_shape=(
            jax.ShapeDtypeStruct((CHUNK, BS), jnp.float32),
            jax.ShapeDtypeStruct((8, BS), jnp.float32),
        ),
        in_specs=[pl.BlockSpec(memory_space=pltpu.HBM)] * 3,
        out_specs=(pl.BlockSpec(memory_space=pltpu.VMEM),) * 2,
        scratch_shapes=[
            room(3, 2, 2, ROWS_N),
            room(3, 2, 2, ROWS_F),
            room(CORE_SLOTS, 2, 2, ROWS_N),
            room(CORE_SLOTS, 2, 2, ROWS_F),
            room(KEEP, 2, ROWS_N),
            room(KEEP, 2, ROWS_F),
            room(SEND_SLOTS, 2, ROWS_N),
            room(SEND_SLOTS, ROWS_N),
            room(SEND_SLOTS, 2, ROWS_F),
            room(PIECES, 2, ROWS_N),
            room(PIECES, ROWS_N),
            room(PIECES, 2, ROWS_F),
            room(SUM_SLOTS, ROWS_N),
            room(SUM_SLOTS, 2, ROWS_F),
            room(PIECES, ROWS_N),
            room(PIECES, ROWS_N),
            room(PIECES, ROWS_F),
            room(PIECES, ROWS_F),
            sems(3, 3),
            sems(PIECES, 3),
            sems(CORE_SLOTS, 3),
            pltpu.SemaphoreType.REGULAR,
            sems(SEND_SLOTS),
            sems(SEND_SLOTS),
            sems(SEND_SLOTS),
            sems(PIECES),
            sems(PIECES),
            sems(PIECES),
            sems(SUM_SLOTS),
            sems(SUM_SLOTS, 2),
            sems(PIECES),
            sems(PIECES),
            sems(PIECES),
            sems(PIECES),
        ],
        compiler_params=pltpu.CompilerParams(
            collective_id=1, has_side_effects=True, vmem_limit_bytes=58 * MIB
        ),
        cost_estimate=pl.CostEstimate(flops=0, bytes_accessed=100 * MIB, transcendentals=0),
        name="reduce_to_owners",
    )(rest, first, final)


MATRICES = [
    (96, 6, 9, 3, True),
    (150, 3, 6, 3, False),
    (168, 6, 12, 3, True),
    (240, 12, 6, 4, False),
    (312, 9, 8, 3, False),
]
LOADS = 4


def unblock_kernel(plan, kinds, blocks_ref, *refs):
    outs, tiles = refs[:kinds], refs[kinds : 2 * kinds]
    loaded, load_sem, store_sem = refs[2 * kinds :]

    def load(i):
        kind, m, first, rows, per_row, row, col = plan[i]
        number = rows * per_row
        return pltpu.make_async_copy(
            blocks_ref.at[m, pl.ds(first, number)],
            loaded.at[i % LOADS, pl.ds(0, number)],
            load_sem.at[i % LOADS],
        )

    def store(i, slot):
        kind, m, first, rows, per_row, row, col = plan[i]
        return pltpu.make_async_copy(
            tiles[kind].at[slot],
            outs[kind].at[pl.ds(row, rows * BS), pl.ds(col, per_row * BS)],
            store_sem.at[kind, slot],
        )

    history = [[] for _ in range(kinds)]
    for i in range(min(LOADS - 1, len(plan))):
        load(i).start()
    for i, (kind, m, first, rows, per_row, row, col) in enumerate(plan):
        if i + LOADS - 1 < len(plan):
            load(i + LOADS - 1).start()
        load(i).wait()
        slot = len(history[kind]) % 2
        if len(history[kind]) >= 2:
            store(*history[kind][-2]).wait()
        for r in range(rows):
            for c in range(per_row):
                tiles[kind][slot, r * BS : (r + 1) * BS, c * BS : (c + 1) * BS] = loaded[
                    i % LOADS, r * per_row + c
                ]
        history[kind].append((i, slot))
        store(i, slot).start()
    for done in history:
        for entry in done[-2:]:
            store(*entry).wait()


def unblock(gathered):
    plan, shapes, tiles = [], [], []
    for kind, (first, rows, per_row, step, beside) in enumerate(MATRICES):
        tall, wide = rows * BS, per_row * BS
        shapes.append((tall, MP * wide) if beside else (MP * tall, wide))
        tiles.append((step * BS, wide))
        for m in range(MP):
            for at in range(0, rows, step):
                row = at * BS + (0 if beside else m * tall)
                plan.append((kind, m, first + at * per_row, step, per_row, row, m * wide if beside else 0))
    anywhere = pl.BlockSpec(memory_space=pl.ANY)
    largest = max(entry[3] * entry[4] for entry in plan)
    return pl.pallas_call(
        functools.partial(unblock_kernel, plan, len(shapes)),
        out_shape=tuple(jax.ShapeDtypeStruct(shape, jnp.bfloat16) for shape in shapes),
        in_specs=[anywhere],
        out_specs=tuple([anywhere] * len(shapes)),
        scratch_shapes=[pltpu.VMEM((2,) + tile, jnp.bfloat16) for tile in tiles]
        + [
            pltpu.VMEM((LOADS, largest, BS, BS), jnp.bfloat16),
            pltpu.SemaphoreType.DMA((LOADS,)),
            pltpu.SemaphoreType.DMA((len(shapes), 2)),
        ],
        compiler_params=pltpu.CompilerParams(vmem_limit_bytes=60 * MIB),
        cost_estimate=pl.CostEstimate(
            flops=0, bytes_accessed=38 * MIB, transcendentals=0
        ),
        name="unblock",
    )(gathered)


def embed_kernel(which_ref, rows_ref, blocks_ref, out_ref, matrix_ref):
    step = pl.program_id(0)
    for r in range(4):
        for c in range(6):
            matrix_ref[r * BS : (r + 1) * BS, c * BS : (c + 1) * BS] = blocks_ref[0, r * 6 + c]
    product = dot_nn(rows_ref[...], matrix_ref[...])

    @pl.when(step == 0)
    def _():
        out_ref[...] = product

    @pl.when(step > 0)
    def _():
        out_ref[...] += product


def embed_other(patches, gathered):
    part = lax.axis_index("mp")
    tall = 4 * BS
    return pl.pallas_call(
        embed_kernel,
        grid_spec=pltpu.PrefetchScalarGridSpec(
            num_scalar_prefetch=1,
            grid=(PV // MP // tall,),
            in_specs=[
                pl.BlockSpec((NTOK, tall), lambda k, which: (which[0], k)),
                pl.BlockSpec((1, 24, BS, BS), lambda k, which: (which[1], k, 0, 0)),
            ],
            out_specs=(
                pl.BlockSpec((NTOK, D), lambda k, which: (0, 0)),
                pl.BlockSpec((tall, D), lambda k, which: (k, 0)),
            ),
        ),
        out_shape=(
            jax.ShapeDtypeStruct((NTOK, D), jnp.float32),
            jax.ShapeDtypeStruct((PV // MP, D), jnp.bfloat16),
        ),
        compiler_params=pltpu.CompilerParams(vmem_limit_bytes=56 * MIB),
        cost_estimate=pl.CostEstimate(
            flops=2 * NTOK * D * PV // MP, bytes_accessed=10 * MIB, transcendentals=0
        ),
        name="embed_other",
    )(jnp.stack([1 - part, part]).astype(jnp.int32), patches, gathered)


def labels_kernel(labels_ref, out_ref):
    side = 2 * GS
    plane = side * side
    rows = jnp.concatenate([labels_ref[:, z * plane : (z + 1) * plane] for z in range(side)], 0)
    cell = lax.broadcasted_iota(jnp.int32, (plane, plane), 0)
    place = lax.broadcasted_iota(jnp.int32, (plane, plane), 1)
    parity, patch = place // (GS * GS), place % (GS * GS)
    match = (cell // side == 2 * (patch // GS) + parity // 2) & (
        cell % side == 2 * (patch % GS) + parity % 2
    )
    low = rows.astype(jnp.float32).astype(jnp.bfloat16)
    moved = dot_nn(low, match.astype(jnp.float32).astype(jnp.bfloat16)).astype(jnp.int32)
    width = GS * GS
    for i in range(2):
        for inner in range(4):
            for a in range(GS):
                out_ref[i * 4 + inner : i * 4 + inner + 1, a * width : (a + 1) * width] = moved[
                    2 * a + i : 2 * a + i + 1, inner * width : (inner + 1) * width
                ]


def arrange_labels(labels):
    return pl.pallas_call(
        labels_kernel,
        out_shape=jax.ShapeDtypeStruct((8, NTOK), jnp.int32),
        in_specs=whole_specs(1),
        out_specs=whole_specs(1)[0],
        cost_estimate=pl.CostEstimate(flops=2 * 16 * 256 * 256, bytes_accessed=65536, transcendentals=0),
        name="arrange_labels",
    )(labels)


def blocks_kernel(first_block, per_row, step_rows, transposed, pairs, *refs):
    out_ref, tiles, sems = refs[-3:]
    m, i = pl.program_id(0), pl.program_id(1)
    steps = pl.num_programs(1)
    at = m * steps + i
    slot = lax.rem(at, 2)
    total = pl.num_programs(0) * steps

    def drain(which):
        pltpu.make_async_copy(tiles.at[which], tiles.at[which], sems.at[which]).wait()

    @pl.when(at >= 2)
    def _():
        drain(slot)

    total_product = None
    for pair in range(pairs):
        x_ref, g_ref = refs[2 * pair], refs[2 * pair + 1]
        term = dot(x_ref[...], g_ref[...], ((0,), (1,) if transposed else (0,)))
        total_product = term if total_product is None else total_product + term
    tiles[slot] = total_product
    for r in range(step_rows):
        for c in range(per_row):
            block = first_block + (i * step_rows + r) * per_row + c
            chunk, at_row = block // 24, lax.rem(block, 24) * BS
            pltpu.make_async_copy(
                tiles.at[slot, r * BS : (r + 1) * BS, c * BS : (c + 1) * BS],
                out_ref.at[m, chunk, pl.ds(pl.multiple_of(at_row, BS), BS)],
                sems.at[slot],
            ).start()

    @pl.when(at == total - 1)
    def _():
        drain(slot)

        @pl.when(total > 1)
        def _():
            drain(1 - slot)


def grad_blocks(xs, gs, parts, rows, per_row, step_rows, first_block, split_x, split_g, buffer, name, chunks, depth, transposed=False, x_stride=None):
    steps = rows // step_rows
    x_stride = x_stride or steps
    tokens = xs[0].shape[0]
    width = per_row * BS
    x_spec = pl.BlockSpec(
        (tokens, step_rows * BS), (lambda m, i: (0, m * x_stride + i)) if split_x else (lambda m, i: (0, i))
    )
    if transposed:
        g_spec = pl.BlockSpec((width, tokens), lambda m, i: (0, 0))
    else:
        g_spec = pl.BlockSpec((tokens, width), (lambda m, i: (0, m)) if split_g else (lambda m, i: (0, 0)))
    anywhere = pl.BlockSpec(memory_space=pltpu.HBM)
    operands = [array for pair in zip(xs, gs) for array in pair] + ([] if buffer is None else [buffer])
    return pl.pallas_call(
        functools.partial(
            blocks_kernel, first_block, per_row, step_rows, transposed, len(xs)
        ),
        grid=(parts, steps),
        out_shape=jax.ShapeDtypeStruct((parts, chunks, depth, BS), jnp.float32),
        in_specs=[x_spec, g_spec] * len(xs) + ([] if buffer is None else [anywhere]),
        out_specs=anywhere,
        input_output_aliases={} if buffer is None else {2 * len(xs): 0},
        scratch_shapes=[
            pltpu.VMEM((2, step_rows * BS, width), jnp.float32),
            pltpu.SemaphoreType.DMA((2,)),
        ],
        compiler_params=pltpu.CompilerParams(vmem_limit_bytes=32 * MIB),
        cost_estimate=pl.CostEstimate(
            flops=2 * len(xs) * tokens * parts * rows * BS * width,
            bytes_accessed=parts * rows * BS * width * 4,
            transcendentals=0,
        ),
        name=name,
    )(*operands)


def fast_mesh():
    return lax.axis_size("dp") == 4 * LAYERS and lax.axis_size("mp") == MP


def gather_weights(blocks):
    low = blocks.astype(jnp.bfloat16)[0, 0]
    if fast_mesh():
        gathered = gather_all(low.reshape(-1, BS), THIRDS, 1, True, (), 2, "gather_weights")
    else:
        gathered = lax.all_gather(low, ("dp", "mp"), axis=0, tiled=False)
        gathered = gathered.reshape((-1, MP) + low.shape).swapaxes(0, 1)
    return gathered.reshape(MP, -1, BS, BS)


def swap_mp(values):
    return lax.ppermute(values, "mp", [(0, 1), (1, 0)])


def reduce_plain(rest, first, final):
    part = lax.axis_index("mp")
    own = (jnp.arange(MP) == part).astype(jnp.float32)
    ends = [piece.reshape(1, -1, BS, BS) * own[:, None, None, None] for piece in (first, final)]
    dp = lax.axis_size("dp")
    every = jnp.concatenate([ends[0], rest, ends[1]], 1)
    every = every.reshape(MP, dp, -1, BS, BS).transpose(1, 0, 2, 3, 4)
    return lax.psum_scatter(
        every.reshape(dp * MP, -1, BS, BS), ("dp", "mp"), scatter_dimension=0, tiled=True
    )[0]


TALL = NTOK + 16
TILES = D // BS
CONV_AT = TILES * TALL
HEAD_AT = CONV_AT + 27 * CF
SMALL_AT = HEAD_AT + CF
DECONV_AT = SMALL_AT + CF
PACKED = DECONV_AT + DEC
AUX_ROOM = 8 * MP * AUX_ROWS
FLAT_ROWS = -(-NAUX // (8 * BS)) * 8


def pack_kernel(zero_ref, *refs):
    vectors, up_ref, conv_ref, head_ref, small_ref, deconv_ref = refs[:8], *refs[8:13]
    out_ref, rows_ref, sems = refs[14:]
    for j in range(TILES):
        lanes_at = slice(j * BS, (j + 1) * BS)
        base = j * TALL
        rows_ref[base : base + NTOK] = zero_ref[:, lanes_at]
        small_rows = [vector[:, lanes_at] for vector in vectors]
        small_rows += [up_ref[:, i * D + j * BS : i * D + (j + 1) * BS] for i in range(FF // D)]
        small_rows += [jnp.zeros((16 - len(small_rows), BS), jnp.float32)]
        rows_ref[base + NTOK : base + TALL] = jnp.concatenate(small_rows, 0)
    lane = lax.broadcasted_iota(jnp.int32, (CF, BS), 1)
    wide_lane = lax.broadcasted_iota(jnp.int32, (DEC, BS), 1)
    rows_ref[CONV_AT:HEAD_AT] = conv_ref[...]
    rows_ref[HEAD_AT:SMALL_AT] = head_ref[...]
    rows_ref[SMALL_AT:DECONV_AT] = jnp.where(lane < 2, small_ref[...], 0.0)
    rows_ref[DECONV_AT:PACKED] = jnp.where(wide_lane < 1, deconv_ref[...], 0.0)
    rows_ref[PACKED:AUX_ROOM] = jnp.zeros((AUX_ROOM - PACKED, BS), jnp.float32)
    copies = [
        pltpu.make_async_copy(
            rows_ref.at[pl.ds((m * 8 + chunk) * AUX_ROWS, AUX_ROWS)],
            out_ref.at[m, chunk, pl.ds(BLOCK_ROWS, AUX_ROWS)],
            sems.at[m * 8 + chunk],
        )
        for m in range(MP)
        for chunk in range(8)
    ]
    for copy in copies:
        copy.start()
    for copy in copies:
        copy.wait()


def pack_aux(zero, vectors, up_bias, conv, head, small, deconv, buffer):
    whole = pl.BlockSpec(memory_space=pltpu.VMEM)
    anywhere = pl.BlockSpec(memory_space=pl.ANY)
    operands = [zero] + [vector.reshape(1, D) for vector in vectors]
    operands += [up_bias.reshape(1, FF), conv, head, small, deconv]
    return pl.pallas_call(
        pack_kernel,
        out_shape=jax.ShapeDtypeStruct(buffer.shape, jnp.float32),
        in_specs=[whole] * len(operands) + [anywhere],
        out_specs=anywhere,
        input_output_aliases={len(operands): 0},
        scratch_shapes=[
            pltpu.VMEM((AUX_ROOM, BS), jnp.float32),
            pltpu.SemaphoreType.DMA((8 * MP,)),
        ],
        compiler_params=pltpu.CompilerParams(vmem_limit_bytes=32 * MIB),
        cost_estimate=pl.CostEstimate(flops=0, bytes_accessed=4 * MIB, transcendentals=0),
        name="pack_aux",
    )(*operands, buffer)


def unpack_kernel(sums_ref, rows_ref, norm_ref, turned):
    def pieces(start, stop):
        at = start
        while at < stop:
            m, chunk = at // (8 * AUX_ROWS), at // AUX_ROWS % 8
            end = min(stop, (at // AUX_ROWS + 1) * AUX_ROWS)
            first = at % AUX_ROWS
            yield at - start, sums_ref[m, 4 + chunk, first : first + end - at]
            at = end

    def packed(start, stop):
        found = [piece for _, piece in pieces(start, stop)]
        return found[0] if len(found) == 1 else jnp.concatenate(found, 0)

    square = jnp.zeros((8, BS), jnp.float32)
    for m in range(MP):
        for owner in range(4 * LAYERS):
            square += sums_ref[m, owner, AUX_ROWS:]
    rows_ref[FLAT_ROWS - 16 :] = jnp.zeros((16, BS), jnp.float32)
    after = NTOK * TILES
    for j in range(TILES):
        token_sum = jnp.zeros((1, BS), jnp.float32)
        for offset, piece in pieces(j * TALL, j * TALL + NTOK):
            rows_ref[pl.ds(offset * TILES + j, piece.shape[0], stride=TILES)] = piece
            token_sum += jnp.sum(piece, 0, keepdims=True)
            square += jnp.sum((piece * piece).reshape(-1, 8, BS), 0)
        vectors = packed(j * TALL + NTOK, (j + 1) * TALL)
        square += jnp.sum((vectors * vectors).reshape(-1, 8, BS), 0)
        square += jnp.concatenate([token_sum * token_sum, jnp.zeros((7, BS), jnp.float32)], 0)
        rows_ref[after + j : after + j + 1] = token_sum
        order = list(range(7)) + list(range(8, 8 + FF // D)) + [7]
        for place, which in enumerate(order):
            at = after + TILES * (1 + place) + j
            rows_ref[at : at + 1] = vectors[which : which + 1]
    at = after + TILES * 13
    deconv = packed(DECONV_AT, PACKED)
    square += jnp.sum((deconv * deconv).reshape(-1, 8, BS), 0)
    rows_ref[at : at + 1] = deconv.T[0:1]
    at += 1
    for o in range(27):
        conv = packed(CONV_AT + o * CF, CONV_AT + (o + 1) * CF)
        square += jnp.sum((conv * conv).reshape(-1, 8, BS), 0)
        turned[:, 0:CF] = conv.T
        for f in range(8):
            rows_ref[at + o * CF : at + (o + 1) * CF, f * CF : (f + 1) * CF] = turned[
                pl.ds(f, CF, stride=8), 0:CF
            ]
    at += 27 * CF
    head = packed(HEAD_AT, SMALL_AT)
    small = packed(SMALL_AT, DECONV_AT)
    square += jnp.sum((head * head + small * small).reshape(-1, 8, BS), 0)
    turned_small = small.T
    segments = [(turned_small[1:2], CF)]
    segments += [(head[row : row + 1], NCLS) for row in range(CF)]
    segments += [(turned_small[0:1], NCLS)]
    lane = 0
    for values, length in segments:
        taken = 0
        while taken < length:
            row, col = lane // BS, lane % BS
            part = min(length - taken, BS - col)
            rows_ref[at + row : at + row + 1, col : col + part] = values[:, taken : taken + part]
            taken += part
            lane += part
    norm = jnp.sqrt(jnp.sum(jnp.sum(square, 0, keepdims=True), 1, keepdims=True))
    clip = clip_value / jnp.maximum(norm, clip_value)
    lanes_of = lax.broadcasted_iota(jnp.int32, (8, BS), 1)
    norm_ref[...] = jnp.where(lanes_of == 0, norm, clip)


def unpack_aux(gathered):
    whole = pl.BlockSpec(memory_space=pltpu.VMEM)
    return pl.pallas_call(
        unpack_kernel,
        out_shape=(
            jax.ShapeDtypeStruct((FLAT_ROWS, BS), jnp.float32),
            jax.ShapeDtypeStruct((8, BS), jnp.float32),
        ),
        in_specs=[whole],
        out_specs=(whole, whole),
        scratch_shapes=[pltpu.VMEM((BS, BS), jnp.float32)],
        compiler_params=pltpu.CompilerParams(vmem_limit_bytes=32 * MIB),
        cost_estimate=pl.CostEstimate(flops=0, bytes_accessed=7 * MIB, transcendentals=0),
        name="unpack_aux",
    )(gathered)


def greet_all(devices):
    me = lax.axis_index("dp") * MP + lax.axis_index("mp")
    barrier = pltpu.get_barrier_semaphore()

    def greet(k, carry):
        peer = lax.rem(me + k, devices)
        place = (peer // MP, lax.rem(peer, MP))
        pl.semaphore_signal(barrier, inc=1, device_id=place, device_id_type=MESH)
        return carry

    lax.fori_loop(1, devices, greet, 0)


def sum_over_all(devices, in_ref, out_ref, slots, send_sem, recv_sem):
    me = lax.axis_index("dp") * MP + lax.axis_index("mp")

    def copy(k, slot):
        peer = lax.rem(me + k, devices)
        place = (peer // MP, lax.rem(peer, MP))
        return remote(in_ref, slots.at[slot], send_sem.at[k], recv_sem.at[slot], place)

    slots[me] = in_ref[...]
    pl.semaphore_wait(pltpu.get_barrier_semaphore(), devices - 1)

    def push(k, carry):
        copy(k, me).start()
        return carry

    def pull(k, carry):
        copy(k, lax.rem(me + devices - k, devices)).wait_recv()
        return carry

    def settle(k, carry):
        copy(k, me).wait_send()
        return carry

    lax.fori_loop(1, devices, push, 0)
    lax.fori_loop(1, devices, pull, 0)
    total = slots[0]
    for i in range(1, devices):
        total = total + slots[i]
    out_ref[...] = total
    lax.fori_loop(1, devices, settle, 0)


def decoder_kernel(
    all_crops,
    devices,
    up_ref,
    deconv_bias_ref,
    conv_ref,
    conv_bias_ref,
    head_ref,
    head_bias_ref,
    labels_ref,
    batch_ref,
    conv_t_ref,
    head_t_ref,
    gu_ref,
    conv_grad_ref,
    head_grad_ref,
    small_ref,
    deconv_grad_ref,
    conv_in,
    grid_slope,
    conv_slope,
    features,
    chance,
    sums,
    conved,
    spread,
    total,
    slots,
    send_sem,
    recv_sem,
):
    greet_all(devices)
    decoder_forward_kernel(
        up_ref,
        deconv_bias_ref,
        conv_ref,
        conv_bias_ref,
        head_ref,
        head_bias_ref,
        labels_ref,
        batch_ref,
        conv_in,
        grid_slope,
        conv_slope,
        features,
        chance,
        sums,
        conved,
    )
    sum_over_all(devices, sums, total, slots, send_sem, recv_sem)
    decoder_backward_kernel(
        all_crops,
        total,
        batch_ref,
        labels_ref,
        chance,
        features,
        conv_slope,
        grid_slope,
        conv_in,
        conv_t_ref,
        head_t_ref,
        gu_ref,
        conv_grad_ref,
        head_grad_ref,
        small_ref,
        deconv_grad_ref,
        spread,
    )


def decoder(all_crops, *operands):
    devices = 4 * LAYERS * MP
    shapes = (
        jax.ShapeDtypeStruct((8 * DEC, NTOK), jnp.bfloat16),
        jax.ShapeDtypeStruct((27 * CF, DEC), jnp.float32),
        jax.ShapeDtypeStruct((CF, CF), jnp.float32),
        jax.ShapeDtypeStruct((CF, BS), jnp.float32),
        jax.ShapeDtypeStruct((DEC, BS), jnp.float32),
    )
    return pl.pallas_call(
        functools.partial(decoder_kernel, all_crops, devices),
        out_shape=shapes,
        in_specs=whole_specs(10),
        out_specs=tuple(whole_specs(5)),
        scratch_shapes=[
            pltpu.VMEM((DEC, CELLS), jnp.bfloat16),
            pltpu.VMEM((DEC, CELLS), jnp.float32),
            pltpu.VMEM((CF, CELLS), jnp.float32),
            pltpu.VMEM((CF, CELLS), jnp.bfloat16),
            pltpu.VMEM((CF, CELLS), jnp.float32),
            pltpu.VMEM((CF, BS), jnp.float32),
            pltpu.VMEM((CF, CELLS), jnp.float32),
            pltpu.VMEM((27 * CF, CELLS), jnp.bfloat16),
            pltpu.VMEM((CF, BS), jnp.float32),
            pltpu.VMEM((devices, CF, BS), jnp.float32),
            pltpu.SemaphoreType.DMA((devices,)),
            pltpu.SemaphoreType.DMA((devices,)),
        ],
        compiler_params=pltpu.CompilerParams(
            collective_id=3, has_side_effects=True, vmem_limit_bytes=40 * MIB
        ),
        cost_estimate=pl.CostEstimate(
            flops=6 * 27 * CF * DEC * CELLS, bytes_accessed=6 * MIB, transcendentals=DEC * CELLS
        ),
        name="decoder",
    )(*operands)


def layer_norm(values):
    center = values - jnp.mean(values, -1, keepdims=True)
    spread = jnp.mean(center * center, -1, keepdims=True)
    inverse = lax.rsqrt(spread + 1e-06)
    return center * inverse, inverse


def layer_norm_back(back, normal, inverse, gain):
    scaled = back * gain
    mean = jnp.mean(scaled, -1, keepdims=True)
    along = jnp.mean(scaled * normal, -1, keepdims=True)
    return inverse * (scaled - mean - normal * along)


def shampoo_kernel(per_step, clip_ref, g_ref, b_ref, s_ref, r_ref, m_ref, v_ref, nb_ref, ns_ref, nm_ref, nv_ref):
    def exact(a, b, dims):
        return lax.dot_general(
            a, b, (dims, ((), ())), precision=HIGHEST, preferred_element_type=jnp.float32
        )

    def mean_square(values):
        total = jnp.sum(jnp.sum(values * values, 0, keepdims=True), 1, keepdims=True)
        return total * (1.0 / (BS * BS))

    for i in range(per_step):
        grads = g_ref[i * BS : (i + 1) * BS] * clip_ref[0, 0]
        ns_ref[0, i] = beta_stat * s_ref[0, i] + (1 - beta_stat) * exact(grads, grads, ((1,), (1,)))
        ns_ref[1, i] = beta_stat * s_ref[1, i] + (1 - beta_stat) * exact(grads, grads, ((0,), (0,)))
        moment = beta_one * m_ref[i] + (1 - beta_one) * grads
        velocity = beta_two * v_ref[i] + (1 - beta_two) * grads * grads
        nm_ref[i] = moment
        nv_ref[i] = velocity
        hat = moment / (1 - beta_one**STEP)
        adam = hat / (jnp.sqrt(velocity / (1 - beta_two**STEP)) + 1e-08)
        left = exact(r_ref[0, i], hat, ((1,), (0,)))
        precond = exact(left, r_ref[1, i], ((1,), (0,)))
        ratio = jnp.sqrt((mean_square(adam) + 1e-06) / (mean_square(precond) + 1e-06))
        blocks = b_ref[i]
        nb_ref[i] = blocks - learn_rate * (precond * ratio + decay_rate * blocks)


def shampoo_step(clip, owned, blocks, stat_pair, root_pair, moment, velocity):
    number = blocks.shape[0]
    per_step = 3 if number % 4 else 4
    one = pl.BlockSpec((per_step, BS, BS), lambda i: (i, 0, 0))
    pair = pl.BlockSpec((2, per_step, BS, BS), lambda i: (0, i, 0, 0))
    single = jax.ShapeDtypeStruct((number, BS, BS), jnp.float32)
    return pl.pallas_call(
        functools.partial(shampoo_kernel, per_step),
        grid=(number // per_step,),
        out_shape=(single, jax.ShapeDtypeStruct((2, number, BS, BS), jnp.float32), single, single),
        in_specs=[
            pl.BlockSpec(memory_space=pltpu.SMEM),
            pl.BlockSpec((per_step * BS, BS), lambda i: (i, 0)),
            one,
            pair,
            pair,
            one,
            one,
        ],
        out_specs=(one, pair, one, one),
        compiler_params=pltpu.CompilerParams(vmem_limit_bytes=60 * MIB),
        cost_estimate=pl.CostEstimate(
            flops=number * 8 * BS**3 * 6, bytes_accessed=number * 12 * BS * BS * 4, transcendentals=0
        ),
        name="shampoo",
    )(clip.reshape(1, 1), owned, blocks, stat_pair, root_pair, moment, velocity)


def adam_step(param, grads, moment, veloc):
    moment_new = beta_one * moment + (1 - beta_one) * grads
    veloc_new = beta_two * veloc + (1 - beta_two) * grads * grads
    direction = (
        moment_new / (1 - beta_one**STEP) / (jnp.sqrt(veloc_new / (1 - beta_two**STEP)) + 1e-08)
    )
    return (param - learn_rate * direction, moment_new, veloc_new)


def halves(matrix):
    return matrix[:, :HALF], matrix[:, HALF:]


def local(
    patches,
    labels,
    batch_ids,
    blocks,
    statistics,
    roots,
    moments,
    velocity,
    aux,
    aux_moment,
    aux_velocity,
):
    part = lax.axis_index("mp")
    all_crops = lax.axis_size("dp") * MP
    pieces = split_aux(aux)
    gain, shift = pieces["norm_gain"], pieces["norm_bias"]

    gathered = gather_weights(blocks)
    other_embedding, w_embed = embed_other(patches, gathered)
    w_qkv, w_proj, w_up, w_down, w_deconv = unblock(gathered)

    def columns(array, which, width, start):
        return lax.dynamic_slice_in_dim(array, which * width + start, width - start, 1)

    down_start = 2 * FF // MP // 3

    other_rows = lax.dynamic_slice_in_dim(patches, (1 - part) * NTOK, NTOK, 0)
    own_rows = lax.dynamic_slice_in_dim(patches, part * NTOK, NTOK, 0)
    received = swap_mp(other_embedding)
    stream_zero = (
        dot_nn(own_rows, w_embed) + received + pieces["positions"] + pieces["embed_bias"]
    )
    normal_one, inverse_one = layer_norm(stream_zero)
    normed_one = (normal_one * gain[0] + shift[0]).astype(jnp.bfloat16)
    q_bias, v_bias = pieces["qv_bias"][0], pieces["qv_bias"][1]
    nothing = jnp.zeros((HALF,), jnp.float32)
    qkv_bias = jnp.concatenate(
        [q_bias[:HALF], nothing, v_bias[:HALF], q_bias[HALF:], nothing, v_bias[HALF:]]
    )
    qkv = (dot_nn(normed_one, w_qkv) + qkv_bias).astype(jnp.bfloat16)
    zero_stream = stream_zero.astype(jnp.bfloat16)
    zero_half = swap_mp(columns(zero_stream, 1 - part, HALF, 0))
    mixed, lse = attention_forward(qkv)
    mixed, zero_half = lax.optimization_barrier((mixed, zero_half))
    stream_one = stream_zero + dot_nn(mixed, w_proj) + pieces["proj_bias"]
    one_stream = stream_one.astype(jnp.bfloat16)
    one_half = swap_mp(columns(one_stream, 1 - part, HALF, 0))
    normal_two, inverse_two = layer_norm(stream_one)
    normed_two = (normal_two * gain[1] + shift[1]).astype(jnp.bfloat16)
    hidden = dot_nn(normed_two, w_up) + pieces["up_bias"]
    active_value, hidden_slope = gelu_and_slope(hidden)
    active = active_value.astype(jnp.bfloat16)
    active, one_half = lax.optimization_barrier((active, one_half))
    active_other = swap_mp(columns(active, 1 - part, FF // MP, down_start))
    stream_two = stream_one + dot_nn(active, w_down) + pieces["down_bias"]
    streams = [zero_stream, one_stream, stream_two.astype(jnp.bfloat16)]
    stacked = jnp.concatenate([halves(s)[m] for m in range(MP) for s in streams], 1)
    up_t = dot(w_deconv, stacked, ((0,), (1,)))

    conv_weight = pieces["conv_weight"].astype(jnp.bfloat16).reshape(27, DEC, CF)
    conv_low = conv_weight.transpose(0, 2, 1).reshape(27 * CF, DEC)
    conv_t = conv_weight.transpose(1, 0, 2).reshape(DEC, 27 * CF)
    head_weight = jnp.pad(pieces["head_weight"], ((0, 0), (0, CF - NCLS))).astype(jnp.bfloat16)
    head_bias = jnp.pad(pieces["head_bias"], (0, CF - NCLS)).reshape(CF, 1)
    grid_labels = arrange_labels(labels)
    batch = jnp.broadcast_to(batch_ids.reshape(1, 1), (1, BS))
    operands = (
        up_t,
        pieces["deconv_bias"].reshape(DEC, 1),
        conv_low,
        pieces["conv_bias"].reshape(CF, 1),
        head_weight.T,
        head_bias,
        grid_labels,
        batch,
    )
    if fast_mesh():
        gu_t, conv_grad, head_grad, small, deconv_bias_grad = decoder(
            all_crops, *operands, conv_t, head_weight
        )
    else:
        conv_in, grid_slope, conv_slope, features, chance, sums = decoder_forward(*operands)
        gu_t, conv_grad, head_grad, small, deconv_bias_grad = decoder_backward(
            all_crops,
            lax.psum(sums, ("dp", "mp")),
            batch,
            grid_labels,
            chance,
            features,
            conv_slope,
            grid_slope,
            conv_in,
            conv_t,
            head_weight,
        )
    gu_t, two_stream, active_other = lax.optimization_barrier((gu_t, streams[2], active_other))
    two_half = swap_mp(columns(two_stream, 1 - part, HALF, 0))
    loss_value = small[0, 2]

    gu_other = swap_mp(gu_t)
    stacked_back = dot(gu_t, w_deconv, ((0,), (1,)))
    back_zero_s, back_one_s, back_two = [
        jnp.concatenate([stacked_back[:, (3 * m + s) * HALF : (3 * m + s + 1) * HALF] for m in range(MP)], 1)
        for s in range(3)
    ]
    grad_down_bias = jnp.sum(back_two, 0)
    two_low = back_two.astype(jnp.bfloat16)
    two_other = swap_mp(two_low)
    back_hidden = (hidden_slope * dot_nt(two_low, w_down)).astype(jnp.bfloat16)
    grad_up_bias = jnp.sum(back_hidden.astype(jnp.float32), 0)
    back_normed_two = dot_nt(back_hidden, w_up)
    grad_gain_two = jnp.sum(back_normed_two * normal_two, 0)
    grad_shift_two = jnp.sum(back_normed_two, 0)
    back_one = (
        back_two + back_one_s + layer_norm_back(back_normed_two, normal_two, inverse_two, gain[1])
    )
    grad_proj_bias = jnp.sum(back_one, 0)
    one_low = back_one.astype(jnp.bfloat16)
    back_mixed = dot_nt(one_low, w_proj).astype(jnp.bfloat16)
    back_q, back_k, back_v = attention_backward(qkv, back_mixed, lse)
    back_qkv = jnp.concatenate(
        [halves(piece)[m] for m in range(MP) for piece in (back_q, back_k, back_v)], 1
    )
    grad_query_bias = jnp.sum(back_q.astype(jnp.float32), 0)
    grad_value_bias = jnp.sum(back_v.astype(jnp.float32), 0)
    back_normed_one = dot_nt(back_qkv, w_qkv)
    grad_gain_one = jnp.sum(back_normed_one * normal_one, 0)
    grad_shift_one = jnp.sum(back_normed_one, 0)
    back_normed_one, two_half, gu_other, two_other = lax.optimization_barrier(
        (back_normed_one, two_half, gu_other, two_other)
    )
    back_zero = (
        back_one + back_zero_s + layer_norm_back(back_normed_one, normal_one, inverse_one, gain[0])
    )
    zero_low = back_zero.astype(jnp.bfloat16)
    other_low = swap_mp(zero_low)

    fast = fast_mesh()
    depth = CHUNK if fast else BLOCK_ROWS
    stacked_own = jnp.concatenate([columns(stream, part, HALF, 0) for stream in streams], 1)
    stacked_other = jnp.concatenate([zero_half, one_half, two_half], 1)
    active_own = columns(active, part, FF // MP, down_start)
    final_grads = grad_blocks(
        [stacked_own, stacked_other], [gu_t, gu_other], 1, 9, 8, 3, 24, True, False, None, "grad_deconv", 4, BLOCK_ROWS, True
    )
    final_grads = grad_blocks(
        [active_own, active_other], [two_low, two_other], 1, 4, 6, 4, 0, True, False, final_grads, "grad_down_last", 4, BLOCK_ROWS
    )
    rest_grads = None
    for name, x, g, rows, per_row, step_rows, start, split_x, split_g, stride in (
        ("grad_down", active, two_low, 8, 6, 4, 144, True, False, 3),
        ("grad_up", normed_two, back_hidden, 6, 12, 3, 72, False, True, None),
        ("grad_proj", mixed, one_low, 3, 6, 3, 54, True, False, None),
        ("grad_qkv", normed_one, back_qkv, 6, 9, 3, 0, False, True, None),
    ):
        rest_grads = grad_blocks(
            [x], [g], MP, rows, per_row, step_rows, start, split_x, split_g, rest_grads, name, 8, depth,
            x_stride=stride,
        )
    first_grads = grad_blocks(
        [own_rows, other_rows], [zero_low, other_low], 1, 16, 6, 4, 0, False, False, None, "grad_embed", 4, BLOCK_ROWS
    )
    vectors = [
        grad_gain_one,
        grad_gain_two,
        grad_shift_one,
        grad_shift_two,
        grad_query_bias,
        grad_value_bias,
        grad_proj_bias,
        grad_down_bias,
    ]
    if fast:
        head_wide = jnp.pad(head_grad, ((0, 0), (0, BS - CF)))
        rest_grads = pack_aux(
            back_zero, vectors, grad_up_bias, conv_grad, head_wide, small, deconv_bias_grad, rest_grads
        )
        owned, squares = reduce_to_owners(
            rest_grads.reshape(MP, 2, 2, 2, CHUNK, BS),
            first_grads.reshape(2, 2, BLOCK_ROWS, BS),
            final_grads.reshape(2, 2, BLOCK_ROWS, BS),
        )
        gathered_aux = gather_all(
            jnp.concatenate([owned[BLOCK_ROWS:], squares]),
            ((0, AUX_ROWS), (AUX_ROWS, 8)),
            1,
            False,
            (0,),
            4,
            "gather_aux",
        )
        in_rows, norm_clip = unpack_aux(gathered_aux)
        aux_total = in_rows.reshape(-1)[:NAUX]
        grad_norm, clip_scale = norm_clip[0, 0], norm_clip[0, 1]
    else:
        owned = reduce_plain(rest_grads.reshape(MP, -1, BS, BS), first_grads, final_grads)
        owned = owned.reshape(-1, BS)
        positions_sum, small_sum = lax.psum(
            (
                back_zero,
                jnp.concatenate(
                    vectors[:7]
                    + [
                        grad_up_bias,
                        grad_down_bias,
                        deconv_bias_grad[:, 0],
                        conv_grad.reshape(27, CF, DEC).transpose(0, 2, 1).reshape(-1),
                        small[:, 1],
                        head_grad[:, :NCLS].reshape(-1),
                        small[:NCLS, 0],
                    ]
                ),
            ),
            ("dp", "mp"),
        )
        aux_total = jnp.concatenate(
            [positions_sum.reshape(-1), jnp.sum(positions_sum, 0), small_sum]
        )
        block_square = lax.psum(jnp.sum(owned * owned), ("dp", "mp"))
        grad_norm = jnp.sqrt(block_square + jnp.sum(aux_total * aux_total))
        clip_scale = clip_value / jnp.maximum(grad_norm, clip_value)
    block_new, stat_new, moment_new, veloc_new = shampoo_step(
        clip_scale,
        owned,
        blocks[0, 0],
        statistics[:, 0, 0],
        roots[:, 0, 0],
        moments[0, 0],
        velocity[0, 0],
    )
    aux_new, aux_moment_new, aux_veloc_new = adam_step(
        aux, aux_total * clip_scale, aux_moment, aux_velocity
    )
    return (
        loss_value,
        grad_norm,
        block_new[None, None],
        stat_new[:, None, None],
        moment_new[None, None],
        veloc_new[None, None],
        aux_new,
        aux_moment_new,
        aux_veloc_new,
    )


def solution(mesh):
    block_spec = P("dp", "mp", None, None, None)
    pair_spec = P(None, "dp", "mp", None, None, None)
    placed = (
        P("dp", "mp"),
        P(("dp", "mp"), None),
        P(("dp", "mp")),
        block_spec,
        pair_spec,
        pair_spec,
        block_spec,
        block_spec,
        P(),
        P(),
        P(),
    )
    return jax.shard_map(
        local,
        mesh=mesh,
        in_specs=placed,
        out_specs=(P(), P(), block_spec, pair_spec, block_spec, block_spec, P(), P(), P()),
        check_vma=False,
    )
```

```python
import functools
import math

import jax
import jax.numpy as jnp
from jax import lax
from jax.experimental import pallas as pl
from jax.experimental.pallas import tpu as pltpu
from jax.sharding import PartitionSpec as P

D = 768
HDIM = 64
FF = 3072
PV = 4096
DEC = 128
CF = 16
NCLS = 14
GS = 8
MB = 4
STEP = 10
BS = 128
NTOK = 512
CELLS = 4096
MP = 2
HALF = D // MP
E_BLOCKS = PV // MP * D // (BS * BS)

HIGHEST = lax.Precision.HIGHEST
MESH = pl.DeviceIdType.MESH
beta_one = 0.9
beta_two = 0.999
beta_stat = 0.95
learn_rate = 0.02
decay_rate = 0.01
clip_value = 0.005
MIB = 1024 * 1024

OFFSETS = [(a, b, c) for a in range(3) for b in range(3) for c in range(3)]
PARITIES = [(i, j, k) for i in range(2) for j in range(2) for k in range(2)]


def dot(a, b, dims):
    return lax.dot_general(a, b, (dims, ((), ())), preferred_element_type=jnp.float32)


def dot_nn(a, b):
    return dot(a, b, ((1,), (0,)))


def dot_nt(a, b):
    return dot(a, b, ((1,), (1,)))


def dot_tn(a, b):
    return dot(a, b, ((0,), (0,)))


def gelu_cdf(v):
    return 0.5 * (1.0 + lax.erf(v * (0.5**0.5)))


def gelu_and_slope(v):
    cdf = gelu_cdf(v)
    density = jnp.exp(-0.5 * v * v) * (1.0 / math.sqrt(2.0 * math.pi))
    return v * cdf, cdf + v * density


def aux_layout():
    return [
        ("positions", (NTOK, D)),
        ("embed_bias", (D,)),
        ("norm_gain", (2, D)),
        ("norm_bias", (2, D)),
        ("qv_bias", (2, D)),
        ("proj_bias", (D,)),
        ("up_bias", (FF,)),
        ("down_bias", (D,)),
        ("deconv_bias", (DEC,)),
        ("conv_weight", (27 * DEC, CF)),
        ("conv_bias", (CF,)),
        ("head_weight", (CF, NCLS)),
        ("head_bias", (NCLS,)),
    ]


NAUX = sum(math.prod(shape) for _, shape in aux_layout())


def split_aux(vector):
    pieces = {}
    offset = 0
    for section_name, section_shape in aux_layout():
        length = math.prod(section_shape)
        pieces[section_name] = vector[offset : offset + length].reshape(section_shape)
        offset += length
    return pieces


def attention_forward_kernel(qkv_q, qkv_k, qkv_v, mixed_ref, lse_ref):
    q, k, v = qkv_q[...], qkv_k[...], qkv_v[...]
    v_t = v.astype(jnp.float32).T.astype(jnp.bfloat16)
    outs = []
    for h in range(2):
        cols = slice(h * HDIM, (h + 1) * HDIM)
        scores = dot_nt(k[:, cols], q[:, cols]) * 0.125
        top = jnp.max(scores, 0, keepdims=True)
        weights = jnp.exp(scores - top)
        total = jnp.sum(weights, 0, keepdims=True)
        attention = (weights * (1.0 / total)).astype(jnp.bfloat16)
        outs.append(dot_nn(v_t[cols], attention))
        lse_ref[0, h : h + 1, :] = top + jnp.log(total)
    mixed_ref[...] = jnp.concatenate(outs, 0).T.astype(jnp.bfloat16)


def attention_backward_kernel(qkv_q, qkv_k, qkv_v, gm_ref, lse_ref, gq_ref, gk_ref, gv_ref):
    q, k, v, gm = qkv_q[...], qkv_k[...], qkv_v[...], gm_ref[...]
    k_t = k.astype(jnp.float32).T.astype(jnp.bfloat16)
    gq_t = []
    for h in range(2):
        cols = slice(h * HDIM, (h + 1) * HDIM)
        scores = dot_nt(k[:, cols], q[:, cols]) * 0.125
        attention = jnp.exp(scores - lse_ref[0, h : h + 1, :])
        back = dot_nt(v[:, cols], gm[:, cols])
        gv_ref[:, cols] = dot_nn(attention.astype(jnp.bfloat16), gm[:, cols]).astype(jnp.bfloat16)
        mean = jnp.sum(back * attention, 0, keepdims=True)
        gs = (attention * (back - mean)).astype(jnp.bfloat16)
        gk_ref[:, cols] = (dot_nn(gs, q[:, cols]) * 0.125).astype(jnp.bfloat16)
        gq_t.append(dot_nn(k_t[cols], gs) * 0.125)
    gq_ref[...] = jnp.concatenate(gq_t, 0).T.astype(jnp.bfloat16)


def qkv_spec(part):
    return pl.BlockSpec((NTOK, BS), lambda i, part=part: (0, (i // 3) * 9 + part * 3 + i % 3))


def attention_forward(qkv):
    return pl.pallas_call(
        attention_forward_kernel,
        grid=(6,),
        out_shape=(
            jax.ShapeDtypeStruct((NTOK, D), jnp.bfloat16),
            jax.ShapeDtypeStruct((6, 2, NTOK), jnp.float32),
        ),
        in_specs=[qkv_spec(0), qkv_spec(1), qkv_spec(2)],
        out_specs=(
            pl.BlockSpec((NTOK, BS), lambda i: (0, i)),
            pl.BlockSpec((1, 2, NTOK), lambda i: (i, 0, 0)),
        ),
        compiler_params=pltpu.CompilerParams(vmem_limit_bytes=32 * MIB),
        cost_estimate=pl.CostEstimate(
            flops=12 * 4 * NTOK * NTOK * HDIM,
            bytes_accessed=NTOK * D * 8,
            transcendentals=12 * NTOK * NTOK,
        ),
        name="attention_forward",
    )(qkv, qkv, qkv)


def attention_backward(qkv, gm, lse):
    pair = pl.BlockSpec((NTOK, BS), lambda i: (0, i))
    return pl.pallas_call(
        attention_backward_kernel,
        grid=(6,),
        out_shape=(jax.ShapeDtypeStruct((NTOK, D), jnp.bfloat16),) * 3,
        in_specs=[
            qkv_spec(0),
            qkv_spec(1),
            qkv_spec(2),
            pair,
            pl.BlockSpec((1, 2, NTOK), lambda i: (i, 0, 0)),
        ],
        out_specs=(pair,) * 3,
        compiler_params=pltpu.CompilerParams(vmem_limit_bytes=32 * MIB),
        cost_estimate=pl.CostEstimate(
            flops=12 * 10 * NTOK * NTOK * HDIM,
            bytes_accessed=NTOK * D * 14,
            transcendentals=12 * NTOK * NTOK,
        ),
        name="attention_backward",
    )(qkv, qkv, qkv, gm, lse)


def source_of(parity, step):
    at = parity + step
    if at < 0:
        return 1, -1
    if at > 1:
        return 0, 1
    return at, 0


def shift_plan(offset, parity, sign):
    found = [source_of(par, sign * (off - 1)) for off, par in zip(offset, parity)]
    bits = [f[0] for f in found]
    steps = [f[1] for f in found]
    return bits[0] * 4 + bits[1] * 2 + bits[2], steps


def token_masks(tokens):
    at = (tokens // (GS * GS), (tokens // GS) % GS, tokens % GS)
    masks = {}
    for axis in range(3):
        masks[axis, 1] = at[axis] < GS - 1
        masks[axis, -1] = at[axis] > 0
    return masks


def shifted(values, steps, masks):
    delta = steps[0] * GS * GS + steps[1] * GS + steps[2]
    if delta == 0 and not any(steps):
        return values
    moved = pltpu.roll(values, (-delta) % NTOK, 1)
    keep = None
    for axis in range(3):
        if steps[axis]:
            mask = masks[axis, steps[axis]]
            keep = mask if keep is None else keep & mask
    return jnp.where(keep, moved, 0.0)


def lanes(parity):
    return slice(parity * NTOK, (parity + 1) * NTOK)


def decoder_forward_kernel(
    up_ref,
    deconv_bias_ref,
    conv_ref,
    conv_bias_ref,
    head_ref,
    head_bias_ref,
    labels_ref,
    batch_ref,
    conv_in_ref,
    grid_slope_ref,
    conv_slope_ref,
    features_ref,
    chance_ref,
    sums_ref,
    conved_ref,
):
    tokens = lax.broadcasted_iota(jnp.int32, (CF, NTOK), 1)
    masks = token_masks(tokens)
    for parity in range(8):
        conved_ref[:, lanes(parity)] = jnp.broadcast_to(conv_bias_ref[...], (CF, NTOK))
    for parity in range(8):
        cell = up_ref[parity * DEC : (parity + 1) * DEC, :] + deconv_bias_ref[...]
        value, slope = gelu_and_slope(cell)
        low = value.astype(jnp.bfloat16)
        conv_in_ref[:, lanes(parity)] = low
        grid_slope_ref[:, lanes(parity)] = slope
        products = dot_nn(conv_ref[...], low)
        for at, offset in enumerate(OFFSETS):
            target, back_steps = shift_plan(offset, PARITIES[parity], -1)
            forward = [-s for s in back_steps]
            piece = shifted(products[at * CF : (at + 1) * CF, :], forward, masks)
            conved_ref[:, lanes(target)] += piece
    rows = lax.broadcasted_iota(jnp.int32, (CF, NTOK), 0)
    hit = jnp.zeros((CF, 1), jnp.float32)
    predicted = jnp.zeros((CF, 1), jnp.float32)
    truth = jnp.zeros((CF, 1), jnp.float32)
    entropy = jnp.zeros((CF, 1), jnp.float32)
    for parity in range(8):
        value, slope = gelu_and_slope(conved_ref[:, lanes(parity)])
        conv_slope_ref[:, lanes(parity)] = slope
        features = value.astype(jnp.bfloat16)
        features_ref[:, lanes(parity)] = features
        logits = dot_nn(head_ref[...], features) + head_bias_ref[...]
        logits = jnp.where(rows < NCLS, logits, -1e30)
        center = logits - jnp.max(logits, 0, keepdims=True)
        log_prob = center - jnp.log(jnp.sum(jnp.exp(center), 0, keepdims=True))
        chance = jnp.exp(log_prob)
        target = (rows == labels_ref[parity : parity + 1, :]).astype(jnp.float32)
        chance_ref[:, lanes(parity)] = chance
        hit += jnp.sum(chance * target, 1, keepdims=True)
        predicted += jnp.sum(chance, 1, keepdims=True)
        truth += jnp.sum(target, 1, keepdims=True)
        entropy -= jnp.sum(jnp.where(target > 0, log_prob, 0.0), 1, keepdims=True)
    lane = lax.broadcasted_iota(jnp.int32, (CF, BS), 1)
    base = batch_ref[...] * 3
    sums_ref[...] = (
        jnp.where(lane == base, hit, 0.0)
        + jnp.where(lane == base + 1, predicted, 0.0)
        + jnp.where(lane == base + 2, truth, 0.0)
        + jnp.where(lane == 3 * MB, entropy, 0.0)
    )


def decoder_backward_kernel(
    all_crops,
    sums_ref,
    batch_ref,
    labels_ref,
    chance_ref,
    features_ref,
    conv_slope_ref,
    grid_slope_ref,
    conv_in_ref,
    conv_t_ref,
    head_t_ref,
    gu_ref,
    conv_grad_ref,
    head_grad_ref,
    small_ref,
    deconv_grad_ref,
    spread_ref,
):
    sums = sums_ref[...]
    lane = lax.broadcasted_iota(jnp.int32, (CF, BS), 1)
    row = lax.broadcasted_iota(jnp.int32, (CF, BS), 0)
    live = (lane < 3 * MB) & (lane % 3 == 0) & (row < NCLS)
    under = pltpu.roll(sums, BS - 1, 1) + pltpu.roll(sums, BS - 2, 1) + 1.0
    under = jnp.where(live, under, 1.0)
    over = 2.0 * sums + 1.0
    dice = jnp.where(live, over / under, 0.0)
    mean_dice = jnp.sum(jnp.sum(dice, 1, keepdims=True), 0, keepdims=True) / (NCLS * MB)
    entropy_lane = jnp.where(lane == 3 * MB, sums, 0.0)
    entropy = jnp.sum(jnp.sum(entropy_lane, 1, keepdims=True), 0, keepdims=True)
    loss = entropy / (all_crops * CELLS) + (1.0 - mean_dice)
    own = live & (lane == batch_ref[...] * 3)
    d_hit = jnp.sum(jnp.where(own, -2.0 / (MB * NCLS) / under, 0.0), 1, keepdims=True)
    d_predicted = jnp.sum(
        jnp.where(own, (1.0 / (MB * NCLS)) * over / (under * under), 0.0), 1, keepdims=True
    )
    tokens = lax.broadcasted_iota(jnp.int32, (CF, NTOK), 1)
    masks = token_masks(tokens)
    rows = lax.broadcasted_iota(jnp.int32, (CF, NTOK), 0)
    head_bias = jnp.zeros((CF, 1), jnp.float32)
    conv_bias = jnp.zeros((CF, 1), jnp.float32)
    head_grad = jnp.zeros((CF, CF), jnp.float32)
    for parity in range(8):
        chance = chance_ref[:, lanes(parity)]
        target = (rows == labels_ref[parity : parity + 1, :]).astype(jnp.float32)
        back = (d_hit * target + d_predicted) * chance - target * (1.0 / (all_crops * CELLS))
        logits = back - chance * jnp.sum(back, 0, keepdims=True)
        head_bias += jnp.sum(logits, 1, keepdims=True)
        low = logits.astype(jnp.bfloat16)
        head_grad += dot_nt(features_ref[:, lanes(parity)], low)
        conved = conv_slope_ref[:, lanes(parity)] * dot_nn(head_t_ref[...], low)
        conv_bias += jnp.sum(conved, 1, keepdims=True)
        rounded = conved.astype(jnp.bfloat16).astype(jnp.float32)
        for at, offset in enumerate(OFFSETS):
            target_cell, steps = shift_plan(offset, PARITIES[parity], 1)
            piece = shifted(rounded, [-s for s in steps], masks)
            spread_ref[at * CF : (at + 1) * CF, lanes(target_cell)] = piece.astype(jnp.bfloat16)
    head_grad_ref[...] = head_grad
    small_ref[...] = (
        jnp.where(lane == 0, head_bias, 0.0)
        + jnp.where(lane == 1, conv_bias, 0.0)
        + jnp.where(lane == 2, loss, 0.0)
    )
    conv_grad = jnp.zeros((27 * CF, DEC), jnp.float32)
    deconv_grad = jnp.zeros((DEC, 1), jnp.float32)
    for parity in range(8):
        spread = spread_ref[:, lanes(parity)]
        conv_grad += dot_nt(spread, conv_in_ref[:, lanes(parity)])
        back = grid_slope_ref[:, lanes(parity)] * dot_nn(conv_t_ref[...], spread)
        deconv_grad += jnp.sum(back, 1, keepdims=True)
        gu_ref[parity * DEC : (parity + 1) * DEC, :] = back.astype(jnp.bfloat16)
    conv_grad_ref[...] = conv_grad
    deconv_grad_ref[...] = jnp.broadcast_to(deconv_grad, (DEC, BS))


def whole_specs(number):
    return [pl.BlockSpec(memory_space=pltpu.VMEM)] * number


def decoder_forward(up_t, deconv_bias, conv_low, conv_bias, head_low, head_bias, labels, batch):
    shapes = (
        jax.ShapeDtypeStruct((DEC, CELLS), jnp.bfloat16),
        jax.ShapeDtypeStruct((DEC, CELLS), jnp.float32),
        jax.ShapeDtypeStruct((CF, CELLS), jnp.float32),
        jax.ShapeDtypeStruct((CF, CELLS), jnp.bfloat16),
        jax.ShapeDtypeStruct((CF, CELLS), jnp.float32),
        jax.ShapeDtypeStruct((CF, BS), jnp.float32),
    )
    return pl.pallas_call(
        decoder_forward_kernel,
        out_shape=shapes,
        in_specs=whole_specs(8),
        out_specs=tuple(whole_specs(6)),
        scratch_shapes=[pltpu.VMEM((CF, CELLS), jnp.float32)],
        compiler_params=pltpu.CompilerParams(vmem_limit_bytes=40 * MIB),
        cost_estimate=pl.CostEstimate(
            flops=2 * 27 * CF * DEC * CELLS, bytes_accessed=6 * MIB, transcendentals=DEC * CELLS
        ),
        name="decoder_forward",
    )(up_t, deconv_bias, conv_low, conv_bias, head_low, head_bias, labels, batch)


def decoder_backward(
    all_crops, sums, batch, labels, chance, features, conv_slope, grid_slope, conv_in, conv_t, head_t
):
    shapes = (
        jax.ShapeDtypeStruct((8 * DEC, NTOK), jnp.bfloat16),
        jax.ShapeDtypeStruct((27 * CF, DEC), jnp.float32),
        jax.ShapeDtypeStruct((CF, CF), jnp.float32),
        jax.ShapeDtypeStruct((CF, BS), jnp.float32),
        jax.ShapeDtypeStruct((DEC, BS), jnp.float32),
    )
    return pl.pallas_call(
        functools.partial(decoder_backward_kernel, all_crops),
        out_shape=shapes,
        in_specs=whole_specs(10),
        out_specs=tuple(whole_specs(5)),
        scratch_shapes=[pltpu.VMEM((27 * CF, CELLS), jnp.bfloat16)],
        compiler_params=pltpu.CompilerParams(vmem_limit_bytes=40 * MIB),
        cost_estimate=pl.CostEstimate(
            flops=4 * 27 * CF * DEC * CELLS, bytes_accessed=6 * MIB, transcendentals=0
        ),
        name="decoder_backward",
    )(sums, batch, labels, chance, features, conv_slope, grid_slope, conv_in, conv_t, head_t)


LAYERS = 4
GATHER_LAG = 2
THIRDS = tuple((8 * BS * i, 8 * BS) for i in range(3))
PIECES = 32
BLOCK_ROWS = 24 * BS
AUX_ROWS = 256
CHUNK = BLOCK_ROWS + AUX_ROWS
ROWS_N = 2 * CHUNK // PIECES
ROWS_F = BLOCK_ROWS // PIECES
LAG = 1
HOP_LAG = 1
AHEAD = 3
CORE_SLOTS = 8
SEND_SLOTS = 4
KEEP = 8
SUM_SLOTS = 12


def remote(src, dst, send_sem, recv_sem, device):
    return pltpu.make_async_remote_copy(
        src_ref=src,
        dst_ref=dst,
        send_sem=send_sem,
        recv_sem=recv_sem,
        device_id=device,
        device_id_type=MESH,
    )


def places():
    dp, x = lax.axis_index("dp"), lax.axis_index("mp")
    z, y, c = dp // 4, (dp // 2) % 2, dp % 2
    return dict(
        dp=dp,
        x=x,
        y=y,
        z=z,
        c=c,
        at_core=(dp + 1 - 2 * c, x),
        at_x=(dp, 1 - x),
        at_y=(dp + 2 - 4 * y, x),
        above=(lax.rem(dp + 4, 4 * LAYERS), x),
        below=(lax.rem(dp + 4 * LAYERS - 4, 4 * LAYERS), x),
    )


def greet_neighbours(at):
    barrier = pltpu.get_barrier_semaphore()
    for name in ("at_core", "at_x", "at_y"):
        pl.semaphore_signal(barrier, inc=1, device_id=at[name], device_id_type=MESH)

    @pl.when(at["z"] < LAYERS - 1)
    def _():
        pl.semaphore_signal(barrier, inc=1, device_id=at["above"], device_id_type=MESH)

    @pl.when(at["z"] > 0)
    def _():
        pl.semaphore_signal(barrier, inc=1, device_id=at["below"], device_id_type=MESH)

    peers = 3 + jnp.minimum(at["z"], 1) + jnp.minimum(LAYERS - 1 - at["z"], 1)
    pl.semaphore_wait(barrier, peers)


def gather_kernel(parts, by_x, skip, middle, in_ref, out_ref, local_sem, up_sem, down_sem, z_recv, x_send, x_recv, y_send, y_recv, core_send, core_recv):
    at = places()
    x, y, z, c = at["x"], at["y"], at["z"], at["c"]
    last = LAYERS - 1

    def spot(l, y_at, c_at, x_at, p):
        return out_ref.at[x_at, l * 4 + y_at * 2 + c_at, pl.ds(*parts[p])]

    def send(ref, send_sem, recv_sem, device):
        return remote(ref, ref, send_sem, recv_sem, device)

    def up(l, p):
        return send(spot(l, y, c, x, p), up_sem.at[l, p], z_recv.at[l, p], at["above"])

    def down(l, p):
        return send(spot(l, y, c, x, p), down_sem.at[l, p], z_recv.at[l, p], at["below"])

    def x_direct(l, p, x_at):
        return send(spot(l, y, c, x_at, p), x_send.at[l, p, 0], x_recv.at[l, p, 0], at["at_x"])

    def y_direct(l, p, y_at):
        return send(spot(l, y_at, c, x, p), y_send.at[l, p, 0], y_recv.at[l, p, 0], at["at_y"])

    def diagonal(l, p, y_at, x_at):
        if p < by_x:
            return send(spot(l, y_at, c, x_at, p), y_send.at[l, p, 1], y_recv.at[l, p, 1], at["at_y"])
        return send(spot(l, y_at, c, x_at, p), x_send.at[l, p, 1], x_recv.at[l, p, 1], at["at_x"])

    def relayed(l, p):
        return diagonal(l, p, y, 1 - x) if p < by_x else diagonal(l, p, 1 - y, x)

    def core(l, p, kind, c_at):
        y_at, x_at = ((y, x), (1 - y, x), (y, 1 - x), (1 - y, 1 - x))[kind]
        return send(
            spot(l, y_at, c_at, x_at, p),
            core_send.at[l, p, kind],
            core_recv.at[l, p, kind],
            at["at_core"],
        )

    def wide(l):
        return (l > 0) if skip else (l >= 0)

    own = pltpu.make_async_copy(in_ref, out_ref.at[x, at["dp"]], local_sem)
    own.start()
    greet_neighbours(at)
    own.wait()

    def arrive(l, p, came_up, came_down):
        if not (came_up and came_down):
            up(l, p).wait_recv()
        if came_up:

            @pl.when(z < last)
            def _():
                up(l, p).start()

        if came_down:

            @pl.when(z > 0)
            def _():
                down(l, p).start()

        @pl.when(wide(l))
        def _():
            x_direct(l, p, x).start()

        y_direct(l, p, y).start()
        core(l, p, 0, c).start()

    def relay(l, p):
        y_direct(l, p, 1 - y).wait_recv()

        @pl.when(wide(l))
        def _():
            if p >= by_x:
                relayed(l, p).start()
            x_direct(l, p, 1 - x).wait_recv()
            if p < by_x:
                relayed(l, p).start()
            core(l, p, 2, c).start()

        core(l, p, 1, c).start()

    def finish(l, p):
        @pl.when(wide(l))
        def _():
            diagonal(l, p, 1 - y, 1 - x).wait_recv()
            core(l, p, 3, c).start()

    def held(l, p):
        return ((l > 0) & (l < last)) if p in middle else ((l >= 0) & (l <= last))

    number = len(parts)

    def both(tick, run):
        if tick < 0 or tick >= LAYERS * number:
            return
        r, p = tick // number, tick % number
        if r == 0:

            @pl.when(held(z, p))
            def _():
                run(z, p, True, True)

            return

        @pl.when(held(z - r, p))
        def _():
            run(z - r, p, True, False)

        @pl.when(held(z + r, p))
        def _():
            run(z + r, p, False, True)

    lag = 4 if middle else GATHER_LAG
    for tick in range(LAYERS * number + 2 * lag):
        both(tick, arrive)
        both(tick - lag, lambda l, p, up_way, down_way: relay(l, p))
        both(tick - 2 * lag, lambda l, p, up_way, down_way: finish(l, p))

    def settle_part(l, p):
        for kind in (0, 1):
            core(l, p, kind, 1 - c).wait_recv()
            core(l, p, kind, c).wait_send()
        y_direct(l, p, y).wait_send()

        @pl.when(wide(l))
        def _():
            for kind in (2, 3):
                core(l, p, kind, 1 - c).wait_recv()
                core(l, p, kind, c).wait_send()
            x_direct(l, p, x).wait_send()
            relayed(l, p).wait_send()

        @pl.when((l <= z) & (z < last))
        def _():
            up(l, p).wait_send()

        @pl.when((l >= z) & (z > 0))
        def _():
            down(l, p).wait_send()

    def settle(l, carry):
        for p in range(number):
            pl.when(held(l, p))(functools.partial(settle_part, l, p))
        return carry

    lax.fori_loop(0, LAYERS, settle, 0)


def gather_all(values, parts, by_x, skip, middle, collective_id, name):
    rows = values.shape[0]
    number = len(parts)

    def sems(*shape):
        return pltpu.SemaphoreType.DMA(shape)

    return pl.pallas_call(
        functools.partial(gather_kernel, parts, by_x, skip, middle),
        out_shape=jax.ShapeDtypeStruct((MP, 4 * LAYERS, rows, BS), values.dtype),
        in_specs=[pl.BlockSpec(memory_space=pl.ANY)],
        out_specs=pl.BlockSpec(memory_space=pl.ANY),
        scratch_shapes=[
            pltpu.SemaphoreType.DMA,
            sems(LAYERS, number),
            sems(LAYERS, number),
            sems(LAYERS, number),
            sems(LAYERS, number, 2),
            sems(LAYERS, number, 2),
            sems(LAYERS, number, 2),
            sems(LAYERS, number, 2),
            sems(LAYERS, number, 4),
            sems(LAYERS, number, 4),
        ],
        compiler_params=pltpu.CompilerParams(
            collective_id=collective_id, has_side_effects=True, vmem_limit_bytes=32 * MIB
        ),
        cost_estimate=pl.CostEstimate(flops=0, bytes_accessed=32 * rows * BS * 4, transcendentals=0),
        name=name,
    )(values)


def reduce_kernel(
    n_ref,
    e_ref,
    f_ref,
    out_ref,
    square_ref,
    own_n,
    own_f,
    core_n,
    core_f,
    keep_n,
    keep_f,
    xs_n,
    ys_n,
    ys_f,
    xr_n,
    yr_n,
    yr_f,
    sum_n,
    sum_f,
    up_n,
    down_n,
    up_f,
    down_e,
    own_sem,
    core_send,
    core_recv,
    credit,
    xs_sem,
    ys_n_sem,
    ys_f_sem,
    xr_sem,
    yr_n_sem,
    yr_f_sem,
    z_n_sem,
    z_f_sem,
    up_n_sem,
    down_n_sem,
    up_f_sem,
    down_e_sem,
):
    at = places()
    x, y, z, c = at["x"], at["y"], at["z"], at["c"]
    last = LAYERS - 1

    def layer_of(s):
        return 1 + lax.rem(s, 2)

    def rows_of(s):
        return pl.ds(pl.multiple_of((s // 2) * ROWS_N, 8), ROWS_N)

    def rows_f(s):
        return pl.ds(pl.multiple_of(s * ROWS_F, 8), ROWS_F)

    def own_loads(s):
        slot = lax.rem(s, 3)
        mine = n_ref.at[:, layer_of(s) - 1, :, c, rows_of(s)]
        return (
            pltpu.make_async_copy(mine, own_n.at[slot], own_sem.at[slot, 0]),
            pltpu.make_async_copy(e_ref.at[:, c, rows_f(s)], own_f.at[slot, 0], own_sem.at[slot, 1]),
            pltpu.make_async_copy(f_ref.at[:, c, rows_f(s)], own_f.at[slot, 1], own_sem.at[slot, 2]),
        )

    def core_copies(s):
        slot = lax.rem(s, CORE_SLOTS)
        sources = (
            n_ref.at[:, layer_of(s) - 1, :, 1 - c, rows_of(s)],
            e_ref.at[:, 1 - c, rows_f(s)],
            f_ref.at[:, 1 - c, rows_f(s)],
        )
        targets = (core_n.at[slot], core_f.at[slot, 0], core_f.at[slot, 1])
        return [
            remote(source, target, core_send.at[s, i], core_recv.at[slot, i], at["at_core"])
            for i, (source, target) in enumerate(zip(sources, targets))
        ]

    def x_copy(s):
        slot = lax.rem(s, SEND_SLOTS)
        return remote(xs_n.at[slot], xr_n.at[s], xs_sem.at[slot], xr_sem.at[s], at["at_x"])

    def y_copy_f(s):
        slot = lax.rem(s, SEND_SLOTS)
        return remote(ys_f.at[slot], yr_f.at[s], ys_f_sem.at[slot], yr_f_sem.at[s], at["at_y"])

    def y_copy(s):
        slot = lax.rem(s, SEND_SLOTS)
        return remote(ys_n.at[slot], yr_n.at[s], ys_n_sem.at[slot], yr_n_sem.at[s], at["at_y"])

    def up_copy(s):
        slot = lax.rem(s, SUM_SLOTS)
        return remote(sum_n.at[slot], up_n.at[s], z_n_sem.at[slot], up_n_sem.at[s], at["above"])

    def down_copy(s):
        slot = lax.rem(s, SUM_SLOTS)
        return remote(sum_n.at[slot], down_n.at[s], z_n_sem.at[slot], down_n_sem.at[s], at["below"])

    def down_copy_e(s):
        slot = lax.rem(s, SUM_SLOTS)
        source, sem = sum_f.at[slot, 0], z_f_sem.at[slot, 0]
        return remote(source, down_e.at[s], sem, down_e_sem.at[s], at["below"])

    def up_copy_f(s):
        slot = lax.rem(s, SUM_SLOTS)
        source, sem = sum_f.at[slot, 1], z_f_sem.at[slot, 1]
        return remote(source, up_f.at[s], sem, up_f_sem.at[s], at["above"])

    def add_squares(values):
        square_ref[...] += jnp.sum((values * values).reshape(-1, 8, BS), 0)

    square_ref[...] = jnp.zeros((8, BS), jnp.float32)
    for s in range(2):
        for copy in own_loads(s):
            copy.start()
    greet_neighbours(at)
    for s in range(AHEAD):
        for copy in core_copies(s):
            copy.start()

    def first(s):
        @pl.when(s + 2 < PIECES)
        def _():
            for copy in own_loads(s + 2):
                copy.start()

        @pl.when(s + AHEAD < PIECES)
        def _():
            @pl.when(s + AHEAD >= CORE_SLOTS)
            def _():
                pl.semaphore_wait(credit, 1)

            for copy in core_copies(s + AHEAD):
                copy.start()

        for copy in own_loads(s):
            copy.wait()
        for copy in core_copies(s):
            copy.wait_recv()

        @pl.when(s >= SEND_SLOTS)
        def _():
            x_copy(s - SEND_SLOTS).wait_send()
            y_copy_f(s - SEND_SLOTS).wait_send()

        own, core = lax.rem(s, 3), lax.rem(s, CORE_SLOTS)
        send, keep = lax.rem(s, SEND_SLOTS), lax.rem(s, KEEP)
        xs_n[send] = own_n[own, 1 - x] + core_n[core, 1 - x]
        x_copy(s).start()
        for kind in range(2):
            ys_f[send, kind] = own_f[own, kind, 1 - y] + core_f[core, kind, 1 - y]
        y_copy_f(s).start()
        keep_n[keep] = own_n[own, x] + core_n[core, x]
        for kind in range(2):
            keep_f[keep, kind] = own_f[own, kind, y] + core_f[core, kind, y]

        @pl.when(s + CORE_SLOTS < PIECES)
        def _():
            pl.semaphore_signal(credit, inc=1, device_id=at["at_core"], device_id_type=MESH)

    def second(s):
        x_copy(s).wait_recv()

        @pl.when(s >= SEND_SLOTS)
        def _():
            y_copy(s - SEND_SLOTS).wait_send()

        send, keep = lax.rem(s, SEND_SLOTS), lax.rem(s, KEEP)
        ys_n[send] = keep_n[keep, 1 - y] + xr_n[s, 1 - y]
        y_copy(s).start()
        keep_n[keep, y] = keep_n[keep, y] + xr_n[s, y]

    def third(s):
        y_copy_f(s).wait_recv()
        y_copy(s).wait_recv()

        @pl.when((s >= SUM_SLOTS) & (z != layer_of(s)))
        def _():
            up_copy(s - SUM_SLOTS).wait_send()

        @pl.when((s >= SUM_SLOTS) & (z > 0))
        def _():
            down_copy_e(s - SUM_SLOTS).wait_send()

        @pl.when((s >= SUM_SLOTS) & (z < last))
        def _():
            up_copy_f(s - SUM_SLOTS).wait_send()

        slot, keep = lax.rem(s, SUM_SLOTS), lax.rem(s, KEEP)
        sum_n[slot] = keep_n[keep, y] + yr_n[s]
        sum_f[slot] = keep_f[keep] + yr_f[s]

    def along(s, hop):
        slot = lax.rem(s, SUM_SLOTS)
        layer = layer_of(s)
        away = jnp.where(z < layer, z, jnp.where(z > layer, last - z, jnp.maximum(z, last - z)))

        @pl.when(away == hop)
        def _():
            @pl.when((z > 0) & (z <= layer))
            def _():
                up_copy(s).wait_recv()
                sum_n[slot] = sum_n[slot] + up_n[s]

            @pl.when((z < last) & (z >= layer))
            def _():
                down_copy(s).wait_recv()
                sum_n[slot] = sum_n[slot] + down_n[s]

            @pl.when(z < layer)
            def _():
                up_copy(s).start()

            @pl.when(z > layer)
            def _():
                down_copy(s).start()

            @pl.when(z == layer)
            def _():
                out_ref[rows_of(s)] = sum_n[slot]
                piece = s // 2
                whole, cut = BLOCK_ROWS // ROWS_N, BLOCK_ROWS % ROWS_N

                @pl.when(piece <= whole)
                def _():
                    add_squares(sum_n[slot, pl.ds(0, cut)])

                @pl.when(piece < whole)
                def _():
                    add_squares(sum_n[slot, pl.ds(cut, ROWS_N - cut)])

        @pl.when(jnp.where(z == 0, last, last - z) == hop)
        def _():
            @pl.when(z < last)
            def _():
                down_copy_e(s).wait_recv()
                sum_f[slot, 0] = sum_f[slot, 0] + down_e[s]

            @pl.when(z > 0)
            def _():
                down_copy_e(s).start()

            @pl.when(z == 0)
            def _():
                out_ref[rows_f(s)] = sum_f[slot, 0]
                add_squares(sum_f[slot, 0])

        @pl.when(z == hop)
        def _():
            @pl.when(z > 0)
            def _():
                up_copy_f(s).wait_recv()
                sum_f[slot, 1] = sum_f[slot, 1] + up_f[s]

            @pl.when(z < last)
            def _():
                up_copy_f(s).start()

            @pl.when(z == last)
            def _():
                out_ref[rows_f(s)] = sum_f[slot, 1]
                add_squares(sum_f[slot, 1])

    def guarded(run, s):
        @pl.when((s >= 0) & (s < PIECES))
        def _():
            run(s)

    def step(t, carry):
        guarded(first, t)
        guarded(second, t - LAG)
        guarded(third, t - 2 * LAG)
        for hop in range(LAYERS):
            guarded(functools.partial(along, hop=hop), t - 2 * LAG - hop * HOP_LAG)
        return carry

    lax.fori_loop(0, PIECES + 2 * LAG + (LAYERS - 1) * HOP_LAG, step, 0)

    def drain_sends(i, carry):
        s = PIECES - SEND_SLOTS + i
        for copy in (x_copy(s), y_copy_f(s), y_copy(s)):
            copy.wait_send()
        return carry

    lax.fori_loop(0, SEND_SLOTS, drain_sends, 0)

    def drain_sums(i, carry):
        s = PIECES - SUM_SLOTS + i

        @pl.when(z != layer_of(s))
        def _():
            up_copy(s).wait_send()

        @pl.when(z > 0)
        def _():
            down_copy_e(s).wait_send()

        @pl.when(z < last)
        def _():
            up_copy_f(s).wait_send()

        return carry

    lax.fori_loop(0, SUM_SLOTS, drain_sums, 0)

    def drain_core(s, carry):
        for copy in core_copies(s):
            copy.wait_send()
        return carry

    lax.fori_loop(0, PIECES, drain_core, 0)

    @pl.when((z == 0) | (z == last))
    def _():
        out_ref[pl.ds(BLOCK_ROWS, AUX_ROWS)] = jnp.zeros((AUX_ROWS, BS), jnp.float32)


def reduce_to_owners(rest, first, final):
    def room(*shape):
        return pltpu.VMEM(shape + (BS,), jnp.float32)

    def sems(*shape):
        return pltpu.SemaphoreType.DMA(shape)

    return pl.pallas_call(
        reduce_kernel,
        out_shape=(
            jax.ShapeDtypeStruct((CHUNK, BS), jnp.float32),
            jax.ShapeDtypeStruct((8, BS), jnp.float32),
        ),
        in_specs=[pl.BlockSpec(memory_space=pltpu.HBM)] * 3,
        out_specs=(pl.BlockSpec(memory_space=pltpu.VMEM),) * 2,
        scratch_shapes=[
            room(3, 2, 2, ROWS_N),
            room(3, 2, 2, ROWS_F),
            room(CORE_SLOTS, 2, 2, ROWS_N),
            room(CORE_SLOTS, 2, 2, ROWS_F),
            room(KEEP, 2, ROWS_N),
            room(KEEP, 2, ROWS_F),
            room(SEND_SLOTS, 2, ROWS_N),
            room(SEND_SLOTS, ROWS_N),
            room(SEND_SLOTS, 2, ROWS_F),
            room(PIECES, 2, ROWS_N),
            room(PIECES, ROWS_N),
            room(PIECES, 2, ROWS_F),
            room(SUM_SLOTS, ROWS_N),
            room(SUM_SLOTS, 2, ROWS_F),
            room(PIECES, ROWS_N),
            room(PIECES, ROWS_N),
            room(PIECES, ROWS_F),
            room(PIECES, ROWS_F),
            sems(3, 3),
            sems(PIECES, 3),
            sems(CORE_SLOTS, 3),
            pltpu.SemaphoreType.REGULAR,
            sems(SEND_SLOTS),
            sems(SEND_SLOTS),
            sems(SEND_SLOTS),
            sems(PIECES),
            sems(PIECES),
            sems(PIECES),
            sems(SUM_SLOTS),
            sems(SUM_SLOTS, 2),
            sems(PIECES),
            sems(PIECES),
            sems(PIECES),
            sems(PIECES),
        ],
        compiler_params=pltpu.CompilerParams(
            collective_id=1, has_side_effects=True, vmem_limit_bytes=58 * MIB
        ),
        cost_estimate=pl.CostEstimate(flops=0, bytes_accessed=100 * MIB, transcendentals=0),
        name="reduce_to_owners",
    )(rest, first, final)


MATRICES = [
    (96, 6, 9, 3, True),
    (150, 3, 6, 3, False),
    (168, 6, 12, 3, True),
    (240, 12, 6, 4, False),
    (312, 9, 8, 3, False),
]
LOADS = 4


def unblock_kernel(plan, kinds, blocks_ref, *refs):
    outs, tiles = refs[:kinds], refs[kinds : 2 * kinds]
    loaded, load_sem, store_sem = refs[2 * kinds :]

    def load(i):
        kind, m, first, rows, per_row, row, col = plan[i]
        number = rows * per_row
        return pltpu.make_async_copy(
            blocks_ref.at[m, pl.ds(first, number)],
            loaded.at[i % LOADS, pl.ds(0, number)],
            load_sem.at[i % LOADS],
        )

    def store(i, slot):
        kind, m, first, rows, per_row, row, col = plan[i]
        return pltpu.make_async_copy(
            tiles[kind].at[slot],
            outs[kind].at[pl.ds(row, rows * BS), pl.ds(col, per_row * BS)],
            store_sem.at[kind, slot],
        )

    history = [[] for _ in range(kinds)]
    for i in range(min(LOADS - 1, len(plan))):
        load(i).start()
    for i, (kind, m, first, rows, per_row, row, col) in enumerate(plan):
        if i + LOADS - 1 < len(plan):
            load(i + LOADS - 1).start()
        load(i).wait()
        slot = len(history[kind]) % 2
        if len(history[kind]) >= 2:
            store(*history[kind][-2]).wait()
        for r in range(rows):
            for c in range(per_row):
                tiles[kind][slot, r * BS : (r + 1) * BS, c * BS : (c + 1) * BS] = loaded[
                    i % LOADS, r * per_row + c
                ]
        history[kind].append((i, slot))
        store(i, slot).start()
    for done in history:
        for entry in done[-2:]:
            store(*entry).wait()


def unblock(gathered):
    plan, shapes, tiles = [], [], []
    for kind, (first, rows, per_row, step, beside) in enumerate(MATRICES):
        tall, wide = rows * BS, per_row * BS
        shapes.append((tall, MP * wide) if beside else (MP * tall, wide))
        tiles.append((step * BS, wide))
        for m in range(MP):
            for at in range(0, rows, step):
                row = at * BS + (0 if beside else m * tall)
                plan.append((kind, m, first + at * per_row, step, per_row, row, m * wide if beside else 0))
    anywhere = pl.BlockSpec(memory_space=pl.ANY)
    largest = max(entry[3] * entry[4] for entry in plan)
    return pl.pallas_call(
        functools.partial(unblock_kernel, plan, len(shapes)),
        out_shape=tuple(jax.ShapeDtypeStruct(shape, jnp.bfloat16) for shape in shapes),
        in_specs=[anywhere],
        out_specs=tuple([anywhere] * len(shapes)),
        scratch_shapes=[pltpu.VMEM((2,) + tile, jnp.bfloat16) for tile in tiles]
        + [
            pltpu.VMEM((LOADS, largest, BS, BS), jnp.bfloat16),
            pltpu.SemaphoreType.DMA((LOADS,)),
            pltpu.SemaphoreType.DMA((len(shapes), 2)),
        ],
        compiler_params=pltpu.CompilerParams(vmem_limit_bytes=60 * MIB),
        cost_estimate=pl.CostEstimate(
            flops=0, bytes_accessed=38 * MIB, transcendentals=0
        ),
        name="unblock",
    )(gathered)


def embed_kernel(which_ref, rows_ref, blocks_ref, out_ref, matrix_ref):
    step = pl.program_id(0)
    for r in range(4):
        for c in range(6):
            matrix_ref[r * BS : (r + 1) * BS, c * BS : (c + 1) * BS] = blocks_ref[0, r * 6 + c]
    product = dot_nn(rows_ref[...], matrix_ref[...])

    @pl.when(step == 0)
    def _():
        out_ref[...] = product

    @pl.when(step > 0)
    def _():
        out_ref[...] += product


def embed_other(patches, gathered):
    part = lax.axis_index("mp")
    tall = 4 * BS
    return pl.pallas_call(
        embed_kernel,
        grid_spec=pltpu.PrefetchScalarGridSpec(
            num_scalar_prefetch=1,
            grid=(PV // MP // tall,),
            in_specs=[
                pl.BlockSpec((NTOK, tall), lambda k, which: (which[0], k)),
                pl.BlockSpec((1, 24, BS, BS), lambda k, which: (which[1], k, 0, 0)),
            ],
            out_specs=(
                pl.BlockSpec((NTOK, D), lambda k, which: (0, 0)),
                pl.BlockSpec((tall, D), lambda k, which: (k, 0)),
            ),
        ),
        out_shape=(
            jax.ShapeDtypeStruct((NTOK, D), jnp.float32),
            jax.ShapeDtypeStruct((PV // MP, D), jnp.bfloat16),
        ),
        compiler_params=pltpu.CompilerParams(vmem_limit_bytes=56 * MIB),
        cost_estimate=pl.CostEstimate(
            flops=2 * NTOK * D * PV // MP, bytes_accessed=10 * MIB, transcendentals=0
        ),
        name="embed_other",
    )(jnp.stack([1 - part, part]).astype(jnp.int32), patches, gathered)


def labels_kernel(labels_ref, out_ref):
    side = 2 * GS
    plane = side * side
    rows = jnp.concatenate([labels_ref[:, z * plane : (z + 1) * plane] for z in range(side)], 0)
    cell = lax.broadcasted_iota(jnp.int32, (plane, plane), 0)
    place = lax.broadcasted_iota(jnp.int32, (plane, plane), 1)
    parity, patch = place // (GS * GS), place % (GS * GS)
    match = (cell // side == 2 * (patch // GS) + parity // 2) & (
        cell % side == 2 * (patch % GS) + parity % 2
    )
    low = rows.astype(jnp.float32).astype(jnp.bfloat16)
    moved = dot_nn(low, match.astype(jnp.float32).astype(jnp.bfloat16)).astype(jnp.int32)
    width = GS * GS
    for i in range(2):
        for inner in range(4):
            for a in range(GS):
                out_ref[i * 4 + inner : i * 4 + inner + 1, a * width : (a + 1) * width] = moved[
                    2 * a + i : 2 * a + i + 1, inner * width : (inner + 1) * width
                ]


def arrange_labels(labels):
    return pl.pallas_call(
        labels_kernel,
        out_shape=jax.ShapeDtypeStruct((8, NTOK), jnp.int32),
        in_specs=whole_specs(1),
        out_specs=whole_specs(1)[0],
        cost_estimate=pl.CostEstimate(flops=2 * 16 * 256 * 256, bytes_accessed=65536, transcendentals=0),
        name="arrange_labels",
    )(labels)


def blocks_kernel(first_block, per_row, step_rows, transposed, pairs, *refs):
    out_ref, tiles, sems = refs[-3:]
    m, i = pl.program_id(0), pl.program_id(1)
    steps = pl.num_programs(1)
    at = m * steps + i
    slot = lax.rem(at, 2)
    total = pl.num_programs(0) * steps

    def drain(which):
        pltpu.make_async_copy(tiles.at[which], tiles.at[which], sems.at[which]).wait()

    @pl.when(at >= 2)
    def _():
        drain(slot)

    total_product = None
    for pair in range(pairs):
        x_ref, g_ref = refs[2 * pair], refs[2 * pair + 1]
        term = dot(x_ref[...], g_ref[...], ((0,), (1,) if transposed else (0,)))
        total_product = term if total_product is None else total_product + term
    tiles[slot] = total_product
    for r in range(step_rows):
        for c in range(per_row):
            block = first_block + (i * step_rows + r) * per_row + c
            chunk, at_row = block // 24, lax.rem(block, 24) * BS
            pltpu.make_async_copy(
                tiles.at[slot, r * BS : (r + 1) * BS, c * BS : (c + 1) * BS],
                out_ref.at[m, chunk, pl.ds(pl.multiple_of(at_row, BS), BS)],
                sems.at[slot],
            ).start()

    @pl.when(at == total - 1)
    def _():
        drain(slot)

        @pl.when(total > 1)
        def _():
            drain(1 - slot)


def grad_blocks(xs, gs, parts, rows, per_row, step_rows, first_block, split_x, split_g, buffer, name, chunks, depth, transposed=False, x_stride=None):
    steps = rows // step_rows
    x_stride = x_stride or steps
    tokens = xs[0].shape[0]
    width = per_row * BS
    x_spec = pl.BlockSpec(
        (tokens, step_rows * BS), (lambda m, i: (0, m * x_stride + i)) if split_x else (lambda m, i: (0, i))
    )
    if transposed:
        g_spec = pl.BlockSpec((width, tokens), lambda m, i: (0, 0))
    else:
        g_spec = pl.BlockSpec((tokens, width), (lambda m, i: (0, m)) if split_g else (lambda m, i: (0, 0)))
    anywhere = pl.BlockSpec(memory_space=pltpu.HBM)
    operands = [array for pair in zip(xs, gs) for array in pair] + ([] if buffer is None else [buffer])
    return pl.pallas_call(
        functools.partial(
            blocks_kernel, first_block, per_row, step_rows, transposed, len(xs)
        ),
        grid=(parts, steps),
        out_shape=jax.ShapeDtypeStruct((parts, chunks, depth, BS), jnp.float32),
        in_specs=[x_spec, g_spec] * len(xs) + ([] if buffer is None else [anywhere]),
        out_specs=anywhere,
        input_output_aliases={} if buffer is None else {2 * len(xs): 0},
        scratch_shapes=[
            pltpu.VMEM((2, step_rows * BS, width), jnp.float32),
            pltpu.SemaphoreType.DMA((2,)),
        ],
        compiler_params=pltpu.CompilerParams(vmem_limit_bytes=32 * MIB),
        cost_estimate=pl.CostEstimate(
            flops=2 * len(xs) * tokens * parts * rows * BS * width,
            bytes_accessed=parts * rows * BS * width * 4,
            transcendentals=0,
        ),
        name=name,
    )(*operands)


def fast_mesh():
    return lax.axis_size("dp") == 4 * LAYERS and lax.axis_size("mp") == MP


def gather_weights(blocks):
    low = blocks.astype(jnp.bfloat16)[0, 0]
    if fast_mesh():
        gathered = gather_all(low.reshape(-1, BS), THIRDS, 1, True, (), 2, "gather_weights")
    else:
        gathered = lax.all_gather(low, ("dp", "mp"), axis=0, tiled=False)
        gathered = gathered.reshape((-1, MP) + low.shape).swapaxes(0, 1)
    return gathered.reshape(MP, -1, BS, BS)


def swap_mp(values):
    return lax.ppermute(values, "mp", [(0, 1), (1, 0)])


def reduce_plain(rest, first, final):
    part = lax.axis_index("mp")
    own = (jnp.arange(MP) == part).astype(jnp.float32)
    ends = [piece.reshape(1, -1, BS, BS) * own[:, None, None, None] for piece in (first, final)]
    dp = lax.axis_size("dp")
    every = jnp.concatenate([ends[0], rest, ends[1]], 1)
    every = every.reshape(MP, dp, -1, BS, BS).transpose(1, 0, 2, 3, 4)
    return lax.psum_scatter(
        every.reshape(dp * MP, -1, BS, BS), ("dp", "mp"), scatter_dimension=0, tiled=True
    )[0]


TALL = NTOK + 16
TILES = D // BS
CONV_AT = TILES * TALL
HEAD_AT = CONV_AT + 27 * CF
SMALL_AT = HEAD_AT + CF
DECONV_AT = SMALL_AT + CF
PACKED = DECONV_AT + DEC
AUX_ROOM = 8 * MP * AUX_ROWS
FLAT_ROWS = -(-NAUX // (8 * BS)) * 8


def pack_kernel(zero_ref, *refs):
    vectors, up_ref, conv_ref, head_ref, small_ref, deconv_ref = refs[:8], *refs[8:13]
    out_ref, rows_ref, sems = refs[14:]
    for j in range(TILES):
        lanes_at = slice(j * BS, (j + 1) * BS)
        base = j * TALL
        rows_ref[base : base + NTOK] = zero_ref[:, lanes_at]
        small_rows = [vector[:, lanes_at] for vector in vectors]
        small_rows += [up_ref[:, i * D + j * BS : i * D + (j + 1) * BS] for i in range(FF // D)]
        small_rows += [jnp.zeros((16 - len(small_rows), BS), jnp.float32)]
        rows_ref[base + NTOK : base + TALL] = jnp.concatenate(small_rows, 0)
    lane = lax.broadcasted_iota(jnp.int32, (CF, BS), 1)
    wide_lane = lax.broadcasted_iota(jnp.int32, (DEC, BS), 1)
    rows_ref[CONV_AT:HEAD_AT] = conv_ref[...]
    rows_ref[HEAD_AT:SMALL_AT] = head_ref[...]
    rows_ref[SMALL_AT:DECONV_AT] = jnp.where(lane < 2, small_ref[...], 0.0)
    rows_ref[DECONV_AT:PACKED] = jnp.where(wide_lane < 1, deconv_ref[...], 0.0)
    rows_ref[PACKED:AUX_ROOM] = jnp.zeros((AUX_ROOM - PACKED, BS), jnp.float32)
    copies = [
        pltpu.make_async_copy(
            rows_ref.at[pl.ds((m * 8 + chunk) * AUX_ROWS, AUX_ROWS)],
            out_ref.at[m, chunk, pl.ds(BLOCK_ROWS, AUX_ROWS)],
            sems.at[m * 8 + chunk],
        )
        for m in range(MP)
        for chunk in range(8)
    ]
    for copy in copies:
        copy.start()
    for copy in copies:
        copy.wait()


def pack_aux(zero, vectors, up_bias, conv, head, small, deconv, buffer):
    whole = pl.BlockSpec(memory_space=pltpu.VMEM)
    anywhere = pl.BlockSpec(memory_space=pl.ANY)
    operands = [zero] + [vector.reshape(1, D) for vector in vectors]
    operands += [up_bias.reshape(1, FF), conv, head, small, deconv]
    return pl.pallas_call(
        pack_kernel,
        out_shape=jax.ShapeDtypeStruct(buffer.shape, jnp.float32),
        in_specs=[whole] * len(operands) + [anywhere],
        out_specs=anywhere,
        input_output_aliases={len(operands): 0},
        scratch_shapes=[
            pltpu.VMEM((AUX_ROOM, BS), jnp.float32),
            pltpu.SemaphoreType.DMA((8 * MP,)),
        ],
        compiler_params=pltpu.CompilerParams(vmem_limit_bytes=32 * MIB),
        cost_estimate=pl.CostEstimate(flops=0, bytes_accessed=4 * MIB, transcendentals=0),
        name="pack_aux",
    )(*operands, buffer)


def unpack_kernel(sums_ref, rows_ref, norm_ref, turned):
    def pieces(start, stop):
        at = start
        while at < stop:
            m, chunk = at // (8 * AUX_ROWS), at // AUX_ROWS % 8
            end = min(stop, (at // AUX_ROWS + 1) * AUX_ROWS)
            first = at % AUX_ROWS
            yield at - start, sums_ref[m, 4 + chunk, first : first + end - at]
            at = end

    def packed(start, stop):
        found = [piece for _, piece in pieces(start, stop)]
        return found[0] if len(found) == 1 else jnp.concatenate(found, 0)

    square = jnp.zeros((8, BS), jnp.float32)
    for m in range(MP):
        for owner in range(4 * LAYERS):
            square += sums_ref[m, owner, AUX_ROWS:]
    rows_ref[FLAT_ROWS - 16 :] = jnp.zeros((16, BS), jnp.float32)
    after = NTOK * TILES
    for j in range(TILES):
        token_sum = jnp.zeros((1, BS), jnp.float32)
        for offset, piece in pieces(j * TALL, j * TALL + NTOK):
            rows_ref[pl.ds(offset * TILES + j, piece.shape[0], stride=TILES)] = piece
            token_sum += jnp.sum(piece, 0, keepdims=True)
            square += jnp.sum((piece * piece).reshape(-1, 8, BS), 0)
        vectors = packed(j * TALL + NTOK, (j + 1) * TALL)
        square += jnp.sum((vectors * vectors).reshape(-1, 8, BS), 0)
        square += jnp.concatenate([token_sum * token_sum, jnp.zeros((7, BS), jnp.float32)], 0)
        rows_ref[after + j : after + j + 1] = token_sum
        order = list(range(7)) + list(range(8, 8 + FF // D)) + [7]
        for place, which in enumerate(order):
            at = after + TILES * (1 + place) + j
            rows_ref[at : at + 1] = vectors[which : which + 1]
    at = after + TILES * 13
    deconv = packed(DECONV_AT, PACKED)
    square += jnp.sum((deconv * deconv).reshape(-1, 8, BS), 0)
    rows_ref[at : at + 1] = deconv.T[0:1]
    at += 1
    for o in range(27):
        conv = packed(CONV_AT + o * CF, CONV_AT + (o + 1) * CF)
        square += jnp.sum((conv * conv).reshape(-1, 8, BS), 0)
        turned[:, 0:CF] = conv.T
        for f in range(8):
            rows_ref[at + o * CF : at + (o + 1) * CF, f * CF : (f + 1) * CF] = turned[
                pl.ds(f, CF, stride=8), 0:CF
            ]
    at += 27 * CF
    head = packed(HEAD_AT, SMALL_AT)
    small = packed(SMALL_AT, DECONV_AT)
    square += jnp.sum((head * head + small * small).reshape(-1, 8, BS), 0)
    turned_small = small.T
    segments = [(turned_small[1:2], CF)]
    segments += [(head[row : row + 1], NCLS) for row in range(CF)]
    segments += [(turned_small[0:1], NCLS)]
    lane = 0
    for values, length in segments:
        taken = 0
        while taken < length:
            row, col = lane // BS, lane % BS
            part = min(length - taken, BS - col)
            rows_ref[at + row : at + row + 1, col : col + part] = values[:, taken : taken + part]
            taken += part
            lane += part
    norm = jnp.sqrt(jnp.sum(jnp.sum(square, 0, keepdims=True), 1, keepdims=True))
    clip = clip_value / jnp.maximum(norm, clip_value)
    lanes_of = lax.broadcasted_iota(jnp.int32, (8, BS), 1)
    norm_ref[...] = jnp.where(lanes_of == 0, norm, clip)


def unpack_aux(gathered):
    whole = pl.BlockSpec(memory_space=pltpu.VMEM)
    return pl.pallas_call(
        unpack_kernel,
        out_shape=(
            jax.ShapeDtypeStruct((FLAT_ROWS, BS), jnp.float32),
            jax.ShapeDtypeStruct((8, BS), jnp.float32),
        ),
        in_specs=[whole],
        out_specs=(whole, whole),
        scratch_shapes=[pltpu.VMEM((BS, BS), jnp.float32)],
        compiler_params=pltpu.CompilerParams(vmem_limit_bytes=32 * MIB),
        cost_estimate=pl.CostEstimate(flops=0, bytes_accessed=7 * MIB, transcendentals=0),
        name="unpack_aux",
    )(gathered)


def greet_all(devices):
    me = lax.axis_index("dp") * MP + lax.axis_index("mp")
    barrier = pltpu.get_barrier_semaphore()

    def greet(k, carry):
        peer = lax.rem(me + k, devices)
        place = (peer // MP, lax.rem(peer, MP))
        pl.semaphore_signal(barrier, inc=1, device_id=place, device_id_type=MESH)
        return carry

    lax.fori_loop(1, devices, greet, 0)


def sum_over_all(devices, in_ref, out_ref, slots, send_sem, recv_sem):
    me = lax.axis_index("dp") * MP + lax.axis_index("mp")

    def copy(k, slot):
        peer = lax.rem(me + k, devices)
        place = (peer // MP, lax.rem(peer, MP))
        return remote(in_ref, slots.at[slot], send_sem.at[k], recv_sem.at[slot], place)

    slots[me] = in_ref[...]
    pl.semaphore_wait(pltpu.get_barrier_semaphore(), devices - 1)

    def push(k, carry):
        copy(k, me).start()
        return carry

    def pull(k, carry):
        copy(k, lax.rem(me + devices - k, devices)).wait_recv()
        return carry

    def settle(k, carry):
        copy(k, me).wait_send()
        return carry

    lax.fori_loop(1, devices, push, 0)
    lax.fori_loop(1, devices, pull, 0)
    total = slots[0]
    for i in range(1, devices):
        total = total + slots[i]
    out_ref[...] = total
    lax.fori_loop(1, devices, settle, 0)


def decoder_kernel(
    all_crops,
    devices,
    up_ref,
    deconv_bias_ref,
    conv_ref,
    conv_bias_ref,
    head_ref,
    head_bias_ref,
    labels_ref,
    batch_ref,
    conv_t_ref,
    head_t_ref,
    gu_ref,
    conv_grad_ref,
    head_grad_ref,
    small_ref,
    deconv_grad_ref,
    conv_in,
    grid_slope,
    conv_slope,
    features,
    chance,
    sums,
    conved,
    spread,
    total,
    slots,
    send_sem,
    recv_sem,
):
    greet_all(devices)
    decoder_forward_kernel(
        up_ref,
        deconv_bias_ref,
        conv_ref,
        conv_bias_ref,
        head_ref,
        head_bias_ref,
        labels_ref,
        batch_ref,
        conv_in,
        grid_slope,
        conv_slope,
        features,
        chance,
        sums,
        conved,
    )
    sum_over_all(devices, sums, total, slots, send_sem, recv_sem)
    decoder_backward_kernel(
        all_crops,
        total,
        batch_ref,
        labels_ref,
        chance,
        features,
        conv_slope,
        grid_slope,
        conv_in,
        conv_t_ref,
        head_t_ref,
        gu_ref,
        conv_grad_ref,
        head_grad_ref,
        small_ref,
        deconv_grad_ref,
        spread,
    )


def decoder(all_crops, *operands):
    devices = 4 * LAYERS * MP
    shapes = (
        jax.ShapeDtypeStruct((8 * DEC, NTOK), jnp.bfloat16),
        jax.ShapeDtypeStruct((27 * CF, DEC), jnp.float32),
        jax.ShapeDtypeStruct((CF, CF), jnp.float32),
        jax.ShapeDtypeStruct((CF, BS), jnp.float32),
        jax.ShapeDtypeStruct((DEC, BS), jnp.float32),
    )
    return pl.pallas_call(
        functools.partial(decoder_kernel, all_crops, devices),
        out_shape=shapes,
        in_specs=whole_specs(10),
        out_specs=tuple(whole_specs(5)),
        scratch_shapes=[
            pltpu.VMEM((DEC, CELLS), jnp.bfloat16),
            pltpu.VMEM((DEC, CELLS), jnp.float32),
            pltpu.VMEM((CF, CELLS), jnp.float32),
            pltpu.VMEM((CF, CELLS), jnp.bfloat16),
            pltpu.VMEM((CF, CELLS), jnp.float32),
            pltpu.VMEM((CF, BS), jnp.float32),
            pltpu.VMEM((CF, CELLS), jnp.float32),
            pltpu.VMEM((27 * CF, CELLS), jnp.bfloat16),
            pltpu.VMEM((CF, BS), jnp.float32),
            pltpu.VMEM((devices, CF, BS), jnp.float32),
            pltpu.SemaphoreType.DMA((devices,)),
            pltpu.SemaphoreType.DMA((devices,)),
        ],
        compiler_params=pltpu.CompilerParams(
            collective_id=3, has_side_effects=True, vmem_limit_bytes=40 * MIB
        ),
        cost_estimate=pl.CostEstimate(
            flops=6 * 27 * CF * DEC * CELLS, bytes_accessed=6 * MIB, transcendentals=DEC * CELLS
        ),
        name="decoder",
    )(*operands)


def layer_norm(values):
    center = values - jnp.mean(values, -1, keepdims=True)
    spread = jnp.mean(center * center, -1, keepdims=True)
    inverse = lax.rsqrt(spread + 1e-06)
    return center * inverse, inverse


def layer_norm_back(back, normal, inverse, gain):
    scaled = back * gain
    mean = jnp.mean(scaled, -1, keepdims=True)
    along = jnp.mean(scaled * normal, -1, keepdims=True)
    return inverse * (scaled - mean - normal * along)


def shampoo_kernel(per_step, clip_ref, g_ref, b_ref, s_ref, r_ref, m_ref, v_ref, nb_ref, ns_ref, nm_ref, nv_ref):
    def exact(a, b, dims):
        return lax.dot_general(
            a, b, (dims, ((), ())), precision=HIGHEST, preferred_element_type=jnp.float32
        )

    def mean_square(values):
        total = jnp.sum(jnp.sum(values * values, 0, keepdims=True), 1, keepdims=True)
        return total * (1.0 / (BS * BS))

    for i in range(per_step):
        grads = g_ref[i * BS : (i + 1) * BS] * clip_ref[0, 0]
        ns_ref[0, i] = beta_stat * s_ref[0, i] + (1 - beta_stat) * exact(grads, grads, ((1,), (1,)))
        ns_ref[1, i] = beta_stat * s_ref[1, i] + (1 - beta_stat) * exact(grads, grads, ((0,), (0,)))
        moment = beta_one * m_ref[i] + (1 - beta_one) * grads
        velocity = beta_two * v_ref[i] + (1 - beta_two) * grads * grads
        nm_ref[i] = moment
        nv_ref[i] = velocity
        hat = moment / (1 - beta_one**STEP)
        adam = hat / (jnp.sqrt(velocity / (1 - beta_two**STEP)) + 1e-08)
        left = exact(r_ref[0, i], hat, ((1,), (0,)))
        precond = exact(left, r_ref[1, i], ((1,), (0,)))
        ratio = jnp.sqrt((mean_square(adam) + 1e-06) / (mean_square(precond) + 1e-06))
        blocks = b_ref[i]
        nb_ref[i] = blocks - learn_rate * (precond * ratio + decay_rate * blocks)


def shampoo_step(clip, owned, blocks, stat_pair, root_pair, moment, velocity):
    number = blocks.shape[0]
    per_step = 3 if number % 4 else 4
    one = pl.BlockSpec((per_step, BS, BS), lambda i: (i, 0, 0))
    pair = pl.BlockSpec((2, per_step, BS, BS), lambda i: (0, i, 0, 0))
    single = jax.ShapeDtypeStruct((number, BS, BS), jnp.float32)
    return pl.pallas_call(
        functools.partial(shampoo_kernel, per_step),
        grid=(number // per_step,),
        out_shape=(single, jax.ShapeDtypeStruct((2, number, BS, BS), jnp.float32), single, single),
        in_specs=[
            pl.BlockSpec(memory_space=pltpu.SMEM),
            pl.BlockSpec((per_step * BS, BS), lambda i: (i, 0)),
            one,
            pair,
            pair,
            one,
            one,
        ],
        out_specs=(one, pair, one, one),
        compiler_params=pltpu.CompilerParams(vmem_limit_bytes=60 * MIB),
        cost_estimate=pl.CostEstimate(
            flops=number * 8 * BS**3 * 6, bytes_accessed=number * 12 * BS * BS * 4, transcendentals=0
        ),
        name="shampoo",
    )(clip.reshape(1, 1), owned, blocks, stat_pair, root_pair, moment, velocity)


def adam_step(param, grads, moment, veloc):
    moment_new = beta_one * moment + (1 - beta_one) * grads
    veloc_new = beta_two * veloc + (1 - beta_two) * grads * grads
    direction = (
        moment_new / (1 - beta_one**STEP) / (jnp.sqrt(veloc_new / (1 - beta_two**STEP)) + 1e-08)
    )
    return (param - learn_rate * direction, moment_new, veloc_new)


def halves(matrix):
    return matrix[:, :HALF], matrix[:, HALF:]


def local(
    patches,
    labels,
    batch_ids,
    blocks,
    statistics,
    roots,
    moments,
    velocity,
    aux,
    aux_moment,
    aux_velocity,
):
    part = lax.axis_index("mp")
    all_crops = lax.axis_size("dp") * MP
    pieces = split_aux(aux)
    gain, shift = pieces["norm_gain"], pieces["norm_bias"]

    gathered = gather_weights(blocks)
    other_embedding, w_embed = embed_other(patches, gathered)
    w_qkv, w_proj, w_up, w_down, w_deconv = unblock(gathered)

    def columns(array, which, width, start):
        return lax.dynamic_slice_in_dim(array, which * width + start, width - start, 1)

    down_start = 2 * FF // MP // 3

    other_rows = lax.dynamic_slice_in_dim(patches, (1 - part) * NTOK, NTOK, 0)
    own_rows = lax.dynamic_slice_in_dim(patches, part * NTOK, NTOK, 0)
    received = swap_mp(other_embedding)
    stream_zero = (
        dot_nn(own_rows, w_embed) + received + pieces["positions"] + pieces["embed_bias"]
    )
    normal_one, inverse_one = layer_norm(stream_zero)
    normed_one = (normal_one * gain[0] + shift[0]).astype(jnp.bfloat16)
    q_bias, v_bias = pieces["qv_bias"][0], pieces["qv_bias"][1]
    nothing = jnp.zeros((HALF,), jnp.float32)
    qkv_bias = jnp.concatenate(
        [q_bias[:HALF], nothing, v_bias[:HALF], q_bias[HALF:], nothing, v_bias[HALF:]]
    )
    qkv = (dot_nn(normed_one, w_qkv) + qkv_bias).astype(jnp.bfloat16)
    zero_stream = stream_zero.astype(jnp.bfloat16)
    zero_half = swap_mp(columns(zero_stream, 1 - part, HALF, 0))
    mixed, lse = attention_forward(qkv)
    mixed, zero_half = lax.optimization_barrier((mixed, zero_half))
    stream_one = stream_zero + dot_nn(mixed, w_proj) + pieces["proj_bias"]
    one_stream = stream_one.astype(jnp.bfloat16)
    one_half = swap_mp(columns(one_stream, 1 - part, HALF, 0))
    normal_two, inverse_two = layer_norm(stream_one)
    normed_two = (normal_two * gain[1] + shift[1]).astype(jnp.bfloat16)
    hidden = dot_nn(normed_two, w_up) + pieces["up_bias"]
    active_value, hidden_slope = gelu_and_slope(hidden)
    active = active_value.astype(jnp.bfloat16)
    active, one_half = lax.optimization_barrier((active, one_half))
    active_other = swap_mp(columns(active, 1 - part, FF // MP, down_start))
    stream_two = stream_one + dot_nn(active, w_down) + pieces["down_bias"]
    streams = [zero_stream, one_stream, stream_two.astype(jnp.bfloat16)]
    stacked = jnp.concatenate([halves(s)[m] for m in range(MP) for s in streams], 1)
    up_t = dot(w_deconv, stacked, ((0,), (1,)))

    conv_weight = pieces["conv_weight"].astype(jnp.bfloat16).reshape(27, DEC, CF)
    conv_low = conv_weight.transpose(0, 2, 1).reshape(27 * CF, DEC)
    conv_t = conv_weight.transpose(1, 0, 2).reshape(DEC, 27 * CF)
    head_weight = jnp.pad(pieces["head_weight"], ((0, 0), (0, CF - NCLS))).astype(jnp.bfloat16)
    head_bias = jnp.pad(pieces["head_bias"], (0, CF - NCLS)).reshape(CF, 1)
    grid_labels = arrange_labels(labels)
    batch = jnp.broadcast_to(batch_ids.reshape(1, 1), (1, BS))
    operands = (
        up_t,
        pieces["deconv_bias"].reshape(DEC, 1),
        conv_low,
        pieces["conv_bias"].reshape(CF, 1),
        head_weight.T,
        head_bias,
        grid_labels,
        batch,
    )
    if fast_mesh():
        gu_t, conv_grad, head_grad, small, deconv_bias_grad = decoder(
            all_crops, *operands, conv_t, head_weight
        )
    else:
        conv_in, grid_slope, conv_slope, features, chance, sums = decoder_forward(*operands)
        gu_t, conv_grad, head_grad, small, deconv_bias_grad = decoder_backward(
            all_crops,
            lax.psum(sums, ("dp", "mp")),
            batch,
            grid_labels,
            chance,
            features,
            conv_slope,
            grid_slope,
            conv_in,
            conv_t,
            head_weight,
        )
    gu_t, two_stream, active_other = lax.optimization_barrier((gu_t, streams[2], active_other))
    two_half = swap_mp(columns(two_stream, 1 - part, HALF, 0))
    loss_value = small[0, 2]

    gu_other = swap_mp(gu_t)
    stacked_back = dot(gu_t, w_deconv, ((0,), (1,)))
    back_zero_s, back_one_s, back_two = [
        jnp.concatenate([stacked_back[:, (3 * m + s) * HALF : (3 * m + s + 1) * HALF] for m in range(MP)], 1)
        for s in range(3)
    ]
    grad_down_bias = jnp.sum(back_two, 0)
    two_low = back_two.astype(jnp.bfloat16)
    two_other = swap_mp(two_low)
    back_hidden = (hidden_slope * dot_nt(two_low, w_down)).astype(jnp.bfloat16)
    grad_up_bias = jnp.sum(back_hidden.astype(jnp.float32), 0)
    back_normed_two = dot_nt(back_hidden, w_up)
    grad_gain_two = jnp.sum(back_normed_two * normal_two, 0)
    grad_shift_two = jnp.sum(back_normed_two, 0)
    back_one = (
        back_two + back_one_s + layer_norm_back(back_normed_two, normal_two, inverse_two, gain[1])
    )
    grad_proj_bias = jnp.sum(back_one, 0)
    one_low = back_one.astype(jnp.bfloat16)
    back_mixed = dot_nt(one_low, w_proj).astype(jnp.bfloat16)
    back_q, back_k, back_v = attention_backward(qkv, back_mixed, lse)
    back_qkv = jnp.concatenate(
        [halves(piece)[m] for m in range(MP) for piece in (back_q, back_k, back_v)], 1
    )
    grad_query_bias = jnp.sum(back_q.astype(jnp.float32), 0)
    grad_value_bias = jnp.sum(back_v.astype(jnp.float32), 0)
    back_normed_one = dot_nt(back_qkv, w_qkv)
    grad_gain_one = jnp.sum(back_normed_one * normal_one, 0)
    grad_shift_one = jnp.sum(back_normed_one, 0)
    back_normed_one, two_half, gu_other, two_other = lax.optimization_barrier(
        (back_normed_one, two_half, gu_other, two_other)
    )
    back_zero = (
        back_one + back_zero_s + layer_norm_back(back_normed_one, normal_one, inverse_one, gain[0])
    )
    zero_low = back_zero.astype(jnp.bfloat16)
    other_low = swap_mp(zero_low)

    fast = fast_mesh()
    depth = CHUNK if fast else BLOCK_ROWS
    stacked_own = jnp.concatenate([columns(stream, part, HALF, 0) for stream in streams], 1)
    stacked_other = jnp.concatenate([zero_half, one_half, two_half], 1)
    active_own = columns(active, part, FF // MP, down_start)
    final_grads = grad_blocks(
        [stacked_own, stacked_other], [gu_t, gu_other], 1, 9, 8, 3, 24, True, False, None, "grad_deconv", 4, BLOCK_ROWS, True
    )
    final_grads = grad_blocks(
        [active_own, active_other], [two_low, two_other], 1, 4, 6, 4, 0, True, False, final_grads, "grad_down_last", 4, BLOCK_ROWS
    )
    rest_grads = None
    for name, x, g, rows, per_row, step_rows, start, split_x, split_g, stride in (
        ("grad_down", active, two_low, 8, 6, 4, 144, True, False, 3),
        ("grad_up", normed_two, back_hidden, 6, 12, 3, 72, False, True, None),
        ("grad_proj", mixed, one_low, 3, 6, 3, 54, True, False, None),
        ("grad_qkv", normed_one, back_qkv, 6, 9, 3, 0, False, True, None),
    ):
        rest_grads = grad_blocks(
            [x], [g], MP, rows, per_row, step_rows, start, split_x, split_g, rest_grads, name, 8, depth,
            x_stride=stride,
        )
    first_grads = grad_blocks(
        [own_rows, other_rows], [zero_low, other_low], 1, 16, 6, 4, 0, False, False, None, "grad_embed", 4, BLOCK_ROWS
    )
    vectors = [
        grad_gain_one,
        grad_gain_two,
        grad_shift_one,
        grad_shift_two,
        grad_query_bias,
        grad_value_bias,
        grad_proj_bias,
        grad_down_bias,
    ]
    if fast:
        head_wide = jnp.pad(head_grad, ((0, 0), (0, BS - CF)))
        rest_grads = pack_aux(
            back_zero, vectors, grad_up_bias, conv_grad, head_wide, small, deconv_bias_grad, rest_grads
        )
        owned, squares = reduce_to_owners(
            rest_grads.reshape(MP, 2, 2, 2, CHUNK, BS),
            first_grads.reshape(2, 2, BLOCK_ROWS, BS),
            final_grads.reshape(2, 2, BLOCK_ROWS, BS),
        )
        gathered_aux = gather_all(
            jnp.concatenate([owned[BLOCK_ROWS:], squares]),
            ((0, AUX_ROWS), (AUX_ROWS, 8)),
            1,
            False,
            (0,),
            4,
            "gather_aux",
        )
        in_rows, norm_clip = unpack_aux(gathered_aux)
        aux_total = in_rows.reshape(-1)[:NAUX]
        grad_norm, clip_scale = norm_clip[0, 0], norm_clip[0, 1]
    else:
        owned = reduce_plain(rest_grads.reshape(MP, -1, BS, BS), first_grads, final_grads)
        owned = owned.reshape(-1, BS)
        positions_sum, small_sum = lax.psum(
            (
                back_zero,
                jnp.concatenate(
                    vectors[:7]
                    + [
                        grad_up_bias,
                        grad_down_bias,
                        deconv_bias_grad[:, 0],
                        conv_grad.reshape(27, CF, DEC).transpose(0, 2, 1).reshape(-1),
                        small[:, 1],
                        head_grad[:, :NCLS].reshape(-1),
                        small[:NCLS, 0],
                    ]
                ),
            ),
            ("dp", "mp"),
        )
        aux_total = jnp.concatenate(
            [positions_sum.reshape(-1), jnp.sum(positions_sum, 0), small_sum]
        )
        block_square = lax.psum(jnp.sum(owned * owned), ("dp", "mp"))
        grad_norm = jnp.sqrt(block_square + jnp.sum(aux_total * aux_total))
        clip_scale = clip_value / jnp.maximum(grad_norm, clip_value)
    block_new, stat_new, moment_new, veloc_new = shampoo_step(
        clip_scale,
        owned,
        blocks[0, 0],
        statistics[:, 0, 0],
        roots[:, 0, 0],
        moments[0, 0],
        velocity[0, 0],
    )
    aux_new, aux_moment_new, aux_veloc_new = adam_step(
        aux, aux_total * clip_scale, aux_moment, aux_velocity
    )
    return (
        loss_value,
        grad_norm,
        block_new[None, None],
        stat_new[:, None, None],
        moment_new[None, None],
        veloc_new[None, None],
        aux_new,
        aux_moment_new,
        aux_veloc_new,
    )


def solution(mesh):
    block_spec = P("dp", "mp", None, None, None)
    pair_spec = P(None, "dp", "mp", None, None, None)
    placed = (
        P("dp", "mp"),
        P(("dp", "mp"), None),
        P(("dp", "mp")),
        block_spec,
        pair_spec,
        pair_spec,
        block_spec,
        block_spec,
        P(),
        P(),
        P(),
    )
    return jax.shard_map(
        local,
        mesh=mesh,
        in_specs=placed,
        out_specs=(P(), P(), block_spec, pair_spec, block_spec, block_spec, P(), P(), P()),
        check_vma=False,
    )
```
